256 devices in a mesh: tm: 32 (over z, x), chan: 8 (over y, core).
Axes of the slice: x: 4, y: 4, z: 8, core: 2. Of those that a mesh axis runs over, the one named last changes fastest.
Arguments:
- spectra: bfloat16 [16384, 8192], P('tm', 'chan'), may hold values from -6 to 6
- chan_weight: float32 [8192], P('chan'), may hold values from 0.25 to 4
- routes: int32 [1024, 1], P('tm'), may hold values from 0 to 31; in each aligned block of 32 rows (0 to 31, 32 to 63, ...) at most 2 rows name the same one
- offsets: int32 [16384], P('tm'), may hold values from 0 to 64
- kernel: bfloat16 [16], replicated, may hold values from 0.19921875 to 1
- gal_pix: int32 [256], replicated, may hold values from 0 to 2047
- gal_chan: int32 [256], replicated, may hold values from 64 to 8127, as said below
Outputs:
- sky_map: bfloat16 [2048, 8192], P('tm', 'chan')
- stacked: float32 [128], replicated
The draws below stay inside these ranges and needn't reach their ends.
Inputs may be any that keep to these rules, and one draw needn't show every extreme that they name: `routes`: among the 32 blocks of one index of tm no tile is named more than 2 times; every tile is named by some block. `gal_chan`: channel of each galaxy's line centre.
All inputs are finite; a program needn't handle non-finite values.
Results may differ from the reference program's by a relative error of at most 0.012.
Values may be sent and summed in bfloat16 or wider, within the bound.
A program may use at most 64 MiB of HBM per device.

```python
import math
import jax
import jax.numpy as jnp
import numpy as np
from jax import lax

CH = 8192
KMODES = 8
BLK = 16
BLOCKS_DEV = 32
TP = 64
MARGIN = 8
KW = 16
SW = 64
NGAL = 256
CAP = 2
SAMPLES = 16384
BLOCKS = 1024
NPIX = 2048
N_TM = 32
N_CHAN = 8


def draw_gal_chan(key, part):
    key = jax.random.fold_in(key, 7)
    key_depth, key_free = jax.random.split(key)
    galaxy = jnp.arange(NGAL, dtype=jnp.int32)
    pair = galaxy // 2
    side = galaxy % 2
    spread = pair % 8 == 7
    edge_count = pair - pair // 8
    boundary = 1 + edge_count % (N_CHAN - 1)
    block_width = CH // N_CHAN
    depth = jax.random.randint(key_depth, (NGAL,), 0, SW, dtype=jnp.int32)
    near_edge = jnp.where(side == 0, boundary * block_width + depth, boundary * block_width - 1 - depth)
    anywhere = jax.random.randint(key_free, (NGAL,), SW, CH - SW, dtype=jnp.int32)
    return jnp.where(spread, anywhere, near_edge).astype(jnp.int32)


def set_ends(drawn, own_key, low, high):
    longest = drawn.shape.index(max(drawn.shape))
    spots = []
    for shift in (0, 1):
        where = [jax.random.randint(jax.random.fold_in(own_key, axis), (), 0, length) for axis, length in enumerate(drawn.shape)]
        where[longest] = (where[longest] + shift) % drawn.shape[longest]
        spots.append(tuple(where))
    return drawn.at[spots[0]].set(low).at[spots[1]].set(high)


def level_of(key, shape, shards, smallest, top_value):
    gain, own = 1.0, jax.random.fold_in(key, 6)
    for position, shards_of in shards:
        draws = jnp.exp(jax.random.uniform(jax.random.fold_in(own, position), (shards_of,), jnp.float32, smallest / len(shards), top_value / len(shards)))
        gain = gain * jnp.repeat(draws, shape[position] // shards_of).reshape([-1 if axis == position else 1 for axis in range(len(shape))])
    return gain


def routed_block(key, own, number, rows, number_of, top, limit, slope):
    ranking = jax.random.permutation(key, number_of)
    packed, common = load_shares(number_of, rows * top, limit, slope, True), load_shares(number_of, rows * top, limit, slope, False)
    places = jnp.arange(number_of)

    def named(tallies, offset_by):
        used = int((tallies > 0).sum())
        fixed = max(1, used // 4)
        moved = fixed + (places - fixed + offset_by * (used - fixed)) % max(1, number_of - fixed)
        return jnp.zeros((number_of,), jnp.int32).at[ranking[jnp.where(places < fixed, places, moved)]].set(jnp.asarray(tallies, jnp.int32))

    tallies = jnp.where(number % 4 == 0, named(packed, number // 4), named(common, number - number // 4 - 1))
    mixed = jax.random.permutation(jax.random.fold_in(own, 3), number_of)
    donor, sink = mixed[0:number_of // 2 * 2:2], mixed[1:number_of // 2 * 2:2]
    margin = jnp.minimum(tallies[donor] - 1, limit - tallies[sink]) // 2
    margin = jnp.where((donor == ranking[0]) | (sink == ranking[0]) | (tallies[sink] == 0), 0, jnp.maximum(margin, 0))
    moved = jax.random.randint(jax.random.fold_in(own, 4), (number_of // 2,), 0, 1 << 20) % (margin + 1)
    tallies = tallies.at[donor].add(-moved).at[sink].add(moved)
    members = jnp.searchsorted(jnp.cumsum(tallies), jnp.arange(rows * top), side="right").astype(jnp.int32)
    table = members.reshape(top, rows).T
    table = table[jax.random.permutation(jax.random.fold_in(own, 1), rows)]
    offset_by = jax.random.randint(jax.random.fold_in(own, 2), (rows, 1), 0, top)
    return jnp.take_along_axis(table, (jnp.arange(top)[None, :] + offset_by) % top, axis=1)


def load_shares(count, total, limit, lean, full):
    weights = [(1 << 20) // math.isqrt(grade ** lean) + 1 for grade in range(1, count + 1)]
    largest = limit if full else min(limit, max(-(-total // count), total * weights[0] // sum(weights)))
    least = 1 if total - largest >= count - 1 else 0
    given, surplus = [largest] + [least] * (count - 1), total - largest - least * (count - 1)
    while surplus > 0:
        free = [i for i in range(1, count) if given[i] < largest] or [i for i in range(1, count) if given[i] < limit]
        pool, remaining = sum([weights[i] for i in free]), surplus
        for i in free:
            more = min(limit - given[i], max(1, remaining * weights[i] // pool), surplus)
            given[i] = given[i] + more
            surplus = surplus - more
    return np.array(given)


def normal_values(own_key, shape, deviation, limit, shards=(), kind=jnp.bfloat16):
    gain = level_of(own_key, shape, shards, -0.22, 0.18) if shards else 1.0
    entries = jax.random.normal(own_key, shape, jnp.float32) * deviation * gain
    return jnp.minimum(jnp.maximum(entries, -limit), limit).astype(kind)


def setup_inputs(seed: int = 0) -> dict:
    arg_keys = jax.random.split(jax.random.key(seed), 8)
    spectra = normal_values(arg_keys[0], (SAMPLES, CH), 1.0, 6.0, ((0, 32), (1, 8)))
    chan_weight = jnp.clip(jnp.exp(math.log(4.0) - 2.7725887 * jax.random.uniform(arg_keys[1], (CH,), jnp.float32) ** level_of(arg_keys[1], (CH,), ((0, 8),), -0.2, 0.2)), 0.25, 4.0)
    routes_keys = jax.random.split(jax.random.fold_in(arg_keys[2], 1), BLOCKS // BLOCKS_DEV)
    routes_turns = jax.random.permutation(jax.random.fold_in(arg_keys[2], 3), BLOCKS // BLOCKS_DEV)
    routes = jax.vmap(lambda own, number: routed_block(jax.random.fold_in(arg_keys[2], 2), own, number, BLOCKS_DEV, N_TM, 1, CAP, 2))(routes_keys, routes_turns).reshape((BLOCKS, 1))
    offsets = set_ends(jax.random.randint(arg_keys[3], (SAMPLES,), 0, TP + 2 * MARGIN - KW + 1), jax.random.fold_in(arg_keys[3], 1), 0, TP + 2 * MARGIN - KW).astype(jnp.int32)
    kernel = jnp.clip(jax.random.uniform(arg_keys[4], (KW,), jnp.float32, 0.19921875, 1.0), 0.19921875, 1.0).astype(jnp.bfloat16)
    gal_pix = set_ends(jax.random.randint(arg_keys[5], (NGAL,), 0, NPIX), jax.random.fold_in(arg_keys[5], 1), 0, NPIX - 1).astype(jnp.int32)
    gal_chan = draw_gal_chan(jax.random.fold_in(arg_keys[7], 71), 0)
    return dict(spectra=spectra, chan_weight=chan_weight, routes=routes, offsets=offsets, kernel=kernel, gal_pix=gal_pix, gal_chan=gal_chan)


two_pi = 6.283185307179586
highest = lax.Precision.HIGHEST

def basis_columns(chan_index, total):
    orders = jnp.arange(1, KMODES + 1, dtype=jnp.int32)
    phase = (chan_index[:, None] * orders[None, :] % total).astype(jnp.float32) * (two_pi / total)
    return jnp.concatenate([jnp.cos(phase), jnp.sin(phase)], axis=1)

def solve_modes(gram, proj):
    lower = jnp.linalg.cholesky(gram)
    middle = lax.linalg.triangular_solve(lower, proj, left_side=False, lower=True, transpose_a=True)
    return lax.linalg.triangular_solve(lower, middle, left_side=False, lower=True, transpose_a=False)

def band_matrix(row_offsets, kernel, width):
    columns = jnp.arange(width, dtype=jnp.int32)
    relative = columns[None, :] - row_offsets[:, None]
    taps = kernel.shape[0]
    inside = (relative >= 0) & (relative < taps)
    looked = jnp.take(kernel, jnp.clip(relative, 0, taps - 1).astype(jnp.int32))
    return jnp.where(inside, looked, jnp.zeros((), kernel.dtype)).astype(jnp.bfloat16)

def reference(spectra, chan_weight, routes, offsets, kernel, gal_pix, gal_chan):
    rows_dev = BLOCKS_DEV * BLK
    extent = TP + 2 * MARGIN
    basis = basis_columns(jnp.arange(CH, dtype=jnp.int32), CH)
    gram = jnp.dot(basis.T * chan_weight[None, :], basis, precision=highest)
    dest_all = routes[:, 0]

    def one_source(source, tiles_sum):
        start = (source * rows_dev).astype(jnp.int32)
        values = lax.dynamic_slice_in_dim(spectra, start, rows_dev, 0).astype(jnp.float32)
        proj = jnp.dot(values * chan_weight[None, :], basis, precision=highest)
        coef = solve_modes(gram, proj)
        cleaned = (values - jnp.dot(coef, basis.T, precision=highest)).astype(jnp.bfloat16)
        row_offsets = lax.dynamic_slice_in_dim(offsets, start, rows_dev, 0)
        dests = lax.dynamic_slice_in_dim(dest_all, (source * BLOCKS_DEV).astype(jnp.int32), BLOCKS_DEV, 0)
        local = jnp.zeros((N_TM, extent, CH), jnp.float32)
        for block in range(BLOCKS_DEV):
            band = band_matrix(row_offsets[block * BLK:(block + 1) * BLK], kernel, extent)
            part = jnp.dot(band.T.astype(jnp.float32), cleaned[block * BLK:(block + 1) * BLK].astype(jnp.float32), preferred_element_type=jnp.float32)
            where = dests[block].astype(jnp.int32)
            current = lax.dynamic_slice_in_dim(local, where, 1, 0)
            local = lax.dynamic_update_slice_in_dim(local, current + part[None], where, 0)
        rounded = lax.optimization_barrier(local.astype(jnp.bfloat16))
        return tiles_sum + rounded.astype(jnp.float32)
    tiles_sum = lax.fori_loop(0, N_TM, one_source, jnp.zeros((N_TM, extent, CH), jnp.float32))
    core = tiles_sum[:, MARGIN:MARGIN + TP]
    left_rim = tiles_sum[:, :MARGIN]
    right_rim = tiles_sum[:, TP + MARGIN:]
    core = core.at[:-1, TP - MARGIN:].add(left_rim[1:])
    core = core.at[1:, :MARGIN].add(right_rim[:-1])
    sky_map = core.reshape(NPIX, CH).astype(jnp.bfloat16)
    picked = sky_map[gal_pix].astype(jnp.float32)
    index = gal_chan[:, None] - SW + jnp.arange(2 * SW, dtype=jnp.int32)[None, :]
    windows = jnp.take_along_axis(picked, index, axis=1)
    stacked = jnp.sum(windows, axis=0) / gal_pix.shape[0]
    return (sky_map, stacked)
```

```python
import jax
import jax.numpy as jnp
from jax import lax
from jax.experimental import pallas as pl
from jax.experimental.pallas import tpu as pltpu
from jax.sharding import PartitionSpec as P

KMODES = 8
MODES = 2 * KMODES
TP = 64
MARGIN = 8
SW = 64
TAPS = 16
NX = 4

two_pi = 6.283185307179586
highest = lax.Precision.HIGHEST
MESH = pl.DeviceIdType.MESH
f32 = jnp.float32
bf16 = jnp.bfloat16


def basis_rows(chan_index, total):
    orders = jnp.arange(1, KMODES + 1, dtype=jnp.int32)
    phase = (orders[:, None] * chan_index[None, :] % total).astype(f32) * (two_pi / total)
    return jnp.concatenate([jnp.cos(phase), jnp.sin(phase)], axis=0)


def split3(value):
    high = value.astype(bf16)
    rest = value - high.astype(f32)
    mid = rest.astype(bf16)
    low = (rest - mid.astype(f32)).astype(bf16)
    return high, mid, low


def iota(shape, dim):
    return lax.broadcasted_iota(jnp.int32, shape, dim)


def make_kernel(tm_size, chan_size, rows, width, nblocks, ngal):
    nz = tm_size // NX
    quarter = width // NX
    npix = tm_size * TP
    zpix = NX * TP
    half = zpix // 2
    block_rows = rows // nblocks
    shifts = quarter + 2 * SW

    def kernel(
        spec, weight, routes, offsets, taps, gal_pix, gal_chan, basis,
        sky, stacked,
        own, pix, raw, gram, proj, ext, coef, band, clean, part, counts,
        zsend, zrecv, final, st1, st2, st3,
        own_sem, pix_s, pix_r, raw_s, raw_r, gram_s, gram_r, proj_s, proj_r, coef_s, coef_r,
        z_s, z_r, fin_s, fin_r, st1_s, st1_r, st2_s, st2_r, st3_s, st3_r,
    ):
        tm = lax.axis_index("tm")
        j = lax.axis_index("chan")
        z = lax.div(tm, NX)
        x = lax.rem(tm, NX)

        def x_peer(r):
            return (z * NX + lax.rem(x + r, NX), j)

        def c_peer(r):
            return (tm, lax.rem(j + r, chan_size))

        def z_peer(r):
            return (lax.rem(z + r, nz) * NX + x, j)

        peers = (
            [x_peer(r) for r in range(1, NX)]
            + [c_peer(r) for r in range(1, chan_size)]
            + [z_peer(r) for r in range(1, nz)]
        )
        barrier = pltpu.get_barrier_semaphore()
        for peer in peers:
            pl.semaphore_signal(barrier, inc=1, device_id=peer, device_id_type=MESH)

        def remote(src, dst, send_sem, recv_sem, peer):
            return pltpu.make_async_remote_copy(
                src_ref=src, dst_ref=dst, send_sem=send_sem, recv_sem=recv_sem,
                device_id=peer, device_id_type=MESH,
            )

        load = pltpu.make_async_copy(spec, own, own_sem)
        load.start()

        inside = iota((nblocks, rows), 1) - block_rows * iota((nblocks, rows), 0)
        owner = (inside >= 0) & (inside < block_rows)
        tile = jnp.sum(jnp.where(owner, routes[...], 0), axis=0, keepdims=True)
        pix[0] = tile * TP + offsets[...] - MARGIN

        weighted = basis[...] * weight[...]
        gram[0] = jnp.zeros((MODES, 128), f32)
        gram[0, :, 0:MODES] = lax.dot_general(
            weighted, basis[...], (((1,), (1,)), ((), ())), precision=highest,
            preferred_element_type=f32,
        )
        w_stack = jnp.concatenate(split3(weighted), axis=0)
        ext[...] = jnp.zeros(ext.shape, f32)

        pl.semaphore_wait(barrier, len(peers))

        sends = []

        def start(copy):
            copy.start()
            sends.append(copy)

        for r in range(1, NX):
            start(remote(pix.at[0], pix.at[NX - r], pix_s.at[r], pix_r.at[NX - r], x_peer(r)))
        for r in (2, 1, 3):
            column = pl.multiple_of(lax.rem(x + r, NX) * quarter, quarter)
            start(remote(
                spec.at[:, pl.ds(column, quarter)], raw.at[NX - r], raw_s.at[r], raw_r.at[NX - r],
                x_peer(r),
            ))
        for r in range(1, chan_size):
            start(remote(
                gram.at[0], gram.at[chan_size - r], gram_s.at[r], gram_r.at[chan_size - r],
                c_peer(r),
            ))

        load.wait()
        products = lax.dot_general(
            w_stack, own[...], (((1,), (1,)), ((), ())), preferred_element_type=f32
        )
        proj[0] = products[:MODES] + products[MODES:2 * MODES] + products[2 * MODES:]
        for r in range(1, chan_size):
            start(remote(
                proj.at[0], proj.at[chan_size - r], proj_s.at[r], proj_r.at[chan_size - r],
                c_peer(r),
            ))

        def build_band(slot):
            first = pix[slot]
            group = jnp.broadcast_to(first >> 4, (TAPS, rows))
            inner = jnp.broadcast_to(first & (TAPS - 1), (TAPS, rows))
            lane = iota((TAPS, rows), 0)
            turn = (lane - inner) & (TAPS - 1)
            tap = jnp.zeros((TAPS, rows), f32)
            values = taps[...].astype(f32)
            for m in range(TAPS):
                tap = jnp.where(turn == m, values[0:1, m:m + 1], tap)
            where = jnp.where(lane < inner, group + 1, group)

            def step(a, carry):
                row = pl.multiple_of(a * TAPS, TAPS)
                band[pl.ds(row, TAPS), slot * rows:(slot + 1) * rows] = jnp.where(
                    where == a, tap, 0.0
                ).astype(bf16)
                return carry

            lax.fori_loop(0, npix // TAPS, step, 0, unroll=4)

        build_band(0)

        for r in range(1, chan_size):
            remote(gram.at[0], gram.at[r], gram_s.at[r], gram_r.at[r], c_peer(r)).wait_recv()
        total = gram[0]
        for r in range(1, chan_size):
            total = total + gram[r]
        row_id = iota((MODES, 128), 0)
        both = jnp.where(iota((MODES, 128), 1) - MODES == row_id, 1.0, total)
        for i in range(MODES):
            pivot = both[i:i + 1, :] / both[i:i + 1, i:i + 1]
            both = jnp.where(row_id == i, pivot, both - both[:, i:i + 1] * pivot)

        for r in range(1, chan_size):
            remote(proj.at[0], proj.at[r], proj_s.at[r], proj_r.at[r], c_peer(r)).wait_recv()
        full = proj[0]
        for r in range(1, chan_size):
            full = full + proj[r]
        ext[MODES:2 * MODES, :] = full
        coef[0] = jnp.dot(both, ext[...], precision=highest, preferred_element_type=f32)
        for r in range(1, NX):
            start(remote(coef.at[0], coef.at[NX - r], coef_s.at[r], coef_r.at[NX - r], x_peer(r)))

        for r in range(1, NX):
            remote(pix.at[0], pix.at[r], pix_s.at[r], pix_r.at[r], x_peer(r)).wait_recv()
            build_band(r)

        begin = gal_chan[...] - SW - (j * width + x * quarter)
        shift_hot = (iota((shifts, ngal), 0) == quarter - 1 - begin).astype(f32).astype(bf16)
        pixel_hot = (iota((npix, ngal), 0) == gal_pix[...]).astype(f32).astype(bf16)
        counts[...] = lax.dot_general(
            shift_hot, pixel_hot, (((1,), (1,)), ((), ())), preferred_element_type=f32
        ).astype(bf16)

        here = pl.multiple_of(x * quarter, quarter)
        b_high, b_mid, b_low = split3(basis[:, pl.ds(here, quarter)])
        b_stack = jnp.concatenate(
            [b_high, b_mid, b_high, b_mid, b_low, b_high, jnp.zeros((2 * MODES, quarter), bf16)],
            axis=0,
        )

        def clean_slot(slot, values):
            c_high, c_mid, c_low = split3(coef[slot])
            c_stack = jnp.concatenate(
                [c_high, c_high, c_mid, c_mid, c_high, c_low, jnp.zeros((2 * MODES, rows), bf16)],
                axis=0,
            )
            ripple = lax.dot_general(
                c_stack, b_stack, (((0,), (0,)), ((), ())), preferred_element_type=f32
            )
            clean[slot * rows:(slot + 1) * rows, :] = (values.astype(f32) - ripple).astype(bf16)

        clean_slot(0, own[:, pl.ds(here, quarter)])
        for r in (1, 3, 2):
            remote(coef.at[0], coef.at[r], coef_s.at[r], coef_r.at[r], x_peer(r)).wait_recv()
            remote(
                spec.at[:, pl.ds(0, quarter)], raw.at[r], raw_s.at[r], raw_r.at[r], x_peer(r)
            ).wait_recv()
            clean_slot(r, raw[r])

        def chunk_row(step):
            return pl.multiple_of(lax.rem(z + step + 2 * nz, nz) * zpix, zpix)

        def grid_chunk(step):
            row = chunk_row(step)
            part[pl.ds(row, zpix), :] = jnp.dot(
                band[pl.ds(row, zpix), :], clean[...], preferred_element_type=f32
            )

        def part_half(step, which):
            row = pl.multiple_of(chunk_row(step) + which * half, half)
            return part[pl.ds(row, half), :]

        far = nz // 2

        def z_copy(way, index):
            return remote(
                zsend.at[way, index], zrecv.at[way, index], z_s.at[way, index],
                z_r.at[way, index], z_peer((1, nz - 1)[way]),
            )

        def z_start(way, index, value):
            zsend[way, index] = value.astype(bf16)
            start(z_copy(way, index))

        def z_take(way, index):
            z_copy(way, index).wait_recv()
            return zrecv[way, index].astype(f32)

        sign = (1, -1)
        grid_chunk(far)
        for way in range(2):
            z_start(way, 0, part_half(far, way))
        for way in range(2):
            grid_chunk(sign[way] * (far - 1))
            z_start(way, far, part_half(sign[way] * (far - 1), 1 - way))

        def grid_rest(i, carry):
            grid_chunk(i + (2 - far))
            return carry

        lax.fori_loop(0, nz - 3, grid_rest, 0)

        picked = jnp.dot(counts[...], part[...].astype(bf16), preferred_element_type=f32)
        wide = jnp.concatenate([picked, jnp.zeros((shifts, 512 - quarter), f32)], axis=1)
        folded = jnp.zeros((8, 512), f32)
        for i in range(shifts // 8):
            folded = folded + pltpu.roll(
                wide[8 * i:8 * i + 8], (513 - quarter + 8 * i) % 512, 1
            )
        window = jnp.zeros((1, 512), f32)
        for i in range(8):
            window = window + (pltpu.roll(folded[i:i + 1], i, 1) if i else folded[i:i + 1])
        st1[x] = window[:, :2 * SW]

        def share(buffer, me, send_sem, recv_sem, peer_of, count):
            for r in range(1, count):
                start(remote(buffer.at[me], buffer.at[me], send_sem.at[r], recv_sem.at[me], peer_of(r)))

        def gather(buffer, me, send_sem, recv_sem, peer_of, count):
            for r in range(1, count):
                other = lax.rem(me + r, count)
                remote(
                    buffer.at[other], buffer.at[other], send_sem.at[r], recv_sem.at[other], peer_of(r)
                ).wait_recv()
            value = buffer[0]
            for i in range(1, count):
                value = value + buffer[i]
            return value

        share(st1, x, st1_s, st1_r, x_peer, NX)

        def long_step(k):
            for way in range(2):
                got = z_take(way, k)
                z_start(way, k + 1, got + part_half(sign[way] * (far - 1 - k), way))

        def short_step(k):
            for way in range(2):
                got = z_take(way, far + k)
                z_start(way, far + k + 1, got + part_half(sign[way] * (far - 2 - k), 1 - way))

        long_step(0)
        st2[j] = gather(st1, x, st1_s, st1_r, x_peer, NX)
        share(st2, j, st2_s, st2_r, c_peer, chan_size)
        short_step(0)
        long_step(1)
        st3[z] = gather(st2, j, st2_s, st2_r, c_peer, chan_size)
        share(st3, z, st3_s, st3_r, z_peer, nz)
        short_step(1)
        long_step(2)
        stacked[...] = gather(st3, z, st3_s, st3_r, z_peer, nz) / ngal

        got = [z_take(way, 2 * far - 2) for way in range(2)]
        for way in range(2):
            value = z_take(way, far - 1) + got[1 - way] + part_half(0, way)
            final[way * half:(way + 1) * half, :] = value.astype(bf16)

        place = sky.at[:, pl.ds(here, quarter)]
        for r in (2, 1, 3):
            row = pl.multiple_of(lax.rem(x + r, NX) * TP, TP)
            start(remote(
                final.at[pl.ds(row, TP), :], place, fin_s.at[r], fin_r.at[NX - r], x_peer(r)
            ))
        sky[:, pl.ds(here, quarter)] = final[pl.ds(pl.multiple_of(x * TP, TP), TP), :]
        for r in range(1, NX):
            column = pl.multiple_of(lax.rem(x + r, NX) * quarter, quarter)
            remote(
                final.at[pl.ds(0, TP), :], sky.at[:, pl.ds(column, quarter)], fin_s.at[r],
                fin_r.at[r], x_peer(r),
            ).wait_recv()
        for copy in sends:
            copy.wait_send()

    dma = pltpu.SemaphoreType.DMA
    scratch = [
        pltpu.VMEM((rows, width), bf16),
        pltpu.VMEM((NX, 1, rows), jnp.int32),
        pltpu.VMEM((NX, rows, quarter), bf16),
        pltpu.VMEM((chan_size, MODES, 128), f32),
        pltpu.VMEM((chan_size, MODES, rows), f32),
        pltpu.VMEM((128, rows), f32),
        pltpu.VMEM((NX, MODES, rows), f32),
        pltpu.VMEM((npix, NX * rows), bf16),
        pltpu.VMEM((NX * rows, quarter), bf16),
        pltpu.VMEM((npix, quarter), f32),
        pltpu.VMEM((shifts, npix), bf16),
        pltpu.VMEM((2, nz - 1, half, quarter), bf16),
        pltpu.VMEM((2, nz - 1, half, quarter), bf16),
        pltpu.VMEM((zpix, quarter), bf16),
        pltpu.VMEM((NX, 1, 2 * SW), f32),
        pltpu.VMEM((chan_size, 1, 2 * SW), f32),
        pltpu.VMEM((nz, 1, 2 * SW), f32),
        dma,
    ]
    for count in (NX, NX, chan_size, chan_size, NX):
        scratch += [dma((count,)), dma((count,))]
    scratch += [dma((2, nz - 1)), dma((2, nz - 1))]
    for count in (NX, NX, chan_size, nz):
        scratch += [dma((count,)), dma((count,))]
    return kernel, scratch


def solution(mesh):
    tm_size, chan_size = mesh.shape["tm"], mesh.shape["chan"]

    def per_device(spectra, chan_weight, routes, offsets, taps, gal_pix, gal_chan):
        rows, width = spectra.shape
        chan_start = lax.axis_index("chan") * width
        basis = basis_rows(
            chan_start + jnp.arange(width, dtype=jnp.int32), width * chan_size
        )
        kernel, scratch = make_kernel(
            tm_size, chan_size, rows, width, routes.shape[0], gal_pix.shape[0]
        )
        vmem = pl.BlockSpec(memory_space=pltpu.VMEM)
        sky, stacked = pl.pallas_call(
            kernel,
            out_shape=(
                jax.ShapeDtypeStruct((TP, width), bf16),
                jax.ShapeDtypeStruct((1, 2 * SW), f32),
            ),
            in_specs=[pl.BlockSpec(memory_space=pl.ANY)] + [vmem] * 7,
            out_specs=(vmem, vmem),
            scratch_shapes=scratch,
            compiler_params=pltpu.CompilerParams(
                collective_id=0, has_side_effects=True, vmem_limit_bytes=48 * 1024 * 1024
            ),
        )(
            spectra, chan_weight[None, :], routes, offsets[None, :], taps[None, :],
            gal_pix[None, :], gal_chan[None, :], basis,
        )
        return sky, stacked[0]

    in_specs = (
        P("tm", "chan"), P("chan"), P("tm", None), P("tm"), P(None), P(None), P(None)
    )
    return jax.shard_map(
        per_device, mesh=mesh, in_specs=in_specs, out_specs=(P("tm", "chan"), P(None)),
        check_vma=False,
    )
```

```python
import jax
import jax.numpy as jnp
import numpy as np
from jax import lax
from jax.experimental import pallas as pl
from jax.experimental.pallas import tpu as pltpu
from jax.sharding import PartitionSpec as P

KMODES = 8
MODES = 2 * KMODES
TP = 64
MARGIN = 8
SW = 64
TAPS = 16
NX = 4
SUBS = 2

highest = lax.Precision.HIGHEST
MESH = pl.DeviceIdType.MESH
f32 = jnp.float32
bf16 = jnp.bfloat16


def basis_table(total):
    orders = np.arange(1, KMODES + 1)[:, None]
    phase = (orders * np.arange(total)[None, :] % total) * (2 * np.pi / total)
    return np.concatenate([np.cos(phase), np.sin(phase)], axis=0).astype(np.float32)


def split3(value):
    high = value.astype(bf16)
    rest = value - high.astype(f32)
    mid = rest.astype(bf16)
    low = (rest - mid.astype(f32)).astype(bf16)
    return high, mid, low


def iota(shape, dim):
    return lax.broadcasted_iota(jnp.int32, shape, dim)


def make_kernel(tm_size, chan_size, rows, width, nblocks, ngal):
    nz = tm_size // NX
    quarter = width // NX
    sub = quarter // SUBS
    npix = tm_size * TP
    zpix = NX * TP
    half = zpix // 2
    block_rows = rows // nblocks
    shifts = quarter + 2 * SW
    far = nz // 2

    def kernel(
        spec, weight_in, routes_in, offsets_in, taps_in, gal_pix_in, gal_chan_in, basis_in,
        sky, stacked,
        own, weight, routes, offsets, taps, gal_pix, gal_chan, basis,
        pix, raw, gram, proj, ext, coef, band, ripple, clean, part, pixel_hot, counts,
        zsend, zrecv, final, st1, st2, st3,
        load_sem, pix_s, pix_r, raw_s, raw_r, gram_s, gram_r, proj_s, proj_r, coef_s, coef_r,
        z_s, z_r, fin_s, fin_r, st1_s, st1_r, st2_s, st2_r, st3_s, st3_r,
    ):
        tm = lax.axis_index("tm")
        j = lax.axis_index("chan")
        z = lax.div(tm, NX)
        x = lax.rem(tm, NX)
        here = pl.multiple_of(x * quarter, quarter)

        def x_peer(r):
            return (z * NX + lax.rem(x + r, NX), j)

        def c_peer(r):
            return (tm, lax.rem(j + r, chan_size))

        def z_peer(r):
            return (lax.rem(z + r, nz) * NX + x, j)

        def remote(src, dst, send_sem, recv_sem, peer):
            return pltpu.make_async_remote_copy(
                src_ref=src, dst_ref=dst, send_sem=send_sem, recv_sem=recv_sem,
                device_id=peer, device_id_type=MESH,
            )

        sends = []

        def start(copy):
            copy.start()
            sends.append(copy)

        peers = (
            [x_peer(r) for r in range(1, NX)]
            + [c_peer(r) for r in range(1, chan_size)]
            + [z_peer(r) for r in range(1, nz)]
        )
        barrier = pltpu.get_barrier_semaphore()
        for peer in peers:
            pl.semaphore_signal(barrier, inc=1, device_id=peer, device_id_type=MESH)
        basis_here = basis_in.at[:, pl.ds(pl.multiple_of(j * width, width), width)]
        loads = [
            pltpu.make_async_copy(source, target, load_sem.at[i])
            for i, (source, target) in enumerate((
                (weight_in, weight), (basis_here, basis), (spec, own), (routes_in, routes),
                (offsets_in, offsets), (taps_in, taps), (gal_pix_in, gal_pix),
                (gal_chan_in, gal_chan),
            ))
        ]
        for load in loads:
            load.start()
        pl.semaphore_wait(barrier, len(peers))

        def raw_copy(s, r):
            column = pl.multiple_of(lax.rem(x + r, NX) * quarter + s * sub, sub)
            return remote(
                spec.at[:, pl.ds(column, sub)], raw.at[s, NX - r], raw_s.at[s, r],
                raw_r.at[s, NX - r], x_peer(r),
            )

        for r in (2, 1, 3):
            start(raw_copy(0, r))

        loads[0].wait()
        loads[1].wait()
        weighted = basis[...] * weight[...]
        gram[0] = jnp.zeros((MODES, 128), f32)
        gram[0, :, 0:MODES] = lax.dot_general(
            weighted, basis[...], (((1,), (1,)), ((), ())), precision=highest,
            preferred_element_type=f32,
        )
        for r in range(1, chan_size):
            start(remote(
                gram.at[0], gram.at[chan_size - r], gram_s.at[r], gram_r.at[chan_size - r],
                c_peer(r),
            ))
        w_stack = jnp.concatenate(split3(weighted), axis=0)
        loads[2].wait()
        products = lax.dot_general(
            w_stack, own[...], (((1,), (1,)), ((), ())), preferred_element_type=f32
        )
        proj[0] = products[:MODES] + products[MODES:2 * MODES] + products[2 * MODES:]
        for r in range(1, chan_size):
            start(remote(
                proj.at[0], proj.at[chan_size - r], proj_s.at[r], proj_r.at[chan_size - r],
                c_peer(r),
            ))

        for i in (3, 4, 5, 6, 7):
            loads[i].wait()
        inside = iota((nblocks, rows), 1) - block_rows * iota((nblocks, rows), 0)
        owner = ((inside >= 0) & (inside < block_rows)).astype(f32).astype(bf16)
        tile = jnp.dot(
            jnp.broadcast_to(routes[...], (16, nblocks)).astype(f32).astype(bf16), owner,
            preferred_element_type=f32,
        )[0:1].astype(jnp.int32)
        pix[0] = tile * TP + offsets[...] - MARGIN
        for r in range(1, NX):
            start(remote(pix.at[0], pix.at[NX - r], pix_s.at[r], pix_r.at[NX - r], x_peer(r)))

        def fill(target, column, group, tap):
            group = group.astype(f32).astype(bf16)
            tap = tap.astype(bf16)
            zero = jnp.zeros(tap.shape, bf16)

            def step(a, carry):
                row = pl.multiple_of(a * TAPS, TAPS)
                now = jnp.full(tap.shape, a.astype(f32), f32).astype(bf16)
                target[pl.ds(row, TAPS), column:column + tap.shape[1]] = jnp.where(
                    group == now, tap, zero
                )
                return carry

            lax.fori_loop(0, npix // TAPS, step, 0, unroll=4)

        def build_band(slot):
            first = pix[slot]
            group = jnp.broadcast_to(first >> 4, (TAPS, rows))
            inner = jnp.broadcast_to(first & (TAPS - 1), (TAPS, rows))
            lane = iota((TAPS, rows), 0)
            turn = (lane - inner) & (TAPS - 1)
            tap = jnp.zeros((TAPS, rows), f32)
            values = taps[...].astype(f32)
            for m in range(TAPS):
                tap = jnp.where(turn == m, values[0:1, m:m + 1], tap)
            fill(band, slot * rows, jnp.where(lane < inner, group + 1, group), tap)

        build_band(0)

        for r in range(1, chan_size):
            remote(gram.at[0], gram.at[r], gram_s.at[r], gram_r.at[r], c_peer(r)).wait_recv()
        total = gram[0]
        for r in range(1, chan_size):
            total = total + gram[r]
        row_id = iota((MODES, 128), 0)
        both = jnp.where(iota((MODES, 128), 1) - MODES == row_id, 1.0, total)
        for i in range(MODES):
            pivot = both[i:i + 1, :] / both[i:i + 1, i:i + 1]
            both = jnp.where(row_id == i, pivot, both - both[:, i:i + 1] * pivot)

        ext[...] = jnp.zeros(ext.shape, f32)
        for r in range(1, chan_size):
            remote(proj.at[0], proj.at[r], proj_s.at[r], proj_r.at[r], c_peer(r)).wait_recv()
        full = proj[0]
        for r in range(1, chan_size):
            full = full + proj[r]
        ext[MODES:2 * MODES, :] = full
        coef[0] = jnp.dot(both, ext[...], precision=highest, preferred_element_type=f32)
        for r in range(1, NX):
            start(remote(coef.at[0], coef.at[NX - r], coef_s.at[r], coef_r.at[NX - r], x_peer(r)))
        for s in range(1, SUBS):
            for r in (2, 1, 3):
                start(raw_copy(s, r))

        b_high, b_mid, b_low = split3(basis[:, pl.ds(here, quarter)])
        b_stack = jnp.concatenate(
            [b_high, b_mid, b_high, b_mid, b_low, b_high, jnp.zeros((2 * MODES, quarter), bf16)],
            axis=0,
        )

        def fit_slot(slot):
            c_high, c_mid, c_low = split3(coef[slot])
            c_stack = jnp.concatenate(
                [c_high, c_high, c_mid, c_mid, c_high, c_low, jnp.zeros((2 * MODES, rows), bf16)],
                axis=0,
            )
            ripple[slot * rows:(slot + 1) * rows, :] = lax.dot_general(
                c_stack, b_stack, (((0,), (0,)), ((), ())), preferred_element_type=f32
            )

        def clean_slot(s, slot, values):
            clean[s, slot * rows:(slot + 1) * rows, :] = (
                values.astype(f32)
                - ripple[slot * rows:(slot + 1) * rows, s * sub:(s + 1) * sub]
            ).astype(bf16)

        fit_slot(0)
        for s in range(SUBS):
            clean_slot(s, 0, own[:, pl.ds(pl.multiple_of(here + s * sub, sub), sub)])
        for r in range(1, NX):
            remote(pix.at[0], pix.at[r], pix_s.at[r], pix_r.at[r], x_peer(r)).wait_recv()
            build_band(r)
        for r in (1, 3, 2):
            remote(coef.at[0], coef.at[r], coef_s.at[r], coef_r.at[r], x_peer(r)).wait_recv()
            fit_slot(r)

        def clean_rest(s):
            for r in (1, 3, 2):
                remote(
                    spec.at[:, pl.ds(0, sub)], raw.at[s, r], raw_s.at[s, r], raw_r.at[s, r],
                    x_peer(r),
                ).wait_recv()
                clean_slot(s, r, raw[s, r])

        def chunk_row(step):
            return pl.multiple_of(lax.rem(z + step + 2 * nz, nz) * zpix, zpix)

        def grid_chunk(s, step):
            row = chunk_row(step)
            part[s, pl.ds(row, zpix), :] = jnp.dot(
                band[pl.ds(row, zpix), :], clean[s], preferred_element_type=f32
            )

        def part_half(s, step, which):
            row = pl.multiple_of(chunk_row(step) + which * half, half)
            return part[s, pl.ds(row, half), :]

        def z_copy(s, way, index):
            return remote(
                zsend.at[s, way, index], zrecv.at[s, way, index], z_s.at[s, way, index],
                z_r.at[s, way, index], z_peer((1, nz - 1)[way]),
            )

        def z_start(s, way, index, value):
            zsend[s, way, index] = value.astype(bf16)
            start(z_copy(s, way, index))

        def z_take(s, way, index):
            z_copy(s, way, index).wait_recv()
            return zrecv[s, way, index].astype(f32)

        sign = (1, -1)

        def first_steps(s):
            grid_chunk(s, far)
            for way in range(2):
                z_start(s, way, 0, part_half(s, far, way))
            for way in range(2):
                grid_chunk(s, sign[way] * (far - 1))
                z_start(s, way, far, part_half(s, sign[way] * (far - 1), 1 - way))

        def grid_rest(s):
            def step(i, carry):
                grid_chunk(s, i + (2 - far))
                return carry

            lax.fori_loop(0, nz - 3, step, 0)

        def long_step(s, k):
            for way in range(2):
                got = z_take(s, way, k)
                z_start(s, way, k + 1, got + part_half(s, sign[way] * (far - 1 - k), way))

        def short_step(s, k):
            for way in range(2):
                got = z_take(s, way, far + k)
                z_start(
                    s, way, far + k + 1, got + part_half(s, sign[way] * (far - 2 - k), 1 - way)
                )

        def finish(s):
            got = [z_take(s, way, 2 * far - 2) for way in range(2)]
            for way in range(2):
                value = z_take(s, way, far - 1) + got[1 - way] + part_half(s, 0, way)
                final[s, way * half:(way + 1) * half, :] = value.astype(bf16)
            column = pl.multiple_of(here + s * sub, sub)
            for r in (2, 1, 3):
                row = pl.multiple_of(lax.rem(x + r, NX) * TP, TP)
                start(remote(
                    final.at[s, pl.ds(row, TP), :], sky.at[:, pl.ds(column, sub)],
                    fin_s.at[s, r], fin_r.at[s, NX - r], x_peer(r),
                ))
            sky[:, pl.ds(column, sub)] = final[s, pl.ds(pl.multiple_of(x * TP, TP), TP), :]

        def share(buffer, me, send_sem, recv_sem, peer_of, count):
            for r in range(1, count):
                start(remote(buffer.at[me], buffer.at[me], send_sem.at[r], recv_sem.at[me], peer_of(r)))

        def gather(buffer, me, send_sem, recv_sem, peer_of, count):
            for r in range(1, count):
                other = lax.rem(me + r, count)
                remote(
                    buffer.at[other], buffer.at[other], send_sem.at[r], recv_sem.at[other], peer_of(r)
                ).wait_recv()
            value = buffer[0]
            for i in range(1, count):
                value = value + buffer[i]
            return value

        clean_rest(0)
        first_steps(0)
        grid_rest(0)
        long_step(0, 0)
        short_step(0, 0)

        begin = gal_chan[...] - SW - (j * width + here)
        shift_hot = (iota((shifts, ngal), 0) == quarter - 1 - begin).astype(f32).astype(bf16)
        gal_row = jnp.broadcast_to(gal_pix[...], (TAPS, ngal))
        fill(
            pixel_hot, 0, gal_row >> 4,
            jnp.where((gal_row & (TAPS - 1)) == iota((TAPS, ngal), 0), 1.0, 0.0).astype(f32),
        )
        counts[...] = lax.dot_general(
            shift_hot, pixel_hot[...], (((1,), (1,)), ((), ())), preferred_element_type=f32
        ).astype(bf16)

        long_step(0, 1)
        short_step(0, 1)
        clean_rest(1)
        first_steps(1)
        long_step(0, 2)
        grid_rest(1)

        wide = jnp.concatenate(
            [
                jnp.dot(counts[...], part[s].astype(bf16), preferred_element_type=f32)
                for s in range(SUBS)
            ]
            + [jnp.zeros((shifts, 512 - quarter), f32)],
            axis=1,
        )
        folded = jnp.zeros((8, 512), f32)
        for i in range(shifts // 8):
            folded = folded + pltpu.roll(
                wide[8 * i:8 * i + 8], (513 - quarter + 8 * i) % 512, 1
            )
        window = jnp.zeros((1, 512), f32)
        for i in range(8):
            window = window + (pltpu.roll(folded[i:i + 1], i, 1) if i else folded[i:i + 1])
        st1[x] = window[:, :2 * SW]
        share(st1, x, st1_s, st1_r, x_peer, NX)

        long_step(1, 0)
        short_step(1, 0)
        finish(0)
        st2[j] = gather(st1, x, st1_s, st1_r, x_peer, NX)
        share(st2, j, st2_s, st2_r, c_peer, chan_size)
        long_step(1, 1)
        short_step(1, 1)
        st3[z] = gather(st2, j, st2_s, st2_r, c_peer, chan_size)
        share(st3, z, st3_s, st3_r, z_peer, nz)
        long_step(1, 2)
        finish(1)
        stacked[...] = gather(st3, z, st3_s, st3_r, z_peer, nz) / ngal

        for s in range(SUBS):
            for r in range(1, NX):
                column = pl.multiple_of(lax.rem(x + r, NX) * quarter + s * sub, sub)
                remote(
                    final.at[s, pl.ds(0, TP), :], sky.at[:, pl.ds(column, sub)],
                    fin_s.at[s, r], fin_r.at[s, r], x_peer(r),
                ).wait_recv()
        for copy in sends:
            copy.wait_send()

    dma = pltpu.SemaphoreType.DMA
    scratch = [
        pltpu.VMEM((rows, width), bf16),
        pltpu.VMEM((1, width), f32),
        pltpu.VMEM((1, nblocks), jnp.int32),
        pltpu.VMEM((1, rows), jnp.int32),
        pltpu.VMEM((1, TAPS), bf16),
        pltpu.VMEM((1, ngal), jnp.int32),
        pltpu.VMEM((1, ngal), jnp.int32),
        pltpu.VMEM((MODES, width), f32),
        pltpu.VMEM((NX, 1, rows), jnp.int32),
        pltpu.VMEM((SUBS, NX, rows, sub), bf16),
        pltpu.VMEM((chan_size, MODES, 128), f32),
        pltpu.VMEM((chan_size, MODES, rows), f32),
        pltpu.VMEM((128, rows), f32),
        pltpu.VMEM((NX, MODES, rows), f32),
        pltpu.VMEM((npix, NX * rows), bf16),
        pltpu.VMEM((NX * rows, quarter), f32),
        pltpu.VMEM((SUBS, NX * rows, sub), bf16),
        pltpu.VMEM((SUBS, npix, sub), f32),
        pltpu.VMEM((npix, ngal), bf16),
        pltpu.VMEM((shifts, npix), bf16),
        pltpu.VMEM((SUBS, 2, nz - 1, half, sub), bf16),
        pltpu.VMEM((SUBS, 2, nz - 1, half, sub), bf16),
        pltpu.VMEM((SUBS, zpix, sub), bf16),
        pltpu.VMEM((NX, 1, 2 * SW), f32),
        pltpu.VMEM((chan_size, 1, 2 * SW), f32),
        pltpu.VMEM((nz, 1, 2 * SW), f32),
        dma((8,)),
    ]
    for shape in (
        (NX,), (SUBS, NX), (chan_size,), (chan_size,), (NX,), (SUBS, 2, nz - 1), (SUBS, NX),
        (NX,), (chan_size,), (nz,),
    ):
        scratch += [dma(shape), dma(shape)]
    return kernel, scratch


def solution(mesh):
    tm_size, chan_size = mesh.shape["tm"], mesh.shape["chan"]

    def per_device(spectra, chan_weight, routes, offsets, taps, gal_pix, gal_chan):
        rows, width = spectra.shape
        nblocks = routes.shape[0]
        kernel, scratch = make_kernel(
            tm_size, chan_size, rows, width, nblocks, gal_pix.shape[0]
        )
        vmem = pl.BlockSpec(memory_space=pltpu.VMEM)
        sky, stacked = pl.pallas_call(
            kernel,
            out_shape=(
                jax.ShapeDtypeStruct((TP, width), bf16),
                jax.ShapeDtypeStruct((1, 2 * SW), f32),
            ),
            in_specs=[pl.BlockSpec(memory_space=pl.ANY)] * 8,
            out_specs=(vmem, vmem),
            scratch_shapes=scratch,
            compiler_params=pltpu.CompilerParams(
                collective_id=0, has_side_effects=True, vmem_limit_bytes=54880 * 1024
            ),
        )(
            spectra, chan_weight[None, :], routes.reshape(1, nblocks), offsets[None, :],
            taps[None, :], gal_pix[None, :], gal_chan[None, :],
            jnp.asarray(basis_table(width * chan_size)),
        )
        return sky, stacked[0]

    in_specs = (
        P("tm", "chan"), P("chan"), P("tm", None), P("tm"), P(None), P(None), P(None)
    )
    return jax.shard_map(
        per_device, mesh=mesh, in_specs=in_specs, out_specs=(P("tm", "chan"), P(None)),
        check_vma=False,
    )
```

```python
import jax
import jax.numpy as jnp
import numpy as np
from jax import lax
from jax.experimental import pallas as pl
from jax.experimental.pallas import tpu as pltpu
from jax.sharding import PartitionSpec as P

KMODES = 8
MODES = 2 * KMODES
TP = 64
MARGIN = 8
SW = 64
TAPS = 16
NX = 4

highest = lax.Precision.HIGHEST
MESH = pl.DeviceIdType.MESH
f32 = jnp.float32
bf16 = jnp.bfloat16


def basis_table(total):
    orders = np.arange(1, KMODES + 1)[:, None]
    phase = (orders * np.arange(total)[None, :] % total) * (2 * np.pi / total)
    return np.concatenate([np.cos(phase), np.sin(phase)], axis=0).astype(np.float32)


def split3(value):
    high = value.astype(bf16)
    rest = value - high.astype(f32)
    mid = rest.astype(bf16)
    low = (rest - mid.astype(f32)).astype(bf16)
    return high, mid, low


def iota(shape, dim):
    return lax.broadcasted_iota(jnp.int32, shape, dim)


def make_kernel(tm_size, chan_size, rows, width, nblocks, ngal):
    nz = tm_size // NX
    quarter = width // NX
    npix = tm_size * TP
    zpix = NX * TP
    half = zpix // 2
    block_rows = rows // nblocks
    shifts = quarter + 2 * SW
    far = nz // 2

    def kernel(
        spec, weight_in, routes_in, offsets_in, taps_in, gal_pix_in, gal_chan_in, basis_in,
        sky, stacked,
        own, weight, routes, offsets, taps, gal_pix, gal_chan, basis,
        pix, raw, gram, proj, ext, coef, band, ripple, clean, part, pixel_hot, counts,
        zsend, zrecv, final, st1, st2, st3,
        load_sem, pix_s, pix_r, raw_s, raw_r, gram_s, gram_r, proj_s, proj_r, coef_s, coef_r,
        z_s, z_r, fin_s, fin_r, st1_s, st1_r, st2_s, st2_r, st3_s, st3_r,
    ):
        tm = lax.axis_index("tm")
        j = lax.axis_index("chan")
        z = lax.div(tm, NX)
        x = lax.rem(tm, NX)
        here = pl.multiple_of(x * quarter, quarter)

        def x_peer(r):
            return (z * NX + lax.rem(x + r, NX), j)

        def c_peer(r):
            return (tm, lax.rem(j + r, chan_size))

        def z_peer(r):
            return (lax.rem(z + r, nz) * NX + x, j)

        def remote(src, dst, send_sem, recv_sem, peer):
            return pltpu.make_async_remote_copy(
                src_ref=src, dst_ref=dst, send_sem=send_sem, recv_sem=recv_sem,
                device_id=peer, device_id_type=MESH,
            )

        sends = []

        def start(copy):
            copy.start()
            sends.append(copy)

        peers = (
            [x_peer(r) for r in range(1, NX)]
            + [c_peer(r) for r in range(1, chan_size)]
            + [z_peer(r) for r in range(1, nz)]
        )
        barrier = pltpu.get_barrier_semaphore()
        for peer in peers:
            pl.semaphore_signal(barrier, inc=1, device_id=peer, device_id_type=MESH)
        basis_here = basis_in.at[:, pl.ds(pl.multiple_of(j * width, width), width)]
        loads = [
            pltpu.make_async_copy(source, target, load_sem.at[i])
            for i, (source, target) in enumerate((
                (weight_in, weight), (basis_here, basis), (spec, own), (routes_in, routes),
                (offsets_in, offsets), (taps_in, taps), (gal_pix_in, gal_pix),
                (gal_chan_in, gal_chan),
            ))
        ]
        for load in loads:
            load.start()
        pl.semaphore_wait(barrier, len(peers))

        for r in (2, 1, 3):
            column = pl.multiple_of(lax.rem(x + r, NX) * quarter, quarter)
            start(remote(
                spec.at[:, pl.ds(column, quarter)], raw.at[NX - r], raw_s.at[r], raw_r.at[NX - r],
                x_peer(r),
            ))

        loads[0].wait()
        loads[1].wait()
        weighted = basis[...] * weight[...]
        gram[0] = jnp.zeros((MODES, 128), f32)
        gram[0, :, 0:MODES] = lax.dot_general(
            weighted, basis[...], (((1,), (1,)), ((), ())), precision=highest,
            preferred_element_type=f32,
        )
        for r in range(1, chan_size):
            start(remote(
                gram.at[0], gram.at[chan_size - r], gram_s.at[r], gram_r.at[chan_size - r],
                c_peer(r),
            ))
        w_stack = jnp.concatenate(split3(weighted), axis=0)
        loads[2].wait()
        products = lax.dot_general(
            w_stack, own[...], (((1,), (1,)), ((), ())), preferred_element_type=f32
        )
        proj[0] = products[:MODES] + products[MODES:2 * MODES] + products[2 * MODES:]
        for r in range(1, chan_size):
            start(remote(
                proj.at[0], proj.at[chan_size - r], proj_s.at[r], proj_r.at[chan_size - r],
                c_peer(r),
            ))

        for i in (3, 4, 5, 6, 7):
            loads[i].wait()
        inside = iota((nblocks, rows), 1) - block_rows * iota((nblocks, rows), 0)
        owner = ((inside >= 0) & (inside < block_rows)).astype(f32).astype(bf16)
        tile = jnp.dot(
            jnp.broadcast_to(routes[...], (16, nblocks)).astype(f32).astype(bf16), owner,
            preferred_element_type=f32,
        )[0:1].astype(jnp.int32)
        pix[0] = tile * TP + offsets[...] - MARGIN
        for r in range(1, NX):
            start(remote(pix.at[0], pix.at[NX - r], pix_s.at[r], pix_r.at[NX - r], x_peer(r)))

        def fill(target, column, group, tap):
            group = group.astype(f32).astype(bf16)
            tap = tap.astype(bf16)
            zero = jnp.zeros(tap.shape, bf16)

            def step(a, carry):
                row = pl.multiple_of(a * TAPS, TAPS)
                now = jnp.full(tap.shape, a.astype(f32), f32).astype(bf16)
                target[pl.ds(row, TAPS), column:column + tap.shape[1]] = jnp.where(
                    group == now, tap, zero
                )
                return carry

            lax.fori_loop(0, npix // TAPS, step, 0, unroll=4)

        def build_band(slot):
            first = pix[slot]
            group = jnp.broadcast_to(first >> 4, (TAPS, rows))
            inner = jnp.broadcast_to(first & (TAPS - 1), (TAPS, rows))
            lane = iota((TAPS, rows), 0)
            turn = (lane - inner) & (TAPS - 1)
            tap = jnp.zeros((TAPS, rows), f32)
            values = taps[...].astype(f32)
            for m in range(TAPS):
                tap = jnp.where(turn == m, values[0:1, m:m + 1], tap)
            fill(band, slot * rows, jnp.where(lane < inner, group + 1, group), tap)

        build_band(0)

        for r in range(1, chan_size):
            remote(gram.at[0], gram.at[r], gram_s.at[r], gram_r.at[r], c_peer(r)).wait_recv()
        total = gram[0]
        for r in range(1, chan_size):
            total = total + gram[r]
        row_id = iota((MODES, 128), 0)
        both = jnp.where(iota((MODES, 128), 1) - MODES == row_id, 1.0, total)
        for i in range(MODES):
            pivot = both[i:i + 1, :] / both[i:i + 1, i:i + 1]
            both = jnp.where(row_id == i, pivot, both - both[:, i:i + 1] * pivot)

        ext[...] = jnp.zeros(ext.shape, f32)
        for r in range(1, chan_size):
            remote(proj.at[0], proj.at[r], proj_s.at[r], proj_r.at[r], c_peer(r)).wait_recv()
        full = proj[0]
        for r in range(1, chan_size):
            full = full + proj[r]
        ext[MODES:2 * MODES, :] = full
        coef[0] = jnp.dot(both, ext[...], precision=highest, preferred_element_type=f32)
        for r in range(1, NX):
            start(remote(coef.at[0], coef.at[NX - r], coef_s.at[r], coef_r.at[NX - r], x_peer(r)))

        b_high, b_mid, b_low = split3(basis[:, pl.ds(here, quarter)])
        b_stack = jnp.concatenate(
            [b_high, b_mid, b_high, b_mid, b_low, b_high, jnp.zeros((2 * MODES, quarter), bf16)],
            axis=0,
        )

        def fit_slot(slot):
            c_high, c_mid, c_low = split3(coef[slot])
            c_stack = jnp.concatenate(
                [c_high, c_high, c_mid, c_mid, c_high, c_low, jnp.zeros((2 * MODES, rows), bf16)],
                axis=0,
            )
            ripple[slot * rows:(slot + 1) * rows, :] = lax.dot_general(
                c_stack, b_stack, (((0,), (0,)), ((), ())), preferred_element_type=f32
            )

        def clean_slot(slot, values):
            clean[slot * rows:(slot + 1) * rows, :] = (
                values.astype(f32) - ripple[slot * rows:(slot + 1) * rows, :]
            ).astype(bf16)

        fit_slot(0)
        clean_slot(0, own[:, pl.ds(here, quarter)])
        for r in range(1, NX):
            remote(pix.at[0], pix.at[r], pix_s.at[r], pix_r.at[r], x_peer(r)).wait_recv()
            build_band(r)
        for r in (1, 3, 2):
            remote(coef.at[0], coef.at[r], coef_s.at[r], coef_r.at[r], x_peer(r)).wait_recv()
            fit_slot(r)
        for r in (1, 3, 2):
            remote(
                spec.at[:, pl.ds(0, quarter)], raw.at[r], raw_s.at[r], raw_r.at[r], x_peer(r)
            ).wait_recv()
            clean_slot(r, raw[r])

        def chunk_row(step):
            return pl.multiple_of(lax.rem(z + step + 2 * nz, nz) * zpix, zpix)

        def part_half(step, which):
            row = pl.multiple_of(chunk_row(step) + which * half, half)
            return part[pl.ds(row, half), :]

        def z_copy(way, index):
            return remote(
                zsend.at[way, index], zrecv.at[way, index], z_s.at[way, index],
                z_r.at[way, index], z_peer((1, nz - 1)[way]),
            )

        def z_start(way, index, value):
            zsend[way, index] = value.astype(bf16)
            z_copy(way, index).start()

        def z_take(way, index):
            z_copy(way, index).wait_recv()
            return zrecv[way, index].astype(f32)

        sign = (1, -1)

        def long_step(k):
            for way in range(2):
                got = z_take(way, k)
                z_start(way, k + 1, got + part_half(sign[way] * (far - 1 - k), way))

        def short_step(k):
            for way in range(2):
                got = z_take(way, far + k)
                z_start(
                    way, far + k + 1, got + part_half(sign[way] * (far - 2 - k), 1 - way)
                )

        def grid_step(n, carry):
            away = lax.div(n + 1, 2)
            row = chunk_row(far + away - 2 * lax.rem(n, 2) * away)
            part[pl.ds(row, zpix), :] = jnp.dot(
                band[pl.ds(row, zpix), :], clean[...], preferred_element_type=f32
            )

            @pl.when(n == 0)
            def _():
                for way in range(2):
                    z_start(way, 0, part_half(far, way))

            @pl.when(n == 2)
            def _():
                for way in range(2):
                    z_start(way, far, part_half(sign[way] * (far - 1), 1 - way))

            @pl.when(n == 4)
            def _():
                long_step(0)
                short_step(0)

            return carry

        def share(buffer, me, send_sem, recv_sem, peer_of, count):
            for r in range(1, count):
                start(remote(buffer.at[me], buffer.at[me], send_sem.at[r], recv_sem.at[me], peer_of(r)))

        def gather(buffer, me, send_sem, recv_sem, peer_of, count):
            for r in range(1, count):
                other = lax.rem(me + r, count)
                remote(
                    buffer.at[other], buffer.at[other], send_sem.at[r], recv_sem.at[other], peer_of(r)
                ).wait_recv()
            value = buffer[0]
            for i in range(1, count):
                value = value + buffer[i]
            return value

        lax.fori_loop(0, nz, grid_step, 0)

        begin = gal_chan[...] - SW - (j * width + here)
        shift_hot = (iota((shifts, ngal), 0) == quarter - 1 - begin).astype(f32).astype(bf16)
        gal_row = jnp.broadcast_to(gal_pix[...], (TAPS, ngal))
        fill(
            pixel_hot, 0, gal_row >> 4,
            jnp.where((gal_row & (TAPS - 1)) == iota((TAPS, ngal), 0), 1.0, 0.0).astype(f32),
        )
        counts[...] = lax.dot_general(
            shift_hot, pixel_hot[...], (((1,), (1,)), ((), ())), preferred_element_type=f32
        ).astype(bf16)

        long_step(1)
        short_step(1)

        wide = jnp.concatenate(
            [
                jnp.dot(counts[...], part[...].astype(bf16), preferred_element_type=f32),
                jnp.zeros((shifts, 512 - quarter), f32),
            ],
            axis=1,
        )
        folded = jnp.zeros((8, 512), f32)
        for i in range(shifts // 8):
            folded = folded + pltpu.roll(
                wide[8 * i:8 * i + 8], (513 - quarter + 8 * i) % 512, 1
            )
        window = jnp.zeros((1, 512), f32)
        for i in range(8):
            window = window + (pltpu.roll(folded[i:i + 1], i, 1) if i else folded[i:i + 1])
        st1[x] = window[:, :2 * SW]
        share(st1, x, st1_s, st1_r, x_peer, NX)

        long_step(2)
        st2[j] = gather(st1, x, st1_s, st1_r, x_peer, NX)
        share(st2, j, st2_s, st2_r, c_peer, chan_size)
        for copy in sends:
            copy.wait_send()
        sends.clear()

        got = [z_take(way, 2 * far - 2) for way in range(2)]
        for way in range(2):
            value = z_take(way, far - 1) + got[1 - way] + part_half(0, way)
            final[way * half:(way + 1) * half, :] = value.astype(bf16)
        for r in (2, 1, 3):
            row = pl.multiple_of(lax.rem(x + r, NX) * TP, TP)
            start(remote(
                final.at[pl.ds(row, TP), :], sky.at[:, pl.ds(here, quarter)], fin_s.at[r],
                fin_r.at[NX - r], x_peer(r),
            ))
        sky[:, pl.ds(here, quarter)] = final[pl.ds(pl.multiple_of(x * TP, TP), TP), :]

        st3[z] = gather(st2, j, st2_s, st2_r, c_peer, chan_size)
        share(st3, z, st3_s, st3_r, z_peer, nz)
        for way in range(2):
            for index in range(2 * far - 1):
                z_copy(way, index).wait_send()
        for r in range(1, NX):
            column = pl.multiple_of(lax.rem(x + r, NX) * quarter, quarter)
            remote(
                final.at[pl.ds(0, TP), :], sky.at[:, pl.ds(column, quarter)], fin_s.at[r],
                fin_r.at[r], x_peer(r),
            ).wait_recv()
        stacked[...] = gather(st3, z, st3_s, st3_r, z_peer, nz) / ngal
        for copy in sends:
            copy.wait_send()

    dma = pltpu.SemaphoreType.DMA
    scratch = [
        pltpu.VMEM((rows, width), bf16),
        pltpu.VMEM((1, width), f32),
        pltpu.VMEM((1, nblocks), jnp.int32),
        pltpu.VMEM((1, rows), jnp.int32),
        pltpu.VMEM((1, TAPS), bf16),
        pltpu.VMEM((1, ngal), jnp.int32),
        pltpu.VMEM((1, ngal), jnp.int32),
        pltpu.VMEM((MODES, width), f32),
        pltpu.VMEM((NX, 1, rows), jnp.int32),
        pltpu.VMEM((NX, rows, quarter), bf16),
        pltpu.VMEM((chan_size, MODES, 128), f32),
        pltpu.VMEM((chan_size, MODES, rows), f32),
        pltpu.VMEM((128, rows), f32),
        pltpu.VMEM((NX, MODES, rows), f32),
        pltpu.VMEM((npix, NX * rows), bf16),
        pltpu.VMEM((NX * rows, quarter), f32),
        pltpu.VMEM((NX * rows, quarter), bf16),
        pltpu.VMEM((npix, quarter), f32),
        pltpu.VMEM((npix, ngal), bf16),
        pltpu.VMEM((shifts, npix), bf16),
        pltpu.VMEM((2, nz - 1, half, quarter), bf16),
        pltpu.VMEM((2, nz - 1, half, quarter), bf16),
        pltpu.VMEM((zpix, quarter), bf16),
        pltpu.VMEM((NX, 1, 2 * SW), f32),
        pltpu.VMEM((chan_size, 1, 2 * SW), f32),
        pltpu.VMEM((nz, 1, 2 * SW), f32),
        dma((8,)),
    ]
    for shape in (
        (NX,), (NX,), (chan_size,), (chan_size,), (NX,), (2, nz - 1), (NX,),
        (NX,), (chan_size,), (nz,),
    ):
        scratch += [dma(shape), dma(shape)]
    return kernel, scratch


def solution(mesh):
    tm_size, chan_size = mesh.shape["tm"], mesh.shape["chan"]

    def per_device(spectra, chan_weight, routes, offsets, taps, gal_pix, gal_chan):
        rows, width = spectra.shape
        nblocks = routes.shape[0]
        kernel, scratch = make_kernel(
            tm_size, chan_size, rows, width, nblocks, gal_pix.shape[0]
        )
        vmem = pl.BlockSpec(memory_space=pltpu.VMEM)
        sky, stacked = pl.pallas_call(
            kernel,
            out_shape=(
                jax.ShapeDtypeStruct((TP, width), bf16),
                jax.ShapeDtypeStruct((1, 2 * SW), f32),
            ),
            in_specs=[pl.BlockSpec(memory_space=pl.ANY)] * 8,
            out_specs=(vmem, vmem),
            scratch_shapes=scratch,
            compiler_params=pltpu.CompilerParams(
                collective_id=0, has_side_effects=True, vmem_limit_bytes=54880 * 1024
            ),
        )(
            spectra, chan_weight[None, :], routes.reshape(1, nblocks), offsets[None, :],
            taps[None, :], gal_pix[None, :], gal_chan[None, :],
            jnp.asarray(basis_table(width * chan_size)),
        )
        return sky, stacked[0]

    in_specs = (
        P("tm", "chan"), P("chan"), P("tm", None), P("tm"), P(None), P(None), P(None)
    )
    return jax.shard_map(
        per_device, mesh=mesh, in_specs=in_specs, out_specs=(P("tm", "chan"), P(None)),
        check_vma=False,
    )
```

```python
import jax
import jax.numpy as jnp
import numpy as np
from jax import lax
from jax.experimental import pallas as pl
from jax.experimental.pallas import tpu as pltpu
from jax.sharding import PartitionSpec as P

KMODES = 8
MODES = 2 * KMODES
TP = 64
MARGIN = 8
SW = 64
TAPS = 16
NX = 4

highest = lax.Precision.HIGHEST
MESH = pl.DeviceIdType.MESH
f32 = jnp.float32
bf16 = jnp.bfloat16


def basis_table(total):
    orders = np.arange(1, KMODES + 1)[:, None]
    phase = (orders * np.arange(total)[None, :] % total) * (2 * np.pi / total)
    return np.concatenate([np.cos(phase), np.sin(phase)], axis=0).astype(np.float32)


def split3(value):
    high = value.astype(bf16)
    rest = value - high.astype(f32)
    mid = rest.astype(bf16)
    low = (rest - mid.astype(f32)).astype(bf16)
    return high, mid, low


def iota(shape, dim):
    return lax.broadcasted_iota(jnp.int32, shape, dim)


def make_kernel(tm_size, chan_size, rows, width, nblocks, ngal):
    nz = tm_size // NX
    quarter = width // NX
    npix = tm_size * TP
    zpix = NX * TP
    half = zpix // 2
    block_rows = rows // nblocks
    shifts = quarter + 2 * SW
    far = nz // 2

    def kernel(
        spec, weight_in, routes_in, offsets_in, taps_in, gal_pix_in, gal_chan_in, basis_in,
        sky, stacked,
        own, weight, routes, offsets, taps, gal_pix, gal_chan, basis,
        pix, raw, gram, proj, ext, coef, band, ripple, clean, part, pixel_hot, counts,
        zsend, zrecv, final, st1, st2, st3,
        load_sem, pix_s, pix_r, raw_s, raw_r, gram_s, gram_r, proj_s, proj_r, coef_s, coef_r,
        z_s, z_r, fin_s, fin_r, st1_s, st1_r, st2_s, st2_r, st3_s, st3_r,
    ):
        tm = lax.axis_index("tm")
        j = lax.axis_index("chan")
        z = lax.div(tm, NX)
        x = lax.rem(tm, NX)
        here = pl.multiple_of(x * quarter, quarter)

        def x_peer(r):
            return (z * NX + lax.rem(x + r, NX), j)

        def c_peer(r):
            return (tm, lax.rem(j + r, chan_size))

        def z_peer(r):
            return (lax.rem(z + r, nz) * NX + x, j)

        def remote(src, dst, send_sem, recv_sem, peer):
            return pltpu.make_async_remote_copy(
                src_ref=src, dst_ref=dst, send_sem=send_sem, recv_sem=recv_sem,
                device_id=peer, device_id_type=MESH,
            )

        sends = []

        def start(copy):
            copy.start()
            sends.append(copy)

        peers = (
            [x_peer(r) for r in range(1, NX)]
            + [c_peer(r) for r in range(1, chan_size)]
            + [z_peer(r) for r in range(1, nz)]
        )
        barrier = pltpu.get_barrier_semaphore()
        for peer in peers:
            pl.semaphore_signal(barrier, inc=1, device_id=peer, device_id_type=MESH)
        basis_here = basis_in.at[:, pl.ds(pl.multiple_of(j * width, width), width)]
        loads = [
            pltpu.make_async_copy(source, target, load_sem.at[i])
            for i, (source, target) in enumerate((
                (weight_in, weight), (basis_here, basis), (spec, own), (routes_in, routes),
                (offsets_in, offsets), (taps_in, taps), (gal_pix_in, gal_pix),
                (gal_chan_in, gal_chan),
            ))
        ]
        for load in loads:
            load.start()
        pl.semaphore_wait(barrier, len(peers))

        for r in (2, 1, 3):
            column = pl.multiple_of(lax.rem(x + r, NX) * quarter, quarter)
            start(remote(
                spec.at[:, pl.ds(column, quarter)], raw.at[NX - r], raw_s.at[r], raw_r.at[NX - r],
                x_peer(r),
            ))

        loads[0].wait()
        loads[1].wait()
        weighted = basis[...] * weight[...]
        gram[0] = jnp.zeros((MODES, 128), f32)
        gram[0, :, 0:MODES] = lax.dot_general(
            weighted, basis[...], (((1,), (1,)), ((), ())), precision=highest,
            preferred_element_type=f32,
        )
        for r in range(1, chan_size):
            start(remote(
                gram.at[0], gram.at[chan_size - r], gram_s.at[r], gram_r.at[chan_size - r],
                c_peer(r),
            ))
        w_stack = jnp.concatenate(split3(weighted), axis=0)
        loads[2].wait()
        products = lax.dot_general(
            w_stack, own[...], (((1,), (1,)), ((), ())), preferred_element_type=f32
        )
        proj[0] = products[:MODES] + products[MODES:2 * MODES] + products[2 * MODES:]
        for r in range(1, chan_size):
            start(remote(
                proj.at[0], proj.at[chan_size - r], proj_s.at[r], proj_r.at[chan_size - r],
                c_peer(r),
            ))

        for i in (3, 4, 5, 6, 7):
            loads[i].wait()
        inside = iota((nblocks, rows), 1) - block_rows * iota((nblocks, rows), 0)
        owner = ((inside >= 0) & (inside < block_rows)).astype(f32).astype(bf16)
        tile = jnp.dot(
            jnp.broadcast_to(routes[...], (16, nblocks)).astype(f32).astype(bf16), owner,
            preferred_element_type=f32,
        )[0:1].astype(jnp.int32)
        pix[0] = tile * TP + offsets[...] - MARGIN
        for r in range(1, NX):
            start(remote(pix.at[0], pix.at[NX - r], pix_s.at[r], pix_r.at[NX - r], x_peer(r)))

        def fill(target, column, group, tap):
            def step(a, carry):
                row = pl.multiple_of(a * TAPS, TAPS)
                target[pl.ds(row, TAPS), column:column + tap.shape[1]] = jnp.where(
                    group == a, tap, 0.0
                ).astype(bf16)
                return carry

            lax.fori_loop(0, npix // TAPS, step, 0, unroll=4)

        def build_band(slot):
            first = pix[slot]
            group = jnp.broadcast_to(first >> 4, (TAPS, rows))
            inner = jnp.broadcast_to(first & (TAPS - 1), (TAPS, rows))
            lane = iota((TAPS, rows), 0)
            turn = (lane - inner) & (TAPS - 1)
            tap = jnp.zeros((TAPS, rows), f32)
            values = taps[...].astype(f32)
            for m in range(TAPS):
                tap = jnp.where(turn == m, values[0:1, m:m + 1], tap)
            fill(band, slot * rows, jnp.where(lane < inner, group + 1, group), tap)

        build_band(0)

        for r in range(1, chan_size):
            remote(gram.at[0], gram.at[r], gram_s.at[r], gram_r.at[r], c_peer(r)).wait_recv()
        total = gram[0]
        for r in range(1, chan_size):
            total = total + gram[r]
        row_id = iota((MODES, 128), 0)
        both = jnp.where(iota((MODES, 128), 1) - MODES == row_id, 1.0, total)
        for i in range(MODES):
            pivot = both[i:i + 1, :] / both[i:i + 1, i:i + 1]
            both = jnp.where(row_id == i, pivot, both - both[:, i:i + 1] * pivot)

        ext[...] = jnp.zeros(ext.shape, f32)
        for r in range(1, chan_size):
            remote(proj.at[0], proj.at[r], proj_s.at[r], proj_r.at[r], c_peer(r)).wait_recv()
        full = proj[0]
        for r in range(1, chan_size):
            full = full + proj[r]
        ext[MODES:2 * MODES, :] = full
        coef[0] = jnp.dot(both, ext[...], precision=highest, preferred_element_type=f32)
        for r in range(1, NX):
            start(remote(coef.at[0], coef.at[NX - r], coef_s.at[r], coef_r.at[NX - r], x_peer(r)))

        b_high, b_mid, b_low = split3(basis[:, pl.ds(here, quarter)])
        b_stack = jnp.concatenate(
            [b_high, b_mid, b_high, b_mid, b_low, b_high, jnp.zeros((2 * MODES, quarter), bf16)],
            axis=0,
        )

        def fit_slot(slot):
            c_high, c_mid, c_low = split3(coef[slot])
            c_stack = jnp.concatenate(
                [c_high, c_high, c_mid, c_mid, c_high, c_low, jnp.zeros((2 * MODES, rows), bf16)],
                axis=0,
            )
            ripple[slot * rows:(slot + 1) * rows, :] = lax.dot_general(
                c_stack, b_stack, (((0,), (0,)), ((), ())), preferred_element_type=f32
            )

        def clean_slot(slot, values):
            clean[slot * rows:(slot + 1) * rows, :] = (
                values.astype(f32) - ripple[slot * rows:(slot + 1) * rows, :]
            ).astype(bf16)

        fit_slot(0)
        clean_slot(0, own[:, pl.ds(here, quarter)])
        for r in range(1, NX):
            remote(pix.at[0], pix.at[r], pix_s.at[r], pix_r.at[r], x_peer(r)).wait_recv()
            build_band(r)
        for r in (1, 3, 2):
            remote(coef.at[0], coef.at[r], coef_s.at[r], coef_r.at[r], x_peer(r)).wait_recv()
            fit_slot(r)
        for r in (1, 3, 2):
            remote(
                spec.at[:, pl.ds(0, quarter)], raw.at[r], raw_s.at[r], raw_r.at[r], x_peer(r)
            ).wait_recv()
            clean_slot(r, raw[r])

        def chunk_row(step):
            return pl.multiple_of(lax.rem(z + step + 2 * nz, nz) * zpix, zpix)

        def part_half(step, which):
            row = pl.multiple_of(chunk_row(step) + which * half, half)
            return part[pl.ds(row, half), :]

        def z_copy(way, index):
            return remote(
                zsend.at[way, index], zrecv.at[way, index], z_s.at[way, index],
                z_r.at[way, index], z_peer((1, nz - 1)[way]),
            )

        def z_start(way, index, value):
            zsend[way, index] = value.astype(bf16)
            z_copy(way, index).start()

        def z_take(way, index):
            z_copy(way, index).wait_recv()
            return zrecv[way, index].astype(f32)

        sign = (1, -1)

        def long_step(k):
            for way in range(2):
                got = z_take(way, k)
                z_start(way, k + 1, got + part_half(sign[way] * (far - 1 - k), way))

        def short_step(k):
            for way in range(2):
                got = z_take(way, far + k)
                z_start(
                    way, far + k + 1, got + part_half(sign[way] * (far - 2 - k), 1 - way)
                )

        def grid_step(n, carry):
            away = lax.div(n + 1, 2)
            row = chunk_row(far + away - 2 * lax.rem(n, 2) * away)
            part[pl.ds(row, zpix), :] = jnp.dot(
                band[pl.ds(row, zpix), :], clean[...], preferred_element_type=f32
            )

            @pl.when(n == 0)
            def _():
                for way in range(2):
                    z_start(way, 0, part_half(far, way))

            @pl.when(n == 2)
            def _():
                for way in range(2):
                    z_start(way, far, part_half(sign[way] * (far - 1), 1 - way))

            @pl.when(n == 4)
            def _():
                long_step(0)
                short_step(0)

            return carry

        def share(buffer, me, send_sem, recv_sem, peer_of, count):
            for r in range(1, count):
                start(remote(buffer.at[me], buffer.at[me], send_sem.at[r], recv_sem.at[me], peer_of(r)))

        def gather(buffer, me, send_sem, recv_sem, peer_of, count):
            for r in range(1, count):
                other = lax.rem(me + r, count)
                remote(
                    buffer.at[other], buffer.at[other], send_sem.at[r], recv_sem.at[other], peer_of(r)
                ).wait_recv()
            value = buffer[0]
            for i in range(1, count):
                value = value + buffer[i]
            return value

        lax.fori_loop(0, nz, grid_step, 0)

        begin = gal_chan[...] - SW - (j * width + here)
        shift_hot = (iota((shifts, ngal), 0) == quarter - 1 - begin).astype(f32).astype(bf16)
        gal_row = jnp.broadcast_to(gal_pix[...], (TAPS, ngal))
        fill(
            pixel_hot, 0, gal_row >> 4,
            jnp.where((gal_row & (TAPS - 1)) == iota((TAPS, ngal), 0), 1.0, 0.0).astype(f32),
        )
        counts[...] = lax.dot_general(
            shift_hot, pixel_hot[...], (((1,), (1,)), ((), ())), preferred_element_type=f32
        ).astype(bf16)

        long_step(1)
        short_step(1)

        wide = jnp.concatenate(
            [
                jnp.dot(counts[...], part[...].astype(bf16), preferred_element_type=f32),
                jnp.zeros((shifts, 512 - quarter), f32),
            ],
            axis=1,
        )
        folded = jnp.zeros((8, 512), f32)
        for i in range(shifts // 8):
            folded = folded + pltpu.roll(
                wide[8 * i:8 * i + 8], (513 - quarter + 8 * i) % 512, 1
            )
        window = jnp.zeros((1, 512), f32)
        for i in range(8):
            window = window + (pltpu.roll(folded[i:i + 1], i, 1) if i else folded[i:i + 1])
        st1[x] = window[:, :2 * SW]
        share(st1, x, st1_s, st1_r, x_peer, NX)

        long_step(2)
        st2[j] = gather(st1, x, st1_s, st1_r, x_peer, NX)
        share(st2, j, st2_s, st2_r, c_peer, chan_size)
        for copy in sends:
            copy.wait_send()
        sends.clear()

        got = [z_take(way, 2 * far - 2) for way in range(2)]
        for way in range(2):
            value = z_take(way, far - 1) + got[1 - way] + part_half(0, way)
            final[way * half:(way + 1) * half, :] = value.astype(bf16)
        for r in (2, 1, 3):
            row = pl.multiple_of(lax.rem(x + r, NX) * TP, TP)
            start(remote(
                final.at[pl.ds(row, TP), :], sky.at[:, pl.ds(here, quarter)], fin_s.at[r],
                fin_r.at[NX - r], x_peer(r),
            ))
        sky[:, pl.ds(here, quarter)] = final[pl.ds(pl.multiple_of(x * TP, TP), TP), :]

        st3[z] = gather(st2, j, st2_s, st2_r, c_peer, chan_size)
        share(st3, z, st3_s, st3_r, z_peer, nz)
        for way in range(2):
            for index in range(2 * far - 1):
                z_copy(way, index).wait_send()
        for r in range(1, NX):
            column = pl.multiple_of(lax.rem(x + r, NX) * quarter, quarter)
            remote(
                final.at[pl.ds(0, TP), :], sky.at[:, pl.ds(column, quarter)], fin_s.at[r],
                fin_r.at[r], x_peer(r),
            ).wait_recv()
        stacked[...] = gather(st3, z, st3_s, st3_r, z_peer, nz) / ngal
        for copy in sends:
            copy.wait_send()

    dma = pltpu.SemaphoreType.DMA
    scratch = [
        pltpu.VMEM((rows, width), bf16),
        pltpu.VMEM((1, width), f32),
        pltpu.VMEM((1, nblocks), jnp.int32),
        pltpu.VMEM((1, rows), jnp.int32),
        pltpu.VMEM((1, TAPS), bf16),
        pltpu.VMEM((1, ngal), jnp.int32),
        pltpu.VMEM((1, ngal), jnp.int32),
        pltpu.VMEM((MODES, width), f32),
        pltpu.VMEM((NX, 1, rows), jnp.int32),
        pltpu.VMEM((NX, rows, quarter), bf16),
        pltpu.VMEM((chan_size, MODES, 128), f32),
        pltpu.VMEM((chan_size, MODES, rows), f32),
        pltpu.VMEM((128, rows), f32),
        pltpu.VMEM((NX, MODES, rows), f32),
        pltpu.VMEM((npix, NX * rows), bf16),
        pltpu.VMEM((NX * rows, quarter), f32),
        pltpu.VMEM((NX * rows, quarter), bf16),
        pltpu.VMEM((npix, quarter), f32),
        pltpu.VMEM((npix, ngal), bf16),
        pltpu.VMEM((shifts, npix), bf16),
        pltpu.VMEM((2, nz - 1, half, quarter), bf16),
        pltpu.VMEM((2, nz - 1, half, quarter), bf16),
        pltpu.VMEM((zpix, quarter), bf16),
        pltpu.VMEM((NX, 1, 2 * SW), f32),
        pltpu.VMEM((chan_size, 1, 2 * SW), f32),
        pltpu.VMEM((nz, 1, 2 * SW), f32),
        dma((8,)),
    ]
    for shape in (
        (NX,), (NX,), (chan_size,), (chan_size,), (NX,), (2, nz - 1), (NX,),
        (NX,), (chan_size,), (nz,),
    ):
        scratch += [dma(shape), dma(shape)]
    return kernel, scratch


def solution(mesh):
    tm_size, chan_size = mesh.shape["tm"], mesh.shape["chan"]

    def per_device(spectra, chan_weight, routes, offsets, taps, gal_pix, gal_chan):
        rows, width = spectra.shape
        nblocks = routes.shape[0]
        kernel, scratch = make_kernel(
            tm_size, chan_size, rows, width, nblocks, gal_pix.shape[0]
        )
        vmem = pl.BlockSpec(memory_space=pltpu.VMEM)
        sky, stacked = pl.pallas_call(
            kernel,
            out_shape=(
                jax.ShapeDtypeStruct((TP, width), bf16),
                jax.ShapeDtypeStruct((1, 2 * SW), f32),
            ),
            in_specs=[pl.BlockSpec(memory_space=pl.ANY)] * 8,
            out_specs=(vmem, vmem),
            scratch_shapes=scratch,
            compiler_params=pltpu.CompilerParams(
                collective_id=0, has_side_effects=True, vmem_limit_bytes=54880 * 1024
            ),
        )(
            spectra, chan_weight[None, :], routes.reshape(1, nblocks), offsets[None, :],
            taps[None, :], gal_pix[None, :], gal_chan[None, :],
            jnp.asarray(basis_table(width * chan_size)),
        )
        return sky, stacked[0]

    in_specs = (
        P("tm", "chan"), P("chan"), P("tm", None), P("tm"), P(None), P(None), P(None)
    )
    return jax.shard_map(
        per_device, mesh=mesh, in_specs=in_specs, out_specs=(P("tm", "chan"), P(None)),
        check_vma=False,
    )
```

```python
import jax
import jax.numpy as jnp
import numpy as np
from jax import lax
from jax.experimental import pallas as pl
from jax.experimental.pallas import tpu as pltpu
from jax.sharding import PartitionSpec as P

KMODES = 8
MODES = 2 * KMODES
TP = 64
MARGIN = 8
SW = 64
TAPS = 16
NX = 4

highest = lax.Precision.HIGHEST
MESH = pl.DeviceIdType.MESH
f32 = jnp.float32
bf16 = jnp.bfloat16


def basis_table(total):
    orders = np.arange(1, KMODES + 1)[:, None]
    phase = (orders * np.arange(total)[None, :] % total) * (2 * np.pi / total)
    return np.concatenate([np.cos(phase), np.sin(phase)], axis=0).astype(np.float32)


def split3(value):
    high = value.astype(bf16)
    rest = value - high.astype(f32)
    mid = rest.astype(bf16)
    low = (rest - mid.astype(f32)).astype(bf16)
    return high, mid, low


def iota(shape, dim):
    return lax.broadcasted_iota(jnp.int32, shape, dim)


def make_kernel(tm_size, chan_size, rows, width, nblocks, ngal):
    nz = tm_size // NX
    quarter = width // NX
    npix = tm_size * TP
    zpix = NX * TP
    half = zpix // 2
    block_rows = rows // nblocks
    shifts = quarter + 2 * SW
    far = nz // 2

    def kernel(
        spec, weight_in, routes_in, offsets_in, taps_in, gal_pix_in, gal_chan_in, basis_in,
        sky, stacked,
        own, weight, routes, offsets, taps, gal_pix, gal_chan, basis,
        pix, raw, gram, proj, ext, coef, band, ripple, clean, part, pixel_hot, counts,
        zsend, zrecv, final, st1, st2, st3,
        load_sem, pix_s, pix_r, raw_s, raw_r, gram_s, gram_r, proj_s, proj_r, coef_s, coef_r,
        z_s, z_r, fin_s, fin_r, st1_s, st1_r, st2_s, st2_r, st3_s, st3_r,
    ):
        tm = lax.axis_index("tm")
        j = lax.axis_index("chan")
        z = lax.div(tm, NX)
        x = lax.rem(tm, NX)
        here = pl.multiple_of(x * quarter, quarter)

        def x_peer(r):
            return (z * NX + lax.rem(x + r, NX), j)

        def c_peer(r):
            return (tm, lax.rem(j + r, chan_size))

        def z_peer(r):
            return (lax.rem(z + r, nz) * NX + x, j)

        def remote(src, dst, send_sem, recv_sem, peer):
            return pltpu.make_async_remote_copy(
                src_ref=src, dst_ref=dst, send_sem=send_sem, recv_sem=recv_sem,
                device_id=peer, device_id_type=MESH,
            )

        sends = []

        def start(copy):
            copy.start()
            sends.append(copy)

        peers = (
            [x_peer(r) for r in range(1, NX)]
            + [c_peer(r) for r in range(1, chan_size)]
            + [z_peer(r) for r in range(1, nz)]
        )
        barrier = pltpu.get_barrier_semaphore()
        for peer in peers:
            pl.semaphore_signal(barrier, inc=1, device_id=peer, device_id_type=MESH)
        basis_here = basis_in.at[:, pl.ds(pl.multiple_of(j * width, width), width)]
        loads = [
            pltpu.make_async_copy(source, target, load_sem.at[i])
            for i, (source, target) in enumerate((
                (spec, own), (weight_in, weight), (basis_here, basis), (routes_in, routes),
                (offsets_in, offsets), (taps_in, taps), (gal_pix_in, gal_pix),
                (gal_chan_in, gal_chan),
            ))
        ]
        for load in loads:
            load.start()
        pl.semaphore_wait(barrier, len(peers))

        loads[0].wait()
        for r in (2, 1, 3):
            column = pl.multiple_of(lax.rem(x + r, NX) * quarter, quarter)
            start(remote(
                own.at[:, pl.ds(column, quarter)], raw.at[NX - r], raw_s.at[r], raw_r.at[NX - r],
                x_peer(r),
            ))

        loads[1].wait()
        loads[2].wait()
        weighted = basis[...] * weight[...]
        gram[0] = jnp.zeros((MODES, 128), f32)
        gram[0, :, 0:MODES] = lax.dot_general(
            weighted, basis[...], (((1,), (1,)), ((), ())), precision=highest,
            preferred_element_type=f32,
        )
        for r in range(1, chan_size):
            start(remote(
                gram.at[0], gram.at[chan_size - r], gram_s.at[r], gram_r.at[chan_size - r],
                c_peer(r),
            ))
        w_stack = jnp.concatenate(split3(weighted), axis=0)
        products = lax.dot_general(
            w_stack, own[...], (((1,), (1,)), ((), ())), preferred_element_type=f32
        )
        proj[0] = products[:MODES] + products[MODES:2 * MODES] + products[2 * MODES:]
        for r in range(1, chan_size):
            start(remote(
                proj.at[0], proj.at[chan_size - r], proj_s.at[r], proj_r.at[chan_size - r],
                c_peer(r),
            ))

        for i in (3, 4, 5, 6, 7):
            loads[i].wait()
        inside = iota((nblocks, rows), 1) - block_rows * iota((nblocks, rows), 0)
        owner = ((inside >= 0) & (inside < block_rows)).astype(f32).astype(bf16)
        tile = jnp.dot(
            jnp.broadcast_to(routes[...], (16, nblocks)).astype(f32).astype(bf16), owner,
            preferred_element_type=f32,
        )[0:1].astype(jnp.int32)
        pix[0] = tile * TP + offsets[...] - MARGIN
        for r in range(1, NX):
            start(remote(pix.at[0], pix.at[NX - r], pix_s.at[r], pix_r.at[NX - r], x_peer(r)))

        def fill(target, column, group, tap):
            def step(a, carry):
                row = pl.multiple_of(a * TAPS, TAPS)
                target[pl.ds(row, TAPS), column:column + tap.shape[1]] = jnp.where(
                    group == a, tap, 0.0
                ).astype(bf16)
                return carry

            lax.fori_loop(0, npix // TAPS, step, 0, unroll=4)

        def build_band(slot):
            first = pix[slot]
            group = jnp.broadcast_to(first >> 4, (TAPS, rows))
            inner = jnp.broadcast_to(first & (TAPS - 1), (TAPS, rows))
            lane = iota((TAPS, rows), 0)
            turn = (lane - inner) & (TAPS - 1)
            tap = jnp.zeros((TAPS, rows), f32)
            values = taps[...].astype(f32)
            for m in range(TAPS):
                tap = jnp.where(turn == m, values[0:1, m:m + 1], tap)
            fill(band, slot * rows, jnp.where(lane < inner, group + 1, group), tap)

        build_band(0)

        for r in range(1, chan_size):
            remote(gram.at[0], gram.at[r], gram_s.at[r], gram_r.at[r], c_peer(r)).wait_recv()
        total = gram[0]
        for r in range(1, chan_size):
            total = total + gram[r]
        row_id = iota((MODES, 128), 0)
        both = jnp.where(iota((MODES, 128), 1) - MODES == row_id, 1.0, total)
        for i in range(MODES):
            pivot = both[i:i + 1, :] / both[i:i + 1, i:i + 1]
            both = jnp.where(row_id == i, pivot, both - both[:, i:i + 1] * pivot)

        ext[...] = jnp.zeros(ext.shape, f32)
        for r in range(1, chan_size):
            remote(proj.at[0], proj.at[r], proj_s.at[r], proj_r.at[r], c_peer(r)).wait_recv()
        full = proj[0]
        for r in range(1, chan_size):
            full = full + proj[r]
        ext[MODES:2 * MODES, :] = full
        coef[0] = jnp.dot(both, ext[...], precision=highest, preferred_element_type=f32)
        for r in range(1, NX):
            start(remote(coef.at[0], coef.at[NX - r], coef_s.at[r], coef_r.at[NX - r], x_peer(r)))

        b_high, b_mid, b_low = split3(basis[:, pl.ds(here, quarter)])
        b_stack = jnp.concatenate(
            [b_high, b_mid, b_high, b_mid, b_low, b_high, jnp.zeros((2 * MODES, quarter), bf16)],
            axis=0,
        )

        def fit_slot(slot):
            c_high, c_mid, c_low = split3(coef[slot])
            c_stack = jnp.concatenate(
                [c_high, c_high, c_mid, c_mid, c_high, c_low, jnp.zeros((2 * MODES, rows), bf16)],
                axis=0,
            )
            ripple[slot * rows:(slot + 1) * rows, :] = lax.dot_general(
                c_stack, b_stack, (((0,), (0,)), ((), ())), preferred_element_type=f32
            )

        def clean_slot(slot, values):
            clean[slot * rows:(slot + 1) * rows, :] = (
                values.astype(f32) - ripple[slot * rows:(slot + 1) * rows, :]
            ).astype(bf16)

        fit_slot(0)
        clean_slot(0, own[:, pl.ds(here, quarter)])
        for r in range(1, NX):
            remote(pix.at[0], pix.at[r], pix_s.at[r], pix_r.at[r], x_peer(r)).wait_recv()
            build_band(r)
        for r in (1, 3, 2):
            remote(coef.at[0], coef.at[r], coef_s.at[r], coef_r.at[r], x_peer(r)).wait_recv()
            fit_slot(r)
        for r in (1, 3, 2):
            remote(
                own.at[:, pl.ds(0, quarter)], raw.at[r], raw_s.at[r], raw_r.at[r], x_peer(r)
            ).wait_recv()
            clean_slot(r, raw[r])

        def chunk_row(step):
            return pl.multiple_of(lax.rem(z + step + 2 * nz, nz) * zpix, zpix)

        def part_half(step, which):
            row = pl.multiple_of(chunk_row(step) + which * half, half)
            return part[pl.ds(row, half), :]

        def z_copy(way, index):
            return remote(
                zsend.at[way, index], zrecv.at[way, index], z_s.at[way, index],
                z_r.at[way, index], z_peer((1, nz - 1)[way]),
            )

        def z_start(way, index, value):
            zsend[way, index] = value.astype(bf16)
            z_copy(way, index).start()

        def z_take(way, index):
            z_copy(way, index).wait_recv()
            return zrecv[way, index].astype(f32)

        sign = (1, -1)

        def long_step(k):
            for way in range(2):
                got = z_take(way, k)
                z_start(way, k + 1, got + part_half(sign[way] * (far - 1 - k), way))

        def short_step(k):
            for way in range(2):
                got = z_take(way, far + k)
                z_start(
                    way, far + k + 1, got + part_half(sign[way] * (far - 2 - k), 1 - way)
                )

        def grid_step(n, carry):
            away = lax.div(n + 1, 2)
            row = chunk_row(far + away - 2 * lax.rem(n, 2) * away)
            part[pl.ds(row, zpix), :] = jnp.dot(
                band[pl.ds(row, zpix), :], clean[...], preferred_element_type=f32
            )

            @pl.when(n == 0)
            def _():
                for way in range(2):
                    z_start(way, 0, part_half(far, way))

            @pl.when(n == 2)
            def _():
                for way in range(2):
                    z_start(way, far, part_half(sign[way] * (far - 1), 1 - way))

            @pl.when(n == 4)
            def _():
                long_step(0)
                short_step(0)

            return carry

        def share(buffer, me, send_sem, recv_sem, peer_of, count):
            for r in range(1, count):
                start(remote(buffer.at[me], buffer.at[me], send_sem.at[r], recv_sem.at[me], peer_of(r)))

        def gather(buffer, me, send_sem, recv_sem, peer_of, count):
            for r in range(1, count):
                other = lax.rem(me + r, count)
                remote(
                    buffer.at[other], buffer.at[other], send_sem.at[r], recv_sem.at[other], peer_of(r)
                ).wait_recv()
            value = buffer[0]
            for i in range(1, count):
                value = value + buffer[i]
            return value

        lax.fori_loop(0, nz, grid_step, 0)

        begin = gal_chan[...] - SW - (j * width + here)
        shift_hot = (iota((shifts, ngal), 0) == quarter - 1 - begin).astype(f32).astype(bf16)
        gal_row = jnp.broadcast_to(gal_pix[...], (TAPS, ngal))
        fill(
            pixel_hot, 0, gal_row >> 4,
            jnp.where((gal_row & (TAPS - 1)) == iota((TAPS, ngal), 0), 1.0, 0.0).astype(f32),
        )
        counts[...] = lax.dot_general(
            shift_hot, pixel_hot[...], (((1,), (1,)), ((), ())), preferred_element_type=f32
        ).astype(bf16)

        long_step(1)
        short_step(1)

        wide = jnp.concatenate(
            [
                jnp.dot(counts[...], part[...].astype(bf16), preferred_element_type=f32),
                jnp.zeros((shifts, 512 - quarter), f32),
            ],
            axis=1,
        )
        folded = jnp.zeros((8, 512), f32)
        for i in range(shifts // 8):
            folded = folded + pltpu.roll(
                wide[8 * i:8 * i + 8], (513 - quarter + 8 * i) % 512, 1
            )
        window = jnp.zeros((1, 512), f32)
        for i in range(8):
            window = window + (pltpu.roll(folded[i:i + 1], i, 1) if i else folded[i:i + 1])
        st1[x] = window[:, :2 * SW]
        share(st1, x, st1_s, st1_r, x_peer, NX)

        long_step(2)
        st2[j] = gather(st1, x, st1_s, st1_r, x_peer, NX)
        share(st2, j, st2_s, st2_r, c_peer, chan_size)
        for copy in sends:
            copy.wait_send()
        sends.clear()

        got = [z_take(way, 2 * far - 2) for way in range(2)]
        for way in range(2):
            value = z_take(way, far - 1) + got[1 - way] + part_half(0, way)
            final[way * half:(way + 1) * half, :] = value.astype(bf16)
        for r in (2, 1, 3):
            row = pl.multiple_of(lax.rem(x + r, NX) * TP, TP)
            start(remote(
                final.at[pl.ds(row, TP), :], sky.at[:, pl.ds(here, quarter)], fin_s.at[r],
                fin_r.at[NX - r], x_peer(r),
            ))
        sky[:, pl.ds(here, quarter)] = final[pl.ds(pl.multiple_of(x * TP, TP), TP), :]

        st3[z] = gather(st2, j, st2_s, st2_r, c_peer, chan_size)
        share(st3, z, st3_s, st3_r, z_peer, nz)
        for way in range(2):
            for index in range(2 * far - 1):
                z_copy(way, index).wait_send()
        for r in range(1, NX):
            column = pl.multiple_of(lax.rem(x + r, NX) * quarter, quarter)
            remote(
                final.at[pl.ds(0, TP), :], sky.at[:, pl.ds(column, quarter)], fin_s.at[r],
                fin_r.at[r], x_peer(r),
            ).wait_recv()
        stacked[...] = gather(st3, z, st3_s, st3_r, z_peer, nz) / ngal
        for copy in sends:
            copy.wait_send()

    dma = pltpu.SemaphoreType.DMA
    scratch = [
        pltpu.VMEM((rows, width), bf16),
        pltpu.VMEM((1, width), f32),
        pltpu.VMEM((1, nblocks), jnp.int32),
        pltpu.VMEM((1, rows), jnp.int32),
        pltpu.VMEM((1, TAPS), bf16),
        pltpu.VMEM((1, ngal), jnp.int32),
        pltpu.VMEM((1, ngal), jnp.int32),
        pltpu.VMEM((MODES, width), f32),
        pltpu.VMEM((NX, 1, rows), jnp.int32),
        pltpu.VMEM((NX, rows, quarter), bf16),
        pltpu.VMEM((chan_size, MODES, 128), f32),
        pltpu.VMEM((chan_size, MODES, rows), f32),
        pltpu.VMEM((128, rows), f32),
        pltpu.VMEM((NX, MODES, rows), f32),
        pltpu.VMEM((npix, NX * rows), bf16),
        pltpu.VMEM((NX * rows, quarter), f32),
        pltpu.VMEM((NX * rows, quarter), bf16),
        pltpu.VMEM((npix, quarter), f32),
        pltpu.VMEM((npix, ngal), bf16),
        pltpu.VMEM((shifts, npix), bf16),
        pltpu.VMEM((2, nz - 1, half, quarter), bf16),
        pltpu.VMEM((2, nz - 1, half, quarter), bf16),
        pltpu.VMEM((zpix, quarter), bf16),
        pltpu.VMEM((NX, 1, 2 * SW), f32),
        pltpu.VMEM((chan_size, 1, 2 * SW), f32),
        pltpu.VMEM((nz, 1, 2 * SW), f32),
        dma((8,)),
    ]
    for shape in (
        (NX,), (NX,), (chan_size,), (chan_size,), (NX,), (2, nz - 1), (NX,),
        (NX,), (chan_size,), (nz,),
    ):
        scratch += [dma(shape), dma(shape)]
    return kernel, scratch


def solution(mesh):
    tm_size, chan_size = mesh.shape["tm"], mesh.shape["chan"]

    def per_device(spectra, chan_weight, routes, offsets, taps, gal_pix, gal_chan):
        rows, width = spectra.shape
        nblocks = routes.shape[0]
        kernel, scratch = make_kernel(
            tm_size, chan_size, rows, width, nblocks, gal_pix.shape[0]
        )
        vmem = pl.BlockSpec(memory_space=pltpu.VMEM)
        sky, stacked = pl.pallas_call(
            kernel,
            out_shape=(
                jax.ShapeDtypeStruct((TP, width), bf16),
                jax.ShapeDtypeStruct((1, 2 * SW), f32),
            ),
            in_specs=[pl.BlockSpec(memory_space=pl.ANY)] * 8,
            out_specs=(vmem, vmem),
            scratch_shapes=scratch,
            compiler_params=pltpu.CompilerParams(
                collective_id=0, has_side_effects=True, vmem_limit_bytes=54880 * 1024
            ),
        )(
            spectra, chan_weight[None, :], routes.reshape(1, nblocks), offsets[None, :],
            taps[None, :], gal_pix[None, :], gal_chan[None, :],
            jnp.asarray(basis_table(width * chan_size)),
        )
        return sky, stacked[0]

    in_specs = (
        P("tm", "chan"), P("chan"), P("tm", None), P("tm"), P(None), P(None), P(None)
    )
    return jax.shard_map(
        per_device, mesh=mesh, in_specs=in_specs, out_specs=(P("tm", "chan"), P(None)),
        check_vma=False,
    )
```

```python
import jax
import jax.numpy as jnp
import numpy as np
from jax import lax
from jax.experimental import pallas as pl
from jax.experimental.pallas import tpu as pltpu
from jax.sharding import PartitionSpec as P

KMODES = 8
MODES = 2 * KMODES
TP = 64
MARGIN = 8
SW = 64
TAPS = 16
NX = 4

highest = lax.Precision.HIGHEST
MESH = pl.DeviceIdType.MESH
f32 = jnp.float32
bf16 = jnp.bfloat16


def basis_table(total):
    orders = np.arange(1, KMODES + 1)[:, None]
    phase = (orders * np.arange(total)[None, :] % total) * (2 * np.pi / total)
    return np.concatenate([np.cos(phase), np.sin(phase)], axis=0).astype(np.float32)


def split3(value):
    high = value.astype(bf16)
    rest = value - high.astype(f32)
    mid = rest.astype(bf16)
    low = (rest - mid.astype(f32)).astype(bf16)
    return high, mid, low


def iota(shape, dim):
    return lax.broadcasted_iota(jnp.int32, shape, dim)


def make_kernel(tm_size, chan_size, rows, width, nblocks, ngal):
    nz = tm_size // NX
    quarter = width // NX
    npix = tm_size * TP
    zpix = NX * TP
    half = zpix // 2
    block_rows = rows // nblocks
    shifts = quarter + 2 * SW
    far = nz // 2

    def kernel(
        spec, weight_in, routes_in, offsets_in, taps_in, gal_pix_in, gal_chan_in, basis_in,
        sky, stacked,
        own, weight, routes, offsets, taps, gal_pix, gal_chan, basis,
        pix, raw, gram, proj, ext, coef, band, ripple, clean, part, pixel_hot, counts,
        zsend, zrecv, final, st1, st2, st3,
        load_sem, pix_s, pix_r, raw_s, raw_r, gram_s, gram_r, proj_s, proj_r, coef_s, coef_r,
        z_s, z_r, fin_s, fin_r, st1_s, st1_r, st2_s, st2_r, st3_s, st3_r,
    ):
        tm = lax.axis_index("tm")
        j = lax.axis_index("chan")
        z = lax.div(tm, NX)
        x = lax.rem(tm, NX)
        here = pl.multiple_of(x * quarter, quarter)

        def x_peer(r):
            return (z * NX + lax.rem(x + r, NX), j)

        def c_peer(r):
            return (tm, lax.rem(j + r, chan_size))

        def z_peer(r):
            return (lax.rem(z + r, nz) * NX + x, j)

        def remote(src, dst, send_sem, recv_sem, peer):
            return pltpu.make_async_remote_copy(
                src_ref=src, dst_ref=dst, send_sem=send_sem, recv_sem=recv_sem,
                device_id=peer, device_id_type=MESH,
            )

        sends = []

        def start(copy):
            copy.start()
            sends.append(copy)

        peers = (
            [x_peer(r) for r in range(1, NX)]
            + [c_peer(r) for r in range(1, chan_size)]
            + [z_peer(r) for r in range(1, nz)]
        )
        barrier = pltpu.get_barrier_semaphore()
        for peer in peers:
            pl.semaphore_signal(barrier, inc=1, device_id=peer, device_id_type=MESH)
        basis_here = basis_in.at[:, pl.ds(pl.multiple_of(j * width, width), width)]
        loads = [
            pltpu.make_async_copy(source, target, load_sem.at[i])
            for i, (source, target) in enumerate((
                (spec, own), (weight_in, weight), (basis_here, basis), (routes_in, routes),
                (offsets_in, offsets), (taps_in, taps), (gal_pix_in, gal_pix),
                (gal_chan_in, gal_chan),
            ))
        ]
        for load in loads:
            load.start()
        pl.semaphore_wait(barrier, len(peers))

        loads[0].wait()
        for r in (2, 1, 3):
            column = pl.multiple_of(lax.rem(x + r, NX) * quarter, quarter)
            start(remote(
                own.at[:, pl.ds(column, quarter)], raw.at[NX - r], raw_s.at[r], raw_r.at[NX - r],
                x_peer(r),
            ))

        loads[1].wait()
        loads[2].wait()
        weighted = basis[...] * weight[...]
        gram[0] = jnp.zeros((MODES, 128), f32)
        gram[0, :, 0:MODES] = lax.dot_general(
            weighted, basis[...], (((1,), (1,)), ((), ())), precision=highest,
            preferred_element_type=f32,
        )
        for r in range(1, chan_size):
            start(remote(
                gram.at[0], gram.at[chan_size - r], gram_s.at[r], gram_r.at[chan_size - r],
                c_peer(r),
            ))
        w_stack = jnp.concatenate(split3(weighted), axis=0)
        products = lax.dot_general(
            w_stack, own[...], (((1,), (1,)), ((), ())), preferred_element_type=f32
        )
        proj[0] = products[:MODES] + products[MODES:2 * MODES] + products[2 * MODES:]
        for r in range(1, chan_size):
            start(remote(
                proj.at[0], proj.at[chan_size - r], proj_s.at[r], proj_r.at[chan_size - r],
                c_peer(r),
            ))

        for i in (3, 4, 5, 6, 7):
            loads[i].wait()
        inside = iota((nblocks, rows), 1) - block_rows * iota((nblocks, rows), 0)
        owner = ((inside >= 0) & (inside < block_rows)).astype(f32).astype(bf16)
        tile = jnp.dot(
            jnp.broadcast_to(routes[...], (16, nblocks)).astype(f32).astype(bf16), owner,
            preferred_element_type=f32,
        )[0:1].astype(jnp.int32)
        pix[0] = tile * TP + offsets[...] - MARGIN
        for r in range(1, NX):
            start(remote(pix.at[0], pix.at[NX - r], pix_s.at[r], pix_r.at[NX - r], x_peer(r)))

        def fill(target, column, group, tap):
            def step(a, carry):
                row = pl.multiple_of(a * TAPS, TAPS)
                target[pl.ds(row, TAPS), column:column + tap.shape[1]] = jnp.where(
                    group == a, tap, 0.0
                ).astype(bf16)
                return carry

            lax.fori_loop(0, npix // TAPS, step, 0, unroll=4)

        def build_band(slot):
            first = pix[slot]
            group = jnp.broadcast_to(first >> 4, (TAPS, rows))
            inner = jnp.broadcast_to(first & (TAPS - 1), (TAPS, rows))
            lane = iota((TAPS, rows), 0)
            turn = (lane - inner) & (TAPS - 1)
            tap = jnp.zeros((TAPS, rows), f32)
            values = taps[...].astype(f32)
            for m in range(TAPS):
                tap = jnp.where(turn == m, values[0:1, m:m + 1], tap)
            fill(band, slot * rows, jnp.where(lane < inner, group + 1, group), tap)

        build_band(0)

        for r in range(1, chan_size):
            remote(gram.at[0], gram.at[r], gram_s.at[r], gram_r.at[r], c_peer(r)).wait_recv()
        total = gram[0]
        for r in range(1, chan_size):
            total = total + gram[r]
        row_id = iota((MODES, 128), 0)
        both = jnp.where(iota((MODES, 128), 1) - MODES == row_id, 1.0, total)
        for i in range(MODES):
            pivot = both[i:i + 1, :] / both[i:i + 1, i:i + 1]
            both = jnp.where(row_id == i, pivot, both - both[:, i:i + 1] * pivot)

        ext[...] = jnp.zeros(ext.shape, f32)
        for r in range(1, chan_size):
            remote(proj.at[0], proj.at[r], proj_s.at[r], proj_r.at[r], c_peer(r)).wait_recv()
        full = proj[0]
        for r in range(1, chan_size):
            full = full + proj[r]
        ext[MODES:2 * MODES, :] = full
        coef[0] = jnp.dot(both, ext[...], precision=highest, preferred_element_type=f32)
        for r in range(1, NX):
            start(remote(coef.at[0], coef.at[NX - r], coef_s.at[r], coef_r.at[NX - r], x_peer(r)))

        b_high, b_mid, b_low = split3(basis[:, pl.ds(here, quarter)])
        b_stack = jnp.concatenate(
            [b_high, b_mid, b_high, b_mid, b_low, b_high, jnp.zeros((2 * MODES, quarter), bf16)],
            axis=0,
        )

        def fit_slot(slot):
            c_high, c_mid, c_low = split3(coef[slot])
            c_stack = jnp.concatenate(
                [c_high, c_high, c_mid, c_mid, c_high, c_low, jnp.zeros((2 * MODES, rows), bf16)],
                axis=0,
            )
            ripple[slot * rows:(slot + 1) * rows, :] = lax.dot_general(
                c_stack, b_stack, (((0,), (0,)), ((), ())), preferred_element_type=f32
            )

        def clean_slot(slot, values):
            clean[slot * rows:(slot + 1) * rows, :] = (
                values.astype(f32) - ripple[slot * rows:(slot + 1) * rows, :]
            ).astype(bf16)

        fit_slot(0)
        clean_slot(0, own[:, pl.ds(here, quarter)])
        begin = gal_chan[...] - SW - (j * width + here)
        shift_hot = (iota((shifts, ngal), 0) == quarter - 1 - begin).astype(f32).astype(bf16)
        gal_row = jnp.broadcast_to(gal_pix[...], (TAPS, ngal))
        fill(
            pixel_hot, 0, gal_row >> 4,
            jnp.where((gal_row & (TAPS - 1)) == iota((TAPS, ngal), 0), 1.0, 0.0).astype(f32),
        )
        counts[...] = lax.dot_general(
            shift_hot, pixel_hot[...], (((1,), (1,)), ((), ())), preferred_element_type=f32
        ).astype(bf16)

        for r in range(1, NX):
            remote(pix.at[0], pix.at[r], pix_s.at[r], pix_r.at[r], x_peer(r)).wait_recv()
            build_band(r)
        for r in (1, 3, 2):
            remote(coef.at[0], coef.at[r], coef_s.at[r], coef_r.at[r], x_peer(r)).wait_recv()
            fit_slot(r)
        for r in (1, 3, 2):
            remote(
                own.at[:, pl.ds(0, quarter)], raw.at[r], raw_s.at[r], raw_r.at[r], x_peer(r)
            ).wait_recv()
            clean_slot(r, raw[r])

        def chunk_row(step):
            return pl.multiple_of(lax.rem(z + step + 2 * nz, nz) * zpix, zpix)

        def part_half(step, which):
            row = pl.multiple_of(chunk_row(step) + which * half, half)
            return part[pl.ds(row, half), :]

        def z_copy(way, index):
            return remote(
                zsend.at[way, index], zrecv.at[way, index], z_s.at[way, index],
                z_r.at[way, index], z_peer((1, nz - 1)[way]),
            )

        def z_start(way, index, value):
            zsend[way, index] = value.astype(bf16)
            z_copy(way, index).start()

        def z_take(way, index):
            z_copy(way, index).wait_recv()
            return zrecv[way, index].astype(f32)

        sign = (1, -1)

        def long_step(k):
            for way in range(2):
                got = z_take(way, k)
                z_start(way, k + 1, got + part_half(sign[way] * (far - 1 - k), way))

        def short_step(k):
            for way in range(2):
                got = z_take(way, far + k)
                z_start(
                    way, far + k + 1, got + part_half(sign[way] * (far - 2 - k), 1 - way)
                )

        def grid_step(n, carry):
            away = lax.div(n + 1, 2)
            row = chunk_row(far + away - 2 * lax.rem(n, 2) * away)
            part[pl.ds(row, zpix), :] = jnp.dot(
                band[pl.ds(row, zpix), :], clean[...], preferred_element_type=f32
            )

            @pl.when(n == 0)
            def _():
                for way in range(2):
                    z_start(way, 0, part_half(far, way))

            @pl.when(n == 2)
            def _():
                for way in range(2):
                    z_start(way, far, part_half(sign[way] * (far - 1), 1 - way))

            @pl.when(n == 4)
            def _():
                long_step(0)
                short_step(0)

            return carry

        def share(buffer, me, send_sem, recv_sem, peer_of, count):
            for r in range(1, count):
                start(remote(buffer.at[me], buffer.at[me], send_sem.at[r], recv_sem.at[me], peer_of(r)))

        def gather(buffer, me, send_sem, recv_sem, peer_of, count):
            for r in range(1, count):
                other = lax.rem(me + r, count)
                remote(
                    buffer.at[other], buffer.at[other], send_sem.at[r], recv_sem.at[other], peer_of(r)
                ).wait_recv()
            value = buffer[0]
            for i in range(1, count):
                value = value + buffer[i]
            return value

        lax.fori_loop(0, nz, grid_step, 0)

        long_step(1)
        short_step(1)

        wide = jnp.concatenate(
            [
                jnp.dot(counts[...], part[...].astype(bf16), preferred_element_type=f32),
                jnp.zeros((shifts, 512 - quarter), f32),
            ],
            axis=1,
        )
        folded = jnp.zeros((8, 512), f32)
        for i in range(shifts // 8):
            folded = folded + pltpu.roll(
                wide[8 * i:8 * i + 8], (513 - quarter + 8 * i) % 512, 1
            )
        window = jnp.zeros((1, 512), f32)
        for i in range(8):
            window = window + (pltpu.roll(folded[i:i + 1], i, 1) if i else folded[i:i + 1])
        st1[x] = window[:, :2 * SW]
        share(st1, x, st1_s, st1_r, x_peer, NX)

        long_step(2)
        st2[j] = gather(st1, x, st1_s, st1_r, x_peer, NX)
        share(st2, j, st2_s, st2_r, c_peer, chan_size)
        for copy in sends:
            copy.wait_send()
        sends.clear()

        got = [z_take(way, 2 * far - 2) for way in range(2)]
        for way in range(2):
            value = z_take(way, far - 1) + got[1 - way] + part_half(0, way)
            final[way * half:(way + 1) * half, :] = value.astype(bf16)
        for r in (2, 1, 3):
            row = pl.multiple_of(lax.rem(x + r, NX) * TP, TP)
            start(remote(
                final.at[pl.ds(row, TP), :], sky.at[:, pl.ds(here, quarter)], fin_s.at[r],
                fin_r.at[NX - r], x_peer(r),
            ))
        sky[:, pl.ds(here, quarter)] = final[pl.ds(pl.multiple_of(x * TP, TP), TP), :]

        st3[z] = gather(st2, j, st2_s, st2_r, c_peer, chan_size)
        share(st3, z, st3_s, st3_r, z_peer, nz)
        for way in range(2):
            for index in range(2 * far - 1):
                z_copy(way, index).wait_send()
        for r in range(1, NX):
            column = pl.multiple_of(lax.rem(x + r, NX) * quarter, quarter)
            remote(
                final.at[pl.ds(0, TP), :], sky.at[:, pl.ds(column, quarter)], fin_s.at[r],
                fin_r.at[r], x_peer(r),
            ).wait_recv()
        stacked[...] = gather(st3, z, st3_s, st3_r, z_peer, nz) / ngal
        for copy in sends:
            copy.wait_send()

    dma = pltpu.SemaphoreType.DMA
    scratch = [
        pltpu.VMEM((rows, width), bf16),
        pltpu.VMEM((1, width), f32),
        pltpu.VMEM((1, nblocks), jnp.int32),
        pltpu.VMEM((1, rows), jnp.int32),
        pltpu.VMEM((1, TAPS), bf16),
        pltpu.VMEM((1, ngal), jnp.int32),
        pltpu.VMEM((1, ngal), jnp.int32),
        pltpu.VMEM((MODES, width), f32),
        pltpu.VMEM((NX, 1, rows), jnp.int32),
        pltpu.VMEM((NX, rows, quarter), bf16),
        pltpu.VMEM((chan_size, MODES, 128), f32),
        pltpu.VMEM((chan_size, MODES, rows), f32),
        pltpu.VMEM((128, rows), f32),
        pltpu.VMEM((NX, MODES, rows), f32),
        pltpu.VMEM((npix, NX * rows), bf16),
        pltpu.VMEM((NX * rows, quarter), f32),
        pltpu.VMEM((NX * rows, quarter), bf16),
        pltpu.VMEM((npix, quarter), f32),
        pltpu.VMEM((npix, ngal), bf16),
        pltpu.VMEM((shifts, npix), bf16),
        pltpu.VMEM((2, nz - 1, half, quarter), bf16),
        pltpu.VMEM((2, nz - 1, half, quarter), bf16),
        pltpu.VMEM((zpix, quarter), bf16),
        pltpu.VMEM((NX, 1, 2 * SW), f32),
        pltpu.VMEM((chan_size, 1, 2 * SW), f32),
        pltpu.VMEM((nz, 1, 2 * SW), f32),
        dma((8,)),
    ]
    for shape in (
        (NX,), (NX,), (chan_size,), (chan_size,), (NX,), (2, nz - 1), (NX,),
        (NX,), (chan_size,), (nz,),
    ):
        scratch += [dma(shape), dma(shape)]
    return kernel, scratch


def solution(mesh):
    tm_size, chan_size = mesh.shape["tm"], mesh.shape["chan"]

    def per_device(spectra, chan_weight, routes, offsets, taps, gal_pix, gal_chan):
        rows, width = spectra.shape
        nblocks = routes.shape[0]
        kernel, scratch = make_kernel(
            tm_size, chan_size, rows, width, nblocks, gal_pix.shape[0]
        )
        vmem = pl.BlockSpec(memory_space=pltpu.VMEM)
        sky, stacked = pl.pallas_call(
            kernel,
            out_shape=(
                jax.ShapeDtypeStruct((TP, width), bf16),
                jax.ShapeDtypeStruct((1, 2 * SW), f32),
            ),
            in_specs=[pl.BlockSpec(memory_space=pl.ANY)] * 8,
            out_specs=(vmem, vmem),
            scratch_shapes=scratch,
            compiler_params=pltpu.CompilerParams(
                collective_id=0, has_side_effects=True, vmem_limit_bytes=54880 * 1024
            ),
        )(
            spectra, chan_weight[None, :], routes.reshape(1, nblocks), offsets[None, :],
            taps[None, :], gal_pix[None, :], gal_chan[None, :],
            jnp.asarray(basis_table(width * chan_size)),
        )
        return sky, stacked[0]

    in_specs = (
        P("tm", "chan"), P("chan"), P("tm", None), P("tm"), P(None), P(None), P(None)
    )
    return jax.shard_map(
        per_device, mesh=mesh, in_specs=in_specs, out_specs=(P("tm", "chan"), P(None)),
        check_vma=False,
    )
```

```python
import jax
import jax.numpy as jnp
import numpy as np
from jax import lax
from jax.experimental import pallas as pl
from jax.experimental.pallas import tpu as pltpu
from jax.sharding import PartitionSpec as P

KMODES = 8
MODES = 2 * KMODES
TP = 64
MARGIN = 8
SW = 64
TAPS = 16
NX = 4

highest = lax.Precision.HIGHEST
MESH = pl.DeviceIdType.MESH
f32 = jnp.float32
bf16 = jnp.bfloat16


def basis_table(total):
    orders = np.arange(1, KMODES + 1)[:, None]
    phase = (orders * np.arange(total)[None, :] % total) * (2 * np.pi / total)
    return np.concatenate([np.cos(phase), np.sin(phase)], axis=0).astype(np.float32)


def split3(value):
    high = value.astype(bf16)
    rest = value - high.astype(f32)
    mid = rest.astype(bf16)
    low = (rest - mid.astype(f32)).astype(bf16)
    return high, mid, low


def iota(shape, dim):
    return lax.broadcasted_iota(jnp.int32, shape, dim)


def make_kernel(tm_size, chan_size, rows, width, nblocks, ngal):
    nz = tm_size // NX
    quarter = width // NX
    npix = tm_size * TP
    zpix = NX * TP
    half = zpix // 2
    block_rows = rows // nblocks
    shifts = quarter + 2 * SW
    far = nz // 2

    def kernel(
        spec, basis_in, weight, routes, offsets, taps, gal_pix, gal_chan,
        sky, stacked,
        own, basis, pix, raw, gram, proj, ext, coef, band, ripple, clean, part, pixel_hot, counts,
        zsend, zrecv, final, st1, st2, st3,
        load_sem, pix_s, pix_r, raw_s, raw_r, gram_s, gram_r, proj_s, proj_r, coef_s, coef_r,
        z_s, z_r, fin_s, fin_r, st1_s, st1_r, st2_s, st2_r, st3_s, st3_r,
    ):
        tm = lax.axis_index("tm")
        j = lax.axis_index("chan")
        z = lax.div(tm, NX)
        x = lax.rem(tm, NX)
        here = pl.multiple_of(x * quarter, quarter)

        def x_peer(r):
            return (z * NX + lax.rem(x + r, NX), j)

        def c_peer(r):
            return (tm, lax.rem(j + r, chan_size))

        def z_peer(r):
            return (lax.rem(z + r, nz) * NX + x, j)

        def remote(src, dst, send_sem, recv_sem, peer):
            return pltpu.make_async_remote_copy(
                src_ref=src, dst_ref=dst, send_sem=send_sem, recv_sem=recv_sem,
                device_id=peer, device_id_type=MESH,
            )

        sends = []

        def start(copy):
            copy.start()
            sends.append(copy)

        peers = (
            [x_peer(r) for r in range(1, NX)]
            + [c_peer(r) for r in range(1, chan_size)]
            + [z_peer(r) for r in range(1, nz)]
        )
        barrier = pltpu.get_barrier_semaphore()
        for peer in peers:
            pl.semaphore_signal(barrier, inc=1, device_id=peer, device_id_type=MESH)
        basis_here = basis_in.at[:, pl.ds(pl.multiple_of(j * width, width), width)]
        loads = [
            pltpu.make_async_copy(source, target, load_sem.at[i])
            for i, (source, target) in enumerate((
                (spec, own), (basis_here, basis),
            ))
        ]
        for load in loads:
            load.start()
        inside = iota((nblocks, rows), 1) - block_rows * iota((nblocks, rows), 0)
        owner = ((inside >= 0) & (inside < block_rows)).astype(f32).astype(bf16)
        tile = jnp.dot(
            jnp.broadcast_to(routes[...], (16, nblocks)).astype(f32).astype(bf16), owner,
            preferred_element_type=f32,
        )[0:1].astype(jnp.int32)
        pix[0] = tile * TP + offsets[...] - MARGIN

        pl.semaphore_wait(barrier, len(peers))
        for r in range(1, NX):
            start(remote(pix.at[0], pix.at[NX - r], pix_s.at[r], pix_r.at[NX - r], x_peer(r)))

        loads[0].wait()
        for r in (2, 1, 3):
            column = pl.multiple_of(lax.rem(x + r, NX) * quarter, quarter)
            start(remote(
                own.at[:, pl.ds(column, quarter)], raw.at[NX - r], raw_s.at[r], raw_r.at[NX - r],
                x_peer(r),
            ))

        loads[1].wait()
        weighted = basis[...] * weight[...]
        gram[0] = jnp.zeros((MODES, 128), f32)
        gram[0, :, 0:MODES] = lax.dot_general(
            weighted, basis[...], (((1,), (1,)), ((), ())), precision=highest,
            preferred_element_type=f32,
        )
        for r in range(1, chan_size):
            start(remote(
                gram.at[0], gram.at[chan_size - r], gram_s.at[r], gram_r.at[chan_size - r],
                c_peer(r),
            ))
        w_stack = jnp.concatenate(split3(weighted), axis=0)
        products = lax.dot_general(
            w_stack, own[...], (((1,), (1,)), ((), ())), preferred_element_type=f32
        )
        proj[0] = products[:MODES] + products[MODES:2 * MODES] + products[2 * MODES:]
        for r in range(1, chan_size):
            start(remote(
                proj.at[0], proj.at[chan_size - r], proj_s.at[r], proj_r.at[chan_size - r],
                c_peer(r),
            ))

        def fill(target, column, group, tap):
            def step(a, carry):
                row = pl.multiple_of(a * TAPS, TAPS)
                target[pl.ds(row, TAPS), column:column + tap.shape[1]] = jnp.where(
                    group == a, tap, 0.0
                ).astype(bf16)
                return carry

            lax.fori_loop(0, npix // TAPS, step, 0, unroll=4)

        def build_band(slot):
            first = pix[slot]
            group = jnp.broadcast_to(first >> 4, (TAPS, rows))
            inner = jnp.broadcast_to(first & (TAPS - 1), (TAPS, rows))
            lane = iota((TAPS, rows), 0)
            turn = (lane - inner) & (TAPS - 1)
            tap = jnp.zeros((TAPS, rows), f32)
            values = taps[...].astype(f32)
            for m in range(TAPS):
                tap = jnp.where(turn == m, values[0:1, m:m + 1], tap)
            fill(band, slot * rows, jnp.where(lane < inner, group + 1, group), tap)

        build_band(0)

        for r in range(1, chan_size):
            remote(gram.at[0], gram.at[r], gram_s.at[r], gram_r.at[r], c_peer(r)).wait_recv()
        total = gram[0]
        for r in range(1, chan_size):
            total = total + gram[r]
        row_id = iota((MODES, 128), 0)
        both = jnp.where(iota((MODES, 128), 1) - MODES == row_id, 1.0, total)
        for i in range(MODES):
            pivot = both[i:i + 1, :] / both[i:i + 1, i:i + 1]
            both = jnp.where(row_id == i, pivot, both - both[:, i:i + 1] * pivot)

        ext[...] = jnp.zeros(ext.shape, f32)
        for r in range(1, chan_size):
            remote(proj.at[0], proj.at[r], proj_s.at[r], proj_r.at[r], c_peer(r)).wait_recv()
        full = proj[0]
        for r in range(1, chan_size):
            full = full + proj[r]
        ext[MODES:2 * MODES, :] = full
        coef[0] = jnp.dot(both, ext[...], precision=highest, preferred_element_type=f32)
        for r in range(1, NX):
            start(remote(coef.at[0], coef.at[NX - r], coef_s.at[r], coef_r.at[NX - r], x_peer(r)))

        b_high, b_mid, b_low = split3(basis[:, pl.ds(here, quarter)])
        b_stack = jnp.concatenate(
            [b_high, b_mid, b_high, b_mid, b_low, b_high, jnp.zeros((2 * MODES, quarter), bf16)],
            axis=0,
        )

        def fit_slot(slot):
            c_high, c_mid, c_low = split3(coef[slot])
            c_stack = jnp.concatenate(
                [c_high, c_high, c_mid, c_mid, c_high, c_low, jnp.zeros((2 * MODES, rows), bf16)],
                axis=0,
            )
            ripple[slot * rows:(slot + 1) * rows, :] = lax.dot_general(
                c_stack, b_stack, (((0,), (0,)), ((), ())), preferred_element_type=f32
            )

        def clean_slot(slot, values):
            clean[slot * rows:(slot + 1) * rows, :] = (
                values.astype(f32) - ripple[slot * rows:(slot + 1) * rows, :]
            ).astype(bf16)

        fit_slot(0)
        clean_slot(0, own[:, pl.ds(here, quarter)])
        begin = gal_chan[...] - SW - (j * width + here)
        shift_hot = (iota((shifts, ngal), 0) == quarter - 1 - begin).astype(f32).astype(bf16)
        gal_row = jnp.broadcast_to(gal_pix[...], (TAPS, ngal))
        fill(
            pixel_hot, 0, gal_row >> 4,
            jnp.where((gal_row & (TAPS - 1)) == iota((TAPS, ngal), 0), 1.0, 0.0).astype(f32),
        )
        counts[...] = lax.dot_general(
            shift_hot, pixel_hot[...], (((1,), (1,)), ((), ())), preferred_element_type=f32
        ).astype(bf16)

        for r in range(1, NX):
            remote(pix.at[0], pix.at[r], pix_s.at[r], pix_r.at[r], x_peer(r)).wait_recv()
            build_band(r)
        for r in (1, 3, 2):
            remote(coef.at[0], coef.at[r], coef_s.at[r], coef_r.at[r], x_peer(r)).wait_recv()
            fit_slot(r)
        for r in (1, 3, 2):
            remote(
                own.at[:, pl.ds(0, quarter)], raw.at[r], raw_s.at[r], raw_r.at[r], x_peer(r)
            ).wait_recv()
            clean_slot(r, raw[r])

        def chunk_row(step):
            return pl.multiple_of(lax.rem(z + step + 2 * nz, nz) * zpix, zpix)

        def part_half(step, which):
            row = pl.multiple_of(chunk_row(step) + which * half, half)
            return part[pl.ds(row, half), :]

        def z_copy(way, index):
            return remote(
                zsend.at[way, index], zrecv.at[way, index], z_s.at[way, index],
                z_r.at[way, index], z_peer((1, nz - 1)[way]),
            )

        def z_start(way, index, value):
            zsend[way, index] = value.astype(bf16)
            z_copy(way, index).start()

        def z_take(way, index):
            z_copy(way, index).wait_recv()
            return zrecv[way, index].astype(f32)

        sign = (1, -1)

        def long_step(k):
            for way in range(2):
                got = z_take(way, k)
                z_start(way, k + 1, got + part_half(sign[way] * (far - 1 - k), way))

        def short_step(k):
            for way in range(2):
                got = z_take(way, far + k)
                z_start(
                    way, far + k + 1, got + part_half(sign[way] * (far - 2 - k), 1 - way)
                )

        def grid_step(n, carry):
            away = lax.div(n + 1, 2)
            row = chunk_row(far + away - 2 * lax.rem(n, 2) * away)
            part[pl.ds(row, zpix), :] = jnp.dot(
                band[pl.ds(row, zpix), :], clean[...], preferred_element_type=f32
            )

            @pl.when(n == 0)
            def _():
                for way in range(2):
                    z_start(way, 0, part_half(far, way))

            @pl.when(n == 2)
            def _():
                for way in range(2):
                    z_start(way, far, part_half(sign[way] * (far - 1), 1 - way))

            @pl.when(n == 4)
            def _():
                long_step(0)
                short_step(0)

            return carry

        def share(buffer, me, send_sem, recv_sem, peer_of, count):
            for r in range(1, count):
                start(remote(buffer.at[me], buffer.at[me], send_sem.at[r], recv_sem.at[me], peer_of(r)))

        def gather(buffer, me, send_sem, recv_sem, peer_of, count):
            for r in range(1, count):
                other = lax.rem(me + r, count)
                remote(
                    buffer.at[other], buffer.at[other], send_sem.at[r], recv_sem.at[other], peer_of(r)
                ).wait_recv()
            value = buffer[0]
            for i in range(1, count):
                value = value + buffer[i]
            return value

        lax.fori_loop(0, nz, grid_step, 0)

        long_step(1)
        short_step(1)

        wide = jnp.concatenate(
            [
                jnp.dot(counts[...], part[...].astype(bf16), preferred_element_type=f32),
                jnp.zeros((shifts, 512 - quarter), f32),
            ],
            axis=1,
        )
        folded = jnp.zeros((8, 512), f32)
        for i in range(shifts // 8):
            folded = folded + pltpu.roll(
                wide[8 * i:8 * i + 8], (513 - quarter + 8 * i) % 512, 1
            )
        window = jnp.zeros((1, 512), f32)
        for i in range(8):
            window = window + (pltpu.roll(folded[i:i + 1], i, 1) if i else folded[i:i + 1])
        st1[x] = window[:, :2 * SW]
        share(st1, x, st1_s, st1_r, x_peer, NX)

        long_step(2)
        st2[j] = gather(st1, x, st1_s, st1_r, x_peer, NX)
        share(st2, j, st2_s, st2_r, c_peer, chan_size)
        for copy in sends:
            copy.wait_send()
        sends.clear()

        got = [z_take(way, 2 * far - 2) for way in range(2)]
        for way in range(2):
            value = z_take(way, far - 1) + got[1 - way] + part_half(0, way)
            final[way * half:(way + 1) * half, :] = value.astype(bf16)
        for r in (2, 1, 3):
            row = pl.multiple_of(lax.rem(x + r, NX) * TP, TP)
            start(remote(
                final.at[pl.ds(row, TP), :], sky.at[:, pl.ds(here, quarter)], fin_s.at[r],
                fin_r.at[NX - r], x_peer(r),
            ))
        sky[:, pl.ds(here, quarter)] = final[pl.ds(pl.multiple_of(x * TP, TP), TP), :]

        st3[z] = gather(st2, j, st2_s, st2_r, c_peer, chan_size)
        share(st3, z, st3_s, st3_r, z_peer, nz)
        for way in range(2):
            for index in range(2 * far - 1):
                z_copy(way, index).wait_send()
        for r in range(1, NX):
            column = pl.multiple_of(lax.rem(x + r, NX) * quarter, quarter)
            remote(
                final.at[pl.ds(0, TP), :], sky.at[:, pl.ds(column, quarter)], fin_s.at[r],
                fin_r.at[r], x_peer(r),
            ).wait_recv()
        stacked[...] = gather(st3, z, st3_s, st3_r, z_peer, nz) / ngal
        for copy in sends:
            copy.wait_send()

    dma = pltpu.SemaphoreType.DMA
    scratch = [
        pltpu.VMEM((rows, width), bf16),
        pltpu.VMEM((MODES, width), f32),
        pltpu.VMEM((NX, 1, rows), jnp.int32),
        pltpu.VMEM((NX, rows, quarter), bf16),
        pltpu.VMEM((chan_size, MODES, 128), f32),
        pltpu.VMEM((chan_size, MODES, rows), f32),
        pltpu.VMEM((128, rows), f32),
        pltpu.VMEM((NX, MODES, rows), f32),
        pltpu.VMEM((npix, NX * rows), bf16),
        pltpu.VMEM((NX * rows, quarter), f32),
        pltpu.VMEM((NX * rows, quarter), bf16),
        pltpu.VMEM((npix, quarter), f32),
        pltpu.VMEM((npix, ngal), bf16),
        pltpu.VMEM((shifts, npix), bf16),
        pltpu.VMEM((2, nz - 1, half, quarter), bf16),
        pltpu.VMEM((2, nz - 1, half, quarter), bf16),
        pltpu.VMEM((zpix, quarter), bf16),
        pltpu.VMEM((NX, 1, 2 * SW), f32),
        pltpu.VMEM((chan_size, 1, 2 * SW), f32),
        pltpu.VMEM((nz, 1, 2 * SW), f32),
        dma((2,)),
    ]
    for shape in (
        (NX,), (NX,), (chan_size,), (chan_size,), (NX,), (2, nz - 1), (NX,),
        (NX,), (chan_size,), (nz,),
    ):
        scratch += [dma(shape), dma(shape)]
    return kernel, scratch


def solution(mesh):
    tm_size, chan_size = mesh.shape["tm"], mesh.shape["chan"]

    def per_device(spectra, chan_weight, routes, offsets, taps, gal_pix, gal_chan):
        rows, width = spectra.shape
        nblocks = routes.shape[0]
        kernel, scratch = make_kernel(
            tm_size, chan_size, rows, width, nblocks, gal_pix.shape[0]
        )
        vmem = pl.BlockSpec(memory_space=pltpu.VMEM)
        sky, stacked = pl.pallas_call(
            kernel,
            out_shape=(
                jax.ShapeDtypeStruct((TP, width), bf16),
                jax.ShapeDtypeStruct((1, 2 * SW), f32),
            ),
            in_specs=[pl.BlockSpec(memory_space=pl.ANY)] * 2 + [vmem] * 6,
            out_specs=(vmem, vmem),
            scratch_shapes=scratch,
            compiler_params=pltpu.CompilerParams(
                collective_id=0, has_side_effects=True, vmem_limit_bytes=54880 * 1024
            ),
        )(
            spectra, jnp.asarray(basis_table(width * chan_size)), chan_weight[None, :],
            routes.reshape(1, nblocks), offsets[None, :], taps[None, :], gal_pix[None, :],
            gal_chan[None, :],
        )
        return sky, stacked[0]

    in_specs = (
        P("tm", "chan"), P("chan"), P("tm", None), P("tm"), P(None), P(None), P(None)
    )
    return jax.shard_map(
        per_device, mesh=mesh, in_specs=in_specs, out_specs=(P("tm", "chan"), P(None)),
        check_vma=False,
    )
```

```python
import jax
import jax.numpy as jnp
import numpy as np
from jax import lax
from jax.experimental import pallas as pl
from jax.experimental.pallas import tpu as pltpu
from jax.sharding import PartitionSpec as P

KMODES = 8
MODES = 2 * KMODES
TP = 64
MARGIN = 8
SW = 64
TAPS = 16
NX = 4

highest = lax.Precision.HIGHEST
MESH = pl.DeviceIdType.MESH
f32 = jnp.float32
bf16 = jnp.bfloat16


def basis_table(total):
    orders = np.arange(1, KMODES + 1)[:, None]
    phase = (orders * np.arange(total)[None, :] % total) * (2 * np.pi / total)
    return np.concatenate([np.cos(phase), np.sin(phase)], axis=0).astype(np.float32)


def split3(value):
    high = value.astype(bf16)
    rest = value - high.astype(f32)
    mid = rest.astype(bf16)
    low = (rest - mid.astype(f32)).astype(bf16)
    return high, mid, low


def iota(shape, dim):
    return lax.broadcasted_iota(jnp.int32, shape, dim)


def make_kernel(tm_size, chan_size, rows, width, nblocks, ngal):
    nz = tm_size // NX
    quarter = width // NX
    npix = tm_size * TP
    zpix = NX * TP
    half = zpix // 2
    block_rows = rows // nblocks
    shifts = quarter + 2 * SW
    far = nz // 2

    def kernel(
        spec, basis_in, weight, routes, offsets, taps, gal_pix, gal_chan,
        sky, stacked,
        own, basis, pix, raw, relay, gram, proj, ext, coef, band, ripple, clean, part, pixel_hot, counts,
        zsend, zrecv, final, st1, st2, st3,
        load_sem, pix_s, pix_r, raw_s, raw_r, relay_s, relay_r, next_s, next_r, gram_s, gram_r, proj_s, proj_r, coef_s, coef_r,
        z_s, z_r, fin_s, fin_r, st1_s, st1_r, st2_s, st2_r, st3_s, st3_r,
    ):
        tm = lax.axis_index("tm")
        j = lax.axis_index("chan")
        z = lax.div(tm, NX)
        x = lax.rem(tm, NX)
        here = pl.multiple_of(x * quarter, quarter)

        def x_peer(r):
            return (z * NX + lax.rem(x + r, NX), j)

        def c_peer(r):
            return (tm, lax.rem(j + r, chan_size))

        def z_peer(r):
            return (lax.rem(z + r, nz) * NX + x, j)

        def remote(src, dst, send_sem, recv_sem, peer):
            return pltpu.make_async_remote_copy(
                src_ref=src, dst_ref=dst, send_sem=send_sem, recv_sem=recv_sem,
                device_id=peer, device_id_type=MESH,
            )

        sends = []

        def start(copy):
            copy.start()
            sends.append(copy)

        peers = (
            [x_peer(r) for r in range(1, NX)]
            + [c_peer(r) for r in range(1, chan_size)]
            + [z_peer(r) for r in range(1, nz)]
        )
        barrier = pltpu.get_barrier_semaphore()
        for peer in peers:
            pl.semaphore_signal(barrier, inc=1, device_id=peer, device_id_type=MESH)
        basis_here = basis_in.at[:, pl.ds(pl.multiple_of(j * width, width), width)]
        loads = [
            pltpu.make_async_copy(source, target, load_sem.at[i])
            for i, (source, target) in enumerate((
                (spec, own), (basis_here, basis),
            ))
        ]
        for load in loads:
            load.start()
        inside = iota((nblocks, rows), 1) - block_rows * iota((nblocks, rows), 0)
        owner = ((inside >= 0) & (inside < block_rows)).astype(f32).astype(bf16)
        tile = jnp.dot(
            jnp.broadcast_to(routes[...], (16, nblocks)).astype(f32).astype(bf16), owner,
            preferred_element_type=f32,
        )[0:1].astype(jnp.int32)
        pix[0] = tile * TP + offsets[...] - MARGIN

        pl.semaphore_wait(barrier, len(peers))
        for r in range(1, NX):
            start(remote(pix.at[0], pix.at[NX - r], pix_s.at[r], pix_r.at[NX - r], x_peer(r)))

        loads[0].wait()
        across = pl.multiple_of(lax.rem(x + 2, NX) * quarter, quarter)
        mid = rows // 2
        for way in range(2):
            start(remote(
                own.at[way * mid:(way + 1) * mid, pl.ds(across, quarter)], relay.at[way],
                relay_s.at[way], relay_r.at[way], x_peer((1, 3)[way]),
            ))
        for r in (1, 3):
            column = pl.multiple_of(lax.rem(x + r, NX) * quarter, quarter)
            start(remote(
                own.at[:, pl.ds(column, quarter)], raw.at[NX - r], raw_s.at[r], raw_r.at[NX - r],
                x_peer(r),
            ))

        def next_copy(way):
            return remote(
                relay.at[way], raw.at[2, way * mid:(way + 1) * mid], next_s.at[way],
                next_r.at[way], x_peer((1, 3)[way]),
            )

        loads[1].wait()
        weighted = basis[...] * weight[...]
        gram[0] = jnp.zeros((MODES, 128), f32)
        gram[0, :, 0:MODES] = lax.dot_general(
            weighted, basis[...], (((1,), (1,)), ((), ())), precision=highest,
            preferred_element_type=f32,
        )
        for r in range(1, chan_size):
            start(remote(
                gram.at[0], gram.at[chan_size - r], gram_s.at[r], gram_r.at[chan_size - r],
                c_peer(r),
            ))
        w_stack = jnp.concatenate(split3(weighted), axis=0)
        products = lax.dot_general(
            w_stack, own[...], (((1,), (1,)), ((), ())), preferred_element_type=f32
        )
        proj[0] = products[:MODES] + products[MODES:2 * MODES] + products[2 * MODES:]
        for r in range(1, chan_size):
            start(remote(
                proj.at[0], proj.at[chan_size - r], proj_s.at[r], proj_r.at[chan_size - r],
                c_peer(r),
            ))

        def fill(target, column, group, tap):
            def step(a, carry):
                row = pl.multiple_of(a * TAPS, TAPS)
                target[pl.ds(row, TAPS), column:column + tap.shape[1]] = jnp.where(
                    group == a, tap, 0.0
                ).astype(bf16)
                return carry

            lax.fori_loop(0, npix // TAPS, step, 0, unroll=4)

        def build_band(slot):
            first = pix[slot]
            group = jnp.broadcast_to(first >> 4, (TAPS, rows))
            inner = jnp.broadcast_to(first & (TAPS - 1), (TAPS, rows))
            lane = iota((TAPS, rows), 0)
            turn = (lane - inner) & (TAPS - 1)
            tap = jnp.zeros((TAPS, rows), f32)
            values = taps[...].astype(f32)
            for m in range(TAPS):
                tap = jnp.where(turn == m, values[0:1, m:m + 1], tap)
            fill(band, slot * rows, jnp.where(lane < inner, group + 1, group), tap)

        build_band(0)
        for way in range(2):
            remote(
                own.at[0:mid, pl.ds(0, quarter)], relay.at[way], relay_s.at[way], relay_r.at[way],
                x_peer((1, 3)[way]),
            ).wait_recv()
            start(next_copy(way))

        for r in range(1, chan_size):
            remote(gram.at[0], gram.at[r], gram_s.at[r], gram_r.at[r], c_peer(r)).wait_recv()
        total = gram[0]
        for r in range(1, chan_size):
            total = total + gram[r]
        row_id = iota((MODES, 128), 0)
        both = jnp.where(iota((MODES, 128), 1) - MODES == row_id, 1.0, total)
        for i in range(MODES):
            pivot = both[i:i + 1, :] / both[i:i + 1, i:i + 1]
            both = jnp.where(row_id == i, pivot, both - both[:, i:i + 1] * pivot)

        ext[...] = jnp.zeros(ext.shape, f32)
        for r in range(1, chan_size):
            remote(proj.at[0], proj.at[r], proj_s.at[r], proj_r.at[r], c_peer(r)).wait_recv()
        full = proj[0]
        for r in range(1, chan_size):
            full = full + proj[r]
        ext[MODES:2 * MODES, :] = full
        coef[0] = jnp.dot(both, ext[...], precision=highest, preferred_element_type=f32)
        for r in range(1, NX):
            start(remote(coef.at[0], coef.at[NX - r], coef_s.at[r], coef_r.at[NX - r], x_peer(r)))

        b_high, b_mid, b_low = split3(basis[:, pl.ds(here, quarter)])
        b_stack = jnp.concatenate(
            [b_high, b_mid, b_high, b_mid, b_low, b_high, jnp.zeros((2 * MODES, quarter), bf16)],
            axis=0,
        )

        def fit_slot(slot):
            c_high, c_mid, c_low = split3(coef[slot])
            c_stack = jnp.concatenate(
                [c_high, c_high, c_mid, c_mid, c_high, c_low, jnp.zeros((2 * MODES, rows), bf16)],
                axis=0,
            )
            ripple[slot * rows:(slot + 1) * rows, :] = lax.dot_general(
                c_stack, b_stack, (((0,), (0,)), ((), ())), preferred_element_type=f32
            )

        def clean_slot(slot, values):
            clean[slot * rows:(slot + 1) * rows, :] = (
                values.astype(f32) - ripple[slot * rows:(slot + 1) * rows, :]
            ).astype(bf16)

        fit_slot(0)
        clean_slot(0, own[:, pl.ds(here, quarter)])
        begin = gal_chan[...] - SW - (j * width + here)
        shift_hot = (iota((shifts, ngal), 0) == quarter - 1 - begin).astype(f32).astype(bf16)
        gal_row = jnp.broadcast_to(gal_pix[...], (TAPS, ngal))
        fill(
            pixel_hot, 0, gal_row >> 4,
            jnp.where((gal_row & (TAPS - 1)) == iota((TAPS, ngal), 0), 1.0, 0.0).astype(f32),
        )
        counts[...] = lax.dot_general(
            shift_hot, pixel_hot[...], (((1,), (1,)), ((), ())), preferred_element_type=f32
        ).astype(bf16)

        for r in range(1, NX):
            remote(pix.at[0], pix.at[r], pix_s.at[r], pix_r.at[r], x_peer(r)).wait_recv()
            build_band(r)
        for r in (1, 3, 2):
            remote(coef.at[0], coef.at[r], coef_s.at[r], coef_r.at[r], x_peer(r)).wait_recv()
            fit_slot(r)
        for r in (1, 3):
            remote(
                own.at[:, pl.ds(0, quarter)], raw.at[r], raw_s.at[r], raw_r.at[r], x_peer(r)
            ).wait_recv()
            clean_slot(r, raw[r])
        for way in range(2):
            next_copy(way).wait_recv()
        clean_slot(2, raw[2])

        def chunk_row(step):
            return pl.multiple_of(lax.rem(z + step + 2 * nz, nz) * zpix, zpix)

        def part_half(step, which):
            row = pl.multiple_of(chunk_row(step) + which * half, half)
            return part[pl.ds(row, half), :]

        def z_copy(way, index):
            return remote(
                zsend.at[way, index], zrecv.at[way, index], z_s.at[way, index],
                z_r.at[way, index], z_peer((1, nz - 1)[way]),
            )

        def z_start(way, index, value):
            zsend[way, index] = value.astype(bf16)
            z_copy(way, index).start()

        def z_take(way, index):
            z_copy(way, index).wait_recv()
            return zrecv[way, index].astype(f32)

        sign = (1, -1)

        def long_step(k):
            for way in range(2):
                got = z_take(way, k)
                z_start(way, k + 1, got + part_half(sign[way] * (far - 1 - k), way))

        def short_step(k):
            for way in range(2):
                got = z_take(way, far + k)
                z_start(
                    way, far + k + 1, got + part_half(sign[way] * (far - 2 - k), 1 - way)
                )

        def grid_step(n, carry):
            away = lax.div(n + 1, 2)
            row = chunk_row(far + away - 2 * lax.rem(n, 2) * away)
            part[pl.ds(row, zpix), :] = jnp.dot(
                band[pl.ds(row, zpix), :], clean[...], preferred_element_type=f32
            )

            @pl.when(n == 0)
            def _():
                for way in range(2):
                    z_start(way, 0, part_half(far, way))

            @pl.when(n == 2)
            def _():
                for way in range(2):
                    z_start(way, far, part_half(sign[way] * (far - 1), 1 - way))

            @pl.when(n == 4)
            def _():
                long_step(0)
                short_step(0)

            return carry

        def share(buffer, me, send_sem, recv_sem, peer_of, count):
            for r in range(1, count):
                start(remote(buffer.at[me], buffer.at[me], send_sem.at[r], recv_sem.at[me], peer_of(r)))

        def gather(buffer, me, send_sem, recv_sem, peer_of, count):
            for r in range(1, count):
                other = lax.rem(me + r, count)
                remote(
                    buffer.at[other], buffer.at[other], send_sem.at[r], recv_sem.at[other], peer_of(r)
                ).wait_recv()
            value = buffer[0]
            for i in range(1, count):
                value = value + buffer[i]
            return value

        lax.fori_loop(0, nz, grid_step, 0)

        long_step(1)
        short_step(1)

        wide = jnp.concatenate(
            [
                jnp.dot(counts[...], part[...].astype(bf16), preferred_element_type=f32),
                jnp.zeros((shifts, 512 - quarter), f32),
            ],
            axis=1,
        )
        folded = jnp.zeros((8, 512), f32)
        for i in range(shifts // 8):
            folded = folded + pltpu.roll(
                wide[8 * i:8 * i + 8], (513 - quarter + 8 * i) % 512, 1
            )
        window = jnp.zeros((1, 512), f32)
        for i in range(8):
            window = window + (pltpu.roll(folded[i:i + 1], i, 1) if i else folded[i:i + 1])
        st1[x] = window[:, :2 * SW]
        share(st1, x, st1_s, st1_r, x_peer, NX)

        long_step(2)
        st2[j] = gather(st1, x, st1_s, st1_r, x_peer, NX)
        share(st2, j, st2_s, st2_r, c_peer, chan_size)
        for copy in sends:
            copy.wait_send()
        sends.clear()

        got = [z_take(way, 2 * far - 2) for way in range(2)]
        for way in range(2):
            value = z_take(way, far - 1) + got[1 - way] + part_half(0, way)
            final[way * half:(way + 1) * half, :] = value.astype(bf16)
        for r in (2, 1, 3):
            row = pl.multiple_of(lax.rem(x + r, NX) * TP, TP)
            start(remote(
                final.at[pl.ds(row, TP), :], sky.at[:, pl.ds(here, quarter)], fin_s.at[r],
                fin_r.at[NX - r], x_peer(r),
            ))
        sky[:, pl.ds(here, quarter)] = final[pl.ds(pl.multiple_of(x * TP, TP), TP), :]

        st3[z] = gather(st2, j, st2_s, st2_r, c_peer, chan_size)
        share(st3, z, st3_s, st3_r, z_peer, nz)
        for way in range(2):
            for index in range(2 * far - 1):
                z_copy(way, index).wait_send()
        for r in range(1, NX):
            column = pl.multiple_of(lax.rem(x + r, NX) * quarter, quarter)
            remote(
                final.at[pl.ds(0, TP), :], sky.at[:, pl.ds(column, quarter)], fin_s.at[r],
                fin_r.at[r], x_peer(r),
            ).wait_recv()
        stacked[...] = gather(st3, z, st3_s, st3_r, z_peer, nz) / ngal
        for copy in sends:
            copy.wait_send()

    dma = pltpu.SemaphoreType.DMA
    scratch = [
        pltpu.VMEM((rows, width), bf16),
        pltpu.VMEM((MODES, width), f32),
        pltpu.VMEM((NX, 1, rows), jnp.int32),
        pltpu.VMEM((NX, rows, quarter), bf16),
        pltpu.VMEM((2, rows // 2, quarter), bf16),
        pltpu.VMEM((chan_size, MODES, 128), f32),
        pltpu.VMEM((chan_size, MODES, rows), f32),
        pltpu.VMEM((128, rows), f32),
        pltpu.VMEM((NX, MODES, rows), f32),
        pltpu.VMEM((npix, NX * rows), bf16),
        pltpu.VMEM((NX * rows, quarter), f32),
        pltpu.VMEM((NX * rows, quarter), bf16),
        pltpu.VMEM((npix, quarter), f32),
        pltpu.VMEM((npix, ngal), bf16),
        pltpu.VMEM((shifts, npix), bf16),
        pltpu.VMEM((2, nz - 1, half, quarter), bf16),
        pltpu.VMEM((2, nz - 1, half, quarter), bf16),
        pltpu.VMEM((zpix, quarter), bf16),
        pltpu.VMEM((NX, 1, 2 * SW), f32),
        pltpu.VMEM((chan_size, 1, 2 * SW), f32),
        pltpu.VMEM((nz, 1, 2 * SW), f32),
        dma((2,)),
    ]
    for shape in (
        (NX,), (NX,), (2,), (2,), (chan_size,), (chan_size,), (NX,), (2, nz - 1), (NX,),
        (NX,), (chan_size,), (nz,),
    ):
        scratch += [dma(shape), dma(shape)]
    return kernel, scratch


def solution(mesh):
    tm_size, chan_size = mesh.shape["tm"], mesh.shape["chan"]

    def per_device(spectra, chan_weight, routes, offsets, taps, gal_pix, gal_chan):
        rows, width = spectra.shape
        nblocks = routes.shape[0]
        kernel, scratch = make_kernel(
            tm_size, chan_size, rows, width, nblocks, gal_pix.shape[0]
        )
        vmem = pl.BlockSpec(memory_space=pltpu.VMEM)
        sky, stacked = pl.pallas_call(
            kernel,
            out_shape=(
                jax.ShapeDtypeStruct((TP, width), bf16),
                jax.ShapeDtypeStruct((1, 2 * SW), f32),
            ),
            in_specs=[pl.BlockSpec(memory_space=pl.ANY)] * 2 + [vmem] * 6,
            out_specs=(vmem, vmem),
            scratch_shapes=scratch,
            compiler_params=pltpu.CompilerParams(
                collective_id=0, has_side_effects=True, vmem_limit_bytes=54880 * 1024
            ),
        )(
            spectra, jnp.asarray(basis_table(width * chan_size)), chan_weight[None, :],
            routes.reshape(1, nblocks), offsets[None, :], taps[None, :], gal_pix[None, :],
            gal_chan[None, :],
        )
        return sky, stacked[0]

    in_specs = (
        P("tm", "chan"), P("chan"), P("tm", None), P("tm"), P(None), P(None), P(None)
    )
    return jax.shard_map(
        per_device, mesh=mesh, in_specs=in_specs, out_specs=(P("tm", "chan"), P(None)),
        check_vma=False,
    )
```

```python
import jax
import jax.numpy as jnp
import numpy as np
from jax import lax
from jax.experimental import pallas as pl
from jax.experimental.pallas import tpu as pltpu
from jax.sharding import PartitionSpec as P

KMODES = 8
MODES = 2 * KMODES
TP = 64
MARGIN = 8
SW = 64
TAPS = 16
NX = 4

highest = lax.Precision.HIGHEST
MESH = pl.DeviceIdType.MESH
f32 = jnp.float32
bf16 = jnp.bfloat16


def basis_table(total):
    orders = np.arange(1, KMODES + 1)[:, None]
    phase = (orders * np.arange(total)[None, :] % total) * (2 * np.pi / total)
    return np.concatenate([np.cos(phase), np.sin(phase)], axis=0).astype(np.float32)


def split3(value):
    high = value.astype(bf16)
    rest = value - high.astype(f32)
    mid = rest.astype(bf16)
    low = (rest - mid.astype(f32)).astype(bf16)
    return high, mid, low


def iota(shape, dim):
    return lax.broadcasted_iota(jnp.int32, shape, dim)


def make_kernel(tm_size, chan_size, rows, width, nblocks, ngal):
    nz = tm_size // NX
    quarter = width // NX
    npix = tm_size * TP
    zpix = NX * TP
    half = zpix // 2
    block_rows = rows // nblocks
    shifts = quarter + 2 * SW
    far = nz // 2

    def kernel(
        spec, basis_in, weight, routes, offsets, taps, gal_pix, gal_chan,
        sky, stacked,
        own, basis, pix, raw, gram, proj, ext, coef, band, ripple, clean, part, pixel_hot, counts,
        zsend, zrecv, final, st1, st2, st3,
        load_sem, pix_s, pix_r, raw_s, raw_r, gram_s, gram_r, proj_s, proj_r, coef_s, coef_r,
        z_s, z_r, fin_s, fin_r, st1_s, st1_r, st2_s, st2_r, st3_s, st3_r,
    ):
        tm = lax.axis_index("tm")
        j = lax.axis_index("chan")
        z = lax.div(tm, NX)
        x = lax.rem(tm, NX)
        here = pl.multiple_of(x * quarter, quarter)

        def x_peer(r):
            return (z * NX + lax.rem(x + r, NX), j)

        def c_peer(r):
            return (tm, lax.rem(j + r, chan_size))

        def z_peer(r):
            return (lax.rem(z + r, nz) * NX + x, j)

        def remote(src, dst, send_sem, recv_sem, peer):
            return pltpu.make_async_remote_copy(
                src_ref=src, dst_ref=dst, send_sem=send_sem, recv_sem=recv_sem,
                device_id=peer, device_id_type=MESH,
            )

        sends = []

        def start(copy):
            copy.start()
            sends.append(copy)

        peers = (
            [x_peer(r) for r in range(1, NX)]
            + [c_peer(r) for r in range(1, chan_size)]
            + [z_peer(r) for r in range(1, nz)]
        )
        barrier = pltpu.get_barrier_semaphore()
        for peer in peers:
            pl.semaphore_signal(barrier, inc=1, device_id=peer, device_id_type=MESH)
        basis_here = basis_in.at[:, pl.ds(pl.multiple_of(j * width, width), width)]
        loads = [
            pltpu.make_async_copy(source, target, load_sem.at[i])
            for i, (source, target) in enumerate((
                (spec, own), (basis_here, basis),
            ))
        ]
        for load in loads:
            load.start()
        inside = iota((nblocks, rows), 1) - block_rows * iota((nblocks, rows), 0)
        owner = ((inside >= 0) & (inside < block_rows)).astype(f32).astype(bf16)
        tile = jnp.dot(
            jnp.broadcast_to(routes[...], (16, nblocks)).astype(f32).astype(bf16), owner,
            preferred_element_type=f32,
        )[0:1].astype(jnp.int32)
        pix[0] = tile * TP + offsets[...] - MARGIN

        pl.semaphore_wait(barrier, len(peers))
        for r in range(1, NX):
            start(remote(pix.at[0], pix.at[NX - r], pix_s.at[r], pix_r.at[NX - r], x_peer(r)))

        loads[1].wait()
        weighted = basis[...] * weight[...]
        w_stack = jnp.concatenate(split3(weighted), axis=0)
        loads[0].wait()
        products = lax.dot_general(
            w_stack, own[...], (((1,), (1,)), ((), ())), preferred_element_type=f32
        )
        proj[0] = products[:MODES] + products[MODES:2 * MODES] + products[2 * MODES:]
        for r in range(1, chan_size):
            start(remote(
                proj.at[0], proj.at[chan_size - r], proj_s.at[r], proj_r.at[chan_size - r],
                c_peer(r),
            ))
        gram[0] = jnp.zeros((MODES, 128), f32)
        gram[0, :, 0:MODES] = lax.dot_general(
            weighted, basis[...], (((1,), (1,)), ((), ())), precision=highest,
            preferred_element_type=f32,
        )
        for r in range(1, chan_size):
            start(remote(
                gram.at[0], gram.at[chan_size - r], gram_s.at[r], gram_r.at[chan_size - r],
                c_peer(r),
            ))

        mid = rows // 2

        def raw_copy(r, piece):
            column = pl.multiple_of(lax.rem(x + r, NX) * quarter, quarter)
            return remote(
                own.at[piece * mid:(piece + 1) * mid, pl.ds(column, quarter)],
                raw.at[NX - r, piece * mid:(piece + 1) * mid], raw_s.at[piece, r],
                raw_r.at[piece, NX - r], x_peer(r),
            )

        for r, piece in ((2, 0), (1, 0), (3, 0), (2, 1)):
            start(raw_copy(r, piece))

        def fill(target, column, group, tap):
            def step(a, carry):
                row = pl.multiple_of(a * TAPS, TAPS)
                target[pl.ds(row, TAPS), column:column + tap.shape[1]] = jnp.where(
                    group == a, tap, 0.0
                ).astype(bf16)
                return carry

            lax.fori_loop(0, npix // TAPS, step, 0, unroll=4)

        def build_band(slot):
            first = pix[slot]
            group = jnp.broadcast_to(first >> 4, (TAPS, rows))
            inner = jnp.broadcast_to(first & (TAPS - 1), (TAPS, rows))
            lane = iota((TAPS, rows), 0)
            turn = (lane - inner) & (TAPS - 1)
            tap = jnp.zeros((TAPS, rows), f32)
            values = taps[...].astype(f32)
            for m in range(TAPS):
                tap = jnp.where(turn == m, values[0:1, m:m + 1], tap)
            fill(band, slot * rows, jnp.where(lane < inner, group + 1, group), tap)

        build_band(0)

        for r in range(1, chan_size):
            remote(gram.at[0], gram.at[r], gram_s.at[r], gram_r.at[r], c_peer(r)).wait_recv()
        total = gram[0]
        for r in range(1, chan_size):
            total = total + gram[r]
        row_id = iota((MODES, 128), 0)
        both = jnp.where(iota((MODES, 128), 1) - MODES == row_id, 1.0, total)
        for i in range(MODES):
            pivot = both[i:i + 1, :] / both[i:i + 1, i:i + 1]
            both = jnp.where(row_id == i, pivot, both - both[:, i:i + 1] * pivot)

        ext[...] = jnp.zeros(ext.shape, f32)
        for r in range(1, chan_size):
            remote(proj.at[0], proj.at[r], proj_s.at[r], proj_r.at[r], c_peer(r)).wait_recv()
        full = proj[0]
        for r in range(1, chan_size):
            full = full + proj[r]
        ext[MODES:2 * MODES, :] = full
        coef[0] = jnp.dot(both, ext[...], precision=highest, preferred_element_type=f32)
        for r in range(1, NX):
            start(remote(coef.at[0], coef.at[NX - r], coef_s.at[r], coef_r.at[NX - r], x_peer(r)))
        for r in (1, 3):
            start(raw_copy(r, 1))

        b_high, b_mid, b_low = split3(basis[:, pl.ds(here, quarter)])
        b_stack = jnp.concatenate(
            [b_high, b_mid, b_high, b_mid, b_low, b_high, jnp.zeros((2 * MODES, quarter), bf16)],
            axis=0,
        )

        def fit_slot(slot):
            c_high, c_mid, c_low = split3(coef[slot])
            c_stack = jnp.concatenate(
                [c_high, c_high, c_mid, c_mid, c_high, c_low, jnp.zeros((2 * MODES, rows), bf16)],
                axis=0,
            )
            ripple[slot * rows:(slot + 1) * rows, :] = lax.dot_general(
                c_stack, b_stack, (((0,), (0,)), ((), ())), preferred_element_type=f32
            )

        def clean_slot(slot, values):
            clean[slot * rows:(slot + 1) * rows, :] = (
                values.astype(f32) - ripple[slot * rows:(slot + 1) * rows, :]
            ).astype(bf16)

        fit_slot(0)
        clean_slot(0, own[:, pl.ds(here, quarter)])
        begin = gal_chan[...] - SW - (j * width + here)
        shift_hot = (iota((shifts, ngal), 0) == quarter - 1 - begin).astype(f32).astype(bf16)
        gal_row = jnp.broadcast_to(gal_pix[...], (TAPS, ngal))
        fill(
            pixel_hot, 0, gal_row >> 4,
            jnp.where((gal_row & (TAPS - 1)) == iota((TAPS, ngal), 0), 1.0, 0.0).astype(f32),
        )
        counts[...] = lax.dot_general(
            shift_hot, pixel_hot[...], (((1,), (1,)), ((), ())), preferred_element_type=f32
        ).astype(bf16)

        for r in range(1, NX):
            remote(pix.at[0], pix.at[r], pix_s.at[r], pix_r.at[r], x_peer(r)).wait_recv()
            build_band(r)
        for r in (1, 3, 2):
            remote(coef.at[0], coef.at[r], coef_s.at[r], coef_r.at[r], x_peer(r)).wait_recv()
            fit_slot(r)
        for r in (2, 1, 3):
            for piece in range(2):
                raw_copy(NX - r, piece).wait_recv()
            clean_slot(r, raw[r])

        def chunk_row(step):
            return pl.multiple_of(lax.rem(z + step + 2 * nz, nz) * zpix, zpix)

        def part_half(step, which):
            row = pl.multiple_of(chunk_row(step) + which * half, half)
            return part[pl.ds(row, half), :]

        def z_copy(way, index):
            return remote(
                zsend.at[way, index], zrecv.at[way, index], z_s.at[way, index],
                z_r.at[way, index], z_peer((1, nz - 1)[way]),
            )

        def z_start(way, index, value):
            zsend[way, index] = value.astype(bf16)
            z_copy(way, index).start()

        def z_take(way, index):
            z_copy(way, index).wait_recv()
            return zrecv[way, index].astype(f32)

        sign = (1, -1)

        def long_step(k):
            for way in range(2):
                got = z_take(way, k)
                z_start(way, k + 1, got + part_half(sign[way] * (far - 1 - k), way))

        def short_step(k):
            for way in range(2):
                got = z_take(way, far + k)
                z_start(
                    way, far + k + 1, got + part_half(sign[way] * (far - 2 - k), 1 - way)
                )

        def grid_step(n, carry):
            away = lax.div(n + 1, 2)
            row = chunk_row(far + away - 2 * lax.rem(n, 2) * away)
            part[pl.ds(row, zpix), :] = jnp.dot(
                band[pl.ds(row, zpix), :], clean[...], preferred_element_type=f32
            )

            @pl.when(n == 0)
            def _():
                for way in range(2):
                    z_start(way, 0, part_half(far, way))

            @pl.when(n == 2)
            def _():
                for way in range(2):
                    z_start(way, far, part_half(sign[way] * (far - 1), 1 - way))

            @pl.when(n == 4)
            def _():
                long_step(0)
                short_step(0)

            return carry

        def share(buffer, me, send_sem, recv_sem, peer_of, count):
            for r in range(1, count):
                start(remote(buffer.at[me], buffer.at[me], send_sem.at[r], recv_sem.at[me], peer_of(r)))

        def gather(buffer, me, send_sem, recv_sem, peer_of, count):
            for r in range(1, count):
                other = lax.rem(me + r, count)
                remote(
                    buffer.at[other], buffer.at[other], send_sem.at[r], recv_sem.at[other], peer_of(r)
                ).wait_recv()
            value = buffer[0]
            for i in range(1, count):
                value = value + buffer[i]
            return value

        lax.fori_loop(0, nz, grid_step, 0)

        long_step(1)
        short_step(1)

        wide = jnp.concatenate(
            [
                jnp.dot(counts[...], part[...].astype(bf16), preferred_element_type=f32),
                jnp.zeros((shifts, 512 - quarter), f32),
            ],
            axis=1,
        )
        folded = jnp.zeros((8, 512), f32)
        for i in range(shifts // 8):
            folded = folded + pltpu.roll(
                wide[8 * i:8 * i + 8], (513 - quarter + 8 * i) % 512, 1
            )
        window = jnp.zeros((1, 512), f32)
        for i in range(8):
            window = window + (pltpu.roll(folded[i:i + 1], i, 1) if i else folded[i:i + 1])
        st1[x] = window[:, :2 * SW]
        share(st1, x, st1_s, st1_r, x_peer, NX)

        long_step(2)
        st2[j] = gather(st1, x, st1_s, st1_r, x_peer, NX)
        share(st2, j, st2_s, st2_r, c_peer, chan_size)
        for copy in sends:
            copy.wait_send()
        sends.clear()

        got = [z_take(way, 2 * far - 2) for way in range(2)]
        for way in range(2):
            value = z_take(way, far - 1) + got[1 - way] + part_half(0, way)
            final[way * half:(way + 1) * half, :] = value.astype(bf16)
        for r in (2, 1, 3):
            row = pl.multiple_of(lax.rem(x + r, NX) * TP, TP)
            start(remote(
                final.at[pl.ds(row, TP), :], sky.at[:, pl.ds(here, quarter)], fin_s.at[r],
                fin_r.at[NX - r], x_peer(r),
            ))
        sky[:, pl.ds(here, quarter)] = final[pl.ds(pl.multiple_of(x * TP, TP), TP), :]

        st3[z] = gather(st2, j, st2_s, st2_r, c_peer, chan_size)
        share(st3, z, st3_s, st3_r, z_peer, nz)
        for way in range(2):
            for index in range(2 * far - 1):
                z_copy(way, index).wait_send()
        for r in range(1, NX):
            column = pl.multiple_of(lax.rem(x + r, NX) * quarter, quarter)
            remote(
                final.at[pl.ds(0, TP), :], sky.at[:, pl.ds(column, quarter)], fin_s.at[r],
                fin_r.at[r], x_peer(r),
            ).wait_recv()
        stacked[...] = gather(st3, z, st3_s, st3_r, z_peer, nz) / ngal
        for copy in sends:
            copy.wait_send()

    dma = pltpu.SemaphoreType.DMA
    scratch = [
        pltpu.VMEM((rows, width), bf16),
        pltpu.VMEM((MODES, width), f32),
        pltpu.VMEM((NX, 1, rows), jnp.int32),
        pltpu.VMEM((NX, rows, quarter), bf16),
        pltpu.VMEM((chan_size, MODES, 128), f32),
        pltpu.VMEM((chan_size, MODES, rows), f32),
        pltpu.VMEM((128, rows), f32),
        pltpu.VMEM((NX, MODES, rows), f32),
        pltpu.VMEM((npix, NX * rows), bf16),
        pltpu.VMEM((NX * rows, quarter), f32),
        pltpu.VMEM((NX * rows, quarter), bf16),
        pltpu.VMEM((npix, quarter), f32),
        pltpu.VMEM((npix, ngal), bf16),
        pltpu.VMEM((shifts, npix), bf16),
        pltpu.VMEM((2, nz - 1, half, quarter), bf16),
        pltpu.VMEM((2, nz - 1, half, quarter), bf16),
        pltpu.VMEM((zpix, quarter), bf16),
        pltpu.VMEM((NX, 1, 2 * SW), f32),
        pltpu.VMEM((chan_size, 1, 2 * SW), f32),
        pltpu.VMEM((nz, 1, 2 * SW), f32),
        dma((2,)),
    ]
    for shape in (
        (NX,), (2, NX), (chan_size,), (chan_size,), (NX,), (2, nz - 1), (NX,),
        (NX,), (chan_size,), (nz,),
    ):
        scratch += [dma(shape), dma(shape)]
    return kernel, scratch


def solution(mesh):
    tm_size, chan_size = mesh.shape["tm"], mesh.shape["chan"]

    def per_device(spectra, chan_weight, routes, offsets, taps, gal_pix, gal_chan):
        rows, width = spectra.shape
        nblocks = routes.shape[0]
        kernel, scratch = make_kernel(
            tm_size, chan_size, rows, width, nblocks, gal_pix.shape[0]
        )
        vmem = pl.BlockSpec(memory_space=pltpu.VMEM)
        sky, stacked = pl.pallas_call(
            kernel,
            out_shape=(
                jax.ShapeDtypeStruct((TP, width), bf16),
                jax.ShapeDtypeStruct((1, 2 * SW), f32),
            ),
            in_specs=[pl.BlockSpec(memory_space=pl.ANY)] * 2 + [vmem] * 6,
            out_specs=(vmem, vmem),
            scratch_shapes=scratch,
            compiler_params=pltpu.CompilerParams(
                collective_id=0, has_side_effects=True, vmem_limit_bytes=54880 * 1024
            ),
        )(
            spectra, jnp.asarray(basis_table(width * chan_size)), chan_weight[None, :],
            routes.reshape(1, nblocks), offsets[None, :], taps[None, :], gal_pix[None, :],
            gal_chan[None, :],
        )
        return sky, stacked[0]

    in_specs = (
        P("tm", "chan"), P("chan"), P("tm", None), P("tm"), P(None), P(None), P(None)
    )
    return jax.shard_map(
        per_device, mesh=mesh, in_specs=in_specs, out_specs=(P("tm", "chan"), P(None)),
        check_vma=False,
    )
```

```python
import jax
import jax.numpy as jnp
import numpy as np
from jax import lax
from jax.experimental import pallas as pl
from jax.experimental.pallas import tpu as pltpu
from jax.sharding import PartitionSpec as P

KMODES = 8
MODES = 2 * KMODES
TP = 64
MARGIN = 8
SW = 64
TAPS = 16
NX = 4

highest = lax.Precision.HIGHEST
MESH = pl.DeviceIdType.MESH
f32 = jnp.float32
bf16 = jnp.bfloat16


def basis_table(total):
    orders = np.arange(1, KMODES + 1)[:, None]
    phase = (orders * np.arange(total)[None, :] % total) * (2 * np.pi / total)
    return np.concatenate([np.cos(phase), np.sin(phase)], axis=0).astype(np.float32)


def split3(value):
    high = value.astype(bf16)
    rest = value - high.astype(f32)
    mid = rest.astype(bf16)
    low = (rest - mid.astype(f32)).astype(bf16)
    return high, mid, low


def iota(shape, dim):
    return lax.broadcasted_iota(jnp.int32, shape, dim)


def make_kernel(tm_size, chan_size, rows, width, nblocks, ngal):
    nz = tm_size // NX
    quarter = width // NX
    npix = tm_size * TP
    zpix = NX * TP
    half = zpix // 2
    block_rows = rows // nblocks
    shifts = quarter + 2 * SW
    far = nz // 2

    def kernel(
        spec, basis_in, weight, routes, offsets, taps, gal_pix, gal_chan,
        sky, stacked,
        own, basis, pix, raw, gram, proj, ext, coef, band, ripple, clean, part, pixel_hot, counts,
        zsend, zrecv, edge, final, mine, st1, st2, st3,
        load_sem, pix_s, pix_r, raw_s, raw_r, gram_s, gram_r, proj_s, proj_r, coef_s, coef_r,
        z_s, z_r, edge_s, edge_r, mine_s, mine_r, st1_s, st1_r, st2_s, st2_r, st3_s, st3_r,
    ):
        tm = lax.axis_index("tm")
        j = lax.axis_index("chan")
        z = lax.div(tm, NX)
        x = lax.rem(tm, NX)
        here = pl.multiple_of(x * quarter, quarter)

        def x_peer(r):
            return (z * NX + lax.rem(x + r, NX), j)

        def c_peer(r):
            return (tm, lax.rem(j + r, chan_size))

        def z_peer(r):
            return (lax.rem(z + r, nz) * NX + x, j)

        def beside(way, place):
            return (lax.rem(place[0] + (NX, (nz - 1) * NX)[way], tm_size), place[1])

        def remote(src, dst, send_sem, recv_sem, peer):
            return pltpu.make_async_remote_copy(
                src_ref=src, dst_ref=dst, send_sem=send_sem, recv_sem=recv_sem,
                device_id=peer, device_id_type=MESH,
            )

        sends = []

        def start(copy):
            copy.start()
            sends.append(copy)

        peers = (
            [x_peer(r) for r in range(1, NX)]
            + [c_peer(r) for r in range(1, chan_size)]
            + [z_peer(r) for r in range(1, nz)]
            + [beside(way, x_peer(r)) for way in range(2) for r in range(1, NX)]
        )
        barrier = pltpu.get_barrier_semaphore()
        for peer in peers:
            pl.semaphore_signal(barrier, inc=1, device_id=peer, device_id_type=MESH)
        basis_here = basis_in.at[:, pl.ds(pl.multiple_of(j * width, width), width)]
        loads = [
            pltpu.make_async_copy(source, target, load_sem.at[i])
            for i, (source, target) in enumerate((
                (spec, own), (basis_here, basis),
            ))
        ]
        for load in loads:
            load.start()
        inside = iota((nblocks, rows), 1) - block_rows * iota((nblocks, rows), 0)
        owner = ((inside >= 0) & (inside < block_rows)).astype(f32).astype(bf16)
        tile = jnp.dot(
            jnp.broadcast_to(routes[...], (16, nblocks)).astype(f32).astype(bf16), owner,
            preferred_element_type=f32,
        )[0:1].astype(jnp.int32)
        pix[0] = tile * TP + offsets[...] - MARGIN

        pl.semaphore_wait(barrier, len(peers))
        for r in range(1, NX):
            start(remote(pix.at[0], pix.at[NX - r], pix_s.at[r], pix_r.at[NX - r], x_peer(r)))

        loads[0].wait()
        for r in (2, 1, 3):
            column = pl.multiple_of(lax.rem(x + r, NX) * quarter, quarter)
            start(remote(
                own.at[:, pl.ds(column, quarter)], raw.at[NX - r], raw_s.at[r], raw_r.at[NX - r],
                x_peer(r),
            ))

        loads[1].wait()
        weighted = basis[...] * weight[...]
        gram[0] = jnp.zeros((MODES, 128), f32)
        gram[0, :, 0:MODES] = lax.dot_general(
            weighted, basis[...], (((1,), (1,)), ((), ())), precision=highest,
            preferred_element_type=f32,
        )
        for r in range(1, chan_size):
            start(remote(
                gram.at[0], gram.at[chan_size - r], gram_s.at[r], gram_r.at[chan_size - r],
                c_peer(r),
            ))
        w_stack = jnp.concatenate(split3(weighted), axis=0)
        products = lax.dot_general(
            w_stack, own[...], (((1,), (1,)), ((), ())), preferred_element_type=f32
        )
        proj[0] = products[:MODES] + products[MODES:2 * MODES] + products[2 * MODES:]
        for r in range(1, chan_size):
            start(remote(
                proj.at[0], proj.at[chan_size - r], proj_s.at[r], proj_r.at[chan_size - r],
                c_peer(r),
            ))

        def fill(target, column, group, tap):
            def step(a, carry):
                row = pl.multiple_of(a * TAPS, TAPS)
                target[pl.ds(row, TAPS), column:column + tap.shape[1]] = jnp.where(
                    group == a, tap, 0.0
                ).astype(bf16)
                return carry

            lax.fori_loop(0, npix // TAPS, step, 0, unroll=4)

        def build_band(slot):
            first = pix[slot]
            group = jnp.broadcast_to(first >> 4, (TAPS, rows))
            inner = jnp.broadcast_to(first & (TAPS - 1), (TAPS, rows))
            lane = iota((TAPS, rows), 0)
            turn = (lane - inner) & (TAPS - 1)
            tap = jnp.zeros((TAPS, rows), f32)
            values = taps[...].astype(f32)
            for m in range(TAPS):
                tap = jnp.where(turn == m, values[0:1, m:m + 1], tap)
            fill(band, slot * rows, jnp.where(lane < inner, group + 1, group), tap)

        build_band(0)

        for r in range(1, chan_size):
            remote(gram.at[0], gram.at[r], gram_s.at[r], gram_r.at[r], c_peer(r)).wait_recv()
        total = gram[0]
        for r in range(1, chan_size):
            total = total + gram[r]
        row_id = iota((MODES, 128), 0)
        both = jnp.where(iota((MODES, 128), 1) - MODES == row_id, 1.0, total)
        for i in range(MODES):
            pivot = both[i:i + 1, :] / both[i:i + 1, i:i + 1]
            both = jnp.where(row_id == i, pivot, both - both[:, i:i + 1] * pivot)

        ext[...] = jnp.zeros(ext.shape, f32)
        for r in range(1, chan_size):
            remote(proj.at[0], proj.at[r], proj_s.at[r], proj_r.at[r], c_peer(r)).wait_recv()
        full = proj[0]
        for r in range(1, chan_size):
            full = full + proj[r]
        ext[MODES:2 * MODES, :] = full
        coef[0] = jnp.dot(both, ext[...], precision=highest, preferred_element_type=f32)
        for r in range(1, NX):
            start(remote(coef.at[0], coef.at[NX - r], coef_s.at[r], coef_r.at[NX - r], x_peer(r)))

        b_high, b_mid, b_low = split3(basis[:, pl.ds(here, quarter)])
        b_stack = jnp.concatenate(
            [b_high, b_mid, b_high, b_mid, b_low, b_high, jnp.zeros((2 * MODES, quarter), bf16)],
            axis=0,
        )

        def fit_slot(slot):
            c_high, c_mid, c_low = split3(coef[slot])
            c_stack = jnp.concatenate(
                [c_high, c_high, c_mid, c_mid, c_high, c_low, jnp.zeros((2 * MODES, rows), bf16)],
                axis=0,
            )
            ripple[slot * rows:(slot + 1) * rows, :] = lax.dot_general(
                c_stack, b_stack, (((0,), (0,)), ((), ())), preferred_element_type=f32
            )

        def clean_slot(slot, values):
            clean[slot * rows:(slot + 1) * rows, :] = (
                values.astype(f32) - ripple[slot * rows:(slot + 1) * rows, :]
            ).astype(bf16)

        fit_slot(0)
        clean_slot(0, own[:, pl.ds(here, quarter)])
        begin = gal_chan[...] - SW - (j * width + here)
        shift_hot = (iota((shifts, ngal), 0) == quarter - 1 - begin).astype(f32).astype(bf16)
        gal_row = jnp.broadcast_to(gal_pix[...], (TAPS, ngal))
        fill(
            pixel_hot, 0, gal_row >> 4,
            jnp.where((gal_row & (TAPS - 1)) == iota((TAPS, ngal), 0), 1.0, 0.0).astype(f32),
        )
        counts[...] = lax.dot_general(
            shift_hot, pixel_hot[...], (((1,), (1,)), ((), ())), preferred_element_type=f32
        ).astype(bf16)

        for r in range(1, NX):
            remote(pix.at[0], pix.at[r], pix_s.at[r], pix_r.at[r], x_peer(r)).wait_recv()
            build_band(r)
        for r in (1, 3, 2):
            remote(coef.at[0], coef.at[r], coef_s.at[r], coef_r.at[r], x_peer(r)).wait_recv()
            fit_slot(r)
        for r in (1, 3, 2):
            remote(
                own.at[:, pl.ds(0, quarter)], raw.at[r], raw_s.at[r], raw_r.at[r], x_peer(r)
            ).wait_recv()
            clean_slot(r, raw[r])

        def chunk_row(step):
            return pl.multiple_of(lax.rem(z + step + 2 * nz, nz) * zpix, zpix)

        def part_half(step, which):
            row = pl.multiple_of(chunk_row(step) + which * half, half)
            return part[pl.ds(row, half), :]

        def z_copy(way, index):
            return remote(
                zsend.at[way, index], zrecv.at[way, index], z_s.at[way, index],
                z_r.at[way, index], z_peer((1, nz - 1)[way]),
            )

        def z_start(way, index, value):
            zsend[way, index] = value.astype(bf16)
            z_copy(way, index).start()

        def z_take(way, index):
            z_copy(way, index).wait_recv()
            return zrecv[way, index].astype(f32)

        sign = (1, -1)

        def edge_copy(way, tile, index):
            return remote(
                zsend.at[way, index, tile % 2 * TP:(tile % 2 + 1) * TP], edge.at[way, x],
                edge_s.at[way, tile], edge_r.at[way, x], beside(way, (z * NX + tile, j)),
            )

        def edge_start(way, index, which, value):
            zsend[way, index] = value.astype(bf16)
            for tile in (2 * which, 2 * which + 1):
                edge_copy(way, tile, index).start()

        def long_step(k):
            for way in range(2):
                value = z_take(way, k) + part_half(sign[way] * (far - 1 - k), way)
                if k < far - 2:
                    z_start(way, k + 1, value)
                else:
                    edge_start(way, k + 1, way, value)

        def short_step(k):
            for way in range(2):
                value = z_take(way, far + k) + part_half(sign[way] * (far - 2 - k), 1 - way)
                if k < far - 3:
                    z_start(way, far + k + 1, value)
                else:
                    edge_start(way, far + k + 1, 1 - way, value)

        def grid_step(n, carry):
            away = lax.div(n + 1, 2)
            row = chunk_row(far + away - 2 * lax.rem(n, 2) * away)
            part[pl.ds(row, zpix), :] = jnp.dot(
                band[pl.ds(row, zpix), :], clean[...], preferred_element_type=f32
            )

            @pl.when(n == 0)
            def _():
                for way in range(2):
                    z_start(way, 0, part_half(far, way))

            @pl.when(n == 2)
            def _():
                for way in range(2):
                    z_start(way, far, part_half(sign[way] * (far - 1), 1 - way))

            @pl.when(n == 4)
            def _():
                long_step(0)
                short_step(0)

            return carry

        def share(buffer, me, send_sem, recv_sem, peer_of, count):
            for r in range(1, count):
                start(remote(buffer.at[me], buffer.at[me], send_sem.at[r], recv_sem.at[me], peer_of(r)))

        def gather(buffer, me, send_sem, recv_sem, peer_of, count):
            for r in range(1, count):
                other = lax.rem(me + r, count)
                remote(
                    buffer.at[other], buffer.at[other], send_sem.at[r], recv_sem.at[other], peer_of(r)
                ).wait_recv()
            value = buffer[0]
            for i in range(1, count):
                value = value + buffer[i]
            return value

        lax.fori_loop(0, nz, grid_step, 0)

        final[...] = part[pl.ds(chunk_row(0), zpix), :].astype(bf16)
        for r in range(1, NX):
            row = pl.multiple_of(lax.rem(x + r, NX) * TP, TP)
            start(remote(
                final.at[pl.ds(row, TP), :], mine.at[NX - r], mine_s.at[r], mine_r.at[NX - r],
                x_peer(r),
            ))

        wide = jnp.concatenate(
            [
                jnp.dot(counts[...], part[...].astype(bf16), preferred_element_type=f32),
                jnp.zeros((shifts, 512 - quarter), f32),
            ],
            axis=1,
        )
        folded = jnp.zeros((8, 512), f32)
        for i in range(shifts // 8):
            folded = folded + pltpu.roll(
                wide[8 * i:8 * i + 8], (513 - quarter + 8 * i) % 512, 1
            )
        window = jnp.zeros((1, 512), f32)
        for i in range(8):
            window = window + (pltpu.roll(folded[i:i + 1], i, 1) if i else folded[i:i + 1])
        st1[x] = window[:, :2 * SW]
        share(st1, x, st1_s, st1_r, x_peer, NX)

        long_step(1)
        st2[j] = gather(st1, x, st1_s, st1_r, x_peer, NX)
        share(st2, j, st2_s, st2_r, c_peer, chan_size)
        short_step(1)
        long_step(2)
        st3[z] = gather(st2, j, st2_s, st2_r, c_peer, chan_size)
        share(st3, z, st3_s, st3_r, z_peer, nz)
        for r in range(1, NX):
            remote(
                final.at[pl.ds(0, TP), :], mine.at[r], mine_s.at[r], mine_r.at[r], x_peer(r)
            ).wait_recv()
        for copy in sends:
            copy.wait_send()
        for way in range(2):
            for index in range(2 * far - 1):
                if index not in (far - 1, 2 * far - 2):
                    z_copy(way, index).wait_send()

        for way in range(2):
            for source in range(NX):
                remote(
                    zsend.at[way, 0, 0:TP], edge.at[way, source], edge_s.at[way, source],
                    edge_r.at[way, source], beside(way, x_peer(0)),
                ).wait_recv()
        for r in range(NX):
            source = lax.rem(x + r, NX)
            if r:
                value = mine[r].astype(f32)
            else:
                value = part[pl.ds(pl.multiple_of(chunk_row(0) + x * TP, TP), TP), :]
            value = value + edge[0, source].astype(f32) + edge[1, source].astype(f32)
            column = pl.multiple_of(source * quarter, quarter)
            sky[:, pl.ds(column, quarter)] = value.astype(bf16)
        stacked[...] = gather(st3, z, st3_s, st3_r, z_peer, nz) / ngal
        for way in range(2):
            for tile in range(NX):
                edge_copy(way, tile, 0).wait_send()

    dma = pltpu.SemaphoreType.DMA
    scratch = [
        pltpu.VMEM((rows, width), bf16),
        pltpu.VMEM((MODES, width), f32),
        pltpu.VMEM((NX, 1, rows), jnp.int32),
        pltpu.VMEM((NX, rows, quarter), bf16),
        pltpu.VMEM((chan_size, MODES, 128), f32),
        pltpu.VMEM((chan_size, MODES, rows), f32),
        pltpu.VMEM((128, rows), f32),
        pltpu.VMEM((NX, MODES, rows), f32),
        pltpu.VMEM((npix, NX * rows), bf16),
        pltpu.VMEM((NX * rows, quarter), f32),
        pltpu.VMEM((NX * rows, quarter), bf16),
        pltpu.VMEM((npix, quarter), f32),
        pltpu.VMEM((npix, ngal), bf16),
        pltpu.VMEM((shifts, npix), bf16),
        pltpu.VMEM((2, nz - 1, half, quarter), bf16),
        pltpu.VMEM((2, nz - 1, half, quarter), bf16),
        pltpu.VMEM((2, NX, TP, quarter), bf16),
        pltpu.VMEM((zpix, quarter), bf16),
        pltpu.VMEM((NX, TP, quarter), bf16),
        pltpu.VMEM((NX, 1, 2 * SW), f32),
        pltpu.VMEM((chan_size, 1, 2 * SW), f32),
        pltpu.VMEM((nz, 1, 2 * SW), f32),
        dma((2,)),
    ]
    for shape in (
        (NX,), (NX,), (chan_size,), (chan_size,), (NX,), (2, nz - 1), (2, NX), (NX,),
        (NX,), (chan_size,), (nz,),
    ):
        scratch += [dma(shape), dma(shape)]
    return kernel, scratch


def solution(mesh):
    tm_size, chan_size = mesh.shape["tm"], mesh.shape["chan"]

    def per_device(spectra, chan_weight, routes, offsets, taps, gal_pix, gal_chan):
        rows, width = spectra.shape
        nblocks = routes.shape[0]
        kernel, scratch = make_kernel(
            tm_size, chan_size, rows, width, nblocks, gal_pix.shape[0]
        )
        vmem = pl.BlockSpec(memory_space=pltpu.VMEM)
        sky, stacked = pl.pallas_call(
            kernel,
            out_shape=(
                jax.ShapeDtypeStruct((TP, width), bf16),
                jax.ShapeDtypeStruct((1, 2 * SW), f32),
            ),
            in_specs=[pl.BlockSpec(memory_space=pl.ANY)] * 2 + [vmem] * 6,
            out_specs=(vmem, vmem),
            scratch_shapes=scratch,
            compiler_params=pltpu.CompilerParams(
                collective_id=0, has_side_effects=True, vmem_limit_bytes=54880 * 1024
            ),
        )(
            spectra, jnp.asarray(basis_table(width * chan_size)), chan_weight[None, :],
            routes.reshape(1, nblocks), offsets[None, :], taps[None, :], gal_pix[None, :],
            gal_chan[None, :],
        )
        return sky, stacked[0]

    in_specs = (
        P("tm", "chan"), P("chan"), P("tm", None), P("tm"), P(None), P(None), P(None)
    )
    return jax.shard_map(
        per_device, mesh=mesh, in_specs=in_specs, out_specs=(P("tm", "chan"), P(None)),
        check_vma=False,
    )
```

```python
import jax
import jax.numpy as jnp
import numpy as np
from jax import lax
from jax.experimental import pallas as pl
from jax.experimental.pallas import tpu as pltpu
from jax.sharding import PartitionSpec as P

KMODES = 8
MODES = 2 * KMODES
TP = 64
MARGIN = 8
SW = 64
TAPS = 16
NX = 4

highest = lax.Precision.HIGHEST
MESH = pl.DeviceIdType.MESH
f32 = jnp.float32
bf16 = jnp.bfloat16


def basis_table(total):
    orders = np.arange(1, KMODES + 1)[:, None]
    phase = (orders * np.arange(total)[None, :] % total) * (2 * np.pi / total)
    return np.concatenate([np.cos(phase), np.sin(phase)], axis=0).astype(np.float32)


def split3(value):
    high = value.astype(bf16)
    rest = value - high.astype(f32)
    mid = rest.astype(bf16)
    low = (rest - mid.astype(f32)).astype(bf16)
    return high, mid, low


def iota(shape, dim):
    return lax.broadcasted_iota(jnp.int32, shape, dim)


def make_kernel(tm_size, chan_size, rows, width, nblocks, ngal):
    nz = tm_size // NX
    quarter = width // NX
    npix = tm_size * TP
    zpix = NX * TP
    half = zpix // 2
    block_rows = rows // nblocks
    shifts = quarter + 2 * SW
    far = nz // 2

    def kernel(
        spec, basis_in, weight, routes, offsets, taps, gal_pix, gal_chan,
        sky, stacked,
        own, basis, pix, raw, gram, proj, ext, coef, band, ripple, clean, part, pixel_hot, counts,
        zsend, zrecv, edge, final, mine, st1, st2, st3,
        load_sem, pix_s, pix_r, raw_s, raw_r, gram_s, gram_r, proj_s, proj_r, coef_s, coef_r,
        z_s, z_r, edge_s, edge_r, mine_s, mine_r, st1_s, st1_r, st2_s, st2_r, st3_s, st3_r,
    ):
        tm = lax.axis_index("tm")
        j = lax.axis_index("chan")
        z = lax.div(tm, NX)
        x = lax.rem(tm, NX)
        here = pl.multiple_of(x * quarter, quarter)

        def x_peer(r):
            return (z * NX + lax.rem(x + r, NX), j)

        def c_peer(r):
            return (tm, lax.rem(j + r, chan_size))

        def z_peer(r):
            return (lax.rem(z + r, nz) * NX + x, j)

        def beside(way, place):
            return (lax.rem(place[0] + (NX, (nz - 1) * NX)[way], tm_size), place[1])

        def remote(src, dst, send_sem, recv_sem, peer):
            return pltpu.make_async_remote_copy(
                src_ref=src, dst_ref=dst, send_sem=send_sem, recv_sem=recv_sem,
                device_id=peer, device_id_type=MESH,
            )

        sends = []

        def start(copy):
            copy.start()
            sends.append(copy)

        peers = (
            [x_peer(r) for r in range(1, NX)]
            + [c_peer(r) for r in range(1, chan_size)]
            + [z_peer(r) for r in range(1, nz)]
            + [beside(way, x_peer(r)) for way in range(2) for r in range(1, NX)]
        )
        barrier = pltpu.get_barrier_semaphore()
        for peer in peers:
            pl.semaphore_signal(barrier, inc=1, device_id=peer, device_id_type=MESH)
        basis_here = basis_in.at[:, pl.ds(pl.multiple_of(j * width, width), width)]
        loads = [
            pltpu.make_async_copy(source, target, load_sem.at[i])
            for i, (source, target) in enumerate((
                (spec, own), (basis_here, basis),
            ))
        ]
        for load in loads:
            load.start()
        inside = iota((nblocks, rows), 1) - block_rows * iota((nblocks, rows), 0)
        owner = ((inside >= 0) & (inside < block_rows)).astype(f32).astype(bf16)
        tile = jnp.dot(
            jnp.broadcast_to(routes[...], (16, nblocks)).astype(f32).astype(bf16), owner,
            preferred_element_type=f32,
        )[0:1].astype(jnp.int32)
        pix[0] = tile * TP + offsets[...] - MARGIN

        loads[1].wait()
        weighted = basis[...] * weight[...]
        w_stack = jnp.concatenate(split3(weighted), axis=0)

        pl.semaphore_wait(barrier, len(peers))
        for r in range(1, NX):
            start(remote(pix.at[0], pix.at[NX - r], pix_s.at[r], pix_r.at[NX - r], x_peer(r)))

        mid = rows // 2

        def raw_copy(r, piece):
            column = pl.multiple_of(lax.rem(x + r, NX) * quarter, quarter)
            return remote(
                own.at[piece * mid:(piece + 1) * mid, pl.ds(column, quarter)],
                raw.at[NX - r, piece * mid:(piece + 1) * mid], raw_s.at[piece, r],
                raw_r.at[piece, NX - r], x_peer(r),
            )

        loads[0].wait()
        for r, piece in ((2, 0), (1, 0), (3, 0), (2, 1)):
            start(raw_copy(r, piece))

        products = lax.dot_general(
            w_stack, own[...], (((1,), (1,)), ((), ())), preferred_element_type=f32
        )
        proj[0] = products[:MODES] + products[MODES:2 * MODES] + products[2 * MODES:]
        for r in range(1, chan_size):
            start(remote(
                proj.at[0], proj.at[chan_size - r], proj_s.at[r], proj_r.at[chan_size - r],
                c_peer(r),
            ))
        gram[0] = jnp.zeros((MODES, 128), f32)
        gram[0, :, 0:MODES] = lax.dot_general(
            weighted, basis[...], (((1,), (1,)), ((), ())), precision=highest,
            preferred_element_type=f32,
        )
        for r in range(1, chan_size):
            start(remote(
                gram.at[0], gram.at[chan_size - r], gram_s.at[r], gram_r.at[chan_size - r],
                c_peer(r),
            ))

        def fill(target, column, group, tap):
            def step(a, carry):
                row = pl.multiple_of(a * TAPS, TAPS)
                target[pl.ds(row, TAPS), column:column + tap.shape[1]] = jnp.where(
                    group == a, tap, 0.0
                ).astype(bf16)
                return carry

            lax.fori_loop(0, npix // TAPS, step, 0, unroll=4)

        def build_band(slot):
            first = pix[slot]
            group = jnp.broadcast_to(first >> 4, (TAPS, rows))
            inner = jnp.broadcast_to(first & (TAPS - 1), (TAPS, rows))
            lane = iota((TAPS, rows), 0)
            turn = (lane - inner) & (TAPS - 1)
            tap = jnp.zeros((TAPS, rows), f32)
            values = taps[...].astype(f32)
            for m in range(TAPS):
                tap = jnp.where(turn == m, values[0:1, m:m + 1], tap)
            fill(band, slot * rows, jnp.where(lane < inner, group + 1, group), tap)

        build_band(0)

        for r in range(1, chan_size):
            remote(gram.at[0], gram.at[r], gram_s.at[r], gram_r.at[r], c_peer(r)).wait_recv()
        total = gram[0]
        for r in range(1, chan_size):
            total = total + gram[r]
        row_id = iota((MODES, 128), 0)
        both = jnp.where(iota((MODES, 128), 1) - MODES == row_id, 1.0, total)
        for i in range(MODES):
            pivot = both[i:i + 1, :] / both[i:i + 1, i:i + 1]
            both = jnp.where(row_id == i, pivot, both - both[:, i:i + 1] * pivot)

        ext[...] = jnp.zeros(ext.shape, f32)
        for r in range(1, chan_size):
            remote(proj.at[0], proj.at[r], proj_s.at[r], proj_r.at[r], c_peer(r)).wait_recv()
        full = proj[0]
        for r in range(1, chan_size):
            full = full + proj[r]
        ext[MODES:2 * MODES, :] = full
        coef[0] = jnp.dot(both, ext[...], precision=highest, preferred_element_type=f32)
        for r in range(1, NX):
            start(remote(coef.at[0], coef.at[NX - r], coef_s.at[r], coef_r.at[NX - r], x_peer(r)))
        for r in (1, 3):
            start(raw_copy(r, 1))

        b_high, b_mid, b_low = split3(basis[:, pl.ds(here, quarter)])
        b_stack = jnp.concatenate(
            [b_high, b_mid, b_high, b_mid, b_low, b_high, jnp.zeros((2 * MODES, quarter), bf16)],
            axis=0,
        )

        def fit_slot(slot):
            c_high, c_mid, c_low = split3(coef[slot])
            c_stack = jnp.concatenate(
                [c_high, c_high, c_mid, c_mid, c_high, c_low, jnp.zeros((2 * MODES, rows), bf16)],
                axis=0,
            )
            ripple[slot * rows:(slot + 1) * rows, :] = lax.dot_general(
                c_stack, b_stack, (((0,), (0,)), ((), ())), preferred_element_type=f32
            )

        def clean_slot(slot, values):
            clean[slot * rows:(slot + 1) * rows, :] = (
                values.astype(f32) - ripple[slot * rows:(slot + 1) * rows, :]
            ).astype(bf16)

        fit_slot(0)
        clean_slot(0, own[:, pl.ds(here, quarter)])
        begin = gal_chan[...] - SW - (j * width + here)
        shift_hot = (iota((shifts, ngal), 0) == quarter - 1 - begin).astype(f32).astype(bf16)
        gal_row = jnp.broadcast_to(gal_pix[...], (TAPS, ngal))
        fill(
            pixel_hot, 0, gal_row >> 4,
            jnp.where((gal_row & (TAPS - 1)) == iota((TAPS, ngal), 0), 1.0, 0.0).astype(f32),
        )
        counts[...] = lax.dot_general(
            shift_hot, pixel_hot[...], (((1,), (1,)), ((), ())), preferred_element_type=f32
        ).astype(bf16)

        for r in range(1, NX):
            remote(pix.at[0], pix.at[r], pix_s.at[r], pix_r.at[r], x_peer(r)).wait_recv()
            build_band(r)
        for r in (1, 3, 2):
            remote(coef.at[0], coef.at[r], coef_s.at[r], coef_r.at[r], x_peer(r)).wait_recv()
            fit_slot(r)
        for r in (2, 1, 3):
            for piece in range(2):
                raw_copy(NX - r, piece).wait_recv()
            clean_slot(r, raw[r])

        def chunk_row(step):
            return pl.multiple_of(lax.rem(z + step + 2 * nz, nz) * zpix, zpix)

        def part_half(step, which):
            row = pl.multiple_of(chunk_row(step) + which * half, half)
            return part[pl.ds(row, half), :]

        def z_copy(way, index):
            return remote(
                zsend.at[way, index], zrecv.at[way, index], z_s.at[way, index],
                z_r.at[way, index], z_peer((1, nz - 1)[way]),
            )

        def z_start(way, index, value):
            zsend[way, index] = value.astype(bf16)
            z_copy(way, index).start()

        def z_take(way, index):
            z_copy(way, index).wait_recv()
            return zrecv[way, index].astype(f32)

        sign = (1, -1)

        def edge_copy(way, tile, index):
            return remote(
                zsend.at[way, index, tile % 2 * TP:(tile % 2 + 1) * TP], edge.at[way, x],
                edge_s.at[way, tile], edge_r.at[way, x], beside(way, (z * NX + tile, j)),
            )

        def edge_start(way, index, which, value):
            zsend[way, index] = value.astype(bf16)
            for tile in (2 * which, 2 * which + 1):
                edge_copy(way, tile, index).start()

        def long_step(k):
            for way in range(2):
                value = z_take(way, k) + part_half(sign[way] * (far - 1 - k), way)
                if k < far - 2:
                    z_start(way, k + 1, value)
                else:
                    edge_start(way, k + 1, way, value)

        def short_step(k):
            for way in range(2):
                value = z_take(way, far + k) + part_half(sign[way] * (far - 2 - k), 1 - way)
                if k < far - 3:
                    z_start(way, far + k + 1, value)
                else:
                    edge_start(way, far + k + 1, 1 - way, value)

        def grid_step(n, carry):
            away = lax.div(n + 1, 2)
            row = chunk_row(far + away - 2 * lax.rem(n, 2) * away)
            part[pl.ds(row, zpix), :] = jnp.dot(
                band[pl.ds(row, zpix), :], clean[...], preferred_element_type=f32
            )

            @pl.when(n == 0)
            def _():
                for way in range(2):
                    z_start(way, 0, part_half(far, way))

            @pl.when(n == 2)
            def _():
                for way in range(2):
                    z_start(way, far, part_half(sign[way] * (far - 1), 1 - way))

            @pl.when(n == 4)
            def _():
                long_step(0)
                short_step(0)

            return carry

        def share(buffer, me, send_sem, recv_sem, peer_of, count):
            for r in range(1, count):
                start(remote(buffer.at[me], buffer.at[me], send_sem.at[r], recv_sem.at[me], peer_of(r)))

        def gather(buffer, me, send_sem, recv_sem, peer_of, count):
            for r in range(1, count):
                other = lax.rem(me + r, count)
                remote(
                    buffer.at[other], buffer.at[other], send_sem.at[r], recv_sem.at[other], peer_of(r)
                ).wait_recv()
            value = buffer[0]
            for i in range(1, count):
                value = value + buffer[i]
            return value

        lax.fori_loop(0, nz, grid_step, 0)

        final[...] = part[pl.ds(chunk_row(0), zpix), :].astype(bf16)
        for r in range(1, NX):
            row = pl.multiple_of(lax.rem(x + r, NX) * TP, TP)
            start(remote(
                final.at[pl.ds(row, TP), :], mine.at[NX - r], mine_s.at[r], mine_r.at[NX - r],
                x_peer(r),
            ))

        wide = jnp.concatenate(
            [
                jnp.dot(counts[...], part[...].astype(bf16), preferred_element_type=f32),
                jnp.zeros((shifts, 512 - quarter), f32),
            ],
            axis=1,
        )
        folded = jnp.zeros((8, 512), f32)
        for i in range(shifts // 8):
            folded = folded + pltpu.roll(
                wide[8 * i:8 * i + 8], (513 - quarter + 8 * i) % 512, 1
            )
        window = jnp.zeros((1, 512), f32)
        for i in range(8):
            window = window + (pltpu.roll(folded[i:i + 1], i, 1) if i else folded[i:i + 1])
        st1[x] = window[:, :2 * SW]
        share(st1, x, st1_s, st1_r, x_peer, NX)

        long_step(1)
        st2[j] = gather(st1, x, st1_s, st1_r, x_peer, NX)
        share(st2, j, st2_s, st2_r, c_peer, chan_size)
        short_step(1)
        long_step(2)
        st3[z] = gather(st2, j, st2_s, st2_r, c_peer, chan_size)
        share(st3, z, st3_s, st3_r, z_peer, nz)
        for r in range(1, NX):
            remote(
                final.at[pl.ds(0, TP), :], mine.at[r], mine_s.at[r], mine_r.at[r], x_peer(r)
            ).wait_recv()
        for copy in sends:
            copy.wait_send()
        for way in range(2):
            for index in range(2 * far - 1):
                if index not in (far - 1, 2 * far - 2):
                    z_copy(way, index).wait_send()

        for way in range(2):
            for source in range(NX):
                remote(
                    zsend.at[way, 0, 0:TP], edge.at[way, source], edge_s.at[way, source],
                    edge_r.at[way, source], beside(way, x_peer(0)),
                ).wait_recv()
        for r in range(NX):
            source = lax.rem(x + r, NX)
            if r:
                value = mine[r].astype(f32)
            else:
                value = part[pl.ds(pl.multiple_of(chunk_row(0) + x * TP, TP), TP), :]
            value = value + edge[0, source].astype(f32) + edge[1, source].astype(f32)
            column = pl.multiple_of(source * quarter, quarter)
            sky[:, pl.ds(column, quarter)] = value.astype(bf16)
        stacked[...] = gather(st3, z, st3_s, st3_r, z_peer, nz) / ngal
        for way in range(2):
            for tile in range(NX):
                edge_copy(way, tile, 0).wait_send()

    dma = pltpu.SemaphoreType.DMA
    scratch = [
        pltpu.VMEM((rows, width), bf16),
        pltpu.VMEM((MODES, width), f32),
        pltpu.VMEM((NX, 1, rows), jnp.int32),
        pltpu.VMEM((NX, rows, quarter), bf16),
        pltpu.VMEM((chan_size, MODES, 128), f32),
        pltpu.VMEM((chan_size, MODES, rows), f32),
        pltpu.VMEM((128, rows), f32),
        pltpu.VMEM((NX, MODES, rows), f32),
        pltpu.VMEM((npix, NX * rows), bf16),
        pltpu.VMEM((NX * rows, quarter), f32),
        pltpu.VMEM((NX * rows, quarter), bf16),
        pltpu.VMEM((npix, quarter), f32),
        pltpu.VMEM((npix, ngal), bf16),
        pltpu.VMEM((shifts, npix), bf16),
        pltpu.VMEM((2, nz - 1, half, quarter), bf16),
        pltpu.VMEM((2, nz - 1, half, quarter), bf16),
        pltpu.VMEM((2, NX, TP, quarter), bf16),
        pltpu.VMEM((zpix, quarter), bf16),
        pltpu.VMEM((NX, TP, quarter), bf16),
        pltpu.VMEM((NX, 1, 2 * SW), f32),
        pltpu.VMEM((chan_size, 1, 2 * SW), f32),
        pltpu.VMEM((nz, 1, 2 * SW), f32),
        dma((2,)),
    ]
    for shape in (
        (NX,), (2, NX), (chan_size,), (chan_size,), (NX,), (2, nz - 1), (2, NX), (NX,),
        (NX,), (chan_size,), (nz,),
    ):
        scratch += [dma(shape), dma(shape)]
    return kernel, scratch


def solution(mesh):
    tm_size, chan_size = mesh.shape["tm"], mesh.shape["chan"]

    def per_device(spectra, chan_weight, routes, offsets, taps, gal_pix, gal_chan):
        rows, width = spectra.shape
        nblocks = routes.shape[0]
        kernel, scratch = make_kernel(
            tm_size, chan_size, rows, width, nblocks, gal_pix.shape[0]
        )
        vmem = pl.BlockSpec(memory_space=pltpu.VMEM)
        sky, stacked = pl.pallas_call(
            kernel,
            out_shape=(
                jax.ShapeDtypeStruct((TP, width), bf16),
                jax.ShapeDtypeStruct((1, 2 * SW), f32),
            ),
            in_specs=[pl.BlockSpec(memory_space=pl.ANY)] * 2 + [vmem] * 6,
            out_specs=(vmem, vmem),
            scratch_shapes=scratch,
            compiler_params=pltpu.CompilerParams(
                collective_id=0, has_side_effects=True, vmem_limit_bytes=54880 * 1024
            ),
        )(
            spectra, jnp.asarray(basis_table(width * chan_size)), chan_weight[None, :],
            routes.reshape(1, nblocks), offsets[None, :], taps[None, :], gal_pix[None, :],
            gal_chan[None, :],
        )
        return sky, stacked[0]

    in_specs = (
        P("tm", "chan"), P("chan"), P("tm", None), P("tm"), P(None), P(None), P(None)
    )
    return jax.shard_map(
        per_device, mesh=mesh, in_specs=in_specs, out_specs=(P("tm", "chan"), P(None)),
        check_vma=False,
    )
```

```python
import jax
import jax.numpy as jnp
import numpy as np
from jax import lax
from jax.experimental import pallas as pl
from jax.experimental.pallas import tpu as pltpu
from jax.sharding import PartitionSpec as P

KMODES = 8
MODES = 2 * KMODES
TP = 64
MARGIN = 8
SW = 64
TAPS = 16
NX = 4

highest = lax.Precision.HIGHEST
MESH = pl.DeviceIdType.MESH
f32 = jnp.float32
bf16 = jnp.bfloat16


def basis_table(total):
    orders = np.arange(1, KMODES + 1)[:, None]
    phase = (orders * np.arange(total)[None, :] % total) * (2 * np.pi / total)
    return np.concatenate([np.cos(phase), np.sin(phase)], axis=0).astype(np.float32)


def split3(value):
    high = value.astype(bf16)
    rest = value - high.astype(f32)
    mid = rest.astype(bf16)
    low = (rest - mid.astype(f32)).astype(bf16)
    return high, mid, low


def iota(shape, dim):
    return lax.broadcasted_iota(jnp.int32, shape, dim)


def make_kernel(tm_size, chan_size, rows, width, nblocks, ngal):
    nz = tm_size // NX
    quarter = width // NX
    npix = tm_size * TP
    zpix = NX * TP
    block_rows = rows // nblocks
    shifts = quarter + 2 * SW
    far = nz // 2

    def kernel(
        spec, basis_in, weight, routes, offsets, taps, gal_pix, gal_chan,
        sky, stacked,
        own, basis, pix, raw, gram, proj, ext, coef, band, ripple, clean, part, pixel_hot, counts,
        zsend, zrecv, edge, final, mine, st1, st2, st3,
        load_sem, pix_s, pix_r, raw_s, raw_r, gram_s, gram_r, proj_s, proj_r, coef_s, coef_r,
        z_s, z_r, edge_r, mine_s, mine_r, st1_s, st1_r, st2_s, st2_r, st3_s, st3_r,
    ):
        tm = lax.axis_index("tm")
        j = lax.axis_index("chan")
        z = lax.div(tm, NX)
        x = lax.rem(tm, NX)
        here = pl.multiple_of(x * quarter, quarter)

        def x_peer(r):
            return (z * NX + lax.rem(x + r, NX), j)

        def c_peer(r):
            return (tm, lax.rem(j + r, chan_size))

        def z_peer(r):
            return (lax.rem(z + r, nz) * NX + x, j)

        def beside(way, place):
            return (lax.rem(place[0] + (NX, (nz - 1) * NX)[way], tm_size), place[1])

        def remote(src, dst, send_sem, recv_sem, peer):
            return pltpu.make_async_remote_copy(
                src_ref=src, dst_ref=dst, send_sem=send_sem, recv_sem=recv_sem,
                device_id=peer, device_id_type=MESH,
            )

        sends = []

        def start(copy):
            copy.start()
            sends.append(copy)

        peers = (
            [x_peer(r) for r in range(1, NX)]
            + [c_peer(r) for r in range(1, chan_size)]
            + [z_peer(r) for r in range(1, nz)]
            + [beside(way, x_peer(r)) for way in range(2) for r in range(1, NX)]
        )
        barrier = pltpu.get_barrier_semaphore()
        for peer in peers:
            pl.semaphore_signal(barrier, inc=1, device_id=peer, device_id_type=MESH)
        basis_here = basis_in.at[:, pl.ds(pl.multiple_of(j * width, width), width)]
        loads = [
            pltpu.make_async_copy(source, target, load_sem.at[i])
            for i, (source, target) in enumerate((
                (spec, own), (basis_here, basis),
            ))
        ]
        for load in loads:
            load.start()
        inside = iota((nblocks, rows), 1) - block_rows * iota((nblocks, rows), 0)
        owner = ((inside >= 0) & (inside < block_rows)).astype(f32).astype(bf16)
        tile = jnp.dot(
            jnp.broadcast_to(routes[...], (16, nblocks)).astype(f32).astype(bf16), owner,
            preferred_element_type=f32,
        )[0:1].astype(jnp.int32)
        pix[0] = tile * TP + offsets[...] - MARGIN

        loads[1].wait()
        weighted = basis[...] * weight[...]
        w_stack = jnp.concatenate(split3(weighted), axis=0)

        pl.semaphore_wait(barrier, len(peers))
        for r in range(1, NX):
            start(remote(pix.at[0], pix.at[NX - r], pix_s.at[r], pix_r.at[NX - r], x_peer(r)))

        late = rows // 4 * 3

        def raw_copy(r, piece):
            column = pl.multiple_of(lax.rem(x + r, NX) * quarter, quarter)
            low, high = ((0, late), (late, rows), (0, rows))[piece]
            return remote(
                own.at[low:high, pl.ds(column, quarter)], raw.at[NX - r, low:high],
                raw_s.at[piece, r], raw_r.at[piece, NX - r], x_peer(r),
            )

        loads[0].wait()
        for r, piece in ((2, 2), (1, 0), (3, 0)):
            start(raw_copy(r, piece))

        products = lax.dot_general(
            w_stack, own[...], (((1,), (1,)), ((), ())), preferred_element_type=f32
        )
        proj[0] = products[:MODES] + products[MODES:2 * MODES] + products[2 * MODES:]
        for r in range(1, chan_size):
            start(remote(
                proj.at[0], proj.at[chan_size - r], proj_s.at[r], proj_r.at[chan_size - r],
                c_peer(r),
            ))
        gram[0] = jnp.zeros((MODES, 128), f32)
        gram[0, :, 0:MODES] = lax.dot_general(
            weighted, basis[...], (((1,), (1,)), ((), ())), precision=highest,
            preferred_element_type=f32,
        )
        for r in range(1, chan_size):
            start(remote(
                gram.at[0], gram.at[chan_size - r], gram_s.at[r], gram_r.at[chan_size - r],
                c_peer(r),
            ))

        def fill(target, column, group, tap):
            def step(a, carry):
                row = pl.multiple_of(a * TAPS, TAPS)
                target[pl.ds(row, TAPS), column:column + tap.shape[1]] = jnp.where(
                    group == a, tap, 0.0
                ).astype(bf16)
                return carry

            lax.fori_loop(0, npix // TAPS, step, 0, unroll=4)

        def build_band(slot):
            first = pix[slot]
            group = jnp.broadcast_to(first >> 4, (TAPS, rows))
            inner = jnp.broadcast_to(first & (TAPS - 1), (TAPS, rows))
            lane = iota((TAPS, rows), 0)
            turn = (lane - inner) & (TAPS - 1)
            tap = jnp.zeros((TAPS, rows), f32)
            values = taps[...].astype(f32)
            for m in range(TAPS):
                tap = jnp.where(turn == m, values[0:1, m:m + 1], tap)
            fill(band, slot * rows, jnp.where(lane < inner, group + 1, group), tap)

        build_band(0)

        for r in range(1, chan_size):
            remote(gram.at[0], gram.at[r], gram_s.at[r], gram_r.at[r], c_peer(r)).wait_recv()
        total = gram[0]
        for r in range(1, chan_size):
            total = total + gram[r]
        row_id = iota((MODES, 128), 0)
        both = jnp.where(iota((MODES, 128), 1) - MODES == row_id, 1.0, total)
        for i in range(MODES):
            pivot = both[i:i + 1, :] / both[i:i + 1, i:i + 1]
            both = jnp.where(row_id == i, pivot, both - both[:, i:i + 1] * pivot)

        ext[...] = jnp.zeros(ext.shape, f32)
        for r in range(1, chan_size):
            remote(proj.at[0], proj.at[r], proj_s.at[r], proj_r.at[r], c_peer(r)).wait_recv()
        full = proj[0]
        for r in range(1, chan_size):
            full = full + proj[r]
        ext[MODES:2 * MODES, :] = full
        coef[0] = jnp.dot(both, ext[...], precision=highest, preferred_element_type=f32)
        for r in range(1, NX):
            start(remote(coef.at[0], coef.at[NX - r], coef_s.at[r], coef_r.at[NX - r], x_peer(r)))
        for r in (1, 3):
            start(raw_copy(r, 1))

        b_high, b_mid, b_low = split3(basis[:, pl.ds(here, quarter)])
        b_stack = jnp.concatenate(
            [b_high, b_mid, b_high, b_mid, b_low, b_high, jnp.zeros((2 * MODES, quarter), bf16)],
            axis=0,
        )

        def fit_slot(slot):
            c_high, c_mid, c_low = split3(coef[slot])
            c_stack = jnp.concatenate(
                [c_high, c_high, c_mid, c_mid, c_high, c_low, jnp.zeros((2 * MODES, rows), bf16)],
                axis=0,
            )
            ripple[slot * rows:(slot + 1) * rows, :] = lax.dot_general(
                c_stack, b_stack, (((0,), (0,)), ((), ())), preferred_element_type=f32
            )

        def clean_slot(slot, values):
            clean[slot * rows:(slot + 1) * rows, :] = (
                values.astype(f32) - ripple[slot * rows:(slot + 1) * rows, :]
            ).astype(bf16)

        fit_slot(0)
        clean_slot(0, own[:, pl.ds(here, quarter)])
        begin = gal_chan[...] - SW - (j * width + here)
        shift_hot = (iota((shifts, ngal), 0) == quarter - 1 - begin).astype(f32).astype(bf16)
        gal_row = jnp.broadcast_to(gal_pix[...], (TAPS, ngal))
        fill(
            pixel_hot, 0, gal_row >> 4,
            jnp.where((gal_row & (TAPS - 1)) == iota((TAPS, ngal), 0), 1.0, 0.0).astype(f32),
        )
        counts[...] = lax.dot_general(
            shift_hot, pixel_hot[...], (((1,), (1,)), ((), ())), preferred_element_type=f32
        ).astype(bf16)

        for r in range(1, NX):
            remote(pix.at[0], pix.at[r], pix_s.at[r], pix_r.at[r], x_peer(r)).wait_recv()
            build_band(r)
        for r in (1, 3, 2):
            remote(coef.at[0], coef.at[r], coef_s.at[r], coef_r.at[r], x_peer(r)).wait_recv()
            fit_slot(r)
        for r, pieces in ((2, (2,)), (1, (0, 1)), (3, (0, 1))):
            for piece in pieces:
                raw_copy(NX - r, piece).wait_recv()
            clean_slot(r, raw[r])

        def chunk_row(step):
            return pl.multiple_of(lax.rem(z + step + 2 * nz, nz) * zpix, zpix)

        def part_tile(step, tile):
            row = pl.multiple_of(chunk_row(step) + tile * TP, TP)
            return part[pl.ds(row, TP), :]

        sign = (1, -1)

        def hops(way, tile):
            return far if tile // 2 == way else far - 1

        def z_copy(way, tile, k):
            if k < hops(way, tile) - 1:
                target, recv_sem = zrecv.at[way, tile, k], z_r.at[way, tile, k]
                peer = z_peer((1, nz - 1)[way])
            else:
                target, recv_sem = edge.at[way, x], edge_r.at[way, x]
                peer = beside(way, (z * NX + tile, j))
            return remote(
                zsend.at[way, tile, k], target, z_s.at[way, tile, k], recv_sem, peer
            )

        def z_step(k, long):
            for lane in range(2):
                for way in range(2):
                    tile = 2 * (way if long else 1 - way) + lane
                    value = part_tile(sign[way] * (hops(way, tile) - k), tile)
                    if k:
                        z_copy(way, tile, k - 1).wait_recv()
                        value = value + zrecv[way, tile, k - 1].astype(f32)
                    zsend[way, tile, k] = value.astype(bf16)
                    z_copy(way, tile, k).start()

        def grid_step(n, carry):
            away = lax.div(n + 1, 2)
            row = chunk_row(far + away - 2 * lax.rem(n, 2) * away)
            part[pl.ds(row, zpix), :] = jnp.dot(
                band[pl.ds(row, zpix), :], clean[...], preferred_element_type=f32
            )

            @pl.when(n == 0)
            def _():
                z_step(0, True)

            @pl.when(n == 2)
            def _():
                z_step(0, False)

            @pl.when(n == 4)
            def _():
                z_step(1, True)
                z_step(1, False)

            return carry

        def share(buffer, me, send_sem, recv_sem, peer_of, count):
            for r in range(1, count):
                start(remote(buffer.at[me], buffer.at[me], send_sem.at[r], recv_sem.at[me], peer_of(r)))

        def gather(buffer, me, send_sem, recv_sem, peer_of, count):
            for r in range(1, count):
                other = lax.rem(me + r, count)
                remote(
                    buffer.at[other], buffer.at[other], send_sem.at[r], recv_sem.at[other], peer_of(r)
                ).wait_recv()
            value = buffer[0]
            for i in range(1, count):
                value = value + buffer[i]
            return value

        lax.fori_loop(0, nz, grid_step, 0)

        final[...] = part[pl.ds(chunk_row(0), zpix), :].astype(bf16)
        for r in range(1, NX):
            row = pl.multiple_of(lax.rem(x + r, NX) * TP, TP)
            start(remote(
                final.at[pl.ds(row, TP), :], mine.at[NX - r], mine_s.at[r], mine_r.at[NX - r],
                x_peer(r),
            ))

        wide = jnp.concatenate(
            [
                jnp.dot(counts[...], part[...].astype(bf16), preferred_element_type=f32),
                jnp.zeros((shifts, 512 - quarter), f32),
            ],
            axis=1,
        )
        folded = jnp.zeros((8, 512), f32)
        for i in range(shifts // 8):
            folded = folded + pltpu.roll(
                wide[8 * i:8 * i + 8], (513 - quarter + 8 * i) % 512, 1
            )
        window = jnp.zeros((1, 512), f32)
        for i in range(8):
            window = window + (pltpu.roll(folded[i:i + 1], i, 1) if i else folded[i:i + 1])
        st1[x] = window[:, :2 * SW]
        share(st1, x, st1_s, st1_r, x_peer, NX)

        z_step(2, True)
        st2[j] = gather(st1, x, st1_s, st1_r, x_peer, NX)
        share(st2, j, st2_s, st2_r, c_peer, chan_size)
        z_step(2, False)
        z_step(3, True)
        st3[z] = gather(st2, j, st2_s, st2_r, c_peer, chan_size)
        share(st3, z, st3_s, st3_r, z_peer, nz)
        for r in range(1, NX):
            remote(
                final.at[pl.ds(0, TP), :], mine.at[r], mine_s.at[r], mine_r.at[r], x_peer(r)
            ).wait_recv()
        for copy in sends:
            copy.wait_send()
        for way in range(2):
            for source in range(NX):
                remote(
                    zsend.at[way, 0, 0], edge.at[way, source], z_s.at[way, 0, 0],
                    edge_r.at[way, source], beside(way, x_peer(0)),
                ).wait_recv()
        for r in range(NX):
            source = lax.rem(x + r, NX)
            if r:
                value = mine[r].astype(f32)
            else:
                value = part[pl.ds(pl.multiple_of(chunk_row(0) + x * TP, TP), TP), :]
            value = value + edge[0, source].astype(f32) + edge[1, source].astype(f32)
            column = pl.multiple_of(source * quarter, quarter)
            sky[:, pl.ds(column, quarter)] = value.astype(bf16)
        stacked[...] = gather(st3, z, st3_s, st3_r, z_peer, nz) / ngal
        for way in range(2):
            for tile in range(NX):
                for k in range(hops(way, tile)):
                    z_copy(way, tile, k).wait_send()

    dma = pltpu.SemaphoreType.DMA
    scratch = [
        pltpu.VMEM((rows, width), bf16),
        pltpu.VMEM((MODES, width), f32),
        pltpu.VMEM((NX, 1, rows), jnp.int32),
        pltpu.VMEM((NX, rows, quarter), bf16),
        pltpu.VMEM((chan_size, MODES, 128), f32),
        pltpu.VMEM((chan_size, MODES, rows), f32),
        pltpu.VMEM((128, rows), f32),
        pltpu.VMEM((NX, MODES, rows), f32),
        pltpu.VMEM((npix, NX * rows), bf16),
        pltpu.VMEM((NX * rows, quarter), f32),
        pltpu.VMEM((NX * rows, quarter), bf16),
        pltpu.VMEM((npix, quarter), f32),
        pltpu.VMEM((npix, ngal), bf16),
        pltpu.VMEM((shifts, npix), bf16),
        pltpu.VMEM((2, NX, far, TP, quarter), bf16),
        pltpu.VMEM((2, NX, far - 1, TP, quarter), bf16),
        pltpu.VMEM((2, NX, TP, quarter), bf16),
        pltpu.VMEM((zpix, quarter), bf16),
        pltpu.VMEM((NX, TP, quarter), bf16),
        pltpu.VMEM((NX, 1, 2 * SW), f32),
        pltpu.VMEM((chan_size, 1, 2 * SW), f32),
        pltpu.VMEM((nz, 1, 2 * SW), f32),
        dma((2,)),
    ]
    for shape in ((NX,), (3, NX), (chan_size,), (chan_size,), (NX,)):
        scratch += [dma(shape), dma(shape)]
    scratch += [dma((2, NX, far)), dma((2, NX, far - 1)), dma((2, NX))]
    for shape in ((NX,), (NX,), (chan_size,), (nz,)):
        scratch += [dma(shape), dma(shape)]
    return kernel, scratch


def solution(mesh):
    tm_size, chan_size = mesh.shape["tm"], mesh.shape["chan"]

    def per_device(spectra, chan_weight, routes, offsets, taps, gal_pix, gal_chan):
        rows, width = spectra.shape
        nblocks = routes.shape[0]
        kernel, scratch = make_kernel(
            tm_size, chan_size, rows, width, nblocks, gal_pix.shape[0]
        )
        vmem = pl.BlockSpec(memory_space=pltpu.VMEM)
        sky, stacked = pl.pallas_call(
            kernel,
            out_shape=(
                jax.ShapeDtypeStruct((TP, width), bf16),
                jax.ShapeDtypeStruct((1, 2 * SW), f32),
            ),
            in_specs=[pl.BlockSpec(memory_space=pl.ANY)] * 2 + [vmem] * 6,
            out_specs=(vmem, vmem),
            scratch_shapes=scratch,
            compiler_params=pltpu.CompilerParams(
                collective_id=0, has_side_effects=True, vmem_limit_bytes=54880 * 1024
            ),
        )(
            spectra, jnp.asarray(basis_table(width * chan_size)), chan_weight[None, :],
            routes.reshape(1, nblocks), offsets[None, :], taps[None, :], gal_pix[None, :],
            gal_chan[None, :],
        )
        return sky, stacked[0]

    in_specs = (
        P("tm", "chan"), P("chan"), P("tm", None), P("tm"), P(None), P(None), P(None)
    )
    return jax.shard_map(
        per_device, mesh=mesh, in_specs=in_specs, out_specs=(P("tm", "chan"), P(None)),
        check_vma=False,
    )
```

```python
import jax
import jax.numpy as jnp
import numpy as np
from jax import lax
from jax.experimental import pallas as pl
from jax.experimental.pallas import tpu as pltpu
from jax.sharding import PartitionSpec as P

KMODES = 8
MODES = 2 * KMODES
TP = 64
MARGIN = 8
SW = 64
TAPS = 16
NX = 4

highest = lax.Precision.HIGHEST
MESH = pl.DeviceIdType.MESH
f32 = jnp.float32
bf16 = jnp.bfloat16


def basis_table(total):
    orders = np.arange(1, KMODES + 1)[:, None]
    phase = (orders * np.arange(total)[None, :] % total) * (2 * np.pi / total)
    return np.concatenate([np.cos(phase), np.sin(phase)], axis=0).astype(np.float32)


def split3(value):
    high = value.astype(bf16)
    rest = value - high.astype(f32)
    mid = rest.astype(bf16)
    low = (rest - mid.astype(f32)).astype(bf16)
    return high, mid, low


def iota(shape, dim):
    return lax.broadcasted_iota(jnp.int32, shape, dim)


def make_kernel(tm_size, chan_size, rows, width, nblocks, ngal):
    nz = tm_size // NX
    quarter = width // NX
    npix = tm_size * TP
    zpix = NX * TP
    block_rows = rows // nblocks
    shifts = quarter + 2 * SW
    far = nz // 2

    def kernel(
        spec, basis_in, weight, routes, offsets, taps, gal_pix, gal_chan,
        sky, stacked,
        own, basis, pix, raw, gram, proj, ext, coef, band, ripple, clean, part, pixel_hot, counts,
        zsend, zrecv, edge, final, mine, st1, st2, st3, st4,
        load_sem, pix_s, pix_r, raw_s, raw_r, gram_s, gram_r, proj_s, proj_r, coef_s, coef_r,
        z_s, z_r, edge_s, edge_r, mine_s, mine_r, st1_s, st1_r, st2_s, st2_r, st3_s, st3_r, st4_s, st4_r,
    ):
        tm = lax.axis_index("tm")
        j = lax.axis_index("chan")
        z = lax.div(tm, NX)
        x = lax.rem(tm, NX)
        y = lax.div(j, 2)
        core = lax.rem(j, 2)
        odd = lax.rem(z, 2)
        here = pl.multiple_of(x * quarter, quarter)

        def x_peer(r):
            return (z * NX + lax.rem(x + r, NX), j)

        def c_peer(r):
            return (tm, lax.rem(j + r, chan_size))

        def y_peer(r):
            return (tm, lax.rem(j + 2 * r, chan_size))

        def z_peer(r):
            return (lax.rem(z + 2 * r, nz) * NX + x, j)

        def pair_peer(r):
            other = lax.rem(2 * core + odd + r, 4)
            return ((z - odd + lax.rem(other, 2)) * NX + x, j - core + lax.div(other, 2))

        def z_next(way, column):
            turn = core if way == 0 else 1 - core
            return (lax.rem(z + 1 + (nz - 2) * turn, nz) * NX + column, j)

        def remote(src, dst, send_sem, recv_sem, peer):
            return pltpu.make_async_remote_copy(
                src_ref=src, dst_ref=dst, send_sem=send_sem, recv_sem=recv_sem,
                device_id=peer, device_id_type=MESH,
            )

        sends = []

        def start(copy):
            copy.start()
            sends.append(copy)

        peers = (
            [x_peer(r) for r in range(1, NX)]
            + [c_peer(r) for r in range(1, chan_size)]
            + [z_peer(r) for r in range(1, nz // 2)]
            + [z_next(way, column) for way in range(2) for column in range(NX)]
            + [(((z + 1 - 2 * odd) * NX + x), j + 1 - 2 * core)]
        )
        barrier = pltpu.get_barrier_semaphore()
        for peer in peers:
            pl.semaphore_signal(barrier, inc=1, device_id=peer, device_id_type=MESH)
        basis_here = basis_in.at[:, pl.ds(pl.multiple_of(j * width, width), width)]
        loads = [
            pltpu.make_async_copy(source, target, load_sem.at[i])
            for i, (source, target) in enumerate((
                (spec, own), (basis_here, basis),
            ))
        ]
        for load in loads:
            load.start()
        inside = iota((nblocks, rows), 1) - block_rows * iota((nblocks, rows), 0)
        owner = ((inside >= 0) & (inside < block_rows)).astype(f32).astype(bf16)
        tile = jnp.dot(
            jnp.broadcast_to(routes[...], (16, nblocks)).astype(f32).astype(bf16), owner,
            preferred_element_type=f32,
        )[0:1].astype(jnp.int32)
        pix[0] = tile * TP + offsets[...] - MARGIN

        loads[1].wait()
        weighted = basis[...] * weight[...]
        w_stack = jnp.concatenate(split3(weighted), axis=0)

        pl.semaphore_wait(barrier, len(peers))
        for r in range(1, NX):
            start(remote(pix.at[0], pix.at[NX - r], pix_s.at[r], pix_r.at[NX - r], x_peer(r)))

        late = rows // 4 * 3

        def raw_copy(r, piece):
            column = pl.multiple_of(lax.rem(x + r, NX) * quarter, quarter)
            low, high = ((0, late), (late, rows), (0, rows))[piece]
            return remote(
                own.at[low:high, pl.ds(column, quarter)], raw.at[NX - r, low:high],
                raw_s.at[piece, r], raw_r.at[piece, NX - r], x_peer(r),
            )

        loads[0].wait()
        for r, piece in ((2, 2), (1, 0), (3, 0)):
            start(raw_copy(r, piece))

        products = lax.dot_general(
            w_stack, own[...], (((1,), (1,)), ((), ())), preferred_element_type=f32
        )
        proj[0] = products[:MODES] + products[MODES:2 * MODES] + products[2 * MODES:]
        for r in range(1, chan_size):
            start(remote(
                proj.at[0], proj.at[chan_size - r], proj_s.at[r], proj_r.at[chan_size - r],
                c_peer(r),
            ))
        gram[0] = jnp.zeros((MODES, 128), f32)
        gram[0, :, 0:MODES] = lax.dot_general(
            weighted, basis[...], (((1,), (1,)), ((), ())), precision=highest,
            preferred_element_type=f32,
        )
        for r in range(1, chan_size):
            start(remote(
                gram.at[0], gram.at[chan_size - r], gram_s.at[r], gram_r.at[chan_size - r],
                c_peer(r),
            ))

        def fill(target, column, group, tap):
            def step(a, carry):
                row = pl.multiple_of(a * TAPS, TAPS)
                target[pl.ds(row, TAPS), column:column + tap.shape[1]] = jnp.where(
                    group == a, tap, 0.0
                ).astype(bf16)
                return carry

            lax.fori_loop(0, npix // TAPS, step, 0, unroll=4)

        def build_band(slot):
            first = pix[slot]
            group = jnp.broadcast_to(first >> 4, (TAPS, rows))
            inner = jnp.broadcast_to(first & (TAPS - 1), (TAPS, rows))
            lane = iota((TAPS, rows), 0)
            turn = (lane - inner) & (TAPS - 1)
            tap = jnp.zeros((TAPS, rows), f32)
            values = taps[...].astype(f32)
            for m in range(TAPS):
                tap = jnp.where(turn == m, values[0:1, m:m + 1], tap)
            fill(band, slot * rows, jnp.where(lane < inner, group + 1, group), tap)

        build_band(0)

        for r in range(1, chan_size):
            remote(gram.at[0], gram.at[r], gram_s.at[r], gram_r.at[r], c_peer(r)).wait_recv()
        total = gram[0]
        for r in range(1, chan_size):
            total = total + gram[r]
        row_id = iota((MODES, 128), 0)
        both = jnp.where(iota((MODES, 128), 1) - MODES == row_id, 1.0, total)
        for i in range(MODES):
            pivot = both[i:i + 1, :] / both[i:i + 1, i:i + 1]
            both = jnp.where(row_id == i, pivot, both - both[:, i:i + 1] * pivot)

        ext[...] = jnp.zeros(ext.shape, f32)
        for r in range(1, chan_size):
            remote(proj.at[0], proj.at[r], proj_s.at[r], proj_r.at[r], c_peer(r)).wait_recv()
        full = proj[0]
        for r in range(1, chan_size):
            full = full + proj[r]
        ext[MODES:2 * MODES, :] = full
        coef[0] = jnp.dot(both, ext[...], precision=highest, preferred_element_type=f32)
        for r in range(1, NX):
            start(remote(coef.at[0], coef.at[NX - r], coef_s.at[r], coef_r.at[NX - r], x_peer(r)))
        for r in (1, 3):
            start(raw_copy(r, 1))

        b_high, b_mid, b_low = split3(basis[:, pl.ds(here, quarter)])
        b_stack = jnp.concatenate(
            [b_high, b_mid, b_high, b_mid, b_low, b_high, jnp.zeros((2 * MODES, quarter), bf16)],
            axis=0,
        )

        def fit_slot(slot):
            c_high, c_mid, c_low = split3(coef[slot])
            c_stack = jnp.concatenate(
                [c_high, c_high, c_mid, c_mid, c_high, c_low, jnp.zeros((2 * MODES, rows), bf16)],
                axis=0,
            )
            ripple[slot * rows:(slot + 1) * rows, :] = lax.dot_general(
                c_stack, b_stack, (((0,), (0,)), ((), ())), preferred_element_type=f32
            )

        def clean_slot(slot, values):
            clean[slot * rows:(slot + 1) * rows, :] = (
                values.astype(f32) - ripple[slot * rows:(slot + 1) * rows, :]
            ).astype(bf16)

        fit_slot(0)
        clean_slot(0, own[:, pl.ds(here, quarter)])
        begin = gal_chan[...] - SW - (j * width + here)
        shift_hot = (iota((shifts, ngal), 0) == quarter - 1 - begin).astype(f32).astype(bf16)
        gal_row = jnp.broadcast_to(gal_pix[...], (TAPS, ngal))
        fill(
            pixel_hot, 0, gal_row >> 4,
            jnp.where((gal_row & (TAPS - 1)) == iota((TAPS, ngal), 0), 1.0, 0.0).astype(f32),
        )
        counts[...] = lax.dot_general(
            shift_hot, pixel_hot[...], (((1,), (1,)), ((), ())), preferred_element_type=f32
        ).astype(bf16)

        for r in range(1, NX):
            remote(pix.at[0], pix.at[r], pix_s.at[r], pix_r.at[r], x_peer(r)).wait_recv()
            build_band(r)
        for r in (1, 3, 2):
            remote(coef.at[0], coef.at[r], coef_s.at[r], coef_r.at[r], x_peer(r)).wait_recv()
            fit_slot(r)
        for r, pieces in ((2, (2,)), (1, (0, 1)), (3, (0, 1))):
            for piece in pieces:
                raw_copy(NX - r, piece).wait_recv()
            clean_slot(r, raw[r])

        def chunk_row(step):
            return pl.multiple_of(lax.rem(z + step + 2 * nz, nz) * zpix, zpix)

        hops = (far, far - 1)

        def z_copy(way, k, tile=None):
            source = zsend.at[way, k]
            if k < hops[way] - 1:
                return remote(
                    source, zrecv.at[way, k], z_s.at[way, k], z_r.at[way, k], z_next(way, x)
                )
            return remote(
                source.at[tile * TP:(tile + 1) * TP], edge.at[way, x], edge_s.at[way, tile],
                edge_r.at[way, x], z_next(way, tile),
            )

        def z_copies(way, k):
            return [z_copy(way, k, tile) for tile in (range(NX) if k == hops[way] - 1 else (None,))]

        def z_step(way, k):
            turn = core if way == 0 else 1 - core
            away = hops[way] - k
            row = chunk_row(away + (nz - 2 * away) * turn)
            value = part[pl.ds(row, zpix), :]
            if k:
                z_copy(way, k - 1).wait_recv()
                value = value + zrecv[way, k - 1].astype(f32)
            zsend[way, k] = value.astype(bf16)
            for copy in z_copies(way, k):
                copy.start()

        def grid_step(n, carry):
            away = lax.div(n + 1, 2)
            row = chunk_row(far + away - 2 * lax.rem(n, 2) * away)
            part[pl.ds(row, zpix), :] = jnp.dot(
                band[pl.ds(row, zpix), :], clean[...], preferred_element_type=f32
            )

            @pl.when(n == 0)
            def _():
                z_step(0, 0)

            @pl.when(n == 2)
            def _():
                z_step(1, 0)

            @pl.when(n == 4)
            def _():
                z_step(0, 1)
                z_step(1, 1)

            return carry

        def share(buffer, me, send_sem, recv_sem, peer_of):
            for r in range(1, 4):
                start(remote(buffer.at[me], buffer.at[me], send_sem.at[r], recv_sem.at[me], peer_of(r)))

        def gather(buffer, me, send_sem, recv_sem, peer_of):
            for r in range(1, 4):
                other = lax.rem(me + r, 4)
                remote(
                    buffer.at[other], buffer.at[other], send_sem.at[r], recv_sem.at[other], peer_of(r)
                ).wait_recv()
            value = buffer[0]
            for i in range(1, 4):
                value = value + buffer[i]
            return value

        lax.fori_loop(0, nz, grid_step, 0)

        final[...] = part[pl.ds(chunk_row(0), zpix), :].astype(bf16)
        for r in range(1, NX):
            row = pl.multiple_of(lax.rem(x + r, NX) * TP, TP)
            start(remote(
                final.at[pl.ds(row, TP), :], mine.at[NX - r], mine_s.at[r], mine_r.at[NX - r],
                x_peer(r),
            ))

        wide = jnp.concatenate(
            [
                jnp.dot(counts[...], part[...].astype(bf16), preferred_element_type=f32),
                jnp.zeros((shifts, 512 - quarter), f32),
            ],
            axis=1,
        )
        folded = jnp.zeros((8, 512), f32)
        for i in range(shifts // 8):
            folded = folded + pltpu.roll(
                wide[8 * i:8 * i + 8], (513 - quarter + 8 * i) % 512, 1
            )
        window = jnp.zeros((1, 512), f32)
        for i in range(8):
            window = window + (pltpu.roll(folded[i:i + 1], i, 1) if i else folded[i:i + 1])
        st1[x] = window[:, :2 * SW]
        share(st1, x, st1_s, st1_r, x_peer)
        z_step(0, 2)
        st2[y] = gather(st1, x, st1_s, st1_r, x_peer)
        share(st2, y, st2_s, st2_r, y_peer)
        z_step(1, 2)
        st3[2 * core + odd] = gather(st2, y, st2_s, st2_r, y_peer)
        share(st3, 2 * core + odd, st3_s, st3_r, pair_peer)
        z_step(0, 3)
        st4[lax.div(z, 2)] = gather(st3, 2 * core + odd, st3_s, st3_r, pair_peer)
        share(st4, lax.div(z, 2), st4_s, st4_r, z_peer)
        for r in range(1, NX):
            remote(
                final.at[pl.ds(0, TP), :], mine.at[r], mine_s.at[r], mine_r.at[r], x_peer(r)
            ).wait_recv()
        for copy in sends:
            copy.wait_send()
        for way in range(2):
            for source in range(NX):
                remote(
                    zsend.at[way, 0, 0:TP], edge.at[way, source], edge_s.at[way, source],
                    edge_r.at[way, source], z_next(way, x),
                ).wait_recv()
        for r in range(NX):
            source = lax.rem(x + r, NX)
            if r:
                value = mine[r].astype(f32)
            else:
                value = part[pl.ds(pl.multiple_of(chunk_row(0) + x * TP, TP), TP), :]
            value = value + edge[0, source].astype(f32) + edge[1, source].astype(f32)
            column = pl.multiple_of(source * quarter, quarter)
            sky[:, pl.ds(column, quarter)] = value.astype(bf16)
        stacked[...] = gather(st4, lax.div(z, 2), st4_s, st4_r, z_peer) / ngal
        for way in range(2):
            for k in range(hops[way]):
                for copy in z_copies(way, k):
                    copy.wait_send()

    dma = pltpu.SemaphoreType.DMA
    scratch = [
        pltpu.VMEM((rows, width), bf16),
        pltpu.VMEM((MODES, width), f32),
        pltpu.VMEM((NX, 1, rows), jnp.int32),
        pltpu.VMEM((NX, rows, quarter), bf16),
        pltpu.VMEM((chan_size, MODES, 128), f32),
        pltpu.VMEM((chan_size, MODES, rows), f32),
        pltpu.VMEM((128, rows), f32),
        pltpu.VMEM((NX, MODES, rows), f32),
        pltpu.VMEM((npix, NX * rows), bf16),
        pltpu.VMEM((NX * rows, quarter), f32),
        pltpu.VMEM((NX * rows, quarter), bf16),
        pltpu.VMEM((npix, quarter), f32),
        pltpu.VMEM((npix, ngal), bf16),
        pltpu.VMEM((shifts, npix), bf16),
        pltpu.VMEM((2, far, zpix, quarter), bf16),
        pltpu.VMEM((2, far - 1, zpix, quarter), bf16),
        pltpu.VMEM((2, NX, TP, quarter), bf16),
        pltpu.VMEM((zpix, quarter), bf16),
        pltpu.VMEM((NX, TP, quarter), bf16),
        *[pltpu.VMEM((4, 1, 2 * SW), f32) for _ in range(4)],
        dma((2,)),
    ]
    for shape in ((NX,), (3, NX), (chan_size,), (chan_size,), (NX,)):
        scratch += [dma(shape), dma(shape)]
    scratch += [dma((2, far)), dma((2, far - 1)), dma((2, NX)), dma((2, NX))]
    for _ in range(5):
        scratch += [dma((NX,)), dma((NX,))]
    return kernel, scratch


def solution(mesh):
    tm_size, chan_size = mesh.shape["tm"], mesh.shape["chan"]

    def per_device(spectra, chan_weight, routes, offsets, taps, gal_pix, gal_chan):
        rows, width = spectra.shape
        nblocks = routes.shape[0]
        kernel, scratch = make_kernel(
            tm_size, chan_size, rows, width, nblocks, gal_pix.shape[0]
        )
        vmem = pl.BlockSpec(memory_space=pltpu.VMEM)
        sky, stacked = pl.pallas_call(
            kernel,
            out_shape=(
                jax.ShapeDtypeStruct((TP, width), bf16),
                jax.ShapeDtypeStruct((1, 2 * SW), f32),
            ),
            in_specs=[pl.BlockSpec(memory_space=pl.ANY)] * 2 + [vmem] * 6,
            out_specs=(vmem, vmem),
            scratch_shapes=scratch,
            compiler_params=pltpu.CompilerParams(
                collective_id=0, has_side_effects=True, vmem_limit_bytes=54880 * 1024
            ),
        )(
            spectra, jnp.asarray(basis_table(width * chan_size)), chan_weight[None, :],
            routes.reshape(1, nblocks), offsets[None, :], taps[None, :], gal_pix[None, :],
            gal_chan[None, :],
        )
        return sky, stacked[0]

    in_specs = (
        P("tm", "chan"), P("chan"), P("tm", None), P("tm"), P(None), P(None), P(None)
    )
    return jax.shard_map(
        per_device, mesh=mesh, in_specs=in_specs, out_specs=(P("tm", "chan"), P(None)),
        check_vma=False,
    )
```

```python
import jax
import jax.numpy as jnp
import numpy as np
from jax import lax
from jax.experimental import pallas as pl
from jax.experimental.pallas import tpu as pltpu
from jax.sharding import PartitionSpec as P

KMODES = 8
MODES = 2 * KMODES
TP = 64
MARGIN = 8
SW = 64
TAPS = 16
NX = 4

highest = lax.Precision.HIGHEST
MESH = pl.DeviceIdType.MESH
f32 = jnp.float32
bf16 = jnp.bfloat16


def basis_table(total):
    orders = np.arange(1, KMODES + 1)[:, None]
    phase = (orders * np.arange(total)[None, :] % total) * (2 * np.pi / total)
    return np.concatenate([np.cos(phase), np.sin(phase)], axis=0).astype(np.float32)


def split3(value):
    high = value.astype(bf16)
    rest = value - high.astype(f32)
    mid = rest.astype(bf16)
    low = (rest - mid.astype(f32)).astype(bf16)
    return high, mid, low


def iota(shape, dim):
    return lax.broadcasted_iota(jnp.int32, shape, dim)


def make_kernel(tm_size, chan_size, rows, width, nblocks, ngal):
    nz = tm_size // NX
    quarter = width // NX
    npix = tm_size * TP
    zpix = NX * TP
    block_rows = rows // nblocks
    shifts = quarter + 2 * SW
    far = nz // 2

    def kernel(
        spec, basis_in, weight, routes, offsets, taps, gal_pix, gal_chan,
        sky, stacked,
        own, basis, pix, raw, gram, proj, ext, coef, band, ripple, clean, part, pixel_hot, counts,
        zsend, zrecv, edge, final, mine, st1, st2, st3,
        load_sem, pix_s, pix_r, raw_s, raw_r, gram_s, gram_r, proj_s, proj_r, coef_s, coef_r,
        z_s, z_r, edge_r, mine_s, mine_r, st1_s, st1_r, st2_s, st2_r, st3_s, st3_r,
    ):
        tm = lax.axis_index("tm")
        j = lax.axis_index("chan")
        z = lax.div(tm, NX)
        x = lax.rem(tm, NX)
        here = pl.multiple_of(x * quarter, quarter)

        def x_peer(r):
            return (z * NX + lax.rem(x + r, NX), j)

        def c_peer(r):
            return (tm, lax.rem(j + r, chan_size))

        def z_peer(r):
            return (lax.rem(z + r, nz) * NX + x, j)

        def beside(way, place):
            return (lax.rem(place[0] + (NX, (nz - 1) * NX)[way], tm_size), place[1])

        def remote(src, dst, send_sem, recv_sem, peer):
            return pltpu.make_async_remote_copy(
                src_ref=src, dst_ref=dst, send_sem=send_sem, recv_sem=recv_sem,
                device_id=peer, device_id_type=MESH,
            )

        sends = []

        def start(copy):
            copy.start()
            sends.append(copy)

        peers = (
            [x_peer(r) for r in range(1, NX)]
            + [c_peer(r) for r in range(1, chan_size)]
            + [z_peer(r) for r in range(1, nz)]
            + [beside(way, x_peer(r)) for way in range(2) for r in range(1, NX)]
        )
        barrier = pltpu.get_barrier_semaphore()
        for peer in peers:
            pl.semaphore_signal(barrier, inc=1, device_id=peer, device_id_type=MESH)
        basis_here = basis_in.at[:, pl.ds(pl.multiple_of(j * width, width), width)]
        loads = [
            pltpu.make_async_copy(source, target, load_sem.at[i])
            for i, (source, target) in enumerate((
                (spec, own), (basis_here, basis),
            ))
        ]
        for load in loads:
            load.start()
        inside = iota((nblocks, rows), 1) - block_rows * iota((nblocks, rows), 0)
        owner = ((inside >= 0) & (inside < block_rows)).astype(f32).astype(bf16)
        tile = jnp.dot(
            jnp.broadcast_to(routes[...], (16, nblocks)).astype(f32).astype(bf16), owner,
            preferred_element_type=f32,
        )[0:1].astype(jnp.int32)
        pix[0] = tile * TP + offsets[...] - MARGIN

        loads[1].wait()
        weighted = basis[...] * weight[...]
        w_stack = jnp.concatenate(split3(weighted), axis=0)

        pl.semaphore_wait(barrier, len(peers))
        for r in range(1, NX):
            start(remote(pix.at[0], pix.at[NX - r], pix_s.at[r], pix_r.at[NX - r], x_peer(r)))

        late = rows // 4 * 3

        def raw_copy(r, piece):
            column = pl.multiple_of(lax.rem(x + r, NX) * quarter, quarter)
            low, high = ((0, late), (late, rows), (0, rows))[piece]
            return remote(
                own.at[low:high, pl.ds(column, quarter)], raw.at[NX - r, low:high],
                raw_s.at[piece, r], raw_r.at[piece, NX - r], x_peer(r),
            )

        loads[0].wait()
        for r, piece in ((2, 2), (1, 0), (3, 0)):
            start(raw_copy(r, piece))

        products = lax.dot_general(
            w_stack, own[...], (((1,), (1,)), ((), ())), preferred_element_type=f32
        )
        proj[0] = products[:MODES] + products[MODES:2 * MODES] + products[2 * MODES:]
        for r in range(1, chan_size):
            start(remote(
                proj.at[0], proj.at[chan_size - r], proj_s.at[r], proj_r.at[chan_size - r],
                c_peer(r),
            ))
        gram[0] = jnp.zeros((MODES, 128), f32)
        gram[0, :, 0:MODES] = lax.dot_general(
            weighted, basis[...], (((1,), (1,)), ((), ())), precision=highest,
            preferred_element_type=f32,
        )
        for r in range(1, chan_size):
            start(remote(
                gram.at[0], gram.at[chan_size - r], gram_s.at[r], gram_r.at[chan_size - r],
                c_peer(r),
            ))

        def fill(target, column, group, tap):
            def step(a, carry):
                row = pl.multiple_of(a * TAPS, TAPS)
                target[pl.ds(row, TAPS), column:column + tap.shape[1]] = jnp.where(
                    group == a, tap, 0.0
                ).astype(bf16)
                return carry

            lax.fori_loop(0, npix // TAPS, step, 0, unroll=4)

        def build_band(slot):
            first = pix[slot]
            group = jnp.broadcast_to(first >> 4, (TAPS, rows))
            inner = jnp.broadcast_to(first & (TAPS - 1), (TAPS, rows))
            lane = iota((TAPS, rows), 0)
            turn = (lane - inner) & (TAPS - 1)
            tap = jnp.zeros((TAPS, rows), f32)
            values = taps[...].astype(f32)
            for m in range(TAPS):
                tap = jnp.where(turn == m, values[0:1, m:m + 1], tap)
            fill(band, slot * rows, jnp.where(lane < inner, group + 1, group), tap)

        build_band(0)

        for r in range(1, chan_size):
            remote(gram.at[0], gram.at[r], gram_s.at[r], gram_r.at[r], c_peer(r)).wait_recv()
        total = gram[0]
        for r in range(1, chan_size):
            total = total + gram[r]
        row_id = iota((MODES, 128), 0)
        both = jnp.where(iota((MODES, 128), 1) - MODES == row_id, 1.0, total)
        for i in range(MODES):
            pivot = both[i:i + 1, :] / both[i:i + 1, i:i + 1]
            both = jnp.where(row_id == i, pivot, both - both[:, i:i + 1] * pivot)

        ext[...] = jnp.zeros(ext.shape, f32)
        for r in range(1, chan_size):
            remote(proj.at[0], proj.at[r], proj_s.at[r], proj_r.at[r], c_peer(r)).wait_recv()
        full = proj[0]
        for r in range(1, chan_size):
            full = full + proj[r]
        ext[MODES:2 * MODES, :] = full
        coef[0] = jnp.dot(both, ext[...], precision=highest, preferred_element_type=f32)
        for r in range(1, NX):
            start(remote(coef.at[0], coef.at[NX - r], coef_s.at[r], coef_r.at[NX - r], x_peer(r)))
        for r in (1, 3):
            start(raw_copy(r, 1))

        b_high, b_mid, b_low = split3(basis[:, pl.ds(here, quarter)])
        b_stack = jnp.concatenate(
            [b_high, b_mid, b_high, b_mid, b_low, b_high, jnp.zeros((2 * MODES, quarter), bf16)],
            axis=0,
        )

        def fit_slot(slot):
            c_high, c_mid, c_low = split3(coef[slot])
            c_stack = jnp.concatenate(
                [c_high, c_high, c_mid, c_mid, c_high, c_low, jnp.zeros((2 * MODES, rows), bf16)],
                axis=0,
            )
            ripple[slot * rows:(slot + 1) * rows, :] = lax.dot_general(
                c_stack, b_stack, (((0,), (0,)), ((), ())), preferred_element_type=f32
            )

        def clean_slot(slot, values):
            clean[slot * rows:(slot + 1) * rows, :] = (
                values.astype(f32) - ripple[slot * rows:(slot + 1) * rows, :]
            ).astype(bf16)

        fit_slot(0)
        clean_slot(0, own[:, pl.ds(here, quarter)])
        begin = gal_chan[...] - SW - (j * width + here)
        shift_hot = (iota((shifts, ngal), 0) == quarter - 1 - begin).astype(f32).astype(bf16)
        gal_row = jnp.broadcast_to(gal_pix[...], (TAPS, ngal))
        fill(
            pixel_hot, 0, gal_row >> 4,
            jnp.where((gal_row & (TAPS - 1)) == iota((TAPS, ngal), 0), 1.0, 0.0).astype(f32),
        )
        counts[...] = lax.dot_general(
            shift_hot, pixel_hot[...], (((1,), (1,)), ((), ())), preferred_element_type=f32
        ).astype(bf16)

        for r in range(1, NX):
            remote(pix.at[0], pix.at[r], pix_s.at[r], pix_r.at[r], x_peer(r)).wait_recv()
            build_band(r)
        for r in (1, 3, 2):
            remote(coef.at[0], coef.at[r], coef_s.at[r], coef_r.at[r], x_peer(r)).wait_recv()
            fit_slot(r)
        for r, pieces in ((2, (2,)), (1, (0, 1)), (3, (0, 1))):
            for piece in pieces:
                raw_copy(NX - r, piece).wait_recv()
            clean_slot(r, raw[r])

        def chunk_row(step):
            return pl.multiple_of(lax.rem(z + step + 2 * nz, nz) * zpix, zpix)

        def part_tile(step, tile):
            row = pl.multiple_of(chunk_row(step) + tile * TP, TP)
            return part[pl.ds(row, TP), :]

        sign = (1, -1)

        def hops(way, tile):
            return far if tile // 2 == way else far - 1

        def z_copy(way, tile, k):
            if k < hops(way, tile) - 1:
                target, recv_sem = zrecv.at[way, tile, k], z_r.at[way, tile, k]
                peer = z_peer((1, nz - 1)[way])
            else:
                target, recv_sem = edge.at[way, x], edge_r.at[way, x]
                peer = beside(way, (z * NX + tile, j))
            return remote(
                zsend.at[way, tile, k], target, z_s.at[way, tile, k], recv_sem, peer
            )

        def z_step(k, long):
            for lane in range(2):
                for way in range(2):
                    tile = 2 * (way if long else 1 - way) + lane
                    value = part_tile(sign[way] * (hops(way, tile) - k), tile)
                    if k:
                        z_copy(way, tile, k - 1).wait_recv()
                        value = value + zrecv[way, tile, k - 1].astype(f32)
                    zsend[way, tile, k] = value.astype(bf16)
                    z_copy(way, tile, k).start()

        def grid_step(n, carry):
            away = lax.div(n + 1, 2)
            row = chunk_row(far + away - 2 * lax.rem(n, 2) * away)
            part[pl.ds(row, zpix), :] = jnp.dot(
                band[pl.ds(row, zpix), :], clean[...], preferred_element_type=f32
            )

            @pl.when(n == 0)
            def _():
                z_step(0, True)

            @pl.when(n == 2)
            def _():
                z_step(0, False)

            return carry

        def share(buffer, me, send_sem, recv_sem, peer_of, count):
            for r in range(1, count):
                start(remote(buffer.at[me], buffer.at[me], send_sem.at[r], recv_sem.at[me], peer_of(r)))

        def gather(buffer, me, send_sem, recv_sem, peer_of, count):
            for r in range(1, count):
                other = lax.rem(me + r, count)
                remote(
                    buffer.at[other], buffer.at[other], send_sem.at[r], recv_sem.at[other], peer_of(r)
                ).wait_recv()
            value = buffer[0]
            for i in range(1, count):
                value = value + buffer[i]
            return value

        lax.fori_loop(0, nz, grid_step, 0)

        wide = jnp.concatenate(
            [
                jnp.dot(counts[...], part[...].astype(bf16), preferred_element_type=f32),
                jnp.zeros((shifts, 512 - quarter), f32),
            ],
            axis=1,
        )
        folded = jnp.zeros((8, 512), f32)
        for i in range(shifts // 8):
            folded = folded + pltpu.roll(
                wide[8 * i:8 * i + 8], (513 - quarter + 8 * i) % 512, 1
            )
        window = jnp.zeros((1, 512), f32)
        for i in range(8):
            window = window + (pltpu.roll(folded[i:i + 1], i, 1) if i else folded[i:i + 1])
        st1[x] = window[:, :2 * SW]
        share(st1, x, st1_s, st1_r, x_peer, NX)

        z_step(1, True)
        z_step(1, False)
        final[...] = part[pl.ds(chunk_row(0), zpix), :].astype(bf16)
        for r in range(1, NX):
            row = pl.multiple_of(lax.rem(x + r, NX) * TP, TP)
            start(remote(
                final.at[pl.ds(row, TP), :], mine.at[NX - r], mine_s.at[r], mine_r.at[NX - r],
                x_peer(r),
            ))
        st2[j] = gather(st1, x, st1_s, st1_r, x_peer, NX)
        share(st2, j, st2_s, st2_r, c_peer, chan_size)
        z_step(2, True)
        z_step(2, False)
        st3[z] = gather(st2, j, st2_s, st2_r, c_peer, chan_size)
        share(st3, z, st3_s, st3_r, z_peer, nz)
        z_step(3, True)
        for r in range(1, NX):
            remote(
                final.at[pl.ds(0, TP), :], mine.at[r], mine_s.at[r], mine_r.at[r], x_peer(r)
            ).wait_recv()
        for copy in sends:
            copy.wait_send()
        for way in range(2):
            for source in range(NX):
                remote(
                    zsend.at[way, 0, 0], edge.at[way, source], z_s.at[way, 0, 0],
                    edge_r.at[way, source], beside(way, x_peer(0)),
                ).wait_recv()
        for r in range(NX):
            source = lax.rem(x + r, NX)
            if r:
                value = mine[r].astype(f32)
            else:
                value = part[pl.ds(pl.multiple_of(chunk_row(0) + x * TP, TP), TP), :]
            value = value + edge[0, source].astype(f32) + edge[1, source].astype(f32)
            column = pl.multiple_of(source * quarter, quarter)
            sky[:, pl.ds(column, quarter)] = value.astype(bf16)
        stacked[...] = gather(st3, z, st3_s, st3_r, z_peer, nz) / ngal
        for way in range(2):
            for tile in range(NX):
                for k in range(hops(way, tile)):
                    z_copy(way, tile, k).wait_send()

    dma = pltpu.SemaphoreType.DMA
    scratch = [
        pltpu.VMEM((rows, width), bf16),
        pltpu.VMEM((MODES, width), f32),
        pltpu.VMEM((NX, 1, rows), jnp.int32),
        pltpu.VMEM((NX, rows, quarter), bf16),
        pltpu.VMEM((chan_size, MODES, 128), f32),
        pltpu.VMEM((chan_size, MODES, rows), f32),
        pltpu.VMEM((128, rows), f32),
        pltpu.VMEM((NX, MODES, rows), f32),
        pltpu.VMEM((npix, NX * rows), bf16),
        pltpu.VMEM((NX * rows, quarter), f32),
        pltpu.VMEM((NX * rows, quarter), bf16),
        pltpu.VMEM((npix, quarter), f32),
        pltpu.VMEM((npix, ngal), bf16),
        pltpu.VMEM((shifts, npix), bf16),
        pltpu.VMEM((2, NX, far, TP, quarter), bf16),
        pltpu.VMEM((2, NX, far - 1, TP, quarter), bf16),
        pltpu.VMEM((2, NX, TP, quarter), bf16),
        pltpu.VMEM((zpix, quarter), bf16),
        pltpu.VMEM((NX, TP, quarter), bf16),
        pltpu.VMEM((NX, 1, 2 * SW), f32),
        pltpu.VMEM((chan_size, 1, 2 * SW), f32),
        pltpu.VMEM((nz, 1, 2 * SW), f32),
        dma((2,)),
    ]
    for shape in ((NX,), (3, NX), (chan_size,), (chan_size,), (NX,)):
        scratch += [dma(shape), dma(shape)]
    scratch += [dma((2, NX, far)), dma((2, NX, far - 1)), dma((2, NX))]
    for shape in ((NX,), (NX,), (chan_size,), (nz,)):
        scratch += [dma(shape), dma(shape)]
    return kernel, scratch


def solution(mesh):
    tm_size, chan_size = mesh.shape["tm"], mesh.shape["chan"]

    def per_device(spectra, chan_weight, routes, offsets, taps, gal_pix, gal_chan):
        rows, width = spectra.shape
        nblocks = routes.shape[0]
        kernel, scratch = make_kernel(
            tm_size, chan_size, rows, width, nblocks, gal_pix.shape[0]
        )
        vmem = pl.BlockSpec(memory_space=pltpu.VMEM)
        sky, stacked = pl.pallas_call(
            kernel,
            out_shape=(
                jax.ShapeDtypeStruct((TP, width), bf16),
                jax.ShapeDtypeStruct((1, 2 * SW), f32),
            ),
            in_specs=[pl.BlockSpec(memory_space=pl.ANY)] * 2 + [vmem] * 6,
            out_specs=(vmem, vmem),
            scratch_shapes=scratch,
            compiler_params=pltpu.CompilerParams(
                collective_id=0, has_side_effects=True, vmem_limit_bytes=54880 * 1024
            ),
        )(
            spectra, jnp.asarray(basis_table(width * chan_size)), chan_weight[None, :],
            routes.reshape(1, nblocks), offsets[None, :], taps[None, :], gal_pix[None, :],
            gal_chan[None, :],
        )
        return sky, stacked[0]

    in_specs = (
        P("tm", "chan"), P("chan"), P("tm", None), P("tm"), P(None), P(None), P(None)
    )
    return jax.shard_map(
        per_device, mesh=mesh, in_specs=in_specs, out_specs=(P("tm", "chan"), P(None)),
        check_vma=False,
    )
```

```python
import jax
import jax.numpy as jnp
import numpy as np
from jax import lax
from jax.experimental import pallas as pl
from jax.experimental.pallas import tpu as pltpu
from jax.sharding import PartitionSpec as P

KMODES = 8
MODES = 2 * KMODES
TP = 64
MARGIN = 8
SW = 64
TAPS = 16
NX = 4

highest = lax.Precision.HIGHEST
MESH = pl.DeviceIdType.MESH
f32 = jnp.float32
bf16 = jnp.bfloat16


def basis_table(total):
    orders = np.arange(1, KMODES + 1)[:, None]
    phase = (orders * np.arange(total)[None, :] % total) * (2 * np.pi / total)
    return np.concatenate([np.cos(phase), np.sin(phase)], axis=0).astype(np.float32)


def split3(value):
    high = value.astype(bf16)
    rest = value - high.astype(f32)
    mid = rest.astype(bf16)
    low = (rest - mid.astype(f32)).astype(bf16)
    return high, mid, low


def iota(shape, dim):
    return lax.broadcasted_iota(jnp.int32, shape, dim)


def make_kernel(tm_size, chan_size, rows, width, nblocks, ngal):
    nz = tm_size // NX
    quarter = width // NX
    npix = tm_size * TP
    zpix = NX * TP
    block_rows = rows // nblocks
    shifts = quarter + 2 * SW
    far = nz // 2

    def kernel(
        spec, basis_in, weight, routes, offsets, taps, gal_pix, gal_chan,
        sky, stacked,
        own, basis, pix, raw, gram, proj, ext, coef, band, ripple, clean, part, pixel_hot, counts,
        zsend, zrecv, edge, final, mine, st1, st2, st3,
        load_sem, pix_s, pix_r, raw_s, raw_r, gram_s, gram_r, proj_s, proj_r, coef_s, coef_r,
        z_s, z_r, edge_r, mine_s, mine_r, st1_s, st1_r, st2_s, st2_r, st3_s, st3_r,
    ):
        tm = lax.axis_index("tm")
        j = lax.axis_index("chan")
        z = lax.div(tm, NX)
        x = lax.rem(tm, NX)
        here = pl.multiple_of(x * quarter, quarter)

        def x_peer(r):
            return (z * NX + lax.rem(x + r, NX), j)

        def c_peer(r):
            return (tm, lax.rem(j + r, chan_size))

        def z_peer(r):
            return (lax.rem(z + r, nz) * NX + x, j)

        def beside(way, place):
            return (lax.rem(place[0] + (NX, (nz - 1) * NX)[way], tm_size), place[1])

        def remote(src, dst, send_sem, recv_sem, peer):
            return pltpu.make_async_remote_copy(
                src_ref=src, dst_ref=dst, send_sem=send_sem, recv_sem=recv_sem,
                device_id=peer, device_id_type=MESH,
            )

        sends = []

        def start(copy):
            copy.start()
            sends.append(copy)

        peers = (
            [x_peer(r) for r in range(1, NX)]
            + [c_peer(r) for r in range(1, chan_size)]
            + [z_peer(r) for r in range(1, nz)]
            + [beside(way, x_peer(r)) for way in range(2) for r in range(1, NX)]
        )
        barrier = pltpu.get_barrier_semaphore()
        for peer in peers:
            pl.semaphore_signal(barrier, inc=1, device_id=peer, device_id_type=MESH)
        basis_here = basis_in.at[:, pl.ds(pl.multiple_of(j * width, width), width)]
        loads = [
            pltpu.make_async_copy(source, target, load_sem.at[i])
            for i, (source, target) in enumerate((
                (spec, own), (basis_here, basis),
            ))
        ]
        for load in loads:
            load.start()
        inside = iota((nblocks, rows), 1) - block_rows * iota((nblocks, rows), 0)
        owner = ((inside >= 0) & (inside < block_rows)).astype(f32).astype(bf16)
        tile = jnp.dot(
            jnp.broadcast_to(routes[...], (16, nblocks)).astype(f32).astype(bf16), owner,
            preferred_element_type=f32,
        )[0:1].astype(jnp.int32)
        pix[0] = tile * TP + offsets[...] - MARGIN

        pl.semaphore_wait(barrier, len(peers))
        for r in range(1, NX):
            start(remote(pix.at[0], pix.at[NX - r], pix_s.at[r], pix_r.at[NX - r], x_peer(r)))

        late = rows // 4 * 3

        def raw_copy(r, piece):
            column = pl.multiple_of(lax.rem(x + r, NX) * quarter, quarter)
            low, high = ((0, late), (late, rows), (0, rows))[piece]
            return remote(
                spec.at[low:high, pl.ds(column, quarter)], raw.at[NX - r, low:high],
                raw_s.at[piece, r], raw_r.at[piece, NX - r], x_peer(r),
            )

        for r, piece in ((2, 2), (1, 0), (3, 0)):
            start(raw_copy(r, piece))

        loads[1].wait()
        weighted = basis[...] * weight[...]
        w_stack = jnp.concatenate(split3(weighted), axis=0)
        loads[0].wait()
        products = lax.dot_general(
            w_stack, own[...], (((1,), (1,)), ((), ())), preferred_element_type=f32
        )
        proj[0] = products[:MODES] + products[MODES:2 * MODES] + products[2 * MODES:]
        for r in range(1, chan_size):
            start(remote(
                proj.at[0], proj.at[chan_size - r], proj_s.at[r], proj_r.at[chan_size - r],
                c_peer(r),
            ))
        gram[0] = jnp.zeros((MODES, 128), f32)
        gram[0, :, 0:MODES] = lax.dot_general(
            weighted, basis[...], (((1,), (1,)), ((), ())), precision=highest,
            preferred_element_type=f32,
        )
        for r in range(1, chan_size):
            start(remote(
                gram.at[0], gram.at[chan_size - r], gram_s.at[r], gram_r.at[chan_size - r],
                c_peer(r),
            ))

        def fill(target, column, group, tap):
            def step(a, carry):
                row = pl.multiple_of(a * TAPS, TAPS)
                target[pl.ds(row, TAPS), column:column + tap.shape[1]] = jnp.where(
                    group == a, tap, 0.0
                ).astype(bf16)
                return carry

            lax.fori_loop(0, npix // TAPS, step, 0, unroll=4)

        def build_band(slot):
            first = pix[slot]
            group = jnp.broadcast_to(first >> 4, (TAPS, rows))
            inner = jnp.broadcast_to(first & (TAPS - 1), (TAPS, rows))
            lane = iota((TAPS, rows), 0)
            turn = (lane - inner) & (TAPS - 1)
            tap = jnp.zeros((TAPS, rows), f32)
            values = taps[...].astype(f32)
            for m in range(TAPS):
                tap = jnp.where(turn == m, values[0:1, m:m + 1], tap)
            fill(band, slot * rows, jnp.where(lane < inner, group + 1, group), tap)

        build_band(0)

        for r in range(1, chan_size):
            remote(gram.at[0], gram.at[r], gram_s.at[r], gram_r.at[r], c_peer(r)).wait_recv()
        total = gram[0]
        for r in range(1, chan_size):
            total = total + gram[r]
        row_id = iota((MODES, 128), 0)
        both = jnp.where(iota((MODES, 128), 1) - MODES == row_id, 1.0, total)
        for i in range(MODES):
            pivot = both[i:i + 1, :] / both[i:i + 1, i:i + 1]
            both = jnp.where(row_id == i, pivot, both - both[:, i:i + 1] * pivot)

        ext[...] = jnp.zeros(ext.shape, f32)
        for r in range(1, chan_size):
            remote(proj.at[0], proj.at[r], proj_s.at[r], proj_r.at[r], c_peer(r)).wait_recv()
        full = proj[0]
        for r in range(1, chan_size):
            full = full + proj[r]
        ext[MODES:2 * MODES, :] = full
        coef[0] = jnp.dot(both, ext[...], precision=highest, preferred_element_type=f32)
        for r in range(1, NX):
            start(remote(coef.at[0], coef.at[NX - r], coef_s.at[r], coef_r.at[NX - r], x_peer(r)))
        for r in (1, 3):
            start(raw_copy(r, 1))

        b_high, b_mid, b_low = split3(basis[:, pl.ds(here, quarter)])
        b_stack = jnp.concatenate(
            [b_high, b_mid, b_high, b_mid, b_low, b_high, jnp.zeros((2 * MODES, quarter), bf16)],
            axis=0,
        )

        def fit_slot(slot):
            c_high, c_mid, c_low = split3(coef[slot])
            c_stack = jnp.concatenate(
                [c_high, c_high, c_mid, c_mid, c_high, c_low, jnp.zeros((2 * MODES, rows), bf16)],
                axis=0,
            )
            ripple[slot * rows:(slot + 1) * rows, :] = lax.dot_general(
                c_stack, b_stack, (((0,), (0,)), ((), ())), preferred_element_type=f32
            )

        def clean_slot(slot, values):
            clean[slot * rows:(slot + 1) * rows, :] = (
                values.astype(f32) - ripple[slot * rows:(slot + 1) * rows, :]
            ).astype(bf16)

        fit_slot(0)
        clean_slot(0, own[:, pl.ds(here, quarter)])
        begin = gal_chan[...] - SW - (j * width + here)
        shift_hot = (iota((shifts, ngal), 0) == quarter - 1 - begin).astype(f32).astype(bf16)
        gal_row = jnp.broadcast_to(gal_pix[...], (TAPS, ngal))
        fill(
            pixel_hot, 0, gal_row >> 4,
            jnp.where((gal_row & (TAPS - 1)) == iota((TAPS, ngal), 0), 1.0, 0.0).astype(f32),
        )
        counts[...] = lax.dot_general(
            shift_hot, pixel_hot[...], (((1,), (1,)), ((), ())), preferred_element_type=f32
        ).astype(bf16)

        for r in range(1, NX):
            remote(pix.at[0], pix.at[r], pix_s.at[r], pix_r.at[r], x_peer(r)).wait_recv()
            build_band(r)
        for r in (1, 3, 2):
            remote(coef.at[0], coef.at[r], coef_s.at[r], coef_r.at[r], x_peer(r)).wait_recv()
            fit_slot(r)
        for r, pieces in ((2, (2,)), (1, (0, 1)), (3, (0, 1))):
            for piece in pieces:
                raw_copy(NX - r, piece).wait_recv()
            clean_slot(r, raw[r])

        def chunk_row(step):
            return pl.multiple_of(lax.rem(z + step + 2 * nz, nz) * zpix, zpix)

        def part_tile(step, tile):
            row = pl.multiple_of(chunk_row(step) + tile * TP, TP)
            return part[pl.ds(row, TP), :]

        sign = (1, -1)

        def hops(way, tile):
            return far if tile // 2 == way else far - 1

        def z_copy(way, tile, k):
            if k < hops(way, tile) - 1:
                target, recv_sem = zrecv.at[way, tile, k], z_r.at[way, tile, k]
                peer = z_peer((1, nz - 1)[way])
            else:
                target, recv_sem = edge.at[way, x], edge_r.at[way, x]
                peer = beside(way, (z * NX + tile, j))
            return remote(
                zsend.at[way, tile, k], target, z_s.at[way, tile, k], recv_sem, peer
            )

        def z_step(k, long):
            for lane in range(2):
                for way in range(2):
                    tile = 2 * (way if long else 1 - way) + lane
                    value = part_tile(sign[way] * (hops(way, tile) - k), tile)
                    if k:
                        z_copy(way, tile, k - 1).wait_recv()
                        value = value + zrecv[way, tile, k - 1].astype(f32)
                    zsend[way, tile, k] = value.astype(bf16)
                    z_copy(way, tile, k).start()

        def z_sent(last):
            for way in range(2):
                for tile in range(NX):
                    count = hops(way, tile)
                    for k in (count - 1,) if last else range(count - 1):
                        z_copy(way, tile, k).wait_send()

        def grid_step(n, carry):
            away = lax.div(n + 1, 2)
            row = chunk_row(far + away - 2 * lax.rem(n, 2) * away)
            part[pl.ds(row, zpix), :] = jnp.dot(
                band[pl.ds(row, zpix), :], clean[...], preferred_element_type=f32
            )

            @pl.when(n == 0)
            def _():
                z_step(0, True)

            @pl.when(n == 2)
            def _():
                z_step(0, False)

            return carry

        def share(buffer, me, send_sem, recv_sem, peer_of, count):
            for r in range(1, count):
                start(remote(buffer.at[me], buffer.at[me], send_sem.at[r], recv_sem.at[me], peer_of(r)))

        def gather(buffer, me, send_sem, recv_sem, peer_of, count):
            for r in range(1, count):
                other = lax.rem(me + r, count)
                remote(
                    buffer.at[other], buffer.at[other], send_sem.at[r], recv_sem.at[other], peer_of(r)
                ).wait_recv()
            value = buffer[0]
            for i in range(1, count):
                value = value + buffer[i]
            return value

        lax.fori_loop(0, nz, grid_step, 0)

        wide = jnp.concatenate(
            [
                jnp.dot(counts[...], part[...].astype(bf16), preferred_element_type=f32),
                jnp.zeros((shifts, 512 - quarter), f32),
            ],
            axis=1,
        )
        folded = jnp.zeros((8, 512), f32)
        for i in range(shifts // 8):
            folded = folded + pltpu.roll(
                wide[8 * i:8 * i + 8], (513 - quarter + 8 * i) % 512, 1
            )
        window = jnp.zeros((1, 512), f32)
        for i in range(8):
            window = window + (pltpu.roll(folded[i:i + 1], i, 1) if i else folded[i:i + 1])
        st1[x] = window[:, :2 * SW]
        share(st1, x, st1_s, st1_r, x_peer, NX)

        z_step(1, True)
        z_step(1, False)
        final[...] = part[pl.ds(chunk_row(0), zpix), :].astype(bf16)
        for r in range(1, NX):
            row = pl.multiple_of(lax.rem(x + r, NX) * TP, TP)
            start(remote(
                final.at[pl.ds(row, TP), :], mine.at[NX - r], mine_s.at[r], mine_r.at[NX - r],
                x_peer(r),
            ))
        st2[j] = gather(st1, x, st1_s, st1_r, x_peer, NX)
        share(st2, j, st2_s, st2_r, c_peer, chan_size)
        z_step(2, True)
        z_step(2, False)
        st3[z] = gather(st2, j, st2_s, st2_r, c_peer, chan_size)
        share(st3, z, st3_s, st3_r, z_peer, nz)
        z_step(3, True)
        for r in range(1, NX):
            remote(
                final.at[pl.ds(0, TP), :], mine.at[r], mine_s.at[r], mine_r.at[r], x_peer(r)
            ).wait_recv()
        for copy in sends:
            copy.wait_send()
        z_sent(False)

        for way in range(2):
            for source in range(NX):
                remote(
                    zsend.at[way, 0, 0], edge.at[way, source], z_s.at[way, 0, 0],
                    edge_r.at[way, source], beside(way, x_peer(0)),
                ).wait_recv()
        for r in range(NX):
            source = lax.rem(x + r, NX)
            if r:
                value = mine[r].astype(f32)
            else:
                value = part[pl.ds(pl.multiple_of(chunk_row(0) + x * TP, TP), TP), :]
            value = value + edge[0, source].astype(f32) + edge[1, source].astype(f32)
            column = pl.multiple_of(source * quarter, quarter)
            sky[:, pl.ds(column, quarter)] = value.astype(bf16)
        stacked[...] = gather(st3, z, st3_s, st3_r, z_peer, nz) / ngal
        z_sent(True)

    dma = pltpu.SemaphoreType.DMA
    scratch = [
        pltpu.VMEM((rows, width), bf16),
        pltpu.VMEM((MODES, width), f32),
        pltpu.VMEM((NX, 1, rows), jnp.int32),
        pltpu.VMEM((NX, rows, quarter), bf16),
        pltpu.VMEM((chan_size, MODES, 128), f32),
        pltpu.VMEM((chan_size, MODES, rows), f32),
        pltpu.VMEM((128, rows), f32),
        pltpu.VMEM((NX, MODES, rows), f32),
        pltpu.VMEM((npix, NX * rows), bf16),
        pltpu.VMEM((NX * rows, quarter), f32),
        pltpu.VMEM((NX * rows, quarter), bf16),
        pltpu.VMEM((npix, quarter), f32),
        pltpu.VMEM((npix, ngal), bf16),
        pltpu.VMEM((shifts, npix), bf16),
        pltpu.VMEM((2, NX, far, TP, quarter), bf16),
        pltpu.VMEM((2, NX, far - 1, TP, quarter), bf16),
        pltpu.VMEM((2, NX, TP, quarter), bf16),
        pltpu.VMEM((zpix, quarter), bf16),
        pltpu.VMEM((NX, TP, quarter), bf16),
        pltpu.VMEM((NX, 1, 2 * SW), f32),
        pltpu.VMEM((chan_size, 1, 2 * SW), f32),
        pltpu.VMEM((nz, 1, 2 * SW), f32),
        dma((2,)),
    ]
    for shape in ((NX,), (3, NX), (chan_size,), (chan_size,), (NX,)):
        scratch += [dma(shape), dma(shape)]
    scratch += [dma((2, NX, far)), dma((2, NX, far - 1)), dma((2, NX))]
    for shape in ((NX,), (NX,), (chan_size,), (nz,)):
        scratch += [dma(shape), dma(shape)]
    return kernel, scratch


def solution(mesh):
    tm_size, chan_size = mesh.shape["tm"], mesh.shape["chan"]

    def per_device(spectra, chan_weight, routes, offsets, taps, gal_pix, gal_chan):
        rows, width = spectra.shape
        nblocks = routes.shape[0]
        kernel, scratch = make_kernel(
            tm_size, chan_size, rows, width, nblocks, gal_pix.shape[0]
        )
        vmem = pl.BlockSpec(memory_space=pltpu.VMEM)
        sky, stacked = pl.pallas_call(
            kernel,
            out_shape=(
                jax.ShapeDtypeStruct((TP, width), bf16),
                jax.ShapeDtypeStruct((1, 2 * SW), f32),
            ),
            in_specs=[pl.BlockSpec(memory_space=pl.ANY)] * 2 + [vmem] * 6,
            out_specs=(vmem, vmem),
            scratch_shapes=scratch,
            compiler_params=pltpu.CompilerParams(
                collective_id=0, has_side_effects=True, vmem_limit_bytes=54880 * 1024
            ),
        )(
            spectra, jnp.asarray(basis_table(width * chan_size)), chan_weight[None, :],
            routes.reshape(1, nblocks), offsets[None, :], taps[None, :], gal_pix[None, :],
            gal_chan[None, :],
        )
        return sky, stacked[0]

    in_specs = (
        P("tm", "chan"), P("chan"), P("tm", None), P("tm"), P(None), P(None), P(None)
    )
    return jax.shard_map(
        per_device, mesh=mesh, in_specs=in_specs, out_specs=(P("tm", "chan"), P(None)),
        check_vma=False,
    )
```

```python
import jax
import jax.numpy as jnp
import numpy as np
from jax import lax
from jax.experimental import pallas as pl
from jax.experimental.pallas import tpu as pltpu
from jax.sharding import PartitionSpec as P

KMODES = 8
MODES = 2 * KMODES
TP = 64
MARGIN = 8
SW = 64
TAPS = 16
NX = 4

highest = lax.Precision.HIGHEST
MESH = pl.DeviceIdType.MESH
f32 = jnp.float32
bf16 = jnp.bfloat16


def basis_table(total):
    orders = np.arange(1, KMODES + 1)[:, None]
    phase = (orders * np.arange(total)[None, :] % total) * (2 * np.pi / total)
    return np.concatenate([np.cos(phase), np.sin(phase)], axis=0).astype(np.float32)


def split3(value):
    high = value.astype(bf16)
    rest = value - high.astype(f32)
    mid = rest.astype(bf16)
    low = (rest - mid.astype(f32)).astype(bf16)
    return high, mid, low


def iota(shape, dim):
    return lax.broadcasted_iota(jnp.int32, shape, dim)


def make_kernel(tm_size, chan_size, rows, width, nblocks, ngal):
    nz = tm_size // NX
    quarter = width // NX
    npix = tm_size * TP
    zpix = NX * TP
    block_rows = rows // nblocks
    shifts = quarter + 2 * SW
    far = nz // 2

    def kernel(
        spec, basis_in, weight, routes, offsets, taps, gal_pix, gal_chan,
        sky, stacked,
        own, basis, pix, raw, gram, proj, ext, coef, band, clean, part, pixel_hot, counts,
        zsend, zrecv, edge, final, mine, st1, st2, st3,
        load_sem, pix_s, pix_r, raw_s, raw_r, gram_s, gram_r, proj_s, proj_r, coef_s, coef_r,
        z_s, z_r, edge_r, mine_s, mine_r, st1_s, st1_r, st2_s, st2_r, st3_s, st3_r,
    ):
        tm = lax.axis_index("tm")
        j = lax.axis_index("chan")
        z = lax.div(tm, NX)
        x = lax.rem(tm, NX)
        here = pl.multiple_of(x * quarter, quarter)

        def x_peer(r):
            return (z * NX + lax.rem(x + r, NX), j)

        def c_peer(r):
            return (tm, lax.rem(j + r, chan_size))

        def z_peer(r):
            return (lax.rem(z + r, nz) * NX + x, j)

        def beside(way, place):
            return (lax.rem(place[0] + (NX, (nz - 1) * NX)[way], tm_size), place[1])

        def remote(src, dst, send_sem, recv_sem, peer):
            return pltpu.make_async_remote_copy(
                src_ref=src, dst_ref=dst, send_sem=send_sem, recv_sem=recv_sem,
                device_id=peer, device_id_type=MESH,
            )

        sends = []

        def start(copy):
            copy.start()
            sends.append(copy)

        peers = (
            [x_peer(r) for r in range(1, NX)]
            + [c_peer(r) for r in range(1, chan_size)]
            + [z_peer(r) for r in range(1, nz)]
            + [beside(way, x_peer(r)) for way in range(2) for r in range(1, NX)]
        )
        barrier = pltpu.get_barrier_semaphore()
        for peer in peers:
            pl.semaphore_signal(barrier, inc=1, device_id=peer, device_id_type=MESH)
        basis_here = basis_in.at[:, pl.ds(pl.multiple_of(j * width, width), width)]
        loads = [
            pltpu.make_async_copy(source, target, load_sem.at[i])
            for i, (source, target) in enumerate((
                (spec, own.at[0:rows]), (basis_here, basis),
            ))
        ]
        for load in loads:
            load.start()
        inside = iota((nblocks, rows), 1) - block_rows * iota((nblocks, rows), 0)
        owner = ((inside >= 0) & (inside < block_rows)).astype(f32).astype(bf16)
        tile = jnp.dot(
            jnp.broadcast_to(routes[...], (16, nblocks)).astype(f32).astype(bf16), owner,
            preferred_element_type=f32,
        )[0:1].astype(jnp.int32)
        pix[0] = tile * TP + offsets[...] - MARGIN

        pl.semaphore_wait(barrier, len(peers))
        for r in range(1, NX):
            start(remote(pix.at[0], pix.at[NX - r], pix_s.at[r], pix_r.at[NX - r], x_peer(r)))

        late = rows // 4 * 3

        def raw_copy(r, piece):
            column = pl.multiple_of(lax.rem(x + r, NX) * quarter, quarter)
            low, high = ((0, late), (late, rows), (0, rows))[piece]
            return remote(
                spec.at[low:high, pl.ds(column, quarter)], raw.at[NX - r, low:high],
                raw_s.at[piece, r], raw_r.at[piece, NX - r], x_peer(r),
            )

        for r, piece in ((2, 2), (1, 0), (3, 0)):
            start(raw_copy(r, piece))

        loads[1].wait()
        weighted = basis[...] * weight[...]
        w_stack = jnp.concatenate(split3(weighted), axis=0)
        own[rows:, :] = jnp.concatenate(
            [*split3(basis[...]), jnp.zeros((128 - 3 * MODES, width), bf16)], axis=0
        )
        loads[0].wait()
        products = lax.dot_general(
            w_stack, own[...], (((1,), (1,)), ((), ())), preferred_element_type=f32
        )
        products = products[:MODES] + products[MODES:2 * MODES] + products[2 * MODES:]
        normal = products[:, rows:]
        normal = (
            normal + pltpu.roll(normal, 128 - MODES, 1) + pltpu.roll(normal, 128 - 2 * MODES, 1)
        )
        gram[0] = jnp.where(iota((MODES, 128), 1) < MODES, normal, 0.0)
        for r in range(1, chan_size):
            start(remote(
                gram.at[0], gram.at[chan_size - r], gram_s.at[r], gram_r.at[chan_size - r],
                c_peer(r),
            ))
        proj[0] = products[:, :rows]
        for r in range(1, chan_size):
            start(remote(
                proj.at[0], proj.at[chan_size - r], proj_s.at[r], proj_r.at[chan_size - r],
                c_peer(r),
            ))

        def fill(target, column, group, tap):
            def step(a, carry):
                row = pl.multiple_of(a * TAPS, TAPS)
                target[pl.ds(row, TAPS), column:column + tap.shape[1]] = jnp.where(
                    group == a, tap, 0.0
                ).astype(bf16)
                return carry

            lax.fori_loop(0, npix // TAPS, step, 0, unroll=4)

        def build_band(slot):
            first = pix[slot]
            group = jnp.broadcast_to(first >> 4, (TAPS, rows))
            inner = jnp.broadcast_to(first & (TAPS - 1), (TAPS, rows))
            lane = iota((TAPS, rows), 0)
            turn = (lane - inner) & (TAPS - 1)
            tap = jnp.zeros((TAPS, rows), f32)
            values = taps[...].astype(f32)
            for m in range(TAPS):
                tap = jnp.where(turn == m, values[0:1, m:m + 1], tap)
            fill(band, slot * rows, jnp.where(lane < inner, group + 1, group), tap)

        build_band(0)

        for r in range(1, chan_size):
            remote(gram.at[0], gram.at[r], gram_s.at[r], gram_r.at[r], c_peer(r)).wait_recv()
        total = gram[0]
        for r in range(1, chan_size):
            total = total + gram[r]
        row_id = iota((MODES, 128), 0)
        both = jnp.where(iota((MODES, 128), 1) - MODES == row_id, 1.0, total)
        for i in range(MODES):
            pivot = both[i:i + 1, :] / both[i:i + 1, i:i + 1]
            both = jnp.where(row_id == i, pivot, both - both[:, i:i + 1] * pivot)

        ext[...] = jnp.zeros(ext.shape, f32)
        for r in range(1, chan_size):
            remote(proj.at[0], proj.at[r], proj_s.at[r], proj_r.at[r], c_peer(r)).wait_recv()
        full = proj[0]
        for r in range(1, chan_size):
            full = full + proj[r]
        ext[MODES:2 * MODES, :] = full
        coef[0] = jnp.dot(both, ext[...], precision=highest, preferred_element_type=f32)
        for r in range(1, NX):
            start(remote(coef.at[0], coef.at[NX - r], coef_s.at[r], coef_r.at[NX - r], x_peer(r)))
        for r in (1, 3):
            start(raw_copy(r, 1))

        b_high, b_mid, b_low = split3(basis[:, pl.ds(here, quarter)])
        b_stack = jnp.concatenate(
            [b_high, b_mid, b_high, b_mid, b_low, b_high, jnp.zeros((2 * MODES, quarter), bf16)],
            axis=0,
        )

        def clean_slot(slot, values):
            c_high, c_mid, c_low = split3(coef[slot])
            c_stack = jnp.concatenate(
                [c_high, c_high, c_mid, c_mid, c_high, c_low, jnp.zeros((2 * MODES, rows), bf16)],
                axis=0,
            )
            ripple = lax.dot_general(
                c_stack, b_stack, (((0,), (0,)), ((), ())), preferred_element_type=f32
            )
            clean[slot * rows:(slot + 1) * rows, :] = (values.astype(f32) - ripple).astype(bf16)

        clean_slot(0, own[0:rows, pl.ds(here, quarter)])

        begin = gal_chan[...] - SW - (j * width + here)
        shift_hot = (iota((shifts, ngal), 0) == quarter - 1 - begin).astype(f32).astype(bf16)
        gal_row = jnp.broadcast_to(gal_pix[...], (TAPS, ngal))
        fill(
            pixel_hot, 0, gal_row >> 4,
            jnp.where((gal_row & (TAPS - 1)) == iota((TAPS, ngal), 0), 1.0, 0.0).astype(f32),
        )
        counts[...] = lax.dot_general(
            shift_hot, pixel_hot[...], (((1,), (1,)), ((), ())), preferred_element_type=f32
        ).astype(bf16)

        for r in range(1, NX):
            remote(pix.at[0], pix.at[r], pix_s.at[r], pix_r.at[r], x_peer(r)).wait_recv()
            build_band(r)
        for r, pieces in ((1, (0, 1)), (3, (0, 1)), (2, (2,))):
            for piece in pieces:
                raw_copy(NX - r, piece).wait_recv()
            remote(coef.at[0], coef.at[r], coef_s.at[r], coef_r.at[r], x_peer(r)).wait_recv()
            clean_slot(r, raw[r])

        def chunk_row(step):
            return pl.multiple_of(lax.rem(z + step + 2 * nz, nz) * zpix, zpix)

        def part_tile(step, tile):
            row = pl.multiple_of(chunk_row(step) + tile * TP, TP)
            return part[pl.ds(row, TP), :]

        sign = (1, -1)

        def hops(way, tile):
            return far if tile // 2 == way else far - 1

        def z_copy(way, tile, k):
            if k < hops(way, tile) - 1:
                target, recv_sem = zrecv.at[way, tile, k], z_r.at[way, tile, k]
                peer = z_peer((1, nz - 1)[way])
            else:
                target, recv_sem = edge.at[way, x], edge_r.at[way, x]
                peer = beside(way, (z * NX + tile, j))
            return remote(
                zsend.at[way, tile, k], target, z_s.at[way, tile, k], recv_sem, peer
            )

        def z_step(k, long):
            for lane in range(2):
                for way in range(2):
                    tile = 2 * (way if long else 1 - way) + lane
                    value = part_tile(sign[way] * (hops(way, tile) - k), tile)
                    if k:
                        z_copy(way, tile, k - 1).wait_recv()
                        value = value + zrecv[way, tile, k - 1].astype(f32)
                    zsend[way, tile, k] = value.astype(bf16)
                    z_copy(way, tile, k).start()

        def z_sent(last):
            for way in range(2):
                for tile in range(NX):
                    count = hops(way, tile)
                    for k in (count - 1,) if last else range(count - 1):
                        z_copy(way, tile, k).wait_send()

        def grid_step(n, carry):
            away = lax.div(n + 1, 2)
            row = chunk_row(far + away - 2 * lax.rem(n, 2) * away)
            part[pl.ds(row, zpix), :] = jnp.dot(
                band[pl.ds(row, zpix), :], clean[...], preferred_element_type=f32
            )

            @pl.when(n == 0)
            def _():
                z_step(0, True)

            @pl.when(n == 2)
            def _():
                z_step(0, False)

            return carry

        def share(buffer, me, send_sem, recv_sem, peer_of, count):
            for r in range(1, count):
                start(remote(buffer.at[me], buffer.at[me], send_sem.at[r], recv_sem.at[me], peer_of(r)))

        def gather(buffer, me, send_sem, recv_sem, peer_of, count):
            for r in range(1, count):
                other = lax.rem(me + r, count)
                remote(
                    buffer.at[other], buffer.at[other], send_sem.at[r], recv_sem.at[other], peer_of(r)
                ).wait_recv()
            value = buffer[0]
            for i in range(1, count):
                value = value + buffer[i]
            return value

        lax.fori_loop(0, nz, grid_step, 0)

        wide = jnp.concatenate(
            [
                jnp.dot(counts[...], part[...].astype(bf16), preferred_element_type=f32),
                jnp.zeros((shifts, 512 - quarter), f32),
            ],
            axis=1,
        )
        folded = jnp.zeros((8, 512), f32)
        for i in range(shifts // 8):
            folded = folded + pltpu.roll(
                wide[8 * i:8 * i + 8], (513 - quarter + 8 * i) % 512, 1
            )
        window = jnp.zeros((1, 512), f32)
        for i in range(8):
            window = window + (pltpu.roll(folded[i:i + 1], i, 1) if i else folded[i:i + 1])
        st1[x] = window[:, :2 * SW]
        share(st1, x, st1_s, st1_r, x_peer, NX)

        z_step(1, True)
        z_step(1, False)
        final[...] = part[pl.ds(chunk_row(0), zpix), :].astype(bf16)
        for r in range(1, NX):
            row = pl.multiple_of(lax.rem(x + r, NX) * TP, TP)
            start(remote(
                final.at[pl.ds(row, TP), :], mine.at[NX - r], mine_s.at[r], mine_r.at[NX - r],
                x_peer(r),
            ))
        st2[j] = gather(st1, x, st1_s, st1_r, x_peer, NX)
        share(st2, j, st2_s, st2_r, c_peer, chan_size)
        z_step(2, True)
        z_step(2, False)
        st3[z] = gather(st2, j, st2_s, st2_r, c_peer, chan_size)
        share(st3, z, st3_s, st3_r, z_peer, nz)
        z_step(3, True)
        for r in range(1, NX):
            remote(
                final.at[pl.ds(0, TP), :], mine.at[r], mine_s.at[r], mine_r.at[r], x_peer(r)
            ).wait_recv()
        for copy in sends:
            copy.wait_send()
        z_sent(False)

        for way in range(2):
            for source in range(NX):
                remote(
                    zsend.at[way, 0, 0], edge.at[way, source], z_s.at[way, 0, 0],
                    edge_r.at[way, source], beside(way, x_peer(0)),
                ).wait_recv()
        for r in range(NX):
            source = lax.rem(x + r, NX)
            if r:
                value = mine[r].astype(f32)
            else:
                value = part[pl.ds(pl.multiple_of(chunk_row(0) + x * TP, TP), TP), :]
            value = value + edge[0, source].astype(f32) + edge[1, source].astype(f32)
            column = pl.multiple_of(source * quarter, quarter)
            sky[:, pl.ds(column, quarter)] = value.astype(bf16)
        stacked[...] = gather(st3, z, st3_s, st3_r, z_peer, nz) / ngal
        z_sent(True)

    dma = pltpu.SemaphoreType.DMA
    scratch = [
        pltpu.VMEM((rows + 128, width), bf16),
        pltpu.VMEM((MODES, width), f32),
        pltpu.VMEM((NX, 1, rows), jnp.int32),
        pltpu.VMEM((NX, rows, quarter), bf16),
        pltpu.VMEM((chan_size, MODES, 128), f32),
        pltpu.VMEM((chan_size, MODES, rows), f32),
        pltpu.VMEM((128, rows), f32),
        pltpu.VMEM((NX, MODES, rows), f32),
        pltpu.VMEM((npix, NX * rows), bf16),
        pltpu.VMEM((NX * rows, quarter), bf16),
        pltpu.VMEM((npix, quarter), f32),
        pltpu.VMEM((npix, ngal), bf16),
        pltpu.VMEM((shifts, npix), bf16),
        pltpu.VMEM((2, NX, far, TP, quarter), bf16),
        pltpu.VMEM((2, NX, far - 1, TP, quarter), bf16),
        pltpu.VMEM((2, NX, TP, quarter), bf16),
        pltpu.VMEM((zpix, quarter), bf16),
        pltpu.VMEM((NX, TP, quarter), bf16),
        pltpu.VMEM((NX, 1, 2 * SW), f32),
        pltpu.VMEM((chan_size, 1, 2 * SW), f32),
        pltpu.VMEM((nz, 1, 2 * SW), f32),
        dma((2,)),
    ]
    for shape in ((NX,), (3, NX), (chan_size,), (chan_size,), (NX,)):
        scratch += [dma(shape), dma(shape)]
    scratch += [dma((2, NX, far)), dma((2, NX, far - 1)), dma((2, NX))]
    for shape in ((NX,), (NX,), (chan_size,), (nz,)):
        scratch += [dma(shape), dma(shape)]
    return kernel, scratch


def solution(mesh):
    tm_size, chan_size = mesh.shape["tm"], mesh.shape["chan"]

    def per_device(spectra, chan_weight, routes, offsets, taps, gal_pix, gal_chan):
        rows, width = spectra.shape
        nblocks = routes.shape[0]
        kernel, scratch = make_kernel(
            tm_size, chan_size, rows, width, nblocks, gal_pix.shape[0]
        )
        vmem = pl.BlockSpec(memory_space=pltpu.VMEM)
        sky, stacked = pl.pallas_call(
            kernel,
            out_shape=(
                jax.ShapeDtypeStruct((TP, width), bf16),
                jax.ShapeDtypeStruct((1, 2 * SW), f32),
            ),
            in_specs=[pl.BlockSpec(memory_space=pl.ANY)] * 2 + [vmem] * 6,
            out_specs=(vmem, vmem),
            scratch_shapes=scratch,
            compiler_params=pltpu.CompilerParams(
                collective_id=0, has_side_effects=True, vmem_limit_bytes=54880 * 1024
            ),
        )(
            spectra, jnp.asarray(basis_table(width * chan_size)), chan_weight[None, :],
            routes.reshape(1, nblocks), offsets[None, :], taps[None, :], gal_pix[None, :],
            gal_chan[None, :],
        )
        return sky, stacked[0]

    in_specs = (
        P("tm", "chan"), P("chan"), P("tm", None), P("tm"), P(None), P(None), P(None)
    )
    return jax.shard_map(
        per_device, mesh=mesh, in_specs=in_specs, out_specs=(P("tm", "chan"), P(None)),
        check_vma=False,
    )
```

```python
import jax
import jax.numpy as jnp
import numpy as np
from jax import lax
from jax.experimental import pallas as pl
from jax.experimental.pallas import tpu as pltpu
from jax.sharding import PartitionSpec as P

KMODES = 8
MODES = 2 * KMODES
TP = 64
MARGIN = 8
SW = 64
TAPS = 16
NX = 4

highest = lax.Precision.HIGHEST
MESH = pl.DeviceIdType.MESH
f32 = jnp.float32
bf16 = jnp.bfloat16


def basis_table(total):
    orders = np.arange(1, KMODES + 1)[:, None]
    phase = (orders * np.arange(total)[None, :] % total) * (2 * np.pi / total)
    return np.concatenate([np.cos(phase), np.sin(phase)], axis=0).astype(np.float32)


def split3(value):
    high = value.astype(bf16)
    rest = value - high.astype(f32)
    mid = rest.astype(bf16)
    low = (rest - mid.astype(f32)).astype(bf16)
    return high, mid, low


def iota(shape, dim):
    return lax.broadcasted_iota(jnp.int32, shape, dim)


def make_kernel(tm_size, chan_size, rows, width, nblocks, ngal):
    nz = tm_size // NX
    quarter = width // NX
    npix = tm_size * TP
    zpix = NX * TP
    block_rows = rows // nblocks
    shifts = quarter + 2 * SW
    far = nz // 2

    def kernel(
        spec, basis_in, weight, routes, offsets, taps, gal_pix, gal_chan,
        sky, stacked,
        own, basis, pix, raw, gram, proj, ext, coef, band, ripple, clean, part, pixel_hot, counts,
        zsend, zrecv, edge, final, mine, st1, st2, st3,
        load_sem, pix_s, pix_r, raw_s, raw_r, gram_s, gram_r, proj_s, proj_r, coef_s, coef_r,
        z_s, z_r, edge_r, mine_s, mine_r, st1_s, st1_r, st2_s, st2_r, st3_s, st3_r,
    ):
        tm = lax.axis_index("tm")
        j = lax.axis_index("chan")
        z = lax.div(tm, NX)
        x = lax.rem(tm, NX)
        here = pl.multiple_of(x * quarter, quarter)

        def x_peer(r):
            return (z * NX + lax.rem(x + r, NX), j)

        def c_peer(r):
            return (tm, lax.rem(j + r, chan_size))

        def z_peer(r):
            return (lax.rem(z + r, nz) * NX + x, j)

        def beside(way, place):
            return (lax.rem(place[0] + (NX, (nz - 1) * NX)[way], tm_size), place[1])

        def remote(src, dst, send_sem, recv_sem, peer):
            return pltpu.make_async_remote_copy(
                src_ref=src, dst_ref=dst, send_sem=send_sem, recv_sem=recv_sem,
                device_id=peer, device_id_type=MESH,
            )

        sends = []

        def start(copy):
            copy.start()
            sends.append(copy)

        peers = (
            [x_peer(r) for r in range(1, NX)]
            + [c_peer(r) for r in range(1, chan_size)]
            + [z_peer(r) for r in range(1, nz)]
            + [beside(way, x_peer(r)) for way in range(2) for r in range(1, NX)]
        )
        barrier = pltpu.get_barrier_semaphore()
        for peer in peers:
            pl.semaphore_signal(barrier, inc=1, device_id=peer, device_id_type=MESH)
        basis_here = basis_in.at[:, pl.ds(pl.multiple_of(j * width, width), width)]
        loads = [
            pltpu.make_async_copy(source, target, load_sem.at[i])
            for i, (source, target) in enumerate((
                (spec, own.at[0:rows]), (basis_here, basis),
            ))
        ]
        for load in loads:
            load.start()
        inside = iota((nblocks, rows), 1) - block_rows * iota((nblocks, rows), 0)
        owner = ((inside >= 0) & (inside < block_rows)).astype(f32).astype(bf16)
        tile = jnp.dot(
            jnp.broadcast_to(routes[...], (16, nblocks)).astype(f32).astype(bf16), owner,
            preferred_element_type=f32,
        )[0:1].astype(jnp.int32)
        pix[0] = tile * TP + offsets[...] - MARGIN

        pl.semaphore_wait(barrier, len(peers))
        for r in range(1, NX):
            start(remote(pix.at[0], pix.at[NX - r], pix_s.at[r], pix_r.at[NX - r], x_peer(r)))

        def raw_copy(r):
            column = pl.multiple_of(lax.rem(x + r, NX) * quarter, quarter)
            return remote(
                spec.at[:, pl.ds(column, quarter)], raw.at[NX - r], raw_s.at[r], raw_r.at[NX - r],
                x_peer(r),
            )

        for r in (2, 1, 3):
            start(raw_copy(r))

        loads[1].wait()
        weighted = basis[...] * weight[...]
        w_stack = jnp.concatenate(split3(weighted), axis=0)
        own[rows:, :] = jnp.concatenate(
            [*split3(basis[...]), jnp.zeros((128 - 3 * MODES, width), bf16)], axis=0
        )
        loads[0].wait()
        products = lax.dot_general(
            w_stack, own[...], (((1,), (1,)), ((), ())), preferred_element_type=f32
        )
        products = products[:MODES] + products[MODES:2 * MODES] + products[2 * MODES:]
        normal = products[:, rows:]
        normal = (
            normal + pltpu.roll(normal, 128 - MODES, 1) + pltpu.roll(normal, 128 - 2 * MODES, 1)
        )
        gram[0] = jnp.where(iota((MODES, 128), 1) < MODES, normal, 0.0)
        for r in range(1, chan_size):
            start(remote(
                gram.at[0], gram.at[chan_size - r], gram_s.at[r], gram_r.at[chan_size - r],
                c_peer(r),
            ))
        proj[0] = products[:, :rows]
        for r in range(1, chan_size):
            start(remote(
                proj.at[0], proj.at[chan_size - r], proj_s.at[r], proj_r.at[chan_size - r],
                c_peer(r),
            ))

        def fill(target, column, group, tap):
            def step(a, carry):
                row = pl.multiple_of(a * TAPS, TAPS)
                target[pl.ds(row, TAPS), column:column + tap.shape[1]] = jnp.where(
                    group == a, tap, 0.0
                ).astype(bf16)
                return carry

            lax.fori_loop(0, npix // TAPS, step, 0, unroll=4)

        def build_band(slot):
            first = pix[slot]
            group = jnp.broadcast_to(first >> 4, (TAPS, rows))
            inner = jnp.broadcast_to(first & (TAPS - 1), (TAPS, rows))
            lane = iota((TAPS, rows), 0)
            turn = (lane - inner) & (TAPS - 1)
            tap = jnp.zeros((TAPS, rows), f32)
            values = taps[...].astype(f32)
            for m in range(TAPS):
                tap = jnp.where(turn == m, values[0:1, m:m + 1], tap)
            fill(band, slot * rows, jnp.where(lane < inner, group + 1, group), tap)

        build_band(0)

        for r in range(1, chan_size):
            remote(gram.at[0], gram.at[r], gram_s.at[r], gram_r.at[r], c_peer(r)).wait_recv()
        total = gram[0]
        for r in range(1, chan_size):
            total = total + gram[r]
        row_id = iota((MODES, 128), 0)
        both = jnp.where(iota((MODES, 128), 1) - MODES == row_id, 1.0, total)
        for i in range(MODES):
            pivot = both[i:i + 1, :] / both[i:i + 1, i:i + 1]
            both = jnp.where(row_id == i, pivot, both - both[:, i:i + 1] * pivot)

        ext[...] = jnp.zeros(ext.shape, f32)
        for r in range(1, chan_size):
            remote(proj.at[0], proj.at[r], proj_s.at[r], proj_r.at[r], c_peer(r)).wait_recv()
        full = proj[0]
        for r in range(1, chan_size):
            full = full + proj[r]
        ext[MODES:2 * MODES, :] = full
        coef[0] = jnp.dot(both, ext[...], precision=highest, preferred_element_type=f32)
        for r in range(1, NX):
            start(remote(coef.at[0], coef.at[NX - r], coef_s.at[r], coef_r.at[NX - r], x_peer(r)))

        b_high, b_mid, b_low = split3(basis[:, pl.ds(here, quarter)])
        b_stack = jnp.concatenate(
            [b_high, b_mid, b_high, b_mid, b_low, b_high, jnp.zeros((2 * MODES, quarter), bf16)],
            axis=0,
        )

        def fit_slot(slot):
            c_high, c_mid, c_low = split3(coef[slot])
            c_stack = jnp.concatenate(
                [c_high, c_high, c_mid, c_mid, c_high, c_low, jnp.zeros((2 * MODES, rows), bf16)],
                axis=0,
            )
            ripple[slot * rows:(slot + 1) * rows, :] = lax.dot_general(
                c_stack, b_stack, (((0,), (0,)), ((), ())), preferred_element_type=f32
            )

        def clean_slot(slot, values):
            clean[slot * rows:(slot + 1) * rows, :] = (
                values.astype(f32) - ripple[slot * rows:(slot + 1) * rows, :]
            ).astype(bf16)

        fit_slot(0)
        clean_slot(0, own[0:rows, pl.ds(here, quarter)])

        begin = gal_chan[...] - SW - (j * width + here)
        shift_hot = (iota((shifts, ngal), 0) == quarter - 1 - begin).astype(f32).astype(bf16)
        gal_row = jnp.broadcast_to(gal_pix[...], (TAPS, ngal))
        fill(
            pixel_hot, 0, gal_row >> 4,
            jnp.where((gal_row & (TAPS - 1)) == iota((TAPS, ngal), 0), 1.0, 0.0).astype(f32),
        )
        counts[...] = lax.dot_general(
            shift_hot, pixel_hot[...], (((1,), (1,)), ((), ())), preferred_element_type=f32
        ).astype(bf16)

        for r in range(1, NX):
            remote(pix.at[0], pix.at[r], pix_s.at[r], pix_r.at[r], x_peer(r)).wait_recv()
            build_band(r)
        for r in (1, 3, 2):
            remote(coef.at[0], coef.at[r], coef_s.at[r], coef_r.at[r], x_peer(r)).wait_recv()
            fit_slot(r)
        for r in (1, 3, 2):
            raw_copy(NX - r).wait_recv()
            clean_slot(r, raw[r])

        def chunk_row(step):
            return pl.multiple_of(lax.rem(z + step + 2 * nz, nz) * zpix, zpix)

        def part_tile(step, tile):
            row = pl.multiple_of(chunk_row(step) + tile * TP, TP)
            return part[pl.ds(row, TP), :]

        sign = (1, -1)

        def hops(way, tile):
            return far if tile // 2 == way else far - 1

        def z_copy(way, tile, k):
            if k < hops(way, tile) - 1:
                target, recv_sem = zrecv.at[way, tile, k], z_r.at[way, tile, k]
                peer = z_peer((1, nz - 1)[way])
            else:
                target, recv_sem = edge.at[way, x], edge_r.at[way, x]
                peer = beside(way, (z * NX + tile, j))
            return remote(
                zsend.at[way, tile, k], target, z_s.at[way, tile, k], recv_sem, peer
            )

        def z_step(k, long):
            for lane in range(2):
                for way in range(2):
                    tile = 2 * (way if long else 1 - way) + lane
                    value = part_tile(sign[way] * (hops(way, tile) - k), tile)
                    if k:
                        z_copy(way, tile, k - 1).wait_recv()
                        value = value + zrecv[way, tile, k - 1].astype(f32)
                    zsend[way, tile, k] = value.astype(bf16)
                    z_copy(way, tile, k).start()

        def z_sent(last):
            for way in range(2):
                for tile in range(NX):
                    count = hops(way, tile)
                    for k in (count - 1,) if last else range(count - 1):
                        z_copy(way, tile, k).wait_send()

        def grid_step(n, carry):
            away = lax.div(n + 1, 2)
            row = chunk_row(far + away - 2 * lax.rem(n, 2) * away)
            part[pl.ds(row, zpix), :] = jnp.dot(
                band[pl.ds(row, zpix), :], clean[...], preferred_element_type=f32
            )

            @pl.when(n == 0)
            def _():
                z_step(0, True)

            @pl.when(n == 2)
            def _():
                z_step(0, False)

            return carry

        def share(buffer, me, send_sem, recv_sem, peer_of, count):
            for r in range(1, count):
                start(remote(buffer.at[me], buffer.at[me], send_sem.at[r], recv_sem.at[me], peer_of(r)))

        def gather(buffer, me, send_sem, recv_sem, peer_of, count):
            for r in range(1, count):
                other = lax.rem(me + r, count)
                remote(
                    buffer.at[other], buffer.at[other], send_sem.at[r], recv_sem.at[other], peer_of(r)
                ).wait_recv()
            value = buffer[0]
            for i in range(1, count):
                value = value + buffer[i]
            return value

        lax.fori_loop(0, nz, grid_step, 0)

        wide = jnp.concatenate(
            [
                jnp.dot(counts[...], part[...].astype(bf16), preferred_element_type=f32),
                jnp.zeros((shifts, 512 - quarter), f32),
            ],
            axis=1,
        )
        folded = jnp.zeros((8, 512), f32)
        for i in range(shifts // 8):
            folded = folded + pltpu.roll(
                wide[8 * i:8 * i + 8], (513 - quarter + 8 * i) % 512, 1
            )
        window = jnp.zeros((1, 512), f32)
        for i in range(8):
            window = window + (pltpu.roll(folded[i:i + 1], i, 1) if i else folded[i:i + 1])
        st1[x] = window[:, :2 * SW]
        share(st1, x, st1_s, st1_r, x_peer, NX)

        z_step(1, True)
        z_step(1, False)
        final[...] = part[pl.ds(chunk_row(0), zpix), :].astype(bf16)
        for r in range(1, NX):
            row = pl.multiple_of(lax.rem(x + r, NX) * TP, TP)
            start(remote(
                final.at[pl.ds(row, TP), :], mine.at[NX - r], mine_s.at[r], mine_r.at[NX - r],
                x_peer(r),
            ))
        st2[j] = gather(st1, x, st1_s, st1_r, x_peer, NX)
        share(st2, j, st2_s, st2_r, c_peer, chan_size)
        z_step(2, True)
        z_step(2, False)
        st3[z] = gather(st2, j, st2_s, st2_r, c_peer, chan_size)
        share(st3, z, st3_s, st3_r, z_peer, nz)
        z_step(3, True)
        for r in range(1, NX):
            remote(
                final.at[pl.ds(0, TP), :], mine.at[r], mine_s.at[r], mine_r.at[r], x_peer(r)
            ).wait_recv()
        for copy in sends:
            copy.wait_send()
        z_sent(False)

        for way in range(2):
            for source in range(NX):
                remote(
                    zsend.at[way, 0, 0], edge.at[way, source], z_s.at[way, 0, 0],
                    edge_r.at[way, source], beside(way, x_peer(0)),
                ).wait_recv()
        for r in range(NX):
            source = lax.rem(x + r, NX)
            if r:
                value = mine[r].astype(f32)
            else:
                value = part[pl.ds(pl.multiple_of(chunk_row(0) + x * TP, TP), TP), :]
            value = value + edge[0, source].astype(f32) + edge[1, source].astype(f32)
            column = pl.multiple_of(source * quarter, quarter)
            sky[:, pl.ds(column, quarter)] = value.astype(bf16)
        stacked[...] = gather(st3, z, st3_s, st3_r, z_peer, nz) / ngal
        z_sent(True)

    dma = pltpu.SemaphoreType.DMA
    scratch = [
        pltpu.VMEM((rows + 128, width), bf16),
        pltpu.VMEM((MODES, width), f32),
        pltpu.VMEM((NX, 1, rows), jnp.int32),
        pltpu.VMEM((NX, rows, quarter), bf16),
        pltpu.VMEM((chan_size, MODES, 128), f32),
        pltpu.VMEM((chan_size, MODES, rows), f32),
        pltpu.VMEM((128, rows), f32),
        pltpu.VMEM((NX, MODES, rows), f32),
        pltpu.VMEM((npix, NX * rows), bf16),
        pltpu.VMEM((NX * rows, quarter), f32),
        pltpu.VMEM((NX * rows, quarter), bf16),
        pltpu.VMEM((npix, quarter), f32),
        pltpu.VMEM((npix, ngal), bf16),
        pltpu.VMEM((shifts, npix), bf16),
        pltpu.VMEM((2, NX, far, TP, quarter), bf16),
        pltpu.VMEM((2, NX, far - 1, TP, quarter), bf16),
        pltpu.VMEM((2, NX, TP, quarter), bf16),
        pltpu.VMEM((zpix, quarter), bf16),
        pltpu.VMEM((NX, TP, quarter), bf16),
        pltpu.VMEM((NX, 1, 2 * SW), f32),
        pltpu.VMEM((chan_size, 1, 2 * SW), f32),
        pltpu.VMEM((nz, 1, 2 * SW), f32),
        dma((2,)),
    ]
    for shape in ((NX,), (NX,), (chan_size,), (chan_size,), (NX,)):
        scratch += [dma(shape), dma(shape)]
    scratch += [dma((2, NX, far)), dma((2, NX, far - 1)), dma((2, NX))]
    for shape in ((NX,), (NX,), (chan_size,), (nz,)):
        scratch += [dma(shape), dma(shape)]
    return kernel, scratch


def solution(mesh):
    tm_size, chan_size = mesh.shape["tm"], mesh.shape["chan"]

    def per_device(spectra, chan_weight, routes, offsets, taps, gal_pix, gal_chan):
        rows, width = spectra.shape
        nblocks = routes.shape[0]
        kernel, scratch = make_kernel(
            tm_size, chan_size, rows, width, nblocks, gal_pix.shape[0]
        )
        vmem = pl.BlockSpec(memory_space=pltpu.VMEM)
        sky, stacked = pl.pallas_call(
            kernel,
            out_shape=(
                jax.ShapeDtypeStruct((TP, width), bf16),
                jax.ShapeDtypeStruct((1, 2 * SW), f32),
            ),
            in_specs=[pl.BlockSpec(memory_space=pl.ANY)] * 2 + [vmem] * 6,
            out_specs=(vmem, vmem),
            scratch_shapes=scratch,
            compiler_params=pltpu.CompilerParams(
                collective_id=0, has_side_effects=True, vmem_limit_bytes=54880 * 1024
            ),
        )(
            spectra, jnp.asarray(basis_table(width * chan_size)), chan_weight[None, :],
            routes.reshape(1, nblocks), offsets[None, :], taps[None, :], gal_pix[None, :],
            gal_chan[None, :],
        )
        return sky, stacked[0]

    in_specs = (
        P("tm", "chan"), P("chan"), P("tm", None), P("tm"), P(None), P(None), P(None)
    )
    return jax.shard_map(
        per_device, mesh=mesh, in_specs=in_specs, out_specs=(P("tm", "chan"), P(None)),
        check_vma=False,
    )
```

```python
import jax
import jax.numpy as jnp
import numpy as np
from jax import lax
from jax.experimental import pallas as pl
from jax.experimental.pallas import tpu as pltpu
from jax.sharding import PartitionSpec as P

KMODES = 8
MODES = 2 * KMODES
TP = 64
MARGIN = 8
SW = 64
TAPS = 16
NX = 4

highest = lax.Precision.HIGHEST
MESH = pl.DeviceIdType.MESH
f32 = jnp.float32
bf16 = jnp.bfloat16


def basis_table(total):
    orders = np.arange(1, KMODES + 1)[:, None]
    phase = (orders * np.arange(total)[None, :] % total) * (2 * np.pi / total)
    return np.concatenate([np.cos(phase), np.sin(phase)], axis=0).astype(np.float32)


def split3(value):
    high = value.astype(bf16)
    rest = value - high.astype(f32)
    mid = rest.astype(bf16)
    low = (rest - mid.astype(f32)).astype(bf16)
    return high, mid, low


def iota(shape, dim):
    return lax.broadcasted_iota(jnp.int32, shape, dim)


def make_kernel(tm_size, chan_size, rows, width, nblocks, ngal):
    nz = tm_size // NX
    quarter = width // NX
    npix = tm_size * TP
    zpix = NX * TP
    block_rows = rows // nblocks
    shifts = quarter + 2 * SW
    far = nz // 2

    def kernel(
        spec, basis_in, weight, routes, offsets, taps, gal_pix, gal_chan,
        sky, stacked,
        own, basis, pix, raw, gram, proj, ext, coef, band, ripple, clean, part, pixel_hot, counts,
        zsend, zrecv, edge, final, mine, st1, st2, st3,
        load_sem, pix_s, pix_r, raw_s, raw_r, gram_s, gram_r, proj_s, proj_r, coef_s, coef_r,
        z_s, z_r, edge_r, mine_s, mine_r, st1_s, st1_r, st2_s, st2_r, st3_s, st3_r,
    ):
        tm = lax.axis_index("tm")
        j = lax.axis_index("chan")
        z = lax.div(tm, NX)
        x = lax.rem(tm, NX)
        here = pl.multiple_of(x * quarter, quarter)

        def x_peer(r):
            return (z * NX + lax.rem(x + r, NX), j)

        def c_peer(r):
            return (tm, lax.rem(j + r, chan_size))

        def z_peer(r):
            return (lax.rem(z + r, nz) * NX + x, j)

        def beside(way, place, away):
            return (lax.rem(place[0] + (away, nz - away)[way] * NX, tm_size), place[1])

        def remote(src, dst, send_sem, recv_sem, peer):
            return pltpu.make_async_remote_copy(
                src_ref=src, dst_ref=dst, send_sem=send_sem, recv_sem=recv_sem,
                device_id=peer, device_id_type=MESH,
            )

        sends = []

        def start(copy):
            copy.start()
            sends.append(copy)

        peers = (
            [x_peer(r) for r in range(1, NX)]
            + [c_peer(r) for r in range(1, chan_size)]
            + [z_peer(r) for r in range(1, nz)]
            + [
                beside(way, x_peer(r), away)
                for away in (1, 2) for way in range(2) for r in range(1, NX)
            ]
        )
        barrier = pltpu.get_barrier_semaphore()
        for peer in peers:
            pl.semaphore_signal(barrier, inc=1, device_id=peer, device_id_type=MESH)
        basis_here = basis_in.at[:, pl.ds(pl.multiple_of(j * width, width), width)]
        loads = [
            pltpu.make_async_copy(source, target, load_sem.at[i])
            for i, (source, target) in enumerate((
                (spec, own), (basis_here, basis),
            ))
        ]
        for load in loads:
            load.start()
        inside = iota((nblocks, rows), 1) - block_rows * iota((nblocks, rows), 0)
        owner = ((inside >= 0) & (inside < block_rows)).astype(f32).astype(bf16)
        tile = jnp.dot(
            jnp.broadcast_to(routes[...], (16, nblocks)).astype(f32).astype(bf16), owner,
            preferred_element_type=f32,
        )[0:1].astype(jnp.int32)
        pix[0] = tile * TP + offsets[...] - MARGIN

        loads[1].wait()
        weighted = basis[...] * weight[...]
        w_stack = jnp.concatenate(split3(weighted), axis=0)

        pl.semaphore_wait(barrier, len(peers))
        for r in range(1, NX):
            start(remote(pix.at[0], pix.at[NX - r], pix_s.at[r], pix_r.at[NX - r], x_peer(r)))

        late = rows // 4 * 3

        def raw_copy(r, piece):
            column = pl.multiple_of(lax.rem(x + r, NX) * quarter, quarter)
            low, high = ((0, late), (late, rows), (0, rows))[piece]
            return remote(
                own.at[low:high, pl.ds(column, quarter)], raw.at[NX - r, low:high],
                raw_s.at[piece, r], raw_r.at[piece, NX - r], x_peer(r),
            )

        loads[0].wait()
        for r, piece in ((2, 2), (1, 0), (3, 0)):
            start(raw_copy(r, piece))

        products = lax.dot_general(
            w_stack, own[...], (((1,), (1,)), ((), ())), preferred_element_type=f32
        )
        proj[0] = products[:MODES] + products[MODES:2 * MODES] + products[2 * MODES:]
        for r in range(1, chan_size):
            start(remote(
                proj.at[0], proj.at[chan_size - r], proj_s.at[r], proj_r.at[chan_size - r],
                c_peer(r),
            ))
        gram[0] = jnp.zeros((MODES, 128), f32)
        gram[0, :, 0:MODES] = lax.dot_general(
            weighted, basis[...], (((1,), (1,)), ((), ())), precision=highest,
            preferred_element_type=f32,
        )
        for r in range(1, chan_size):
            start(remote(
                gram.at[0], gram.at[chan_size - r], gram_s.at[r], gram_r.at[chan_size - r],
                c_peer(r),
            ))

        def fill(target, column, group, tap):
            def step(a, carry):
                row = pl.multiple_of(a * TAPS, TAPS)
                target[pl.ds(row, TAPS), column:column + tap.shape[1]] = jnp.where(
                    group == a, tap, 0.0
                ).astype(bf16)
                return carry

            lax.fori_loop(0, npix // TAPS, step, 0, unroll=4)

        def build_band(slot):
            first = pix[slot]
            group = jnp.broadcast_to(first >> 4, (TAPS, rows))
            inner = jnp.broadcast_to(first & (TAPS - 1), (TAPS, rows))
            lane = iota((TAPS, rows), 0)
            turn = (lane - inner) & (TAPS - 1)
            tap = jnp.zeros((TAPS, rows), f32)
            values = taps[...].astype(f32)
            for m in range(TAPS):
                tap = jnp.where(turn == m, values[0:1, m:m + 1], tap)
            fill(band, slot * rows, jnp.where(lane < inner, group + 1, group), tap)

        build_band(0)

        for r in range(1, chan_size):
            remote(gram.at[0], gram.at[r], gram_s.at[r], gram_r.at[r], c_peer(r)).wait_recv()
        total = gram[0]
        for r in range(1, chan_size):
            total = total + gram[r]
        row_id = iota((MODES, 128), 0)
        both = jnp.where(iota((MODES, 128), 1) - MODES == row_id, 1.0, total)
        for i in range(MODES):
            pivot = both[i:i + 1, :] / both[i:i + 1, i:i + 1]
            both = jnp.where(row_id == i, pivot, both - both[:, i:i + 1] * pivot)

        ext[...] = jnp.zeros(ext.shape, f32)
        for r in range(1, chan_size):
            remote(proj.at[0], proj.at[r], proj_s.at[r], proj_r.at[r], c_peer(r)).wait_recv()
        full = proj[0]
        for r in range(1, chan_size):
            full = full + proj[r]
        ext[MODES:2 * MODES, :] = full
        coef[0] = jnp.dot(both, ext[...], precision=highest, preferred_element_type=f32)
        for r in range(1, NX):
            start(remote(coef.at[0], coef.at[NX - r], coef_s.at[r], coef_r.at[NX - r], x_peer(r)))
        for r in (1, 3):
            start(raw_copy(r, 1))

        b_high, b_mid, b_low = split3(basis[:, pl.ds(here, quarter)])
        b_stack = jnp.concatenate(
            [b_high, b_mid, b_high, b_mid, b_low, b_high, jnp.zeros((2 * MODES, quarter), bf16)],
            axis=0,
        )

        def fit_slot(slot):
            c_high, c_mid, c_low = split3(coef[slot])
            c_stack = jnp.concatenate(
                [c_high, c_high, c_mid, c_mid, c_high, c_low, jnp.zeros((2 * MODES, rows), bf16)],
                axis=0,
            )
            ripple[slot * rows:(slot + 1) * rows, :] = lax.dot_general(
                c_stack, b_stack, (((0,), (0,)), ((), ())), preferred_element_type=f32
            )

        def clean_slot(slot, values):
            clean[slot * rows:(slot + 1) * rows, :] = (
                values.astype(f32) - ripple[slot * rows:(slot + 1) * rows, :]
            ).astype(bf16)

        fit_slot(0)
        clean_slot(0, own[:, pl.ds(here, quarter)])
        begin = gal_chan[...] - SW - (j * width + here)
        shift_hot = (iota((shifts, ngal), 0) == quarter - 1 - begin).astype(f32).astype(bf16)
        gal_row = jnp.broadcast_to(gal_pix[...], (TAPS, ngal))
        fill(
            pixel_hot, 0, gal_row >> 4,
            jnp.where((gal_row & (TAPS - 1)) == iota((TAPS, ngal), 0), 1.0, 0.0).astype(f32),
        )
        counts[...] = lax.dot_general(
            shift_hot, pixel_hot[...], (((1,), (1,)), ((), ())), preferred_element_type=f32
        ).astype(bf16)

        for r in range(1, NX):
            remote(pix.at[0], pix.at[r], pix_s.at[r], pix_r.at[r], x_peer(r)).wait_recv()
            build_band(r)
        for r in (1, 3, 2):
            remote(coef.at[0], coef.at[r], coef_s.at[r], coef_r.at[r], x_peer(r)).wait_recv()
            fit_slot(r)
        for r, pieces in ((2, (2,)), (1, (0, 1)), (3, (0, 1))):
            for piece in pieces:
                raw_copy(NX - r, piece).wait_recv()
            clean_slot(r, raw[r])

        def chunk_row(step):
            return pl.multiple_of(lax.rem(z + step + 2 * nz, nz) * zpix, zpix)

        def part_tile(step, tile):
            row = pl.multiple_of(chunk_row(step) + tile * TP, TP)
            return part[pl.ds(row, TP), :]

        sign = (1, -1)

        def distance(way, tile, k):
            long = tile // 2 == way
            return (far, far - 1, far - 2, 1)[k] if long else (far - 1, far - 2, 1)[k]

        def steps(way, tile):
            return 4 if tile // 2 == way else 3

        def z_copy(way, tile, k):
            if k < 2:
                target, recv_sem = zrecv.at[way, tile, k], z_r.at[way, tile, k]
                peer = z_peer((1, nz - 1)[way])
            else:
                slot = way if k == 2 else 2
                target, recv_sem = edge.at[slot, x], edge_r.at[slot, x]
                peer = beside(way, (z * NX + tile, j), distance(way, tile, k))
            return remote(
                zsend.at[way, tile, k], target, z_s.at[way, tile, k], recv_sem, peer
            )

        def z_step(k, long):
            for lane in range(2):
                for way in range(2):
                    tile = 2 * (way if long else 1 - way) + lane
                    value = part_tile(sign[way] * distance(way, tile, k), tile)
                    if k in (1, 2):
                        z_copy(way, tile, k - 1).wait_recv()
                        value = value + zrecv[way, tile, k - 1].astype(f32)
                    zsend[way, tile, k] = value.astype(bf16)
                    z_copy(way, tile, k).start()

        def z_sent(ks):
            for way in range(2):
                for tile in range(NX):
                    for k in ks:
                        if k < steps(way, tile):
                            z_copy(way, tile, k).wait_send()

        def grid_step(n, carry):
            away = lax.div(n + 1, 2)
            row = chunk_row(far + away - 2 * lax.rem(n, 2) * away)
            part[pl.ds(row, zpix), :] = jnp.dot(
                band[pl.ds(row, zpix), :], clean[...], preferred_element_type=f32
            )

            @pl.when(n == 0)
            def _():
                z_step(0, True)

            @pl.when(n == 2)
            def _():
                z_step(0, False)

            return carry

        def share(buffer, me, send_sem, recv_sem, peer_of, count):
            for r in range(1, count):
                start(remote(buffer.at[me], buffer.at[me], send_sem.at[r], recv_sem.at[me], peer_of(r)))

        def gather(buffer, me, send_sem, recv_sem, peer_of, count):
            for r in range(1, count):
                other = lax.rem(me + r, count)
                remote(
                    buffer.at[other], buffer.at[other], send_sem.at[r], recv_sem.at[other], peer_of(r)
                ).wait_recv()
            value = buffer[0]
            for i in range(1, count):
                value = value + buffer[i]
            return value

        lax.fori_loop(0, nz, grid_step, 0)

        wide = jnp.concatenate(
            [
                jnp.dot(counts[...], part[...].astype(bf16), preferred_element_type=f32),
                jnp.zeros((shifts, 512 - quarter), f32),
            ],
            axis=1,
        )
        folded = jnp.zeros((8, 512), f32)
        for i in range(shifts // 8):
            folded = folded + pltpu.roll(
                wide[8 * i:8 * i + 8], (513 - quarter + 8 * i) % 512, 1
            )
        window = jnp.zeros((1, 512), f32)
        for i in range(8):
            window = window + (pltpu.roll(folded[i:i + 1], i, 1) if i else folded[i:i + 1])
        st1[x] = window[:, :2 * SW]
        share(st1, x, st1_s, st1_r, x_peer, NX)

        z_step(1, True)
        z_step(1, False)
        final[...] = part[pl.ds(chunk_row(0), zpix), :].astype(bf16)
        for r in range(1, NX):
            row = pl.multiple_of(lax.rem(x + r, NX) * TP, TP)
            start(remote(
                final.at[pl.ds(row, TP), :], mine.at[NX - r], mine_s.at[r], mine_r.at[NX - r],
                x_peer(r),
            ))
        st2[j] = gather(st1, x, st1_s, st1_r, x_peer, NX)
        share(st2, j, st2_s, st2_r, c_peer, chan_size)
        z_step(2, True)
        z_step(2, False)
        z_step(3, True)
        st3[z] = gather(st2, j, st2_s, st2_r, c_peer, chan_size)
        share(st3, z, st3_s, st3_r, z_peer, nz)
        for r in range(1, NX):
            remote(
                final.at[pl.ds(0, TP), :], mine.at[r], mine_s.at[r], mine_r.at[r], x_peer(r)
            ).wait_recv()
        for copy in sends:
            copy.wait_send()
        z_sent((0, 1))

        for slot in range(3):
            for source in range(NX):
                remote(
                    zsend.at[0, 0, 0], edge.at[slot, source], z_s.at[0, 0, 0],
                    edge_r.at[slot, source], beside(0, x_peer(0), 1),
                ).wait_recv()
        for r in range(NX):
            source = lax.rem(x + r, NX)
            if r:
                value = mine[r].astype(f32)
            else:
                value = part[pl.ds(pl.multiple_of(chunk_row(0) + x * TP, TP), TP), :]
            for slot in range(3):
                value = value + edge[slot, source].astype(f32)
            column = pl.multiple_of(source * quarter, quarter)
            sky[:, pl.ds(column, quarter)] = value.astype(bf16)
        stacked[...] = gather(st3, z, st3_s, st3_r, z_peer, nz) / ngal
        z_sent((2, 3))

    dma = pltpu.SemaphoreType.DMA
    scratch = [
        pltpu.VMEM((rows, width), bf16),
        pltpu.VMEM((MODES, width), f32),
        pltpu.VMEM((NX, 1, rows), jnp.int32),
        pltpu.VMEM((NX, rows, quarter), bf16),
        pltpu.VMEM((chan_size, MODES, 128), f32),
        pltpu.VMEM((chan_size, MODES, rows), f32),
        pltpu.VMEM((128, rows), f32),
        pltpu.VMEM((NX, MODES, rows), f32),
        pltpu.VMEM((npix, NX * rows), bf16),
        pltpu.VMEM((NX * rows, quarter), f32),
        pltpu.VMEM((NX * rows, quarter), bf16),
        pltpu.VMEM((npix, quarter), f32),
        pltpu.VMEM((npix, ngal), bf16),
        pltpu.VMEM((shifts, npix), bf16),
        pltpu.VMEM((2, NX, far, TP, quarter), bf16),
        pltpu.VMEM((2, NX, 2, TP, quarter), bf16),
        pltpu.VMEM((3, NX, TP, quarter), bf16),
        pltpu.VMEM((zpix, quarter), bf16),
        pltpu.VMEM((NX, TP, quarter), bf16),
        pltpu.VMEM((NX, 1, 2 * SW), f32),
        pltpu.VMEM((chan_size, 1, 2 * SW), f32),
        pltpu.VMEM((nz, 1, 2 * SW), f32),
        dma((2,)),
    ]
    for shape in ((NX,), (3, NX), (chan_size,), (chan_size,), (NX,)):
        scratch += [dma(shape), dma(shape)]
    scratch += [dma((2, NX, far)), dma((2, NX, 2)), dma((3, NX))]
    for shape in ((NX,), (NX,), (chan_size,), (nz,)):
        scratch += [dma(shape), dma(shape)]
    return kernel, scratch


def solution(mesh):
    tm_size, chan_size = mesh.shape["tm"], mesh.shape["chan"]

    def per_device(spectra, chan_weight, routes, offsets, taps, gal_pix, gal_chan):
        rows, width = spectra.shape
        nblocks = routes.shape[0]
        kernel, scratch = make_kernel(
            tm_size, chan_size, rows, width, nblocks, gal_pix.shape[0]
        )
        vmem = pl.BlockSpec(memory_space=pltpu.VMEM)
        sky, stacked = pl.pallas_call(
            kernel,
            out_shape=(
                jax.ShapeDtypeStruct((TP, width), bf16),
                jax.ShapeDtypeStruct((1, 2 * SW), f32),
            ),
            in_specs=[pl.BlockSpec(memory_space=pl.ANY)] * 2 + [vmem] * 6,
            out_specs=(vmem, vmem),
            scratch_shapes=scratch,
            compiler_params=pltpu.CompilerParams(
                collective_id=0, has_side_effects=True, vmem_limit_bytes=54880 * 1024
            ),
        )(
            spectra, jnp.asarray(basis_table(width * chan_size)), chan_weight[None, :],
            routes.reshape(1, nblocks), offsets[None, :], taps[None, :], gal_pix[None, :],
            gal_chan[None, :],
        )
        return sky, stacked[0]

    in_specs = (
        P("tm", "chan"), P("chan"), P("tm", None), P("tm"), P(None), P(None), P(None)
    )
    return jax.shard_map(
        per_device, mesh=mesh, in_specs=in_specs, out_specs=(P("tm", "chan"), P(None)),
        check_vma=False,
    )
```

```python
import jax
import jax.numpy as jnp
import numpy as np
from jax import lax
from jax.experimental import pallas as pl
from jax.experimental.pallas import tpu as pltpu
from jax.sharding import PartitionSpec as P

KMODES = 8
MODES = 2 * KMODES
TP = 64
MARGIN = 8
SW = 64
TAPS = 16
NX = 4

highest = lax.Precision.HIGHEST
MESH = pl.DeviceIdType.MESH
f32 = jnp.float32
bf16 = jnp.bfloat16


def basis_table(total):
    orders = np.arange(1, KMODES + 1)[:, None]
    phase = (orders * np.arange(total)[None, :] % total) * (2 * np.pi / total)
    return np.concatenate([np.cos(phase), np.sin(phase)], axis=0).astype(np.float32)


def split3(value):
    high = value.astype(bf16)
    rest = value - high.astype(f32)
    mid = rest.astype(bf16)
    low = (rest - mid.astype(f32)).astype(bf16)
    return high, mid, low


def iota(shape, dim):
    return lax.broadcasted_iota(jnp.int32, shape, dim)


def make_kernel(tm_size, chan_size, rows, width, nblocks, ngal):
    nz = tm_size // NX
    quarter = width // NX
    npix = tm_size * TP
    zpix = NX * TP
    block_rows = rows // nblocks
    shifts = quarter + 2 * SW
    far = nz // 2

    def kernel(
        spec, basis_in, weight, routes, offsets, taps, gal_pix, gal_chan,
        sky, stacked,
        own, basis, pix, raw, gram, proj, ext, coef, band, ripple, clean, part, pixel_hot, counts, seen,
        zsend, zrecv, edge, final, mine, st1, st2, st3,
        load_sem, pix_s, pix_r, raw_s, raw_r, gram_s, gram_r, proj_s, proj_r, coef_s, coef_r,
        z_s, z_r, edge_r, mine_s, mine_r, st1_s, st1_r, st2_s, st2_r, st3_s, st3_r,
    ):
        tm = lax.axis_index("tm")
        j = lax.axis_index("chan")
        z = lax.div(tm, NX)
        x = lax.rem(tm, NX)
        here = pl.multiple_of(x * quarter, quarter)

        def x_peer(r):
            return (z * NX + lax.rem(x + r, NX), j)

        def c_peer(r):
            return (tm, lax.rem(j + r, chan_size))

        def z_peer(r):
            return (lax.rem(z + r, nz) * NX + x, j)

        def beside(way, place):
            return (lax.rem(place[0] + (NX, (nz - 1) * NX)[way], tm_size), place[1])

        def remote(src, dst, send_sem, recv_sem, peer):
            return pltpu.make_async_remote_copy(
                src_ref=src, dst_ref=dst, send_sem=send_sem, recv_sem=recv_sem,
                device_id=peer, device_id_type=MESH,
            )

        sends = []

        def start(copy):
            copy.start()
            sends.append(copy)

        peers = (
            [x_peer(r) for r in range(1, NX)]
            + [c_peer(r) for r in range(1, chan_size)]
            + [z_peer(r) for r in range(1, nz)]
            + [beside(way, x_peer(r)) for way in range(2) for r in range(1, NX)]
        )
        barrier = pltpu.get_barrier_semaphore()
        for peer in peers:
            pl.semaphore_signal(barrier, inc=1, device_id=peer, device_id_type=MESH)
        basis_here = basis_in.at[:, pl.ds(pl.multiple_of(j * width, width), width)]
        loads = [
            pltpu.make_async_copy(source, target, load_sem.at[i])
            for i, (source, target) in enumerate((
                (spec, own), (basis_here, basis),
            ))
        ]
        for load in loads:
            load.start()
        inside = iota((nblocks, rows), 1) - block_rows * iota((nblocks, rows), 0)
        owner = ((inside >= 0) & (inside < block_rows)).astype(f32).astype(bf16)
        tile = jnp.dot(
            jnp.broadcast_to(routes[...], (16, nblocks)).astype(f32).astype(bf16), owner,
            preferred_element_type=f32,
        )[0:1].astype(jnp.int32)
        pix[0] = tile * TP + offsets[...] - MARGIN

        loads[1].wait()
        weighted = basis[...] * weight[...]
        w_stack = jnp.concatenate(split3(weighted), axis=0)

        pl.semaphore_wait(barrier, len(peers))
        for r in range(1, NX):
            start(remote(pix.at[0], pix.at[NX - r], pix_s.at[r], pix_r.at[NX - r], x_peer(r)))

        late = rows // 4 * 3

        def raw_copy(r, piece):
            column = pl.multiple_of(lax.rem(x + r, NX) * quarter, quarter)
            low, high = ((0, late), (late, rows), (0, rows))[piece]
            return remote(
                own.at[low:high, pl.ds(column, quarter)], raw.at[NX - r, low:high],
                raw_s.at[piece, r], raw_r.at[piece, NX - r], x_peer(r),
            )

        loads[0].wait()
        for r, piece in ((2, 2), (1, 0), (3, 0)):
            start(raw_copy(r, piece))

        products = lax.dot_general(
            w_stack, own[...], (((1,), (1,)), ((), ())), preferred_element_type=f32
        )
        proj[0] = products[:MODES] + products[MODES:2 * MODES] + products[2 * MODES:]
        for r in range(1, chan_size):
            start(remote(
                proj.at[0], proj.at[chan_size - r], proj_s.at[r], proj_r.at[chan_size - r],
                c_peer(r),
            ))
        gram[0] = jnp.zeros((MODES, 128), f32)
        gram[0, :, 0:MODES] = lax.dot_general(
            weighted, basis[...], (((1,), (1,)), ((), ())), precision=highest,
            preferred_element_type=f32,
        )
        for r in range(1, chan_size):
            start(remote(
                gram.at[0], gram.at[chan_size - r], gram_s.at[r], gram_r.at[chan_size - r],
                c_peer(r),
            ))

        def fill(target, column, group, tap):
            def step(a, carry):
                row = pl.multiple_of(a * TAPS, TAPS)
                target[pl.ds(row, TAPS), column:column + tap.shape[1]] = jnp.where(
                    group == a, tap, 0.0
                ).astype(bf16)
                return carry

            lax.fori_loop(0, npix // TAPS, step, 0, unroll=4)

        def build_band(slot):
            first = pix[slot]
            group = jnp.broadcast_to(first >> 4, (TAPS, rows))
            inner = jnp.broadcast_to(first & (TAPS - 1), (TAPS, rows))
            lane = iota((TAPS, rows), 0)
            turn = (lane - inner) & (TAPS - 1)
            tap = jnp.zeros((TAPS, rows), f32)
            values = taps[...].astype(f32)
            for m in range(TAPS):
                tap = jnp.where(turn == m, values[0:1, m:m + 1], tap)
            fill(band, slot * rows, jnp.where(lane < inner, group + 1, group), tap)

        build_band(0)

        for r in range(1, chan_size):
            remote(gram.at[0], gram.at[r], gram_s.at[r], gram_r.at[r], c_peer(r)).wait_recv()
        total = gram[0]
        for r in range(1, chan_size):
            total = total + gram[r]
        row_id = iota((MODES, 128), 0)
        both = jnp.where(iota((MODES, 128), 1) - MODES == row_id, 1.0, total)
        for i in range(MODES):
            pivot = both[i:i + 1, :] / both[i:i + 1, i:i + 1]
            both = jnp.where(row_id == i, pivot, both - both[:, i:i + 1] * pivot)

        ext[...] = jnp.zeros(ext.shape, f32)
        for r in range(1, chan_size):
            remote(proj.at[0], proj.at[r], proj_s.at[r], proj_r.at[r], c_peer(r)).wait_recv()
        full = proj[0]
        for r in range(1, chan_size):
            full = full + proj[r]
        ext[MODES:2 * MODES, :] = full
        coef[0] = jnp.dot(both, ext[...], precision=highest, preferred_element_type=f32)
        for r in range(1, NX):
            start(remote(coef.at[0], coef.at[NX - r], coef_s.at[r], coef_r.at[NX - r], x_peer(r)))
        for r in (1, 3):
            start(raw_copy(r, 1))

        b_high, b_mid, b_low = split3(basis[:, pl.ds(here, quarter)])
        b_stack = jnp.concatenate(
            [b_high, b_mid, b_high, b_mid, b_low, b_high, jnp.zeros((2 * MODES, quarter), bf16)],
            axis=0,
        )

        def fit_slot(slot):
            c_high, c_mid, c_low = split3(coef[slot])
            c_stack = jnp.concatenate(
                [c_high, c_high, c_mid, c_mid, c_high, c_low, jnp.zeros((2 * MODES, rows), bf16)],
                axis=0,
            )
            ripple[slot * rows:(slot + 1) * rows, :] = lax.dot_general(
                c_stack, b_stack, (((0,), (0,)), ((), ())), preferred_element_type=f32
            )

        def clean_slot(slot, values):
            clean[slot * rows:(slot + 1) * rows, :] = (
                values.astype(f32) - ripple[slot * rows:(slot + 1) * rows, :]
            ).astype(bf16)

        fit_slot(0)
        clean_slot(0, own[:, pl.ds(here, quarter)])
        begin = gal_chan[...] - SW - (j * width + here)
        shift_hot = (iota((shifts, ngal), 0) == quarter - 1 - begin).astype(f32).astype(bf16)
        gal_row = jnp.broadcast_to(gal_pix[...], (TAPS, ngal))
        fill(
            pixel_hot, 0, gal_row >> 4,
            jnp.where((gal_row & (TAPS - 1)) == iota((TAPS, ngal), 0), 1.0, 0.0).astype(f32),
        )
        counts[...] = lax.dot_general(
            shift_hot, pixel_hot[...], (((1,), (1,)), ((), ())), preferred_element_type=f32
        ).astype(bf16)

        for r in range(1, NX):
            remote(pix.at[0], pix.at[r], pix_s.at[r], pix_r.at[r], x_peer(r)).wait_recv()
            build_band(r)
        def weigh(slot, carry):
            column = pl.multiple_of(slot * rows, rows)
            seen[:, pl.ds(column, rows)] = jnp.dot(
                counts[...], band[:, pl.ds(column, rows)], preferred_element_type=f32
            ).astype(bf16)
            return carry

        lax.fori_loop(0, NX, weigh, 0)
        for r in (1, 3, 2):
            remote(coef.at[0], coef.at[r], coef_s.at[r], coef_r.at[r], x_peer(r)).wait_recv()
            fit_slot(r)
        for r, pieces in ((2, (2,)), (1, (0, 1)), (3, (0, 1))):
            for piece in pieces:
                raw_copy(NX - r, piece).wait_recv()
            clean_slot(r, raw[r])

        def chunk_row(step):
            return pl.multiple_of(lax.rem(z + step + 2 * nz, nz) * zpix, zpix)

        def part_tile(step, tile):
            row = pl.multiple_of(chunk_row(step) + tile * TP, TP)
            return part[pl.ds(row, TP), :]

        sign = (1, -1)

        def hops(way, tile):
            return far if tile // 2 == way else far - 1

        def z_copy(way, tile, k):
            if k < hops(way, tile) - 1:
                target, recv_sem = zrecv.at[way, tile, k], z_r.at[way, tile, k]
                peer = z_peer((1, nz - 1)[way])
            else:
                target, recv_sem = edge.at[way, x], edge_r.at[way, x]
                peer = beside(way, (z * NX + tile, j))
            return remote(
                zsend.at[way, tile, k], target, z_s.at[way, tile, k], recv_sem, peer
            )

        def z_step(k, long):
            for lane in range(2):
                for way in range(2):
                    tile = 2 * (way if long else 1 - way) + lane
                    value = part_tile(sign[way] * (hops(way, tile) - k), tile)
                    if k:
                        z_copy(way, tile, k - 1).wait_recv()
                        value = value + zrecv[way, tile, k - 1].astype(f32)
                    zsend[way, tile, k] = value.astype(bf16)
                    z_copy(way, tile, k).start()

        def share(buffer, me, send_sem, recv_sem, peer_of, count):
            for r in range(1, count):
                remote(
                    buffer.at[me], buffer.at[me], send_sem.at[r], recv_sem.at[me], peer_of(r)
                ).start()

        def shared(buffer, me, send_sem, recv_sem, peer_of, count):
            for r in range(1, count):
                remote(
                    buffer.at[me], buffer.at[me], send_sem.at[r], recv_sem.at[me], peer_of(r)
                ).wait_send()

        def gather(buffer, me, send_sem, recv_sem, peer_of, count):
            for r in range(1, count):
                other = lax.rem(me + r, count)
                remote(
                    buffer.at[other], buffer.at[other], send_sem.at[r], recv_sem.at[other], peer_of(r)
                ).wait_recv()
            value = buffer[0]
            for i in range(1, count):
                value = value + buffer[i]
            return value

        def stack_part():
            wide = jnp.concatenate(
                [
                    jnp.dot(seen[...], clean[...], preferred_element_type=f32),
                    jnp.zeros((shifts, 512 - quarter), f32),
                ],
                axis=1,
            )
            folded = jnp.zeros((8, 512), f32)
            for i in range(shifts // 8):
                folded = folded + pltpu.roll(
                    wide[8 * i:8 * i + 8], (513 - quarter + 8 * i) % 512, 1
                )
            window = jnp.zeros((1, 512), f32)
            for i in range(8):
                window = window + (pltpu.roll(folded[i:i + 1], i, 1) if i else folded[i:i + 1])
            st1[x] = window[:, :2 * SW]
            share(st1, x, st1_s, st1_r, x_peer, NX)

        def z_sent(last):
            for way in range(2):
                for tile in range(NX):
                    count = hops(way, tile)
                    for k in (count - 1,) if last else range(count - 1):
                        z_copy(way, tile, k).wait_send()

        def grid_step(n, carry):
            away = lax.div(n + 1, 2)
            row = chunk_row(far + away - 2 * lax.rem(n, 2) * away)
            part[pl.ds(row, zpix), :] = jnp.dot(
                band[pl.ds(row, zpix), :], clean[...], preferred_element_type=f32
            )

            @pl.when(n == 0)
            def _():
                z_step(0, True)
                stack_part()

            @pl.when(n == 2)
            def _():
                z_step(0, False)

            return carry

        lax.fori_loop(0, nz, grid_step, 0)

        z_step(1, True)
        z_step(1, False)
        final[...] = part[pl.ds(chunk_row(0), zpix), :].astype(bf16)
        for r in range(1, NX):
            row = pl.multiple_of(lax.rem(x + r, NX) * TP, TP)
            start(remote(
                final.at[pl.ds(row, TP), :], mine.at[NX - r], mine_s.at[r], mine_r.at[NX - r],
                x_peer(r),
            ))
        st2[j] = gather(st1, x, st1_s, st1_r, x_peer, NX)
        share(st2, j, st2_s, st2_r, c_peer, chan_size)
        z_step(2, True)
        z_step(2, False)
        st3[z] = gather(st2, j, st2_s, st2_r, c_peer, chan_size)
        share(st3, z, st3_s, st3_r, z_peer, nz)
        z_step(3, True)
        for r in range(1, NX):
            remote(
                final.at[pl.ds(0, TP), :], mine.at[r], mine_s.at[r], mine_r.at[r], x_peer(r)
            ).wait_recv()
        for copy in sends:
            copy.wait_send()
        shared(st1, x, st1_s, st1_r, x_peer, NX)
        shared(st2, j, st2_s, st2_r, c_peer, chan_size)
        z_sent(False)

        for way in range(2):
            for source in range(NX):
                remote(
                    zsend.at[way, 0, 0], edge.at[way, source], z_s.at[way, 0, 0],
                    edge_r.at[way, source], beside(way, x_peer(0)),
                ).wait_recv()
        for r in range(NX):
            source = lax.rem(x + r, NX)
            if r:
                value = mine[r].astype(f32)
            else:
                value = part[pl.ds(pl.multiple_of(chunk_row(0) + x * TP, TP), TP), :]
            value = value + edge[0, source].astype(f32) + edge[1, source].astype(f32)
            column = pl.multiple_of(source * quarter, quarter)
            sky[:, pl.ds(column, quarter)] = value.astype(bf16)
        stacked[...] = gather(st3, z, st3_s, st3_r, z_peer, nz) / ngal
        z_sent(True)
        shared(st3, z, st3_s, st3_r, z_peer, nz)

    dma = pltpu.SemaphoreType.DMA
    scratch = [
        pltpu.VMEM((rows, width), bf16),
        pltpu.VMEM((MODES, width), f32),
        pltpu.VMEM((NX, 1, rows), jnp.int32),
        pltpu.VMEM((NX, rows, quarter), bf16),
        pltpu.VMEM((chan_size, MODES, 128), f32),
        pltpu.VMEM((chan_size, MODES, rows), f32),
        pltpu.VMEM((128, rows), f32),
        pltpu.VMEM((NX, MODES, rows), f32),
        pltpu.VMEM((npix, NX * rows), bf16),
        pltpu.VMEM((NX * rows, quarter), f32),
        pltpu.VMEM((NX * rows, quarter), bf16),
        pltpu.VMEM((npix, quarter), f32),
        pltpu.VMEM((npix, ngal), bf16),
        pltpu.VMEM((shifts, npix), bf16),
        pltpu.VMEM((shifts, NX * rows), bf16),
        pltpu.VMEM((2, NX, far, TP, quarter), bf16),
        pltpu.VMEM((2, NX, far - 1, TP, quarter), bf16),
        pltpu.VMEM((2, NX, TP, quarter), bf16),
        pltpu.VMEM((zpix, quarter), bf16),
        pltpu.VMEM((NX, TP, quarter), bf16),
        pltpu.VMEM((NX, 1, 2 * SW), f32),
        pltpu.VMEM((chan_size, 1, 2 * SW), f32),
        pltpu.VMEM((nz, 1, 2 * SW), f32),
        dma((2,)),
    ]
    for shape in ((NX,), (3, NX), (chan_size,), (chan_size,), (NX,)):
        scratch += [dma(shape), dma(shape)]
    scratch += [dma((2, NX, far)), dma((2, NX, far - 1)), dma((2, NX))]
    for shape in ((NX,), (NX,), (chan_size,), (nz,)):
        scratch += [dma(shape), dma(shape)]
    return kernel, scratch


def solution(mesh):
    tm_size, chan_size = mesh.shape["tm"], mesh.shape["chan"]

    def per_device(spectra, chan_weight, routes, offsets, taps, gal_pix, gal_chan):
        rows, width = spectra.shape
        nblocks = routes.shape[0]
        kernel, scratch = make_kernel(
            tm_size, chan_size, rows, width, nblocks, gal_pix.shape[0]
        )
        vmem = pl.BlockSpec(memory_space=pltpu.VMEM)
        sky, stacked = pl.pallas_call(
            kernel,
            out_shape=(
                jax.ShapeDtypeStruct((TP, width), bf16),
                jax.ShapeDtypeStruct((1, 2 * SW), f32),
            ),
            in_specs=[pl.BlockSpec(memory_space=pl.ANY)] * 2 + [vmem] * 6,
            out_specs=(vmem, vmem),
            scratch_shapes=scratch,
            compiler_params=pltpu.CompilerParams(
                collective_id=0, has_side_effects=True, vmem_limit_bytes=54880 * 1024
            ),
        )(
            spectra, jnp.asarray(basis_table(width * chan_size)), chan_weight[None, :],
            routes.reshape(1, nblocks), offsets[None, :], taps[None, :], gal_pix[None, :],
            gal_chan[None, :],
        )
        return sky, stacked[0]

    in_specs = (
        P("tm", "chan"), P("chan"), P("tm", None), P("tm"), P(None), P(None), P(None)
    )
    return jax.shard_map(
        per_device, mesh=mesh, in_specs=in_specs, out_specs=(P("tm", "chan"), P(None)),
        check_vma=False,
    )
```

```python
import jax
import jax.numpy as jnp
import numpy as np
from jax import lax
from jax.experimental import pallas as pl
from jax.experimental.pallas import tpu as pltpu
from jax.sharding import PartitionSpec as P

KMODES = 8
MODES = 2 * KMODES
TP = 64
MARGIN = 8
SW = 64
TAPS = 16
NX = 4

highest = lax.Precision.HIGHEST
MESH = pl.DeviceIdType.MESH
f32 = jnp.float32
bf16 = jnp.bfloat16


def basis_table(total):
    orders = np.arange(1, KMODES + 1)[:, None]
    phase = (orders * np.arange(total)[None, :] % total) * (2 * np.pi / total)
    return np.concatenate([np.cos(phase), np.sin(phase)], axis=0).astype(np.float32)


def split3(value):
    high = value.astype(bf16)
    rest = value - high.astype(f32)
    mid = rest.astype(bf16)
    low = (rest - mid.astype(f32)).astype(bf16)
    return high, mid, low


def iota(shape, dim):
    return lax.broadcasted_iota(jnp.int32, shape, dim)


def make_kernel(tm_size, chan_size, rows, width, nblocks, ngal):
    nz = tm_size // NX
    quarter = width // NX
    npix = tm_size * TP
    zpix = NX * TP
    block_rows = rows // nblocks
    shifts = quarter + 2 * SW
    far = nz // 2

    def kernel(
        spec, basis_in, weight, routes, offsets, taps, gal_pix, gal_chan,
        sky, stacked,
        own, basis, pix, raw, gram, proj, ext, coef, band, ripple, clean, part, pixel_hot, counts,
        zsend, zrecv, edge, final, mine, st1, st2, st3,
        load_sem, pix_s, pix_r, raw_s, raw_r, gram_s, gram_r, proj_s, proj_r, coef_s, coef_r,
        z_s, z_r, edge_r, mine_s, mine_r, st1_s, st1_r, st2_s, st2_r, st3_s, st3_r,
    ):
        tm = lax.axis_index("tm")
        j = lax.axis_index("chan")
        z = lax.div(tm, NX)
        x = lax.rem(tm, NX)
        here = pl.multiple_of(x * quarter, quarter)

        def x_peer(r):
            return (z * NX + lax.rem(x + r, NX), j)

        def c_peer(r):
            return (tm, lax.rem(j + r, chan_size))

        def z_peer(r):
            return (lax.rem(z + r, nz) * NX + x, j)

        def beside(way, place):
            return (lax.rem(place[0] + (NX, (nz - 1) * NX)[way], tm_size), place[1])

        def remote(src, dst, send_sem, recv_sem, peer):
            return pltpu.make_async_remote_copy(
                src_ref=src, dst_ref=dst, send_sem=send_sem, recv_sem=recv_sem,
                device_id=peer, device_id_type=MESH,
            )

        sends = []

        def start(copy):
            copy.start()
            sends.append(copy)

        peers = (
            [x_peer(r) for r in range(1, NX)]
            + [c_peer(r) for r in range(1, chan_size)]
            + [z_peer(r) for r in range(1, nz)]
            + [beside(way, x_peer(r)) for way in range(2) for r in range(1, NX)]
        )
        barrier = pltpu.get_barrier_semaphore()
        for peer in peers:
            pl.semaphore_signal(barrier, inc=1, device_id=peer, device_id_type=MESH)
        basis_here = basis_in.at[:, pl.ds(pl.multiple_of(j * width, width), width)]
        loads = [
            pltpu.make_async_copy(source, target, load_sem.at[i])
            for i, (source, target) in enumerate((
                (spec, own.at[0:rows]), (basis_here, basis),
            ))
        ]
        for load in loads:
            load.start()
        inside = iota((nblocks, rows), 1) - block_rows * iota((nblocks, rows), 0)
        owner = ((inside >= 0) & (inside < block_rows)).astype(f32).astype(bf16)
        tile = jnp.dot(
            jnp.broadcast_to(routes[...], (16, nblocks)).astype(f32).astype(bf16), owner,
            preferred_element_type=f32,
        )[0:1].astype(jnp.int32)
        pix[0] = tile * TP + offsets[...] - MARGIN

        pl.semaphore_wait(barrier, len(peers))
        for r in range(1, NX):
            start(remote(pix.at[0], pix.at[NX - r], pix_s.at[r], pix_r.at[NX - r], x_peer(r)))

        late = rows // 4 * 3

        def raw_copy(r, piece):
            column = pl.multiple_of(lax.rem(x + r, NX) * quarter, quarter)
            low, high = ((0, late), (late, rows), (0, rows))[piece]
            return remote(
                spec.at[low:high, pl.ds(column, quarter)], raw.at[NX - r, low:high],
                raw_s.at[piece, r], raw_r.at[piece, NX - r], x_peer(r),
            )

        for r, piece in ((2, 2), (1, 0), (3, 0)):
            start(raw_copy(r, piece))

        loads[1].wait()
        weighted = basis[...] * weight[...]
        w_stack = jnp.concatenate(split3(weighted), axis=0)
        own[rows:, :] = jnp.concatenate(
            [*split3(basis[...]), jnp.zeros((128 - 3 * MODES, width), bf16)], axis=0
        )
        loads[0].wait()
        products = lax.dot_general(
            w_stack, own[...], (((1,), (1,)), ((), ())), preferred_element_type=f32
        )
        products = products[:MODES] + products[MODES:2 * MODES] + products[2 * MODES:]
        normal = products[:, rows:]
        normal = (
            normal + pltpu.roll(normal, 128 - MODES, 1) + pltpu.roll(normal, 128 - 2 * MODES, 1)
        )
        gram[0] = jnp.where(iota((MODES, 128), 1) < MODES, normal, 0.0)
        for r in range(1, chan_size):
            start(remote(
                gram.at[0], gram.at[chan_size - r], gram_s.at[r], gram_r.at[chan_size - r],
                c_peer(r),
            ))
        proj[0] = products[:, :rows]
        for r in range(1, chan_size):
            start(remote(
                proj.at[0], proj.at[chan_size - r], proj_s.at[r], proj_r.at[chan_size - r],
                c_peer(r),
            ))

        def fill(target, column, group, tap):
            def step(a, carry):
                row = pl.multiple_of(a * TAPS, TAPS)
                target[pl.ds(row, TAPS), column:column + tap.shape[1]] = jnp.where(
                    group == a, tap, 0.0
                ).astype(bf16)
                return carry

            lax.fori_loop(0, npix // TAPS, step, 0, unroll=4)

        def build_band(slot):
            first = pix[slot]
            group = jnp.broadcast_to(first >> 4, (TAPS, rows))
            inner = jnp.broadcast_to(first & (TAPS - 1), (TAPS, rows))
            lane = iota((TAPS, rows), 0)
            turn = (lane - inner) & (TAPS - 1)
            tap = jnp.zeros((TAPS, rows), f32)
            values = taps[...].astype(f32)
            for m in range(TAPS):
                tap = jnp.where(turn == m, values[0:1, m:m + 1], tap)
            fill(band, slot * rows, jnp.where(lane < inner, group + 1, group), tap)

        build_band(0)

        begin = gal_chan[...] - SW - (j * width + here)
        shift_hot = (iota((shifts, ngal), 0) == quarter - 1 - begin).astype(f32).astype(bf16)
        gal_row = jnp.broadcast_to(gal_pix[...], (TAPS, ngal))
        fill(
            pixel_hot, 0, gal_row >> 4,
            jnp.where((gal_row & (TAPS - 1)) == iota((TAPS, ngal), 0), 1.0, 0.0).astype(f32),
        )
        counts[...] = lax.dot_general(
            shift_hot, pixel_hot[...], (((1,), (1,)), ((), ())), preferred_element_type=f32
        ).astype(bf16)

        for r in range(1, NX):
            remote(pix.at[0], pix.at[r], pix_s.at[r], pix_r.at[r], x_peer(r)).wait_recv()
            build_band(r)

        for r in range(1, chan_size):
            remote(gram.at[0], gram.at[r], gram_s.at[r], gram_r.at[r], c_peer(r)).wait_recv()
        total = gram[0]
        for r in range(1, chan_size):
            total = total + gram[r]
        row_id = iota((MODES, 128), 0)
        both = jnp.where(iota((MODES, 128), 1) - MODES == row_id, 1.0, total)
        for i in range(MODES):
            pivot = both[i:i + 1, :] / both[i:i + 1, i:i + 1]
            both = jnp.where(row_id == i, pivot, both - both[:, i:i + 1] * pivot)

        ext[...] = jnp.zeros(ext.shape, f32)
        for r in range(1, chan_size):
            remote(proj.at[0], proj.at[r], proj_s.at[r], proj_r.at[r], c_peer(r)).wait_recv()
        full = proj[0]
        for r in range(1, chan_size):
            full = full + proj[r]
        ext[MODES:2 * MODES, :] = full
        coef[0] = jnp.dot(both, ext[...], precision=highest, preferred_element_type=f32)
        for r in range(1, NX):
            start(remote(coef.at[0], coef.at[NX - r], coef_s.at[r], coef_r.at[NX - r], x_peer(r)))

        for r in (1, 3):
            start(raw_copy(r, 1))

        b_high, b_mid, b_low = split3(basis[:, pl.ds(here, quarter)])
        b_stack = jnp.concatenate(
            [b_high, b_mid, b_high, b_mid, b_low, b_high, jnp.zeros((2 * MODES, quarter), bf16)],
            axis=0,
        )

        def fit_slot(slot):
            c_high, c_mid, c_low = split3(coef[slot])
            c_stack = jnp.concatenate(
                [c_high, c_high, c_mid, c_mid, c_high, c_low, jnp.zeros((2 * MODES, rows), bf16)],
                axis=0,
            )
            ripple[slot * rows:(slot + 1) * rows, :] = lax.dot_general(
                c_stack, b_stack, (((0,), (0,)), ((), ())), preferred_element_type=f32
            )

        def clean_slot(slot, values):
            clean[slot * rows:(slot + 1) * rows, :] = (
                values.astype(f32) - ripple[slot * rows:(slot + 1) * rows, :]
            ).astype(bf16)

        fit_slot(0)
        clean_slot(0, own[0:rows, pl.ds(here, quarter)])

        for r in (1, 3, 2):
            remote(coef.at[0], coef.at[r], coef_s.at[r], coef_r.at[r], x_peer(r)).wait_recv()
            fit_slot(r)
        for r, pieces in ((2, (2,)), (1, (0, 1)), (3, (0, 1))):
            for piece in pieces:
                raw_copy(NX - r, piece).wait_recv()
            clean_slot(r, raw[r])

        def chunk_row(step):
            return pl.multiple_of(lax.rem(z + step + 2 * nz, nz) * zpix, zpix)

        def part_tile(step, tile):
            row = pl.multiple_of(chunk_row(step) + tile * TP, TP)
            return part[pl.ds(row, TP), :]

        sign = (1, -1)

        def hops(way, tile):
            return far if tile // 2 == way else far - 1

        def z_copy(way, tile, k):
            if k < hops(way, tile) - 1:
                target, recv_sem = zrecv.at[way, tile, k], z_r.at[way, tile, k]
                peer = z_peer((1, nz - 1)[way])
            else:
                target, recv_sem = edge.at[way, x], edge_r.at[way, x]
                peer = beside(way, (z * NX + tile, j))
            return remote(
                zsend.at[way, tile, k], target, z_s.at[way, tile, k], recv_sem, peer
            )

        def z_step(k, long):
            for lane in range(2):
                for way in range(2):
                    tile = 2 * (way if long else 1 - way) + lane
                    value = part_tile(sign[way] * (hops(way, tile) - k), tile)
                    if k:
                        z_copy(way, tile, k - 1).wait_recv()
                        value = value + zrecv[way, tile, k - 1].astype(f32)
                    zsend[way, tile, k] = value.astype(bf16)
                    z_copy(way, tile, k).start()

        def z_sent(last):
            for way in range(2):
                for tile in range(NX):
                    count = hops(way, tile)
                    for k in (count - 1,) if last else range(count - 1):
                        z_copy(way, tile, k).wait_send()

        def grid_step(n, carry):
            away = lax.div(n + 1, 2)
            row = chunk_row(far + away - 2 * lax.rem(n, 2) * away)
            part[pl.ds(row, zpix), :] = jnp.dot(
                band[pl.ds(row, zpix), :], clean[...], preferred_element_type=f32
            )

            @pl.when(n == 0)
            def _():
                z_step(0, True)

            @pl.when(n == 2)
            def _():
                z_step(0, False)

            return carry

        def share(buffer, me, send_sem, recv_sem, peer_of, count):
            for r in range(1, count):
                start(remote(buffer.at[me], buffer.at[me], send_sem.at[r], recv_sem.at[me], peer_of(r)))

        def gather(buffer, me, send_sem, recv_sem, peer_of, count):
            for r in range(1, count):
                other = lax.rem(me + r, count)
                remote(
                    buffer.at[other], buffer.at[other], send_sem.at[r], recv_sem.at[other], peer_of(r)
                ).wait_recv()
            value = buffer[0]
            for i in range(1, count):
                value = value + buffer[i]
            return value

        lax.fori_loop(0, nz, grid_step, 0)

        wide = jnp.concatenate(
            [
                jnp.dot(counts[...], part[...].astype(bf16), preferred_element_type=f32),
                jnp.zeros((shifts, 512 - quarter), f32),
            ],
            axis=1,
        )
        folded = jnp.zeros((8, 512), f32)
        for i in range(shifts // 8):
            folded = folded + pltpu.roll(
                wide[8 * i:8 * i + 8], (513 - quarter + 8 * i) % 512, 1
            )
        window = jnp.zeros((1, 512), f32)
        for i in range(8):
            window = window + (pltpu.roll(folded[i:i + 1], i, 1) if i else folded[i:i + 1])
        st1[x] = window[:, :2 * SW]
        share(st1, x, st1_s, st1_r, x_peer, NX)

        z_step(1, True)
        z_step(1, False)
        final[...] = part[pl.ds(chunk_row(0), zpix), :].astype(bf16)
        for r in range(1, NX):
            row = pl.multiple_of(lax.rem(x + r, NX) * TP, TP)
            start(remote(
                final.at[pl.ds(row, TP), :], mine.at[NX - r], mine_s.at[r], mine_r.at[NX - r],
                x_peer(r),
            ))
        st2[j] = gather(st1, x, st1_s, st1_r, x_peer, NX)
        share(st2, j, st2_s, st2_r, c_peer, chan_size)
        z_step(2, True)
        z_step(2, False)
        st3[z] = gather(st2, j, st2_s, st2_r, c_peer, chan_size)
        share(st3, z, st3_s, st3_r, z_peer, nz)
        z_step(3, True)
        for r in range(1, NX):
            remote(
                final.at[pl.ds(0, TP), :], mine.at[r], mine_s.at[r], mine_r.at[r], x_peer(r)
            ).wait_recv()
        for copy in sends:
            copy.wait_send()
        z_sent(False)

        for way in range(2):
            for source in range(NX):
                remote(
                    zsend.at[way, 0, 0], edge.at[way, source], z_s.at[way, 0, 0],
                    edge_r.at[way, source], beside(way, x_peer(0)),
                ).wait_recv()
        for r in range(NX):
            source = lax.rem(x + r, NX)
            if r:
                value = mine[r].astype(f32)
            else:
                value = part[pl.ds(pl.multiple_of(chunk_row(0) + x * TP, TP), TP), :]
            value = value + edge[0, source].astype(f32) + edge[1, source].astype(f32)
            column = pl.multiple_of(source * quarter, quarter)
            sky[:, pl.ds(column, quarter)] = value.astype(bf16)
        stacked[...] = gather(st3, z, st3_s, st3_r, z_peer, nz) / ngal
        z_sent(True)

    dma = pltpu.SemaphoreType.DMA
    scratch = [
        pltpu.VMEM((rows + 128, width), bf16),
        pltpu.VMEM((MODES, width), f32),
        pltpu.VMEM((NX, 1, rows), jnp.int32),
        pltpu.VMEM((NX, rows, quarter), bf16),
        pltpu.VMEM((chan_size, MODES, 128), f32),
        pltpu.VMEM((chan_size, MODES, rows), f32),
        pltpu.VMEM((128, rows), f32),
        pltpu.VMEM((NX, MODES, rows), f32),
        pltpu.VMEM((npix, NX * rows), bf16),
        pltpu.VMEM((NX * rows, quarter), f32),
        pltpu.VMEM((NX * rows, quarter), bf16),
        pltpu.VMEM((npix, quarter), f32),
        pltpu.VMEM((npix, ngal), bf16),
        pltpu.VMEM((shifts, npix), bf16),
        pltpu.VMEM((2, NX, far, TP, quarter), bf16),
        pltpu.VMEM((2, NX, far - 1, TP, quarter), bf16),
        pltpu.VMEM((2, NX, TP, quarter), bf16),
        pltpu.VMEM((zpix, quarter), bf16),
        pltpu.VMEM((NX, TP, quarter), bf16),
        pltpu.VMEM((NX, 1, 2 * SW), f32),
        pltpu.VMEM((chan_size, 1, 2 * SW), f32),
        pltpu.VMEM((nz, 1, 2 * SW), f32),
        dma((2,)),
    ]
    for shape in ((NX,), (3, NX), (chan_size,), (chan_size,), (NX,)):
        scratch += [dma(shape), dma(shape)]
    scratch += [dma((2, NX, far)), dma((2, NX, far - 1)), dma((2, NX))]
    for shape in ((NX,), (NX,), (chan_size,), (nz,)):
        scratch += [dma(shape), dma(shape)]
    return kernel, scratch


def solution(mesh):
    tm_size, chan_size = mesh.shape["tm"], mesh.shape["chan"]

    def per_device(spectra, chan_weight, routes, offsets, taps, gal_pix, gal_chan):
        rows, width = spectra.shape
        nblocks = routes.shape[0]
        kernel, scratch = make_kernel(
            tm_size, chan_size, rows, width, nblocks, gal_pix.shape[0]
        )
        vmem = pl.BlockSpec(memory_space=pltpu.VMEM)
        sky, stacked = pl.pallas_call(
            kernel,
            out_shape=(
                jax.ShapeDtypeStruct((TP, width), bf16),
                jax.ShapeDtypeStruct((1, 2 * SW), f32),
            ),
            in_specs=[pl.BlockSpec(memory_space=pl.ANY)] * 2 + [vmem] * 6,
            out_specs=(vmem, vmem),
            scratch_shapes=scratch,
            compiler_params=pltpu.CompilerParams(
                collective_id=0, has_side_effects=True, vmem_limit_bytes=54880 * 1024
            ),
        )(
            spectra, jnp.asarray(basis_table(width * chan_size)), chan_weight[None, :],
            routes.reshape(1, nblocks), offsets[None, :], taps[None, :], gal_pix[None, :],
            gal_chan[None, :],
        )
        return sky, stacked[0]

    in_specs = (
        P("tm", "chan"), P("chan"), P("tm", None), P("tm"), P(None), P(None), P(None)
    )
    return jax.shard_map(
        per_device, mesh=mesh, in_specs=in_specs, out_specs=(P("tm", "chan"), P(None)),
        check_vma=False,
    )
```

```python
import jax
import jax.numpy as jnp
import numpy as np
from jax import lax
from jax.experimental import pallas as pl
from jax.experimental.pallas import tpu as pltpu
from jax.sharding import PartitionSpec as P

KMODES = 8
MODES = 2 * KMODES
TP = 64
MARGIN = 8
SW = 64
TAPS = 16
NX = 4

highest = lax.Precision.HIGHEST
MESH = pl.DeviceIdType.MESH
f32 = jnp.float32
bf16 = jnp.bfloat16


def basis_table(total):
    orders = np.arange(1, KMODES + 1)[:, None]
    phase = (orders * np.arange(total)[None, :] % total) * (2 * np.pi / total)
    return np.concatenate([np.cos(phase), np.sin(phase)], axis=0).astype(np.float32)


def split3(value):
    high = value.astype(bf16)
    rest = value - high.astype(f32)
    mid = rest.astype(bf16)
    low = (rest - mid.astype(f32)).astype(bf16)
    return high, mid, low


def iota(shape, dim):
    return lax.broadcasted_iota(jnp.int32, shape, dim)


def make_kernel(tm_size, chan_size, rows, width, nblocks, ngal):
    nz = tm_size // NX
    quarter = width // NX
    npix = tm_size * TP
    zpix = NX * TP
    block_rows = rows // nblocks
    shifts = quarter + 2 * SW
    far = nz // 2

    def kernel(
        spec, basis_in, weight, routes, offsets, taps, gal_pix, gal_chan,
        sky, stacked,
        own, basis, pix, raw, gram, proj, coef, band, ripple, clean, part, pixel_hot, counts,
        zsend, zrecv, edge, final, mine, st1, st2, st3,
        load_sem, pix_s, pix_r, raw_s, raw_r, gram_s, gram_r, proj_s, proj_r, coef_s, coef_r,
        z_s, z_r, edge_r, mine_s, mine_r, st1_s, st1_r, st2_s, st2_r, st3_s, st3_r,
    ):
        tm = lax.axis_index("tm")
        j = lax.axis_index("chan")
        z = lax.div(tm, NX)
        x = lax.rem(tm, NX)
        here = pl.multiple_of(x * quarter, quarter)

        def x_peer(r):
            return (z * NX + lax.rem(x + r, NX), j)

        def c_peer(r):
            return (tm, lax.rem(j + r, chan_size))

        def z_peer(r):
            return (lax.rem(z + r, nz) * NX + x, j)

        def beside(way, place):
            return (lax.rem(place[0] + (NX, (nz - 1) * NX)[way], tm_size), place[1])

        def remote(src, dst, send_sem, recv_sem, peer):
            return pltpu.make_async_remote_copy(
                src_ref=src, dst_ref=dst, send_sem=send_sem, recv_sem=recv_sem,
                device_id=peer, device_id_type=MESH,
            )

        sends = []

        def start(copy):
            copy.start()
            sends.append(copy)

        peers = (
            [x_peer(r) for r in range(1, NX)]
            + [c_peer(r) for r in range(1, chan_size)]
            + [z_peer(r) for r in range(1, nz)]
            + [beside(way, x_peer(r)) for way in range(2) for r in range(1, NX)]
        )
        barrier = pltpu.get_barrier_semaphore()
        for peer in peers:
            pl.semaphore_signal(barrier, inc=1, device_id=peer, device_id_type=MESH)
        basis_here = basis_in.at[:, pl.ds(pl.multiple_of(j * width, width), width)]
        loads = [
            pltpu.make_async_copy(source, target, load_sem.at[i])
            for i, (source, target) in enumerate((
                (spec, own.at[0:rows]), (basis_here, basis),
            ))
        ]
        for load in loads:
            load.start()
        inside = iota((nblocks, rows), 1) - block_rows * iota((nblocks, rows), 0)
        owner = ((inside >= 0) & (inside < block_rows)).astype(f32).astype(bf16)
        tile = jnp.dot(
            jnp.broadcast_to(routes[...], (16, nblocks)).astype(f32).astype(bf16), owner,
            preferred_element_type=f32,
        )[0:1].astype(jnp.int32)
        pix[0] = tile * TP + offsets[...] - MARGIN

        pl.semaphore_wait(barrier, len(peers))
        for r in range(1, NX):
            start(remote(pix.at[0], pix.at[NX - r], pix_s.at[r], pix_r.at[NX - r], x_peer(r)))

        late = rows // 4 * 3

        def raw_copy(r, piece):
            column = pl.multiple_of(lax.rem(x + r, NX) * quarter, quarter)
            low, high = ((0, late), (late, rows), (0, rows))[piece]
            return remote(
                spec.at[low:high, pl.ds(column, quarter)], raw.at[NX - r, low:high],
                raw_s.at[piece, r], raw_r.at[piece, NX - r], x_peer(r),
            )

        for r, piece in ((2, 2), (1, 0), (3, 0)):
            start(raw_copy(r, piece))

        loads[1].wait()
        weighted = basis[...] * weight[...]
        w_stack = jnp.concatenate(split3(weighted), axis=0)
        own[rows:, :] = jnp.concatenate(
            [*split3(basis[...]), jnp.zeros((128 - 3 * MODES, width), bf16)], axis=0
        )
        loads[0].wait()
        products = lax.dot_general(
            w_stack, own[...], (((1,), (1,)), ((), ())), preferred_element_type=f32
        )
        products = products[:MODES] + products[MODES:2 * MODES] + products[2 * MODES:]
        normal = products[:, rows:]
        normal = (
            normal + pltpu.roll(normal, 128 - MODES, 1) + pltpu.roll(normal, 128 - 2 * MODES, 1)
        )
        gram[0] = jnp.where(iota((MODES, 128), 1) < MODES, normal, 0.0)
        for r in range(1, chan_size):
            start(remote(
                gram.at[0], gram.at[chan_size - r], gram_s.at[r], gram_r.at[chan_size - r],
                c_peer(r),
            ))
        proj[0] = products[:, :rows]
        for r in range(1, chan_size):
            start(remote(
                proj.at[0], proj.at[chan_size - r], proj_s.at[r], proj_r.at[chan_size - r],
                c_peer(r),
            ))

        def fill(target, column, group, tap):
            def step(a, carry):
                row = pl.multiple_of(a * TAPS, TAPS)
                target[pl.ds(row, TAPS), column:column + tap.shape[1]] = jnp.where(
                    group == a, tap, 0.0
                ).astype(bf16)
                return carry

            lax.fori_loop(0, npix // TAPS, step, 0, unroll=8)

        def build_band(slot):
            first = pix[slot]
            group = jnp.broadcast_to(first >> 4, (TAPS, rows))
            inner = jnp.broadcast_to(first & (TAPS - 1), (TAPS, rows))
            lane = iota((TAPS, rows), 0)
            turn = (lane - inner) & (TAPS - 1)
            tap = jnp.zeros((TAPS, rows), f32)
            values = taps[...].astype(f32)
            for m in range(TAPS):
                tap = jnp.where(turn == m, values[0:1, m:m + 1], tap)
            fill(band, slot * rows, jnp.where(lane < inner, group + 1, group), tap)

        build_band(0)

        begin = gal_chan[...] - SW - (j * width + here)
        shift_hot = (iota((shifts, ngal), 0) == quarter - 1 - begin).astype(f32).astype(bf16)
        gal_column = jnp.broadcast_to(gal_pix[...].astype(f32), (128, ngal)).T.astype(jnp.int32)
        for i in range(npix // 128):
            pixel_hot[:, 128 * i:128 * (i + 1)] = jnp.where(
                gal_column - 128 * i == iota((ngal, 128), 1), 1.0, 0.0
            ).astype(bf16)
        counts[...] = jnp.dot(
            shift_hot, pixel_hot[...], preferred_element_type=f32
        ).astype(bf16)

        for r in range(1, NX):
            remote(pix.at[0], pix.at[r], pix_s.at[r], pix_r.at[r], x_peer(r)).wait_recv()
            build_band(r)

        for r in range(1, chan_size):
            remote(gram.at[0], gram.at[r], gram_s.at[r], gram_r.at[r], c_peer(r)).wait_recv()
        total = gram[0]
        for r in range(1, chan_size):
            total = total + gram[r]
        row_id = iota((MODES, 128), 0)
        both = jnp.where(iota((MODES, 128), 1) - MODES == row_id, 1.0, total)
        for i in range(MODES):
            pivot = both[i:i + 1, :] / both[i:i + 1, i:i + 1]
            both = jnp.where(row_id == i, pivot, both - both[:, i:i + 1] * pivot)

        for r in range(1, chan_size):
            remote(proj.at[0], proj.at[r], proj_s.at[r], proj_r.at[r], c_peer(r)).wait_recv()
        full = proj[0]
        for r in range(1, chan_size):
            full = full + proj[r]
        solved = both[:, MODES:MODES + 1] * full[0:1, :]
        for i in range(1, MODES):
            solved = solved + both[:, MODES + i:MODES + i + 1] * full[i:i + 1, :]
        coef[0] = solved
        for r in range(1, NX):
            start(remote(coef.at[0], coef.at[NX - r], coef_s.at[r], coef_r.at[NX - r], x_peer(r)))

        for r in (1, 3):
            start(raw_copy(r, 1))

        b_high, b_mid, b_low = split3(basis[:, pl.ds(here, quarter)])
        b_stack = jnp.concatenate(
            [b_high, b_mid, b_high, b_mid, b_low, b_high, jnp.zeros((2 * MODES, quarter), bf16)],
            axis=0,
        )

        def fit_slot(slot):
            c_high, c_mid, c_low = split3(coef[slot])
            c_stack = jnp.concatenate(
                [c_high, c_high, c_mid, c_mid, c_high, c_low, jnp.zeros((2 * MODES, rows), bf16)],
                axis=0,
            )
            ripple[slot * rows:(slot + 1) * rows, :] = lax.dot_general(
                c_stack, b_stack, (((0,), (0,)), ((), ())), preferred_element_type=f32
            )

        def clean_slot(slot, values):
            clean[slot * rows:(slot + 1) * rows, :] = (
                values.astype(f32) - ripple[slot * rows:(slot + 1) * rows, :]
            ).astype(bf16)

        fit_slot(0)
        clean_slot(0, own[0:rows, pl.ds(here, quarter)])

        for r in (1, 3, 2):
            remote(coef.at[0], coef.at[r], coef_s.at[r], coef_r.at[r], x_peer(r)).wait_recv()
            fit_slot(r)
        for r, pieces in ((2, (2,)), (1, (0, 1)), (3, (0, 1))):
            for piece in pieces:
                raw_copy(NX - r, piece).wait_recv()
            clean_slot(r, raw[r])

        def chunk_row(step):
            return pl.multiple_of(lax.rem(z + step + 2 * nz, nz) * zpix, zpix)

        def part_tile(step, tile):
            row = pl.multiple_of(chunk_row(step) + tile * TP, TP)
            return part[pl.ds(row, TP), :]

        sign = (1, -1)

        def hops(way, tile):
            return far if tile // 2 == way else far - 1

        def z_copy(way, tile, k):
            if k < hops(way, tile) - 1:
                target, recv_sem = zrecv.at[way, tile, k], z_r.at[way, tile, k]
                peer = z_peer((1, nz - 1)[way])
            else:
                target, recv_sem = edge.at[way, x], edge_r.at[way, x]
                peer = beside(way, (z * NX + tile, j))
            return remote(
                zsend.at[way, tile, k], target, z_s.at[way, tile, k], recv_sem, peer
            )

        def z_step(k, long):
            for lane in range(2):
                for way in range(2):
                    tile = 2 * (way if long else 1 - way) + lane
                    value = part_tile(sign[way] * (hops(way, tile) - k), tile)
                    if k:
                        z_copy(way, tile, k - 1).wait_recv()
                        value = value + zrecv[way, tile, k - 1].astype(f32)
                    zsend[way, tile, k] = value.astype(bf16)
                    z_copy(way, tile, k).start()

        def z_sent(last):
            for way in range(2):
                for tile in range(NX):
                    count = hops(way, tile)
                    for k in (count - 1,) if last else range(count - 1):
                        z_copy(way, tile, k).wait_send()

        def grid_step(n, carry):
            away = lax.div(n + 1, 2)
            row = chunk_row(far + away - 2 * lax.rem(n, 2) * away)
            part[pl.ds(row, zpix), :] = jnp.dot(
                band[pl.ds(row, zpix), :], clean[...], preferred_element_type=f32
            )

            @pl.when(n == 0)
            def _():
                z_step(0, True)

            @pl.when(n == 2)
            def _():
                z_step(0, False)

            return carry

        def share(buffer, me, send_sem, recv_sem, peer_of, count):
            for r in range(1, count):
                start(remote(buffer.at[me], buffer.at[me], send_sem.at[r], recv_sem.at[me], peer_of(r)))

        def gather(buffer, me, send_sem, recv_sem, peer_of, count):
            for r in range(1, count):
                other = lax.rem(me + r, count)
                remote(
                    buffer.at[other], buffer.at[other], send_sem.at[r], recv_sem.at[other], peer_of(r)
                ).wait_recv()
            value = buffer[0]
            for i in range(1, count):
                value = value + buffer[i]
            return value

        lax.fori_loop(0, nz, grid_step, 0)

        wide = jnp.concatenate(
            [
                jnp.dot(counts[...], part[...].astype(bf16), preferred_element_type=f32),
                jnp.zeros((shifts, 512 - quarter), f32),
            ],
            axis=1,
        )
        folded = jnp.zeros((8, 512), f32)
        for i in range(shifts // 8):
            folded = folded + pltpu.roll(
                wide[8 * i:8 * i + 8], (513 - quarter + 8 * i) % 512, 1
            )
        window = jnp.zeros((1, 512), f32)
        for i in range(8):
            window = window + (pltpu.roll(folded[i:i + 1], i, 1) if i else folded[i:i + 1])
        st1[x] = window[:, :2 * SW]
        share(st1, x, st1_s, st1_r, x_peer, NX)

        z_step(1, True)
        z_step(1, False)
        final[...] = part[pl.ds(chunk_row(0), zpix), :].astype(bf16)
        for r in range(1, NX):
            row = pl.multiple_of(lax.rem(x + r, NX) * TP, TP)
            start(remote(
                final.at[pl.ds(row, TP), :], mine.at[NX - r], mine_s.at[r], mine_r.at[NX - r],
                x_peer(r),
            ))
        st2[j] = gather(st1, x, st1_s, st1_r, x_peer, NX)
        share(st2, j, st2_s, st2_r, c_peer, chan_size)
        z_step(2, True)
        z_step(2, False)
        st3[z] = gather(st2, j, st2_s, st2_r, c_peer, chan_size)
        share(st3, z, st3_s, st3_r, z_peer, nz)
        z_step(3, True)
        for r in range(1, NX):
            remote(
                final.at[pl.ds(0, TP), :], mine.at[r], mine_s.at[r], mine_r.at[r], x_peer(r)
            ).wait_recv()
        for copy in sends:
            copy.wait_send()
        z_sent(False)

        for way in range(2):
            for source in range(NX):
                remote(
                    zsend.at[way, 0, 0], edge.at[way, source], z_s.at[way, 0, 0],
                    edge_r.at[way, source], beside(way, x_peer(0)),
                ).wait_recv()
        for r in range(NX):
            source = lax.rem(x + r, NX)
            if r:
                value = mine[r].astype(f32)
            else:
                value = part[pl.ds(pl.multiple_of(chunk_row(0) + x * TP, TP), TP), :]
            value = value + edge[0, source].astype(f32) + edge[1, source].astype(f32)
            column = pl.multiple_of(source * quarter, quarter)
            sky[:, pl.ds(column, quarter)] = value.astype(bf16)
        stacked[...] = gather(st3, z, st3_s, st3_r, z_peer, nz) / ngal
        z_sent(True)

    dma = pltpu.SemaphoreType.DMA
    scratch = [
        pltpu.VMEM((rows + 128, width), bf16),
        pltpu.VMEM((MODES, width), f32),
        pltpu.VMEM((NX, 1, rows), jnp.int32),
        pltpu.VMEM((NX, rows, quarter), bf16),
        pltpu.VMEM((chan_size, MODES, 128), f32),
        pltpu.VMEM((chan_size, MODES, rows), f32),
        pltpu.VMEM((NX, MODES, rows), f32),
        pltpu.VMEM((npix, NX * rows), bf16),
        pltpu.VMEM((NX * rows, quarter), f32),
        pltpu.VMEM((NX * rows, quarter), bf16),
        pltpu.VMEM((npix, quarter), f32),
        pltpu.VMEM((ngal, npix), bf16),
        pltpu.VMEM((shifts, npix), bf16),
        pltpu.VMEM((2, NX, far, TP, quarter), bf16),
        pltpu.VMEM((2, NX, far - 1, TP, quarter), bf16),
        pltpu.VMEM((2, NX, TP, quarter), bf16),
        pltpu.VMEM((zpix, quarter), bf16),
        pltpu.VMEM((NX, TP, quarter), bf16),
        pltpu.VMEM((NX, 1, 2 * SW), f32),
        pltpu.VMEM((chan_size, 1, 2 * SW), f32),
        pltpu.VMEM((nz, 1, 2 * SW), f32),
        dma((2,)),
    ]
    for shape in ((NX,), (3, NX), (chan_size,), (chan_size,), (NX,)):
        scratch += [dma(shape), dma(shape)]
    scratch += [dma((2, NX, far)), dma((2, NX, far - 1)), dma((2, NX))]
    for shape in ((NX,), (NX,), (chan_size,), (nz,)):
        scratch += [dma(shape), dma(shape)]
    return kernel, scratch


def solution(mesh):
    tm_size, chan_size = mesh.shape["tm"], mesh.shape["chan"]

    def per_device(spectra, chan_weight, routes, offsets, taps, gal_pix, gal_chan):
        rows, width = spectra.shape
        nblocks = routes.shape[0]
        kernel, scratch = make_kernel(
            tm_size, chan_size, rows, width, nblocks, gal_pix.shape[0]
        )
        vmem = pl.BlockSpec(memory_space=pltpu.VMEM)
        sky, stacked = pl.pallas_call(
            kernel,
            out_shape=(
                jax.ShapeDtypeStruct((TP, width), bf16),
                jax.ShapeDtypeStruct((1, 2 * SW), f32),
            ),
            in_specs=[pl.BlockSpec(memory_space=pl.ANY)] * 2 + [vmem] * 6,
            out_specs=(vmem, vmem),
            scratch_shapes=scratch,
            compiler_params=pltpu.CompilerParams(
                collective_id=0, has_side_effects=True, vmem_limit_bytes=54880 * 1024
            ),
        )(
            spectra, jnp.asarray(basis_table(width * chan_size)), chan_weight[None, :],
            routes.reshape(1, nblocks), offsets[None, :], taps[None, :], gal_pix[None, :],
            gal_chan[None, :],
        )
        return sky, stacked[0]

    in_specs = (
        P("tm", "chan"), P("chan"), P("tm", None), P("tm"), P(None), P(None), P(None)
    )
    return jax.shard_map(
        per_device, mesh=mesh, in_specs=in_specs, out_specs=(P("tm", "chan"), P(None)),
        check_vma=False,
    )
```

```python
import jax
import jax.numpy as jnp
import numpy as np
from jax import lax
from jax.experimental import pallas as pl
from jax.experimental.pallas import tpu as pltpu
from jax.sharding import PartitionSpec as P

KMODES = 8
MODES = 2 * KMODES
TP = 64
MARGIN = 8
SW = 64
TAPS = 16
NX = 4

highest = lax.Precision.HIGHEST
MESH = pl.DeviceIdType.MESH
f32 = jnp.float32
bf16 = jnp.bfloat16


def basis_table(total):
    orders = np.arange(1, KMODES + 1)[:, None]
    phase = (orders * np.arange(total)[None, :] % total) * (2 * np.pi / total)
    return np.concatenate([np.cos(phase), np.sin(phase)], axis=0).astype(np.float32)


def split3(value):
    high = value.astype(bf16)
    rest = value - high.astype(f32)
    mid = rest.astype(bf16)
    low = (rest - mid.astype(f32)).astype(bf16)
    return high, mid, low


def iota(shape, dim):
    return lax.broadcasted_iota(jnp.int32, shape, dim)


def make_kernel(tm_size, chan_size, rows, width, nblocks, ngal):
    nz = tm_size // NX
    quarter = width // NX
    npix = tm_size * TP
    zpix = NX * TP
    block_rows = rows // nblocks
    shifts = quarter + 2 * SW
    far = nz // 2

    def kernel(
        spec, basis_in, weight, routes, offsets, taps, gal_pix, gal_chan,
        sky, stacked,
        own, basis, pix, raw, gram, proj, coef, band, ripple, clean, part, pixel_hot, counts,
        zsend, zrecv, edge, final, mine, st1, st2, st3,
        load_sem, pix_s, pix_r, raw_s, raw_r, gram_s, gram_r, proj_s, proj_r, coef_s, coef_r,
        z_s, z_r, edge_r, mine_s, mine_r, st1_s, st1_r, st2_s, st2_r, st3_s, st3_r,
    ):
        tm = lax.axis_index("tm")
        j = lax.axis_index("chan")
        z = lax.div(tm, NX)
        x = lax.rem(tm, NX)
        here = pl.multiple_of(x * quarter, quarter)

        def x_peer(r):
            return (z * NX + lax.rem(x + r, NX), j)

        def c_peer(r):
            return (tm, lax.rem(j + r, chan_size))

        def z_peer(r):
            return (lax.rem(z + r, nz) * NX + x, j)

        def beside(way, place, away):
            return (lax.rem(place[0] + (away, nz - away)[way] * NX, tm_size), place[1])

        def remote(src, dst, send_sem, recv_sem, peer):
            return pltpu.make_async_remote_copy(
                src_ref=src, dst_ref=dst, send_sem=send_sem, recv_sem=recv_sem,
                device_id=peer, device_id_type=MESH,
            )

        sends = []

        def start(copy):
            copy.start()
            sends.append(copy)

        peers = (
            [x_peer(r) for r in range(1, NX)]
            + [c_peer(r) for r in range(1, chan_size)]
            + [z_peer(r) for r in range(1, nz)]
            + [beside(way, x_peer(r), 1) for way in range(2) for r in range(1, NX)]
            + [
                (lax.rem(z + nz - 2 + 4 * lax.div(x, 2), nz) * NX + lax.rem(x + r, NX), j)
                for r in range(1, NX)
            ]
        )
        barrier = pltpu.get_barrier_semaphore()
        for peer in peers:
            pl.semaphore_signal(barrier, inc=1, device_id=peer, device_id_type=MESH)
        basis_here = basis_in.at[:, pl.ds(pl.multiple_of(j * width, width), width)]
        loads = [
            pltpu.make_async_copy(source, target, load_sem.at[i])
            for i, (source, target) in enumerate((
                (spec, own.at[0:rows]), (basis_here, basis),
            ))
        ]
        for load in loads:
            load.start()
        inside = iota((nblocks, rows), 1) - block_rows * iota((nblocks, rows), 0)
        owner = ((inside >= 0) & (inside < block_rows)).astype(f32).astype(bf16)
        tile = jnp.dot(
            jnp.broadcast_to(routes[...], (16, nblocks)).astype(f32).astype(bf16), owner,
            preferred_element_type=f32,
        )[0:1].astype(jnp.int32)
        pix[0] = tile * TP + offsets[...] - MARGIN

        pl.semaphore_wait(barrier, len(peers))
        for r in range(1, NX):
            start(remote(pix.at[0], pix.at[NX - r], pix_s.at[r], pix_r.at[NX - r], x_peer(r)))

        late = rows // 4 * 3

        def raw_copy(r, piece):
            column = pl.multiple_of(lax.rem(x + r, NX) * quarter, quarter)
            low, high = ((0, late), (late, rows), (0, rows))[piece]
            return remote(
                spec.at[low:high, pl.ds(column, quarter)], raw.at[NX - r, low:high],
                raw_s.at[piece, r], raw_r.at[piece, NX - r], x_peer(r),
            )

        for r, piece in ((2, 2), (1, 0), (3, 0)):
            start(raw_copy(r, piece))

        loads[1].wait()
        weighted = basis[...] * weight[...]
        w_stack = jnp.concatenate(split3(weighted), axis=0)
        own[rows:, :] = jnp.concatenate(
            [*split3(basis[...]), jnp.zeros((128 - 3 * MODES, width), bf16)], axis=0
        )
        loads[0].wait()
        products = lax.dot_general(
            w_stack, own[...], (((1,), (1,)), ((), ())), preferred_element_type=f32
        )
        products = products[:MODES] + products[MODES:2 * MODES] + products[2 * MODES:]
        normal = products[:, rows:]
        normal = (
            normal + pltpu.roll(normal, 128 - MODES, 1) + pltpu.roll(normal, 128 - 2 * MODES, 1)
        )
        gram[0] = jnp.where(iota((MODES, 128), 1) < MODES, normal, 0.0)
        for r in range(1, chan_size):
            start(remote(
                gram.at[0], gram.at[chan_size - r], gram_s.at[r], gram_r.at[chan_size - r],
                c_peer(r),
            ))
        proj[0] = products[:, :rows]
        for r in range(1, chan_size):
            start(remote(
                proj.at[0], proj.at[chan_size - r], proj_s.at[r], proj_r.at[chan_size - r],
                c_peer(r),
            ))

        def fill(target, column, group, tap):
            def step(a, carry):
                row = pl.multiple_of(a * TAPS, TAPS)
                target[pl.ds(row, TAPS), column:column + tap.shape[1]] = jnp.where(
                    group == a, tap, 0.0
                ).astype(bf16)
                return carry

            lax.fori_loop(0, npix // TAPS, step, 0, unroll=8)

        def build_band(slot):
            first = pix[slot]
            group = jnp.broadcast_to(first >> 4, (TAPS, rows))
            inner = jnp.broadcast_to(first & (TAPS - 1), (TAPS, rows))
            lane = iota((TAPS, rows), 0)
            turn = (lane - inner) & (TAPS - 1)
            tap = jnp.zeros((TAPS, rows), f32)
            values = taps[...].astype(f32)
            for m in range(TAPS):
                tap = jnp.where(turn == m, values[0:1, m:m + 1], tap)
            fill(band, slot * rows, jnp.where(lane < inner, group + 1, group), tap)

        build_band(0)

        begin = gal_chan[...] - SW - (j * width + here)
        shift_hot = (iota((shifts, ngal), 0) == quarter - 1 - begin).astype(f32).astype(bf16)
        gal_column = jnp.broadcast_to(gal_pix[...].astype(f32), (128, ngal)).T.astype(jnp.int32)
        for i in range(npix // 128):
            pixel_hot[:, 128 * i:128 * (i + 1)] = jnp.where(
                gal_column - 128 * i == iota((ngal, 128), 1), 1.0, 0.0
            ).astype(bf16)
        counts[...] = jnp.dot(
            shift_hot, pixel_hot[...], preferred_element_type=f32
        ).astype(bf16)

        for r in range(1, NX):
            remote(pix.at[0], pix.at[r], pix_s.at[r], pix_r.at[r], x_peer(r)).wait_recv()
            build_band(r)

        for r in range(1, chan_size):
            remote(gram.at[0], gram.at[r], gram_s.at[r], gram_r.at[r], c_peer(r)).wait_recv()
        total = gram[0]
        for r in range(1, chan_size):
            total = total + gram[r]
        row_id = iota((MODES, 128), 0)
        both = jnp.where(iota((MODES, 128), 1) - MODES == row_id, 1.0, total)
        for i in range(MODES):
            pivot = both[i:i + 1, :] / both[i:i + 1, i:i + 1]
            both = jnp.where(row_id == i, pivot, both - both[:, i:i + 1] * pivot)

        for r in range(1, chan_size):
            remote(proj.at[0], proj.at[r], proj_s.at[r], proj_r.at[r], c_peer(r)).wait_recv()
        full = proj[0]
        for r in range(1, chan_size):
            full = full + proj[r]
        solved = both[:, MODES:MODES + 1] * full[0:1, :]
        for i in range(1, MODES):
            solved = solved + both[:, MODES + i:MODES + i + 1] * full[i:i + 1, :]
        coef[0] = solved
        for r in range(1, NX):
            start(remote(coef.at[0], coef.at[NX - r], coef_s.at[r], coef_r.at[NX - r], x_peer(r)))

        for r in (1, 3):
            start(raw_copy(r, 1))

        b_high, b_mid, b_low = split3(basis[:, pl.ds(here, quarter)])
        b_stack = jnp.concatenate(
            [b_high, b_mid, b_high, b_mid, b_low, b_high, jnp.zeros((2 * MODES, quarter), bf16)],
            axis=0,
        )

        def fit_slot(slot):
            c_high, c_mid, c_low = split3(coef[slot])
            c_stack = jnp.concatenate(
                [c_high, c_high, c_mid, c_mid, c_high, c_low, jnp.zeros((2 * MODES, rows), bf16)],
                axis=0,
            )
            ripple[slot * rows:(slot + 1) * rows, :] = lax.dot_general(
                c_stack, b_stack, (((0,), (0,)), ((), ())), preferred_element_type=f32
            )

        def clean_slot(slot, values):
            clean[slot * rows:(slot + 1) * rows, :] = (
                values.astype(f32) - ripple[slot * rows:(slot + 1) * rows, :]
            ).astype(bf16)

        fit_slot(0)
        clean_slot(0, own[0:rows, pl.ds(here, quarter)])

        for r in (1, 3, 2):
            remote(coef.at[0], coef.at[r], coef_s.at[r], coef_r.at[r], x_peer(r)).wait_recv()
            fit_slot(r)
        for r, pieces in ((2, (2,)), (1, (0, 1)), (3, (0, 1))):
            for piece in pieces:
                raw_copy(NX - r, piece).wait_recv()
            clean_slot(r, raw[r])

        def chunk_row(step):
            return pl.multiple_of(lax.rem(z + step + 2 * nz, nz) * zpix, zpix)

        def part_tile(step, tile):
            row = pl.multiple_of(chunk_row(step) + tile * TP, TP)
            return part[pl.ds(row, TP), :]

        sign = (1, -1)

        def distance(way, tile, k):
            long = tile // 2 == way
            return (far, far - 1, far - 2, 1)[k] if long else (far - 1, far - 2, 1)[k]

        def steps(way, tile):
            return 4 if tile // 2 == way else 3

        def z_copy(way, tile, k):
            if k < 2:
                target, recv_sem = zrecv.at[way, tile, k], z_r.at[way, tile, k]
                peer = z_peer((1, nz - 1)[way])
            else:
                slot = way if k == 2 else 2
                target, recv_sem = edge.at[slot, x], edge_r.at[slot, x]
                peer = beside(way, (z * NX + tile, j), distance(way, tile, k))
            return remote(
                zsend.at[way, tile, k], target, z_s.at[way, tile, k], recv_sem, peer
            )

        def z_step(k, long):
            for lane in range(2):
                for way in range(2):
                    tile = 2 * (way if long else 1 - way) + lane
                    value = part_tile(sign[way] * distance(way, tile, k), tile)
                    if k in (1, 2):
                        z_copy(way, tile, k - 1).wait_recv()
                        value = value + zrecv[way, tile, k - 1].astype(f32)
                    zsend[way, tile, k] = value.astype(bf16)
                    z_copy(way, tile, k).start()

        def z_sent(ks):
            for way in range(2):
                for tile in range(NX):
                    for k in ks:
                        if k < steps(way, tile):
                            z_copy(way, tile, k).wait_send()

        def grid_step(n, carry):
            away = lax.div(n + 1, 2)
            row = chunk_row(far + away - 2 * lax.rem(n, 2) * away)
            part[pl.ds(row, zpix), :] = jnp.dot(
                band[pl.ds(row, zpix), :], clean[...], preferred_element_type=f32
            )

            @pl.when(n == 0)
            def _():
                z_step(0, True)

            @pl.when(n == 2)
            def _():
                z_step(0, False)

            @pl.when(n == 6)
            def _():
                z_step(3, True)

            return carry

        def share(buffer, me, send_sem, recv_sem, peer_of, count):
            for r in range(1, count):
                start(remote(buffer.at[me], buffer.at[me], send_sem.at[r], recv_sem.at[me], peer_of(r)))

        def gather(buffer, me, send_sem, recv_sem, peer_of, count):
            for r in range(1, count):
                other = lax.rem(me + r, count)
                remote(
                    buffer.at[other], buffer.at[other], send_sem.at[r], recv_sem.at[other], peer_of(r)
                ).wait_recv()
            value = buffer[0]
            for i in range(1, count):
                value = value + buffer[i]
            return value

        lax.fori_loop(0, nz, grid_step, 0)

        wide = jnp.concatenate(
            [
                jnp.dot(counts[...], part[...].astype(bf16), preferred_element_type=f32),
                jnp.zeros((shifts, 512 - quarter), f32),
            ],
            axis=1,
        )
        folded = jnp.zeros((8, 512), f32)
        for i in range(shifts // 8):
            folded = folded + pltpu.roll(
                wide[8 * i:8 * i + 8], (513 - quarter + 8 * i) % 512, 1
            )
        window = jnp.zeros((1, 512), f32)
        for i in range(8):
            window = window + (pltpu.roll(folded[i:i + 1], i, 1) if i else folded[i:i + 1])
        st1[x] = window[:, :2 * SW]
        share(st1, x, st1_s, st1_r, x_peer, NX)

        z_step(1, True)
        z_step(1, False)
        final[...] = part[pl.ds(chunk_row(0), zpix), :].astype(bf16)
        for r in range(1, NX):
            row = pl.multiple_of(lax.rem(x + r, NX) * TP, TP)
            start(remote(
                final.at[pl.ds(row, TP), :], mine.at[NX - r], mine_s.at[r], mine_r.at[NX - r],
                x_peer(r),
            ))
        st2[j] = gather(st1, x, st1_s, st1_r, x_peer, NX)
        share(st2, j, st2_s, st2_r, c_peer, chan_size)
        z_step(2, True)
        z_step(2, False)
        st3[z] = gather(st2, j, st2_s, st2_r, c_peer, chan_size)
        share(st3, z, st3_s, st3_r, z_peer, nz)
        for r in range(1, NX):
            remote(
                final.at[pl.ds(0, TP), :], mine.at[r], mine_s.at[r], mine_r.at[r], x_peer(r)
            ).wait_recv()
        for copy in sends:
            copy.wait_send()
        z_sent((0, 1, 3))

        for slot in range(3):
            for source in range(NX):
                remote(
                    zsend.at[0, 0, 0], edge.at[slot, source], z_s.at[0, 0, 0],
                    edge_r.at[slot, source], beside(0, x_peer(0), 1),
                ).wait_recv()
        for r in range(NX):
            source = lax.rem(x + r, NX)
            if r:
                value = mine[r].astype(f32)
            else:
                value = part[pl.ds(pl.multiple_of(chunk_row(0) + x * TP, TP), TP), :]
            for slot in range(3):
                value = value + edge[slot, source].astype(f32)
            column = pl.multiple_of(source * quarter, quarter)
            sky[:, pl.ds(column, quarter)] = value.astype(bf16)
        stacked[...] = gather(st3, z, st3_s, st3_r, z_peer, nz) / ngal
        z_sent((2,))

    dma = pltpu.SemaphoreType.DMA
    scratch = [
        pltpu.VMEM((rows + 128, width), bf16),
        pltpu.VMEM((MODES, width), f32),
        pltpu.VMEM((NX, 1, rows), jnp.int32),
        pltpu.VMEM((NX, rows, quarter), bf16),
        pltpu.VMEM((chan_size, MODES, 128), f32),
        pltpu.VMEM((chan_size, MODES, rows), f32),
        pltpu.VMEM((NX, MODES, rows), f32),
        pltpu.VMEM((npix, NX * rows), bf16),
        pltpu.VMEM((NX * rows, quarter), f32),
        pltpu.VMEM((NX * rows, quarter), bf16),
        pltpu.VMEM((npix, quarter), f32),
        pltpu.VMEM((ngal, npix), bf16),
        pltpu.VMEM((shifts, npix), bf16),
        pltpu.VMEM((2, NX, far, TP, quarter), bf16),
        pltpu.VMEM((2, NX, 2, TP, quarter), bf16),
        pltpu.VMEM((3, NX, TP, quarter), bf16),
        pltpu.VMEM((zpix, quarter), bf16),
        pltpu.VMEM((NX, TP, quarter), bf16),
        pltpu.VMEM((NX, 1, 2 * SW), f32),
        pltpu.VMEM((chan_size, 1, 2 * SW), f32),
        pltpu.VMEM((nz, 1, 2 * SW), f32),
        dma((2,)),
    ]
    for shape in ((NX,), (3, NX), (chan_size,), (chan_size,), (NX,)):
        scratch += [dma(shape), dma(shape)]
    scratch += [dma((2, NX, far)), dma((2, NX, 2)), dma((3, NX))]
    for shape in ((NX,), (NX,), (chan_size,), (nz,)):
        scratch += [dma(shape), dma(shape)]
    return kernel, scratch


def solution(mesh):
    tm_size, chan_size = mesh.shape["tm"], mesh.shape["chan"]

    def per_device(spectra, chan_weight, routes, offsets, taps, gal_pix, gal_chan):
        rows, width = spectra.shape
        nblocks = routes.shape[0]
        kernel, scratch = make_kernel(
            tm_size, chan_size, rows, width, nblocks, gal_pix.shape[0]
        )
        vmem = pl.BlockSpec(memory_space=pltpu.VMEM)
        sky, stacked = pl.pallas_call(
            kernel,
            out_shape=(
                jax.ShapeDtypeStruct((TP, width), bf16),
                jax.ShapeDtypeStruct((1, 2 * SW), f32),
            ),
            in_specs=[pl.BlockSpec(memory_space=pl.ANY)] * 2 + [vmem] * 6,
            out_specs=(vmem, vmem),
            scratch_shapes=scratch,
            compiler_params=pltpu.CompilerParams(
                collective_id=0, has_side_effects=True, vmem_limit_bytes=54880 * 1024
            ),
        )(
            spectra, jnp.asarray(basis_table(width * chan_size)), chan_weight[None, :],
            routes.reshape(1, nblocks), offsets[None, :], taps[None, :], gal_pix[None, :],
            gal_chan[None, :],
        )
        return sky, stacked[0]

    in_specs = (
        P("tm", "chan"), P("chan"), P("tm", None), P("tm"), P(None), P(None), P(None)
    )
    return jax.shard_map(
        per_device, mesh=mesh, in_specs=in_specs, out_specs=(P("tm", "chan"), P(None)),
        check_vma=False,
    )
```

```python
import jax
import jax.numpy as jnp
import numpy as np
from jax import lax
from jax.experimental import pallas as pl
from jax.experimental.pallas import tpu as pltpu
from jax.sharding import PartitionSpec as P

KMODES = 8
MODES = 2 * KMODES
TP = 64
MARGIN = 8
SW = 64
TAPS = 16
NX = 4

highest = lax.Precision.HIGHEST
MESH = pl.DeviceIdType.MESH
f32 = jnp.float32
bf16 = jnp.bfloat16


def basis_table(total):
    orders = np.arange(1, KMODES + 1)[:, None]
    phase = (orders * np.arange(total)[None, :] % total) * (2 * np.pi / total)
    return np.concatenate([np.cos(phase), np.sin(phase)], axis=0).astype(np.float32)


def split3(value):
    high = value.astype(bf16)
    rest = value - high.astype(f32)
    mid = rest.astype(bf16)
    low = (rest - mid.astype(f32)).astype(bf16)
    return high, mid, low


def iota(shape, dim):
    return lax.broadcasted_iota(jnp.int32, shape, dim)


def make_kernel(tm_size, chan_size, rows, width, nblocks, ngal):
    nz = tm_size // NX
    quarter = width // NX
    npix = tm_size * TP
    zpix = NX * TP
    block_rows = rows // nblocks
    shifts = quarter + 2 * SW
    far = nz // 2

    def kernel(
        spec, basis_in, weight, routes, offsets, taps, gal_pix, gal_chan,
        sky, stacked,
        own, basis, pix, raw, gram, proj, coef, band, ripple, clean, part, rounded, pixel_hot, shift_hot,
        zsend, zrecv, edge, final, mine, st1, st2, st3,
        load_sem, pix_s, pix_r, raw_s, raw_r, gram_s, gram_r, proj_s, proj_r, coef_s, coef_r,
        z_s, z_r, edge_r, mine_s, mine_r, st1_s, st1_r, st2_s, st2_r, st3_s, st3_r,
    ):
        tm = lax.axis_index("tm")
        j = lax.axis_index("chan")
        z = lax.div(tm, NX)
        x = lax.rem(tm, NX)
        here = pl.multiple_of(x * quarter, quarter)

        def x_peer(r):
            return (z * NX + lax.rem(x + r, NX), j)

        def c_peer(r):
            return (tm, lax.rem(j + r, chan_size))

        def z_peer(r):
            return (lax.rem(z + r, nz) * NX + x, j)

        def beside(way, place):
            return (lax.rem(place[0] + (NX, (nz - 1) * NX)[way], tm_size), place[1])

        def remote(src, dst, send_sem, recv_sem, peer):
            return pltpu.make_async_remote_copy(
                src_ref=src, dst_ref=dst, send_sem=send_sem, recv_sem=recv_sem,
                device_id=peer, device_id_type=MESH,
            )

        sends = []

        def start(copy):
            copy.start()
            sends.append(copy)

        peers = (
            [x_peer(r) for r in range(1, NX)]
            + [c_peer(r) for r in range(1, chan_size)]
            + [z_peer(r) for r in range(1, nz)]
            + [beside(way, x_peer(r)) for way in range(2) for r in range(1, NX)]
        )
        barrier = pltpu.get_barrier_semaphore()
        for peer in peers:
            pl.semaphore_signal(barrier, inc=1, device_id=peer, device_id_type=MESH)
        basis_here = basis_in.at[:, pl.ds(pl.multiple_of(j * width, width), width)]
        loads = [
            pltpu.make_async_copy(source, target, load_sem.at[i])
            for i, (source, target) in enumerate((
                (spec, own.at[0:rows]), (basis_here, basis),
            ))
        ]
        for load in loads:
            load.start()
        inside = iota((nblocks, rows), 1) - block_rows * iota((nblocks, rows), 0)
        owner = ((inside >= 0) & (inside < block_rows)).astype(f32).astype(bf16)
        tile = jnp.dot(
            jnp.broadcast_to(routes[...], (16, nblocks)).astype(f32).astype(bf16), owner,
            preferred_element_type=f32,
        )[0:1].astype(jnp.int32)
        pix[0] = tile * TP + offsets[...] - MARGIN

        pl.semaphore_wait(barrier, len(peers))
        for r in range(1, NX):
            start(remote(pix.at[0], pix.at[NX - r], pix_s.at[r], pix_r.at[NX - r], x_peer(r)))

        late = rows // 4 * 3

        def raw_copy(r, piece):
            column = pl.multiple_of(lax.rem(x + r, NX) * quarter, quarter)
            low, high = ((0, late), (late, rows), (0, rows))[piece]
            return remote(
                spec.at[low:high, pl.ds(column, quarter)], raw.at[NX - r, low:high],
                raw_s.at[piece, r], raw_r.at[piece, NX - r], x_peer(r),
            )

        for r, piece in ((2, 2), (1, 0), (3, 0)):
            start(raw_copy(r, piece))

        loads[1].wait()
        weighted = basis[...] * weight[...]
        w_stack = jnp.concatenate(split3(weighted), axis=0)
        own[rows:, :] = jnp.concatenate(
            [*split3(basis[...]), jnp.zeros((128 - 3 * MODES, width), bf16)], axis=0
        )
        loads[0].wait()
        products = lax.dot_general(
            w_stack, own[...], (((1,), (1,)), ((), ())), preferred_element_type=f32
        )
        products = products[:MODES] + products[MODES:2 * MODES] + products[2 * MODES:]
        normal = products[:, rows:]
        normal = (
            normal + pltpu.roll(normal, 128 - MODES, 1) + pltpu.roll(normal, 128 - 2 * MODES, 1)
        )
        gram[0] = jnp.where(iota((MODES, 128), 1) < MODES, normal, 0.0)
        for r in range(1, chan_size):
            start(remote(
                gram.at[0], gram.at[chan_size - r], gram_s.at[r], gram_r.at[chan_size - r],
                c_peer(r),
            ))
        proj[0] = products[:, :rows]
        for r in range(1, chan_size):
            start(remote(
                proj.at[0], proj.at[chan_size - r], proj_s.at[r], proj_r.at[chan_size - r],
                c_peer(r),
            ))

        def fill(target, column, group, tap):
            def step(a, carry):
                row = pl.multiple_of(a * TAPS, TAPS)
                target[pl.ds(row, TAPS), column:column + tap.shape[1]] = jnp.where(
                    group == a, tap, 0.0
                ).astype(bf16)
                return carry

            lax.fori_loop(0, npix // TAPS, step, 0, unroll=8)

        def build_band(slot):
            first = pix[slot]
            group = jnp.broadcast_to(first >> 4, (TAPS, rows))
            inner = jnp.broadcast_to(first & (TAPS - 1), (TAPS, rows))
            lane = iota((TAPS, rows), 0)
            turn = (lane - inner) & (TAPS - 1)
            tap = jnp.zeros((TAPS, rows), f32)
            values = taps[...].astype(f32)
            for m in range(TAPS):
                tap = jnp.where(turn == m, values[0:1, m:m + 1], tap)
            fill(band, slot * rows, jnp.where(lane < inner, group + 1, group), tap)

        build_band(0)

        begin = gal_chan[...] - SW - (j * width + here)
        shift_hot[...] = (iota((shifts, ngal), 0) == quarter - 1 - begin).astype(f32).astype(bf16)
        gal_column = jnp.broadcast_to(gal_pix[...].astype(f32), (128, ngal)).T.astype(jnp.int32)
        for i in range(npix // 128):
            pixel_hot[:, 128 * i:128 * (i + 1)] = jnp.where(
                gal_column - 128 * i == iota((ngal, 128), 1), 1.0, 0.0
            ).astype(bf16)
        for r in range(1, NX):
            remote(pix.at[0], pix.at[r], pix_s.at[r], pix_r.at[r], x_peer(r)).wait_recv()
            build_band(r)

        for r in range(1, chan_size):
            remote(gram.at[0], gram.at[r], gram_s.at[r], gram_r.at[r], c_peer(r)).wait_recv()
        total = gram[0]
        for r in range(1, chan_size):
            total = total + gram[r]
        row_id = iota((MODES, 128), 0)
        both = jnp.where(iota((MODES, 128), 1) - MODES == row_id, 1.0, total)
        for i in range(MODES):
            pivot = both[i:i + 1, :] / both[i:i + 1, i:i + 1]
            both = jnp.where(row_id == i, pivot, both - both[:, i:i + 1] * pivot)

        for r in range(1, chan_size):
            remote(proj.at[0], proj.at[r], proj_s.at[r], proj_r.at[r], c_peer(r)).wait_recv()
        full = proj[0]
        for r in range(1, chan_size):
            full = full + proj[r]
        solved = both[:, MODES:MODES + 1] * full[0:1, :]
        for i in range(1, MODES):
            solved = solved + both[:, MODES + i:MODES + i + 1] * full[i:i + 1, :]
        coef[0] = solved
        for r in range(1, NX):
            start(remote(coef.at[0], coef.at[NX - r], coef_s.at[r], coef_r.at[NX - r], x_peer(r)))

        for r in (1, 3):
            start(raw_copy(r, 1))

        b_high, b_mid, b_low = split3(basis[:, pl.ds(here, quarter)])
        b_stack = jnp.concatenate(
            [b_high, b_mid, b_high, b_mid, b_low, b_high, jnp.zeros((2 * MODES, quarter), bf16)],
            axis=0,
        )

        def fit_slot(slot):
            c_high, c_mid, c_low = split3(coef[slot])
            c_stack = jnp.concatenate(
                [c_high, c_high, c_mid, c_mid, c_high, c_low, jnp.zeros((2 * MODES, rows), bf16)],
                axis=0,
            )
            ripple[slot * rows:(slot + 1) * rows, :] = lax.dot_general(
                c_stack, b_stack, (((0,), (0,)), ((), ())), preferred_element_type=f32
            )

        def clean_slot(slot, values):
            clean[slot * rows:(slot + 1) * rows, :] = (
                values.astype(f32) - ripple[slot * rows:(slot + 1) * rows, :]
            ).astype(bf16)

        fit_slot(0)
        clean_slot(0, own[0:rows, pl.ds(here, quarter)])

        for r in (1, 3, 2):
            remote(coef.at[0], coef.at[r], coef_s.at[r], coef_r.at[r], x_peer(r)).wait_recv()
            fit_slot(r)
        for r, pieces in ((2, (2,)), (1, (0, 1)), (3, (0, 1))):
            for piece in pieces:
                raw_copy(NX - r, piece).wait_recv()
            clean_slot(r, raw[r])

        def chunk_row(step):
            return pl.multiple_of(lax.rem(z + step + 2 * nz, nz) * zpix, zpix)

        def part_tile(step, tile):
            row = pl.multiple_of(chunk_row(step) + tile * TP, TP)
            return part[pl.ds(row, TP), :]

        sign = (1, -1)

        def hops(way, tile):
            return far if tile // 2 == way else far - 1

        def z_copy(way, tile, k):
            if k < hops(way, tile) - 1:
                target, recv_sem = zrecv.at[way, tile, k], z_r.at[way, tile, k]
                peer = z_peer((1, nz - 1)[way])
            else:
                target, recv_sem = edge.at[way, x], edge_r.at[way, x]
                peer = beside(way, (z * NX + tile, j))
            return remote(
                zsend.at[way, tile, k], target, z_s.at[way, tile, k], recv_sem, peer
            )

        def z_step(k, long):
            for lane in range(2):
                for way in range(2):
                    tile = 2 * (way if long else 1 - way) + lane
                    value = part_tile(sign[way] * (hops(way, tile) - k), tile)
                    if k:
                        z_copy(way, tile, k - 1).wait_recv()
                        value = value + zrecv[way, tile, k - 1].astype(f32)
                    zsend[way, tile, k] = value.astype(bf16)
                    z_copy(way, tile, k).start()

        def z_sent(last):
            for way in range(2):
                for tile in range(NX):
                    count = hops(way, tile)
                    for k in (count - 1,) if last else range(count - 1):
                        z_copy(way, tile, k).wait_send()

        def grid_step(n, carry):
            away = lax.div(n + 1, 2)
            row = chunk_row(far + away - 2 * lax.rem(n, 2) * away)
            chunk = jnp.dot(
                band[pl.ds(row, zpix), :], clean[...], preferred_element_type=f32
            )
            part[pl.ds(row, zpix), :] = chunk
            rounded[pl.ds(row, zpix), :] = chunk.astype(bf16)

            @pl.when(n == 0)
            def _():
                z_step(0, True)

            @pl.when(n == 2)
            def _():
                z_step(0, False)

            return carry

        def share(buffer, me, send_sem, recv_sem, peer_of, count):
            for r in range(1, count):
                start(remote(buffer.at[me], buffer.at[me], send_sem.at[r], recv_sem.at[me], peer_of(r)))

        def gather(buffer, me, send_sem, recv_sem, peer_of, count):
            for r in range(1, count):
                other = lax.rem(me + r, count)
                remote(
                    buffer.at[other], buffer.at[other], send_sem.at[r], recv_sem.at[other], peer_of(r)
                ).wait_recv()
            value = buffer[0]
            for i in range(1, count):
                value = value + buffer[i]
            return value

        lax.fori_loop(0, nz, grid_step, 0)

        picked = jnp.dot(
            pixel_hot[...], rounded[...], preferred_element_type=f32
        ).astype(bf16)
        wide = jnp.concatenate(
            [
                jnp.dot(shift_hot[...], picked, preferred_element_type=f32),
                jnp.zeros((shifts, 512 - quarter), f32),
            ],
            axis=1,
        )
        folded = jnp.zeros((8, 512), f32)
        for i in range(shifts // 8):
            folded = folded + pltpu.roll(
                wide[8 * i:8 * i + 8], (513 - quarter + 8 * i) % 512, 1
            )
        window = jnp.zeros((1, 512), f32)
        for i in range(8):
            window = window + (pltpu.roll(folded[i:i + 1], i, 1) if i else folded[i:i + 1])
        st1[x] = window[:, :2 * SW]
        share(st1, x, st1_s, st1_r, x_peer, NX)

        z_step(1, True)
        z_step(1, False)
        final[...] = rounded[pl.ds(chunk_row(0), zpix), :]
        for r in range(1, NX):
            row = pl.multiple_of(lax.rem(x + r, NX) * TP, TP)
            start(remote(
                final.at[pl.ds(row, TP), :], mine.at[NX - r], mine_s.at[r], mine_r.at[NX - r],
                x_peer(r),
            ))
        st2[j] = gather(st1, x, st1_s, st1_r, x_peer, NX)
        share(st2, j, st2_s, st2_r, c_peer, chan_size)
        z_step(2, True)
        z_step(2, False)
        st3[z] = gather(st2, j, st2_s, st2_r, c_peer, chan_size)
        share(st3, z, st3_s, st3_r, z_peer, nz)
        z_step(3, True)
        for r in range(1, NX):
            remote(
                final.at[pl.ds(0, TP), :], mine.at[r], mine_s.at[r], mine_r.at[r], x_peer(r)
            ).wait_recv()
        for copy in sends:
            copy.wait_send()
        z_sent(False)

        for way in range(2):
            for source in range(NX):
                remote(
                    zsend.at[way, 0, 0], edge.at[way, source], z_s.at[way, 0, 0],
                    edge_r.at[way, source], beside(way, x_peer(0)),
                ).wait_recv()
        for r in range(NX):
            source = lax.rem(x + r, NX)
            if r:
                value = mine[r].astype(f32)
            else:
                value = part[pl.ds(pl.multiple_of(chunk_row(0) + x * TP, TP), TP), :]
            value = value + edge[0, source].astype(f32) + edge[1, source].astype(f32)
            column = pl.multiple_of(source * quarter, quarter)
            sky[:, pl.ds(column, quarter)] = value.astype(bf16)
        stacked[...] = gather(st3, z, st3_s, st3_r, z_peer, nz) / ngal
        z_sent(True)

    dma = pltpu.SemaphoreType.DMA
    scratch = [
        pltpu.VMEM((rows + 128, width), bf16),
        pltpu.VMEM((MODES, width), f32),
        pltpu.VMEM((NX, 1, rows), jnp.int32),
        pltpu.VMEM((NX, rows, quarter), bf16),
        pltpu.VMEM((chan_size, MODES, 128), f32),
        pltpu.VMEM((chan_size, MODES, rows), f32),
        pltpu.VMEM((NX, MODES, rows), f32),
        pltpu.VMEM((npix, NX * rows), bf16),
        pltpu.VMEM((NX * rows, quarter), f32),
        pltpu.VMEM((NX * rows, quarter), bf16),
        pltpu.VMEM((npix, quarter), f32),
        pltpu.VMEM((npix, quarter), bf16),
        pltpu.VMEM((ngal, npix), bf16),
        pltpu.VMEM((shifts, ngal), bf16),
        pltpu.VMEM((2, NX, far, TP, quarter), bf16),
        pltpu.VMEM((2, NX, far - 1, TP, quarter), bf16),
        pltpu.VMEM((2, NX, TP, quarter), bf16),
        pltpu.VMEM((zpix, quarter), bf16),
        pltpu.VMEM((NX, TP, quarter), bf16),
        pltpu.VMEM((NX, 1, 2 * SW), f32),
        pltpu.VMEM((chan_size, 1, 2 * SW), f32),
        pltpu.VMEM((nz, 1, 2 * SW), f32),
        dma((2,)),
    ]
    for shape in ((NX,), (3, NX), (chan_size,), (chan_size,), (NX,)):
        scratch += [dma(shape), dma(shape)]
    scratch += [dma((2, NX, far)), dma((2, NX, far - 1)), dma((2, NX))]
    for shape in ((NX,), (NX,), (chan_size,), (nz,)):
        scratch += [dma(shape), dma(shape)]
    return kernel, scratch


def solution(mesh):
    tm_size, chan_size = mesh.shape["tm"], mesh.shape["chan"]

    def per_device(spectra, chan_weight, routes, offsets, taps, gal_pix, gal_chan):
        rows, width = spectra.shape
        nblocks = routes.shape[0]
        kernel, scratch = make_kernel(
            tm_size, chan_size, rows, width, nblocks, gal_pix.shape[0]
        )
        vmem = pl.BlockSpec(memory_space=pltpu.VMEM)
        sky, stacked = pl.pallas_call(
            kernel,
            out_shape=(
                jax.ShapeDtypeStruct((TP, width), bf16),
                jax.ShapeDtypeStruct((1, 2 * SW), f32),
            ),
            in_specs=[pl.BlockSpec(memory_space=pl.ANY)] * 2 + [vmem] * 6,
            out_specs=(vmem, vmem),
            scratch_shapes=scratch,
            compiler_params=pltpu.CompilerParams(
                collective_id=0, has_side_effects=True, vmem_limit_bytes=54880 * 1024
            ),
        )(
            spectra, jnp.asarray(basis_table(width * chan_size)), chan_weight[None, :],
            routes.reshape(1, nblocks), offsets[None, :], taps[None, :], gal_pix[None, :],
            gal_chan[None, :],
        )
        return sky, stacked[0]

    in_specs = (
        P("tm", "chan"), P("chan"), P("tm", None), P("tm"), P(None), P(None), P(None)
    )
    return jax.shard_map(
        per_device, mesh=mesh, in_specs=in_specs, out_specs=(P("tm", "chan"), P(None)),
        check_vma=False,
    )
```

```python
import jax
import jax.numpy as jnp
import numpy as np
from jax import lax
from jax.experimental import pallas as pl
from jax.experimental.pallas import tpu as pltpu
from jax.sharding import PartitionSpec as P

KMODES = 8
MODES = 2 * KMODES
TP = 64
MARGIN = 8
SW = 64
TAPS = 16
NX = 4

highest = lax.Precision.HIGHEST
MESH = pl.DeviceIdType.MESH
f32 = jnp.float32
bf16 = jnp.bfloat16


def basis_table(total):
    orders = np.arange(1, KMODES + 1)[:, None]
    phase = (orders * np.arange(total)[None, :] % total) * (2 * np.pi / total)
    return np.concatenate([np.cos(phase), np.sin(phase)], axis=0).astype(np.float32)


def split3(value):
    high = value.astype(bf16)
    rest = value - high.astype(f32)
    mid = rest.astype(bf16)
    low = (rest - mid.astype(f32)).astype(bf16)
    return high, mid, low


def iota(shape, dim):
    return lax.broadcasted_iota(jnp.int32, shape, dim)


def make_kernel(tm_size, chan_size, rows, width, nblocks, ngal):
    nz = tm_size // NX
    quarter = width // NX
    npix = tm_size * TP
    zpix = NX * TP
    block_rows = rows // nblocks
    shifts = quarter + 2 * SW
    far = nz // 2

    def kernel(
        spec, basis_in, weight, routes, offsets, taps, gal_pix, gal_chan,
        sky, stacked,
        own, basis, pix, raw, relay, gram, proj, coef, band, ripple, clean, part, rounded, pixel_hot, shift_hot,
        zsend, zrecv, edge, final, mine, st1, st2, st3,
        load_sem, pix_s, pix_r, raw_s, raw_r, relay_s, relay_r, next_s, next_r, gram_s, gram_r, proj_s, proj_r, coef_s, coef_r,
        z_s, z_r, edge_r, mine_s, mine_r, st1_s, st1_r, st2_s, st2_r, st3_s, st3_r,
    ):
        tm = lax.axis_index("tm")
        j = lax.axis_index("chan")
        z = lax.div(tm, NX)
        x = lax.rem(tm, NX)
        here = pl.multiple_of(x * quarter, quarter)

        def x_peer(r):
            return (z * NX + lax.rem(x + r, NX), j)

        def c_peer(r):
            return (tm, lax.rem(j + r, chan_size))

        def z_peer(r):
            return (lax.rem(z + r, nz) * NX + x, j)

        def beside(way, place):
            return (lax.rem(place[0] + (NX, (nz - 1) * NX)[way], tm_size), place[1])

        def remote(src, dst, send_sem, recv_sem, peer):
            return pltpu.make_async_remote_copy(
                src_ref=src, dst_ref=dst, send_sem=send_sem, recv_sem=recv_sem,
                device_id=peer, device_id_type=MESH,
            )

        sends = []

        def start(copy):
            copy.start()
            sends.append(copy)

        peers = (
            [x_peer(r) for r in range(1, NX)]
            + [c_peer(r) for r in range(1, chan_size)]
            + [z_peer(r) for r in range(1, nz)]
            + [beside(way, x_peer(r)) for way in range(2) for r in range(1, NX)]
        )
        barrier = pltpu.get_barrier_semaphore()
        for peer in peers:
            pl.semaphore_signal(barrier, inc=1, device_id=peer, device_id_type=MESH)
        basis_here = basis_in.at[:, pl.ds(pl.multiple_of(j * width, width), width)]
        loads = [
            pltpu.make_async_copy(source, target, load_sem.at[i])
            for i, (source, target) in enumerate((
                (spec, own.at[0:rows]), (basis_here, basis),
            ))
        ]
        for load in loads:
            load.start()
        inside = iota((nblocks, rows), 1) - block_rows * iota((nblocks, rows), 0)
        owner = ((inside >= 0) & (inside < block_rows)).astype(f32).astype(bf16)
        tile = jnp.dot(
            jnp.broadcast_to(routes[...], (16, nblocks)).astype(f32).astype(bf16), owner,
            preferred_element_type=f32,
        )[0:1].astype(jnp.int32)
        pix[0] = tile * TP + offsets[...] - MARGIN

        pl.semaphore_wait(barrier, len(peers))
        for r in range(1, NX):
            start(remote(pix.at[0], pix.at[NX - r], pix_s.at[r], pix_r.at[NX - r], x_peer(r)))

        late = rows // 4 * 3

        def raw_copy(r, piece):
            column = pl.multiple_of(lax.rem(x + r, NX) * quarter, quarter)
            low, high = ((0, late), (late, rows))[piece]
            return remote(
                spec.at[low:high, pl.ds(column, quarter)], raw.at[NX - r, low:high],
                raw_s.at[piece, r], raw_r.at[piece, NX - r], x_peer(r),
            )

        mid = rows // 2
        across = pl.multiple_of(lax.rem(x + 2, NX) * quarter, quarter)

        def relay_copy(way):
            return remote(
                spec.at[way * mid:(way + 1) * mid, pl.ds(across, quarter)], relay.at[way],
                relay_s.at[way], relay_r.at[way], x_peer((1, 3)[way]),
            )

        def next_copy(way):
            return remote(
                relay.at[way], raw.at[2, way * mid:(way + 1) * mid], next_s.at[way],
                next_r.at[way], x_peer((1, 3)[way]),
            )

        for way in range(2):
            start(relay_copy(way))
        for r in (1, 3):
            start(raw_copy(r, 0))

        loads[1].wait()
        weighted = basis[...] * weight[...]
        w_stack = jnp.concatenate(split3(weighted), axis=0)
        own[rows:, :] = jnp.concatenate(
            [*split3(basis[...]), jnp.zeros((128 - 3 * MODES, width), bf16)], axis=0
        )
        loads[0].wait()
        products = lax.dot_general(
            w_stack, own[...], (((1,), (1,)), ((), ())), preferred_element_type=f32
        )
        products = products[:MODES] + products[MODES:2 * MODES] + products[2 * MODES:]
        normal = products[:, rows:]
        normal = (
            normal + pltpu.roll(normal, 128 - MODES, 1) + pltpu.roll(normal, 128 - 2 * MODES, 1)
        )
        gram[0] = jnp.where(iota((MODES, 128), 1) < MODES, normal, 0.0)
        for r in range(1, chan_size):
            start(remote(
                gram.at[0], gram.at[chan_size - r], gram_s.at[r], gram_r.at[chan_size - r],
                c_peer(r),
            ))
        proj[0] = products[:, :rows]
        for r in range(1, chan_size):
            start(remote(
                proj.at[0], proj.at[chan_size - r], proj_s.at[r], proj_r.at[chan_size - r],
                c_peer(r),
            ))

        def fill(target, column, group, tap):
            def step(a, carry):
                row = pl.multiple_of(a * TAPS, TAPS)
                target[pl.ds(row, TAPS), column:column + tap.shape[1]] = jnp.where(
                    group == a, tap, 0.0
                ).astype(bf16)
                return carry

            lax.fori_loop(0, npix // TAPS, step, 0, unroll=8)

        def build_band(slot):
            first = pix[slot]
            group = jnp.broadcast_to(first >> 4, (TAPS, rows))
            inner = jnp.broadcast_to(first & (TAPS - 1), (TAPS, rows))
            lane = iota((TAPS, rows), 0)
            turn = (lane - inner) & (TAPS - 1)
            tap = jnp.zeros((TAPS, rows), f32)
            values = taps[...].astype(f32)
            for m in range(TAPS):
                tap = jnp.where(turn == m, values[0:1, m:m + 1], tap)
            fill(band, slot * rows, jnp.where(lane < inner, group + 1, group), tap)

        build_band(0)

        begin = gal_chan[...] - SW - (j * width + here)
        shift_hot[...] = (iota((shifts, ngal), 0) == quarter - 1 - begin).astype(f32).astype(bf16)
        gal_column = jnp.broadcast_to(gal_pix[...].astype(f32), (128, ngal)).T.astype(jnp.int32)
        for i in range(npix // 128):
            pixel_hot[:, 128 * i:128 * (i + 1)] = jnp.where(
                gal_column - 128 * i == iota((ngal, 128), 1), 1.0, 0.0
            ).astype(bf16)
        for r in range(1, NX):
            remote(pix.at[0], pix.at[r], pix_s.at[r], pix_r.at[r], x_peer(r)).wait_recv()
            build_band(r)
            if r == 1:
                for way in range(2):
                    relay_copy(way).wait_recv()
                    start(next_copy(way))

        for r in range(1, chan_size):
            remote(gram.at[0], gram.at[r], gram_s.at[r], gram_r.at[r], c_peer(r)).wait_recv()
        total = gram[0]
        for r in range(1, chan_size):
            total = total + gram[r]
        row_id = iota((MODES, 128), 0)
        both = jnp.where(iota((MODES, 128), 1) - MODES == row_id, 1.0, total)
        for i in range(MODES):
            pivot = both[i:i + 1, :] / both[i:i + 1, i:i + 1]
            both = jnp.where(row_id == i, pivot, both - both[:, i:i + 1] * pivot)

        for r in range(1, chan_size):
            remote(proj.at[0], proj.at[r], proj_s.at[r], proj_r.at[r], c_peer(r)).wait_recv()
        full = proj[0]
        for r in range(1, chan_size):
            full = full + proj[r]
        solved = both[:, MODES:MODES + 1] * full[0:1, :]
        for i in range(1, MODES):
            solved = solved + both[:, MODES + i:MODES + i + 1] * full[i:i + 1, :]
        coef[0] = solved
        for r in range(1, NX):
            start(remote(coef.at[0], coef.at[NX - r], coef_s.at[r], coef_r.at[NX - r], x_peer(r)))

        for r in (1, 3):
            start(raw_copy(r, 1))

        b_high, b_mid, b_low = split3(basis[:, pl.ds(here, quarter)])
        b_stack = jnp.concatenate(
            [b_high, b_mid, b_high, b_mid, b_low, b_high, jnp.zeros((2 * MODES, quarter), bf16)],
            axis=0,
        )

        def fit_slot(slot):
            c_high, c_mid, c_low = split3(coef[slot])
            c_stack = jnp.concatenate(
                [c_high, c_high, c_mid, c_mid, c_high, c_low, jnp.zeros((2 * MODES, rows), bf16)],
                axis=0,
            )
            ripple[slot * rows:(slot + 1) * rows, :] = lax.dot_general(
                c_stack, b_stack, (((0,), (0,)), ((), ())), preferred_element_type=f32
            )

        def clean_slot(slot, values):
            clean[slot * rows:(slot + 1) * rows, :] = (
                values.astype(f32) - ripple[slot * rows:(slot + 1) * rows, :]
            ).astype(bf16)

        fit_slot(0)
        clean_slot(0, own[0:rows, pl.ds(here, quarter)])

        for r in (1, 3, 2):
            remote(coef.at[0], coef.at[r], coef_s.at[r], coef_r.at[r], x_peer(r)).wait_recv()
            fit_slot(r)
        for way in range(2):
            next_copy(way).wait_recv()
        clean_slot(2, raw[2])
        for r in (1, 3):
            for piece in range(2):
                raw_copy(NX - r, piece).wait_recv()
            clean_slot(r, raw[r])

        def chunk_row(step):
            return pl.multiple_of(lax.rem(z + step + 2 * nz, nz) * zpix, zpix)

        def part_tile(step, tile):
            row = pl.multiple_of(chunk_row(step) + tile * TP, TP)
            return part[pl.ds(row, TP), :]

        sign = (1, -1)

        def hops(way, tile):
            return far if tile // 2 == way else far - 1

        def z_copy(way, tile, k):
            if k < hops(way, tile) - 1:
                target, recv_sem = zrecv.at[way, tile, k], z_r.at[way, tile, k]
                peer = z_peer((1, nz - 1)[way])
            else:
                target, recv_sem = edge.at[way, x], edge_r.at[way, x]
                peer = beside(way, (z * NX + tile, j))
            return remote(
                zsend.at[way, tile, k], target, z_s.at[way, tile, k], recv_sem, peer
            )

        def z_step(k, long):
            for lane in range(2):
                for way in range(2):
                    tile = 2 * (way if long else 1 - way) + lane
                    value = part_tile(sign[way] * (hops(way, tile) - k), tile)
                    if k:
                        z_copy(way, tile, k - 1).wait_recv()
                        value = value + zrecv[way, tile, k - 1].astype(f32)
                    zsend[way, tile, k] = value.astype(bf16)
                    z_copy(way, tile, k).start()

        def z_sent(last):
            for way in range(2):
                for tile in range(NX):
                    count = hops(way, tile)
                    for k in (count - 1,) if last else range(count - 1):
                        z_copy(way, tile, k).wait_send()

        def grid_step(n, carry):
            away = lax.div(n + 1, 2)
            row = chunk_row(far + away - 2 * lax.rem(n, 2) * away)
            chunk = jnp.dot(
                band[pl.ds(row, zpix), :], clean[...], preferred_element_type=f32
            )
            part[pl.ds(row, zpix), :] = chunk
            rounded[pl.ds(row, zpix), :] = chunk.astype(bf16)

            @pl.when(n == 0)
            def _():
                z_step(0, True)

            @pl.when(n == 2)
            def _():
                z_step(0, False)

            return carry

        def share(buffer, me, send_sem, recv_sem, peer_of, count):
            for r in range(1, count):
                start(remote(buffer.at[me], buffer.at[me], send_sem.at[r], recv_sem.at[me], peer_of(r)))

        def gather(buffer, me, send_sem, recv_sem, peer_of, count):
            for r in range(1, count):
                other = lax.rem(me + r, count)
                remote(
                    buffer.at[other], buffer.at[other], send_sem.at[r], recv_sem.at[other], peer_of(r)
                ).wait_recv()
            value = buffer[0]
            for i in range(1, count):
                value = value + buffer[i]
            return value

        lax.fori_loop(0, nz, grid_step, 0)

        picked = jnp.dot(
            pixel_hot[...], rounded[...], preferred_element_type=f32
        ).astype(bf16)
        wide = jnp.concatenate(
            [
                jnp.dot(shift_hot[...], picked, preferred_element_type=f32),
                jnp.zeros((shifts, 512 - quarter), f32),
            ],
            axis=1,
        )
        folded = jnp.zeros((8, 512), f32)
        for i in range(shifts // 8):
            folded = folded + pltpu.roll(
                wide[8 * i:8 * i + 8], (513 - quarter + 8 * i) % 512, 1
            )
        window = jnp.zeros((1, 512), f32)
        for i in range(8):
            window = window + (pltpu.roll(folded[i:i + 1], i, 1) if i else folded[i:i + 1])
        st1[x] = window[:, :2 * SW]
        share(st1, x, st1_s, st1_r, x_peer, NX)

        z_step(1, True)
        z_step(1, False)
        final[...] = rounded[pl.ds(chunk_row(0), zpix), :]
        for r in range(1, NX):
            row = pl.multiple_of(lax.rem(x + r, NX) * TP, TP)
            start(remote(
                final.at[pl.ds(row, TP), :], mine.at[NX - r], mine_s.at[r], mine_r.at[NX - r],
                x_peer(r),
            ))
        st2[j] = gather(st1, x, st1_s, st1_r, x_peer, NX)
        share(st2, j, st2_s, st2_r, c_peer, chan_size)
        z_step(2, True)
        z_step(2, False)
        st3[z] = gather(st2, j, st2_s, st2_r, c_peer, chan_size)
        share(st3, z, st3_s, st3_r, z_peer, nz)
        z_step(3, True)
        for r in range(1, NX):
            remote(
                final.at[pl.ds(0, TP), :], mine.at[r], mine_s.at[r], mine_r.at[r], x_peer(r)
            ).wait_recv()
        for copy in sends:
            copy.wait_send()
        z_sent(False)

        for way in range(2):
            for source in range(NX):
                remote(
                    zsend.at[way, 0, 0], edge.at[way, source], z_s.at[way, 0, 0],
                    edge_r.at[way, source], beside(way, x_peer(0)),
                ).wait_recv()
        for r in range(NX):
            source = lax.rem(x + r, NX)
            if r:
                value = mine[r].astype(f32)
            else:
                value = part[pl.ds(pl.multiple_of(chunk_row(0) + x * TP, TP), TP), :]
            value = value + edge[0, source].astype(f32) + edge[1, source].astype(f32)
            column = pl.multiple_of(source * quarter, quarter)
            sky[:, pl.ds(column, quarter)] = value.astype(bf16)
        stacked[...] = gather(st3, z, st3_s, st3_r, z_peer, nz) / ngal
        z_sent(True)

    dma = pltpu.SemaphoreType.DMA
    scratch = [
        pltpu.VMEM((rows + 128, width), bf16),
        pltpu.VMEM((MODES, width), f32),
        pltpu.VMEM((NX, 1, rows), jnp.int32),
        pltpu.VMEM((NX, rows, quarter), bf16),
        pltpu.VMEM((2, rows // 2, quarter), bf16),
        pltpu.VMEM((chan_size, MODES, 128), f32),
        pltpu.VMEM((chan_size, MODES, rows), f32),
        pltpu.VMEM((NX, MODES, rows), f32),
        pltpu.VMEM((npix, NX * rows), bf16),
        pltpu.VMEM((NX * rows, quarter), f32),
        pltpu.VMEM((NX * rows, quarter), bf16),
        pltpu.VMEM((npix, quarter), f32),
        pltpu.VMEM((npix, quarter), bf16),
        pltpu.VMEM((ngal, npix), bf16),
        pltpu.VMEM((shifts, ngal), bf16),
        pltpu.VMEM((2, NX, far, TP, quarter), bf16),
        pltpu.VMEM((2, NX, far - 1, TP, quarter), bf16),
        pltpu.VMEM((2, NX, TP, quarter), bf16),
        pltpu.VMEM((zpix, quarter), bf16),
        pltpu.VMEM((NX, TP, quarter), bf16),
        pltpu.VMEM((NX, 1, 2 * SW), f32),
        pltpu.VMEM((chan_size, 1, 2 * SW), f32),
        pltpu.VMEM((nz, 1, 2 * SW), f32),
        dma((2,)),
    ]
    for shape in ((NX,), (2, NX), (2,), (2,), (chan_size,), (chan_size,), (NX,)):
        scratch += [dma(shape), dma(shape)]
    scratch += [dma((2, NX, far)), dma((2, NX, far - 1)), dma((2, NX))]
    for shape in ((NX,), (NX,), (chan_size,), (nz,)):
        scratch += [dma(shape), dma(shape)]
    return kernel, scratch


def solution(mesh):
    tm_size, chan_size = mesh.shape["tm"], mesh.shape["chan"]

    def per_device(spectra, chan_weight, routes, offsets, taps, gal_pix, gal_chan):
        rows, width = spectra.shape
        nblocks = routes.shape[0]
        kernel, scratch = make_kernel(
            tm_size, chan_size, rows, width, nblocks, gal_pix.shape[0]
        )
        vmem = pl.BlockSpec(memory_space=pltpu.VMEM)
        sky, stacked = pl.pallas_call(
            kernel,
            out_shape=(
                jax.ShapeDtypeStruct((TP, width), bf16),
                jax.ShapeDtypeStruct((1, 2 * SW), f32),
            ),
            in_specs=[pl.BlockSpec(memory_space=pl.ANY)] * 2 + [vmem] * 6,
            out_specs=(vmem, vmem),
            scratch_shapes=scratch,
            compiler_params=pltpu.CompilerParams(
                collective_id=0, has_side_effects=True, vmem_limit_bytes=54880 * 1024
            ),
        )(
            spectra, jnp.asarray(basis_table(width * chan_size)), chan_weight[None, :],
            routes.reshape(1, nblocks), offsets[None, :], taps[None, :], gal_pix[None, :],
            gal_chan[None, :],
        )
        return sky, stacked[0]

    in_specs = (
        P("tm", "chan"), P("chan"), P("tm", None), P("tm"), P(None), P(None), P(None)
    )
    return jax.shard_map(
        per_device, mesh=mesh, in_specs=in_specs, out_specs=(P("tm", "chan"), P(None)),
        check_vma=False,
    )
```

```python
import jax
import jax.numpy as jnp
import numpy as np
from jax import lax
from jax.experimental import pallas as pl
from jax.experimental.pallas import tpu as pltpu
from jax.sharding import PartitionSpec as P

KMODES = 8
MODES = 2 * KMODES
TP = 64
MARGIN = 8
SW = 64
TAPS = 16
NX = 4

highest = lax.Precision.HIGHEST
MESH = pl.DeviceIdType.MESH
f32 = jnp.float32
bf16 = jnp.bfloat16


def basis_table(total):
    orders = np.arange(1, KMODES + 1)[:, None]
    phase = (orders * np.arange(total)[None, :] % total) * (2 * np.pi / total)
    return np.concatenate([np.cos(phase), np.sin(phase)], axis=0).astype(np.float32)


def split3(value):
    high = value.astype(bf16)
    rest = value - high.astype(f32)
    mid = rest.astype(bf16)
    low = (rest - mid.astype(f32)).astype(bf16)
    return high, mid, low


def iota(shape, dim):
    return lax.broadcasted_iota(jnp.int32, shape, dim)


def make_kernel(tm_size, chan_size, rows, width, nblocks, ngal):
    nz = tm_size // NX
    quarter = width // NX
    npix = tm_size * TP
    zpix = NX * TP
    block_rows = rows // nblocks
    shifts = quarter + 2 * SW
    far = nz // 2

    def kernel(
        spec, basis_in, weight, routes, offsets, taps, gal_pix, gal_chan,
        sky, stacked,
        own, basis, pix, raw, gram, proj, coef, band, ripple, clean, part, rounded, pixel_hot, shift_hot,
        zsend, zrecv, edge, final, mine, st1, st2, st3,
        load_sem, pix_s, pix_r, raw_s, raw_r, gram_s, gram_r, proj_s, proj_r, coef_s, coef_r,
        z_s, z_r, edge_r, mine_s, mine_r, st1_s, st1_r, st2_s, st2_r, st3_s, st3_r,
    ):
        tm = lax.axis_index("tm")
        j = lax.axis_index("chan")
        z = lax.div(tm, NX)
        x = lax.rem(tm, NX)
        here = pl.multiple_of(x * quarter, quarter)

        def x_peer(r):
            return (z * NX + lax.rem(x + r, NX), j)

        def c_peer(r):
            return (tm, lax.rem(j + r, chan_size))

        def z_peer(r):
            return (lax.rem(z + r, nz) * NX + x, j)

        def beside(way, place, away):
            return (lax.rem(place[0] + (away, nz - away)[way] * NX, tm_size), place[1])

        def remote(src, dst, send_sem, recv_sem, peer):
            return pltpu.make_async_remote_copy(
                src_ref=src, dst_ref=dst, send_sem=send_sem, recv_sem=recv_sem,
                device_id=peer, device_id_type=MESH,
            )

        sends = []

        def start(copy):
            copy.start()
            sends.append(copy)

        peers = (
            [x_peer(r) for r in range(1, NX)]
            + [c_peer(r) for r in range(1, chan_size)]
            + [z_peer(r) for r in range(1, nz)]
            + [beside(way, x_peer(r), 1) for way in range(2) for r in range(1, NX)]
            + [
                (lax.rem(z + nz - 2 + 4 * lax.div(x, 2), nz) * NX + lax.rem(x + r, NX), j)
                for r in range(1, NX)
            ]
        )
        barrier = pltpu.get_barrier_semaphore()
        for peer in peers:
            pl.semaphore_signal(barrier, inc=1, device_id=peer, device_id_type=MESH)
        basis_here = basis_in.at[:, pl.ds(pl.multiple_of(j * width, width), width)]
        loads = [
            pltpu.make_async_copy(source, target, load_sem.at[i])
            for i, (source, target) in enumerate((
                (spec, own.at[0:rows]), (basis_here, basis),
            ))
        ]
        for load in loads:
            load.start()
        inside = iota((nblocks, rows), 1) - block_rows * iota((nblocks, rows), 0)
        owner = ((inside >= 0) & (inside < block_rows)).astype(f32).astype(bf16)
        tile = jnp.dot(
            jnp.broadcast_to(routes[...], (16, nblocks)).astype(f32).astype(bf16), owner,
            preferred_element_type=f32,
        )[0:1].astype(jnp.int32)
        pix[0] = tile * TP + offsets[...] - MARGIN

        pl.semaphore_wait(barrier, len(peers))
        for r in range(1, NX):
            start(remote(pix.at[0], pix.at[NX - r], pix_s.at[r], pix_r.at[NX - r], x_peer(r)))

        late = rows // 4 * 3

        def raw_copy(r, piece):
            column = pl.multiple_of(lax.rem(x + r, NX) * quarter, quarter)
            low, high = ((0, late), (late, rows), (0, rows))[piece]
            return remote(
                spec.at[low:high, pl.ds(column, quarter)], raw.at[NX - r, low:high],
                raw_s.at[piece, r], raw_r.at[piece, NX - r], x_peer(r),
            )

        for r, piece in ((2, 2), (1, 0), (3, 0)):
            start(raw_copy(r, piece))

        loads[1].wait()
        weighted = basis[...] * weight[...]
        w_stack = jnp.concatenate(split3(weighted), axis=0)
        own[rows:, :] = jnp.concatenate(
            [*split3(basis[...]), jnp.zeros((128 - 3 * MODES, width), bf16)], axis=0
        )
        loads[0].wait()
        products = lax.dot_general(
            w_stack, own[...], (((1,), (1,)), ((), ())), preferred_element_type=f32
        )
        products = products[:MODES] + products[MODES:2 * MODES] + products[2 * MODES:]
        normal = products[:, rows:]
        normal = (
            normal + pltpu.roll(normal, 128 - MODES, 1) + pltpu.roll(normal, 128 - 2 * MODES, 1)
        )
        gram[0] = jnp.where(iota((MODES, 128), 1) < MODES, normal, 0.0)
        for r in range(1, chan_size):
            start(remote(
                gram.at[0], gram.at[chan_size - r], gram_s.at[r], gram_r.at[chan_size - r],
                c_peer(r),
            ))
        proj[0] = products[:, :rows]
        for r in range(1, chan_size):
            start(remote(
                proj.at[0], proj.at[chan_size - r], proj_s.at[r], proj_r.at[chan_size - r],
                c_peer(r),
            ))

        def fill(target, column, group, tap):
            def step(a, carry):
                row = pl.multiple_of(a * TAPS, TAPS)
                target[pl.ds(row, TAPS), column:column + tap.shape[1]] = jnp.where(
                    group == a, tap, 0.0
                ).astype(bf16)
                return carry

            lax.fori_loop(0, npix // TAPS, step, 0, unroll=8)

        def build_band(slot):
            first = pix[slot]
            group = jnp.broadcast_to(first >> 4, (TAPS, rows))
            inner = jnp.broadcast_to(first & (TAPS - 1), (TAPS, rows))
            lane = iota((TAPS, rows), 0)
            turn = (lane - inner) & (TAPS - 1)
            tap = jnp.zeros((TAPS, rows), f32)
            values = taps[...].astype(f32)
            for m in range(TAPS):
                tap = jnp.where(turn == m, values[0:1, m:m + 1], tap)
            fill(band, slot * rows, jnp.where(lane < inner, group + 1, group), tap)

        build_band(0)

        begin = gal_chan[...] - SW - (j * width + here)
        shift_hot[...] = (iota((shifts, ngal), 0) == quarter - 1 - begin).astype(f32).astype(bf16)
        gal_column = jnp.broadcast_to(gal_pix[...].astype(f32), (128, ngal)).T.astype(jnp.int32)
        for i in range(npix // 128):
            pixel_hot[:, 128 * i:128 * (i + 1)] = jnp.where(
                gal_column - 128 * i == iota((ngal, 128), 1), 1.0, 0.0
            ).astype(bf16)
        for r in range(1, NX):
            remote(pix.at[0], pix.at[r], pix_s.at[r], pix_r.at[r], x_peer(r)).wait_recv()
            build_band(r)

        for r in range(1, chan_size):
            remote(gram.at[0], gram.at[r], gram_s.at[r], gram_r.at[r], c_peer(r)).wait_recv()
        total = gram[0]
        for r in range(1, chan_size):
            total = total + gram[r]
        row_id = iota((MODES, 128), 0)
        both = jnp.where(iota((MODES, 128), 1) - MODES == row_id, 1.0, total)
        for i in range(MODES):
            pivot = both[i:i + 1, :] / both[i:i + 1, i:i + 1]
            both = jnp.where(row_id == i, pivot, both - both[:, i:i + 1] * pivot)

        for r in range(1, chan_size):
            remote(proj.at[0], proj.at[r], proj_s.at[r], proj_r.at[r], c_peer(r)).wait_recv()
        full = proj[0]
        for r in range(1, chan_size):
            full = full + proj[r]
        solved = both[:, MODES:MODES + 1] * full[0:1, :]
        for i in range(1, MODES):
            solved = solved + both[:, MODES + i:MODES + i + 1] * full[i:i + 1, :]
        coef[0] = solved
        for r in range(1, NX):
            start(remote(coef.at[0], coef.at[NX - r], coef_s.at[r], coef_r.at[NX - r], x_peer(r)))

        for r in (1, 3):
            start(raw_copy(r, 1))

        b_high, b_mid, b_low = split3(basis[:, pl.ds(here, quarter)])
        b_stack = jnp.concatenate(
            [b_high, b_mid, b_high, b_mid, b_low, b_high, jnp.zeros((2 * MODES, quarter), bf16)],
            axis=0,
        )

        def fit_slot(slot):
            c_high, c_mid, c_low = split3(coef[slot])
            c_stack = jnp.concatenate(
                [c_high, c_high, c_mid, c_mid, c_high, c_low, jnp.zeros((2 * MODES, rows), bf16)],
                axis=0,
            )
            ripple[slot * rows:(slot + 1) * rows, :] = lax.dot_general(
                c_stack, b_stack, (((0,), (0,)), ((), ())), preferred_element_type=f32
            )

        def clean_slot(slot, values):
            clean[slot * rows:(slot + 1) * rows, :] = (
                values.astype(f32) - ripple[slot * rows:(slot + 1) * rows, :]
            ).astype(bf16)

        fit_slot(0)
        clean_slot(0, own[0:rows, pl.ds(here, quarter)])

        for r in (1, 3, 2):
            remote(coef.at[0], coef.at[r], coef_s.at[r], coef_r.at[r], x_peer(r)).wait_recv()
            fit_slot(r)
        for r, pieces in ((2, (2,)), (1, (0, 1)), (3, (0, 1))):
            for piece in pieces:
                raw_copy(NX - r, piece).wait_recv()
            clean_slot(r, raw[r])

        def chunk_row(step):
            return pl.multiple_of(lax.rem(z + step + 2 * nz, nz) * zpix, zpix)

        def part_tile(step, tile):
            row = pl.multiple_of(chunk_row(step) + tile * TP, TP)
            return part[pl.ds(row, TP), :]

        sign = (1, -1)

        def distance(way, tile, k):
            long = tile // 2 == way
            return (far, far - 1, far - 2, 1)[k] if long else (far - 1, far - 2, 1)[k]

        def steps(way, tile):
            return 4 if tile // 2 == way else 3

        def z_copy(way, tile, k):
            if k < 2:
                target, recv_sem = zrecv.at[way, tile, k], z_r.at[way, tile, k]
                peer = z_peer((1, nz - 1)[way])
            else:
                slot = way if k == 2 else 2
                target, recv_sem = edge.at[slot, x], edge_r.at[slot, x]
                peer = beside(way, (z * NX + tile, j), distance(way, tile, k))
            return remote(
                zsend.at[way, tile, k], target, z_s.at[way, tile, k], recv_sem, peer
            )

        def z_step(k, long):
            for lane in range(2):
                for way in range(2):
                    tile = 2 * (way if long else 1 - way) + lane
                    value = part_tile(sign[way] * distance(way, tile, k), tile)
                    if k in (1, 2):
                        z_copy(way, tile, k - 1).wait_recv()
                        value = value + zrecv[way, tile, k - 1].astype(f32)
                    zsend[way, tile, k] = value.astype(bf16)
                    z_copy(way, tile, k).start()

        def z_sent(ks):
            for way in range(2):
                for tile in range(NX):
                    for k in ks:
                        if k < steps(way, tile):
                            z_copy(way, tile, k).wait_send()

        def grid_step(n, carry):
            away = lax.div(n + 1, 2)
            row = chunk_row(far + away - 2 * lax.rem(n, 2) * away)
            chunk = jnp.dot(
                band[pl.ds(row, zpix), :], clean[...], preferred_element_type=f32
            )
            part[pl.ds(row, zpix), :] = chunk
            rounded[pl.ds(row, zpix), :] = chunk.astype(bf16)

            @pl.when(n == 0)
            def _():
                z_step(0, True)

            @pl.when(n == 2)
            def _():
                z_step(0, False)

            @pl.when(n == 6)
            def _():
                z_step(3, True)

            return carry

        def share(buffer, me, send_sem, recv_sem, peer_of, count):
            for r in range(1, count):
                start(remote(buffer.at[me], buffer.at[me], send_sem.at[r], recv_sem.at[me], peer_of(r)))

        def gather(buffer, me, send_sem, recv_sem, peer_of, count):
            for r in range(1, count):
                other = lax.rem(me + r, count)
                remote(
                    buffer.at[other], buffer.at[other], send_sem.at[r], recv_sem.at[other], peer_of(r)
                ).wait_recv()
            value = buffer[0]
            for i in range(1, count):
                value = value + buffer[i]
            return value

        lax.fori_loop(0, nz, grid_step, 0)

        picked = jnp.dot(
            pixel_hot[...], rounded[...], preferred_element_type=f32
        ).astype(bf16)
        wide = jnp.concatenate(
            [
                jnp.dot(shift_hot[...], picked, preferred_element_type=f32),
                jnp.zeros((shifts, 512 - quarter), f32),
            ],
            axis=1,
        )
        folded = jnp.zeros((8, 512), f32)
        for i in range(shifts // 8):
            folded = folded + pltpu.roll(
                wide[8 * i:8 * i + 8], (513 - quarter + 8 * i) % 512, 1
            )
        window = jnp.zeros((1, 512), f32)
        for i in range(8):
            window = window + (pltpu.roll(folded[i:i + 1], i, 1) if i else folded[i:i + 1])
        st1[x] = window[:, :2 * SW]
        share(st1, x, st1_s, st1_r, x_peer, NX)

        z_step(1, True)
        z_step(1, False)
        final[...] = rounded[pl.ds(chunk_row(0), zpix), :]
        for r in range(1, NX):
            row = pl.multiple_of(lax.rem(x + r, NX) * TP, TP)
            start(remote(
                final.at[pl.ds(row, TP), :], mine.at[NX - r], mine_s.at[r], mine_r.at[NX - r],
                x_peer(r),
            ))
        st2[j] = gather(st1, x, st1_s, st1_r, x_peer, NX)
        share(st2, j, st2_s, st2_r, c_peer, chan_size)
        z_step(2, True)
        z_step(2, False)
        st3[z] = gather(st2, j, st2_s, st2_r, c_peer, chan_size)
        share(st3, z, st3_s, st3_r, z_peer, nz)
        for r in range(1, NX):
            remote(
                final.at[pl.ds(0, TP), :], mine.at[r], mine_s.at[r], mine_r.at[r], x_peer(r)
            ).wait_recv()
        for copy in sends:
            copy.wait_send()
        z_sent((0, 1, 3))

        for slot in range(3):
            for source in range(NX):
                remote(
                    zsend.at[0, 0, 0], edge.at[slot, source], z_s.at[0, 0, 0],
                    edge_r.at[slot, source], beside(0, x_peer(0), 1),
                ).wait_recv()
        for r in range(NX):
            source = lax.rem(x + r, NX)
            if r:
                value = mine[r].astype(f32)
            else:
                value = part[pl.ds(pl.multiple_of(chunk_row(0) + x * TP, TP), TP), :]
            for slot in range(3):
                value = value + edge[slot, source].astype(f32)
            column = pl.multiple_of(source * quarter, quarter)
            sky[:, pl.ds(column, quarter)] = value.astype(bf16)
        stacked[...] = gather(st3, z, st3_s, st3_r, z_peer, nz) / ngal
        z_sent((2,))

    dma = pltpu.SemaphoreType.DMA
    scratch = [
        pltpu.VMEM((rows + 128, width), bf16),
        pltpu.VMEM((MODES, width), f32),
        pltpu.VMEM((NX, 1, rows), jnp.int32),
        pltpu.VMEM((NX, rows, quarter), bf16),
        pltpu.VMEM((chan_size, MODES, 128), f32),
        pltpu.VMEM((chan_size, MODES, rows), f32),
        pltpu.VMEM((NX, MODES, rows), f32),
        pltpu.VMEM((npix, NX * rows), bf16),
        pltpu.VMEM((NX * rows, quarter), f32),
        pltpu.VMEM((NX * rows, quarter), bf16),
        pltpu.VMEM((npix, quarter), f32),
        pltpu.VMEM((npix, quarter), bf16),
        pltpu.VMEM((ngal, npix), bf16),
        pltpu.VMEM((shifts, ngal), bf16),
        pltpu.VMEM((2, NX, far, TP, quarter), bf16),
        pltpu.VMEM((2, NX, 2, TP, quarter), bf16),
        pltpu.VMEM((3, NX, TP, quarter), bf16),
        pltpu.VMEM((zpix, quarter), bf16),
        pltpu.VMEM((NX, TP, quarter), bf16),
        pltpu.VMEM((NX, 1, 2 * SW), f32),
        pltpu.VMEM((chan_size, 1, 2 * SW), f32),
        pltpu.VMEM((nz, 1, 2 * SW), f32),
        dma((2,)),
    ]
    for shape in ((NX,), (3, NX), (chan_size,), (chan_size,), (NX,)):
        scratch += [dma(shape), dma(shape)]
    scratch += [dma((2, NX, far)), dma((2, NX, 2)), dma((3, NX))]
    for shape in ((NX,), (NX,), (chan_size,), (nz,)):
        scratch += [dma(shape), dma(shape)]
    return kernel, scratch


def solution(mesh):
    tm_size, chan_size = mesh.shape["tm"], mesh.shape["chan"]

    def per_device(spectra, chan_weight, routes, offsets, taps, gal_pix, gal_chan):
        rows, width = spectra.shape
        nblocks = routes.shape[0]
        kernel, scratch = make_kernel(
            tm_size, chan_size, rows, width, nblocks, gal_pix.shape[0]
        )
        vmem = pl.BlockSpec(memory_space=pltpu.VMEM)
        sky, stacked = pl.pallas_call(
            kernel,
            out_shape=(
                jax.ShapeDtypeStruct((TP, width), bf16),
                jax.ShapeDtypeStruct((1, 2 * SW), f32),
            ),
            in_specs=[pl.BlockSpec(memory_space=pl.ANY)] * 2 + [vmem] * 6,
            out_specs=(vmem, vmem),
            scratch_shapes=scratch,
            compiler_params=pltpu.CompilerParams(
                collective_id=0, has_side_effects=True, vmem_limit_bytes=54880 * 1024
            ),
        )(
            spectra, jnp.asarray(basis_table(width * chan_size)), chan_weight[None, :],
            routes.reshape(1, nblocks), offsets[None, :], taps[None, :], gal_pix[None, :],
            gal_chan[None, :],
        )
        return sky, stacked[0]

    in_specs = (
        P("tm", "chan"), P("chan"), P("tm", None), P("tm"), P(None), P(None), P(None)
    )
    return jax.shard_map(
        per_device, mesh=mesh, in_specs=in_specs, out_specs=(P("tm", "chan"), P(None)),
        check_vma=False,
    )
```

```python
import jax
import jax.numpy as jnp
import numpy as np
from jax import lax
from jax.experimental import pallas as pl
from jax.experimental.pallas import tpu as pltpu
from jax.sharding import PartitionSpec as P

KMODES = 8
MODES = 2 * KMODES
TP = 64
MARGIN = 8
SW = 64
TAPS = 16
NX = 4

highest = lax.Precision.HIGHEST
MESH = pl.DeviceIdType.MESH
f32 = jnp.float32
bf16 = jnp.bfloat16


def basis_table(total):
    orders = np.arange(1, KMODES + 1)[:, None]
    phase = (orders * np.arange(total)[None, :] % total) * (2 * np.pi / total)
    return np.concatenate([np.cos(phase), np.sin(phase)], axis=0).astype(np.float32)


def split3(value):
    high = value.astype(bf16)
    rest = value - high.astype(f32)
    mid = rest.astype(bf16)
    low = (rest - mid.astype(f32)).astype(bf16)
    return high, mid, low


def iota(shape, dim):
    return lax.broadcasted_iota(jnp.int32, shape, dim)


def make_kernel(tm_size, chan_size, rows, width, nblocks, ngal):
    nz = tm_size // NX
    quarter = width // NX
    npix = tm_size * TP
    zpix = NX * TP
    block_rows = rows // nblocks
    shifts = quarter + 2 * SW
    far = nz // 2

    def kernel(
        spec, basis_in, weight, routes, offsets, taps, gal_pix, gal_chan,
        sky, stacked,
        own, basis, pix, raw, gram, proj, coef, band, ripple, clean, part, rounded, pixel_hot, shift_hot,
        zsend, zrecv, edge, final, mine, st1, st2, st3,
        load_sem, pix_s, pix_r, raw_s, raw_r, gram_s, gram_r, proj_s, proj_r, coef_s, coef_r,
        z_s, z_r, edge_s, edge_r, mine_s, mine_r, st1_s, st1_r, st2_s, st2_r, st3_s, st3_r,
    ):
        tm = lax.axis_index("tm")
        j = lax.axis_index("chan")
        z = lax.div(tm, NX)
        x = lax.rem(tm, NX)
        here = pl.multiple_of(x * quarter, quarter)

        def x_peer(r):
            return (z * NX + lax.rem(x + r, NX), j)

        def c_peer(r):
            return (tm, lax.rem(j + r, chan_size))

        def z_peer(r):
            return (lax.rem(z + r, nz) * NX + x, j)

        def beside(way, place):
            return (lax.rem(place[0] + (NX, (nz - 1) * NX)[way], tm_size), place[1])

        def remote(src, dst, send_sem, recv_sem, peer):
            return pltpu.make_async_remote_copy(
                src_ref=src, dst_ref=dst, send_sem=send_sem, recv_sem=recv_sem,
                device_id=peer, device_id_type=MESH,
            )

        sends = []

        def start(copy):
            copy.start()
            sends.append(copy)

        peers = (
            [x_peer(r) for r in range(1, NX)]
            + [c_peer(r) for r in range(1, chan_size)]
            + [z_peer(r) for r in range(1, nz)]
            + [beside(way, x_peer(r)) for way in range(2) for r in range(1, NX)]
        )
        barrier = pltpu.get_barrier_semaphore()
        for peer in peers:
            pl.semaphore_signal(barrier, inc=1, device_id=peer, device_id_type=MESH)
        basis_here = basis_in.at[:, pl.ds(pl.multiple_of(j * width, width), width)]
        loads = [
            pltpu.make_async_copy(source, target, load_sem.at[i])
            for i, (source, target) in enumerate((
                (spec, own.at[0:rows]), (basis_here, basis),
            ))
        ]
        for load in loads:
            load.start()
        inside = iota((nblocks, rows), 1) - block_rows * iota((nblocks, rows), 0)
        owner = ((inside >= 0) & (inside < block_rows)).astype(f32).astype(bf16)
        tile = jnp.dot(
            jnp.broadcast_to(routes[...], (16, nblocks)).astype(f32).astype(bf16), owner,
            preferred_element_type=f32,
        )[0:1].astype(jnp.int32)
        pix[0] = tile * TP + offsets[...] - MARGIN

        pl.semaphore_wait(barrier, len(peers))
        for r in range(1, NX):
            start(remote(pix.at[0], pix.at[NX - r], pix_s.at[r], pix_r.at[NX - r], x_peer(r)))

        late = rows // 4 * 3

        def raw_copy(r, piece):
            column = pl.multiple_of(lax.rem(x + r, NX) * quarter, quarter)
            low, high = ((0, late), (late, rows), (0, rows))[piece]
            return remote(
                spec.at[low:high, pl.ds(column, quarter)], raw.at[NX - r, low:high],
                raw_s.at[piece, r], raw_r.at[piece, NX - r], x_peer(r),
            )

        for r, piece in ((2, 2), (1, 0), (3, 0)):
            start(raw_copy(r, piece))

        loads[1].wait()
        weighted = basis[...] * weight[...]
        w_stack = jnp.concatenate(split3(weighted), axis=0)
        own[rows:, :] = jnp.concatenate(
            [*split3(basis[...]), jnp.zeros((128 - 3 * MODES, width), bf16)], axis=0
        )
        loads[0].wait()
        products = lax.dot_general(
            w_stack, own[...], (((1,), (1,)), ((), ())), preferred_element_type=f32
        )
        products = products[:MODES] + products[MODES:2 * MODES] + products[2 * MODES:]
        normal = products[:, rows:]
        normal = (
            normal + pltpu.roll(normal, 128 - MODES, 1) + pltpu.roll(normal, 128 - 2 * MODES, 1)
        )
        gram[0] = jnp.where(iota((MODES, 128), 1) < MODES, normal, 0.0)
        for r in range(1, chan_size):
            start(remote(
                gram.at[0], gram.at[chan_size - r], gram_s.at[r], gram_r.at[chan_size - r],
                c_peer(r),
            ))
        proj[0] = products[:, :rows]
        for r in range(1, chan_size):
            start(remote(
                proj.at[0], proj.at[chan_size - r], proj_s.at[r], proj_r.at[chan_size - r],
                c_peer(r),
            ))

        def fill(target, column, group, tap):
            def step(a, carry):
                row = pl.multiple_of(a * TAPS, TAPS)
                target[pl.ds(row, TAPS), column:column + tap.shape[1]] = jnp.where(
                    group == a, tap, 0.0
                ).astype(bf16)
                return carry

            lax.fori_loop(0, npix // TAPS, step, 0, unroll=8)

        def build_band(slot):
            first = pix[slot]
            group = jnp.broadcast_to(first >> 4, (TAPS, rows))
            inner = jnp.broadcast_to(first & (TAPS - 1), (TAPS, rows))
            lane = iota((TAPS, rows), 0)
            turn = (lane - inner) & (TAPS - 1)
            tap = jnp.zeros((TAPS, rows), f32)
            values = taps[...].astype(f32)
            for m in range(TAPS):
                tap = jnp.where(turn == m, values[0:1, m:m + 1], tap)
            fill(band, slot * rows, jnp.where(lane < inner, group + 1, group), tap)

        build_band(0)

        begin = gal_chan[...] - SW - (j * width + here)
        shift_hot[...] = (iota((shifts, ngal), 0) == quarter - 1 - begin).astype(f32).astype(bf16)
        gal_column = jnp.broadcast_to(gal_pix[...].astype(f32), (128, ngal)).T.astype(jnp.int32)
        for i in range(npix // 128):
            pixel_hot[:, 128 * i:128 * (i + 1)] = jnp.where(
                gal_column - 128 * i == iota((ngal, 128), 1), 1.0, 0.0
            ).astype(bf16)
        for r in range(1, NX):
            remote(pix.at[0], pix.at[r], pix_s.at[r], pix_r.at[r], x_peer(r)).wait_recv()
            build_band(r)

        for r in range(1, chan_size):
            remote(gram.at[0], gram.at[r], gram_s.at[r], gram_r.at[r], c_peer(r)).wait_recv()
        total = gram[0]
        for r in range(1, chan_size):
            total = total + gram[r]
        row_id = iota((MODES, 128), 0)
        both = jnp.where(iota((MODES, 128), 1) - MODES == row_id, 1.0, total)
        for i in range(MODES):
            pivot = both[i:i + 1, :] / both[i:i + 1, i:i + 1]
            both = jnp.where(row_id == i, pivot, both - both[:, i:i + 1] * pivot)

        for r in range(1, chan_size):
            remote(proj.at[0], proj.at[r], proj_s.at[r], proj_r.at[r], c_peer(r)).wait_recv()
        full = proj[0]
        for r in range(1, chan_size):
            full = full + proj[r]
        solved = both[:, MODES:MODES + 1] * full[0:1, :]
        for i in range(1, MODES):
            solved = solved + both[:, MODES + i:MODES + i + 1] * full[i:i + 1, :]
        coef[0] = solved
        for r in range(1, NX):
            start(remote(coef.at[0], coef.at[NX - r], coef_s.at[r], coef_r.at[NX - r], x_peer(r)))

        for r in (1, 3):
            start(raw_copy(r, 1))

        b_high, b_mid, b_low = split3(basis[:, pl.ds(here, quarter)])
        b_stack = jnp.concatenate(
            [b_high, b_mid, b_high, b_mid, b_low, b_high, jnp.zeros((2 * MODES, quarter), bf16)],
            axis=0,
        )

        def fit_slot(slot):
            c_high, c_mid, c_low = split3(coef[slot])
            c_stack = jnp.concatenate(
                [c_high, c_high, c_mid, c_mid, c_high, c_low, jnp.zeros((2 * MODES, rows), bf16)],
                axis=0,
            )
            ripple[slot * rows:(slot + 1) * rows, :] = lax.dot_general(
                c_stack, b_stack, (((0,), (0,)), ((), ())), preferred_element_type=f32
            )

        def clean_slot(slot, values):
            clean[slot * rows:(slot + 1) * rows, :] = (
                values.astype(f32) - ripple[slot * rows:(slot + 1) * rows, :]
            ).astype(bf16)

        fit_slot(0)
        clean_slot(0, own[0:rows, pl.ds(here, quarter)])

        for r in (1, 3, 2):
            remote(coef.at[0], coef.at[r], coef_s.at[r], coef_r.at[r], x_peer(r)).wait_recv()
            fit_slot(r)
        for r, pieces in ((2, (2,)), (1, (0, 1)), (3, (0, 1))):
            for piece in pieces:
                raw_copy(NX - r, piece).wait_recv()
            clean_slot(r, raw[r])

        def chunk_row(step):
            return pl.multiple_of(lax.rem(z + step + 2 * nz, nz) * zpix, zpix)

        def part_half(step, which):
            row = pl.multiple_of(chunk_row(step) + which * 2 * TP, 2 * TP)
            return part[pl.ds(row, 2 * TP), :]

        sign = (1, -1)

        def z_copies(way, long, k):
            hops = far if long else far - 1
            kind = 0 if long else 1
            source = zsend.at[way, kind, k]
            if k < hops - 1:
                return [remote(
                    source, zrecv.at[way, kind, k], z_s.at[way, kind, k], z_r.at[way, kind, k],
                    z_peer((1, nz - 1)[way]),
                )]
            first = 2 * (way if long else 1 - way)
            return [
                remote(
                    source.at[i * TP:(i + 1) * TP], edge.at[way, x], edge_s.at[way, first + i],
                    edge_r.at[way, x], beside(way, (z * NX + first + i, j)),
                )
                for i in range(2)
            ]

        def z_step(k, long):
            hops = far if long else far - 1
            kind = 0 if long else 1
            for way in range(2):
                value = part_half(sign[way] * (hops - k), way if long else 1 - way)
                if k:
                    z_copies(way, long, k - 1)[0].wait_recv()
                    value = value + zrecv[way, kind, k - 1].astype(f32)
                zsend[way, kind, k] = value.astype(bf16)
                for copy in z_copies(way, long, k):
                    copy.start()

        def z_sent(last):
            for way in range(2):
                for long in (True, False):
                    hops = far if long else far - 1
                    for k in (hops - 1,) if last else range(hops - 1):
                        for copy in z_copies(way, long, k):
                            copy.wait_send()

        def grid_step(n, carry):
            away = lax.div(n + 1, 2)
            row = chunk_row(far + away - 2 * lax.rem(n, 2) * away)
            chunk = jnp.dot(
                band[pl.ds(row, zpix), :], clean[...], preferred_element_type=f32
            )
            part[pl.ds(row, zpix), :] = chunk
            rounded[pl.ds(row, zpix), :] = chunk.astype(bf16)

            @pl.when(n == 0)
            def _():
                z_step(0, True)

            @pl.when(n == 2)
            def _():
                z_step(0, False)

            return carry

        def share(buffer, me, send_sem, recv_sem, peer_of, count):
            for r in range(1, count):
                start(remote(buffer.at[me], buffer.at[me], send_sem.at[r], recv_sem.at[me], peer_of(r)))

        def gather(buffer, me, send_sem, recv_sem, peer_of, count):
            for r in range(1, count):
                other = lax.rem(me + r, count)
                remote(
                    buffer.at[other], buffer.at[other], send_sem.at[r], recv_sem.at[other], peer_of(r)
                ).wait_recv()
            value = buffer[0]
            for i in range(1, count):
                value = value + buffer[i]
            return value

        lax.fori_loop(0, nz, grid_step, 0)

        picked = jnp.dot(
            pixel_hot[...], rounded[...], preferred_element_type=f32
        ).astype(bf16)
        wide = jnp.concatenate(
            [
                jnp.dot(shift_hot[...], picked, preferred_element_type=f32),
                jnp.zeros((shifts, 512 - quarter), f32),
            ],
            axis=1,
        )
        folded = jnp.zeros((8, 512), f32)
        for i in range(shifts // 8):
            folded = folded + pltpu.roll(
                wide[8 * i:8 * i + 8], (513 - quarter + 8 * i) % 512, 1
            )
        window = jnp.zeros((1, 512), f32)
        for i in range(8):
            window = window + (pltpu.roll(folded[i:i + 1], i, 1) if i else folded[i:i + 1])
        st1[x] = window[:, :2 * SW]
        share(st1, x, st1_s, st1_r, x_peer, NX)

        z_step(1, True)
        z_step(1, False)
        final[...] = rounded[pl.ds(chunk_row(0), zpix), :]
        for r in range(1, NX):
            row = pl.multiple_of(lax.rem(x + r, NX) * TP, TP)
            start(remote(
                final.at[pl.ds(row, TP), :], mine.at[NX - r], mine_s.at[r], mine_r.at[NX - r],
                x_peer(r),
            ))
        st2[j] = gather(st1, x, st1_s, st1_r, x_peer, NX)
        share(st2, j, st2_s, st2_r, c_peer, chan_size)
        z_step(2, True)
        z_step(2, False)
        st3[z] = gather(st2, j, st2_s, st2_r, c_peer, chan_size)
        share(st3, z, st3_s, st3_r, z_peer, nz)
        z_step(3, True)
        for r in range(1, NX):
            remote(
                final.at[pl.ds(0, TP), :], mine.at[r], mine_s.at[r], mine_r.at[r], x_peer(r)
            ).wait_recv()
        for copy in sends:
            copy.wait_send()
        z_sent(False)

        for way in range(2):
            for source in range(NX):
                remote(
                    zsend.at[way, 0, 0, 0:TP], edge.at[way, source], edge_s.at[way, source],
                    edge_r.at[way, source], beside(way, x_peer(0)),
                ).wait_recv()
        for r in range(NX):
            source = lax.rem(x + r, NX)
            if r:
                value = mine[r].astype(f32)
            else:
                value = part[pl.ds(pl.multiple_of(chunk_row(0) + x * TP, TP), TP), :]
            value = value + edge[0, source].astype(f32) + edge[1, source].astype(f32)
            column = pl.multiple_of(source * quarter, quarter)
            sky[:, pl.ds(column, quarter)] = value.astype(bf16)
        stacked[...] = gather(st3, z, st3_s, st3_r, z_peer, nz) / ngal
        z_sent(True)

    dma = pltpu.SemaphoreType.DMA
    scratch = [
        pltpu.VMEM((rows + 128, width), bf16),
        pltpu.VMEM((MODES, width), f32),
        pltpu.VMEM((NX, 1, rows), jnp.int32),
        pltpu.VMEM((NX, rows, quarter), bf16),
        pltpu.VMEM((chan_size, MODES, 128), f32),
        pltpu.VMEM((chan_size, MODES, rows), f32),
        pltpu.VMEM((NX, MODES, rows), f32),
        pltpu.VMEM((npix, NX * rows), bf16),
        pltpu.VMEM((NX * rows, quarter), f32),
        pltpu.VMEM((NX * rows, quarter), bf16),
        pltpu.VMEM((npix, quarter), f32),
        pltpu.VMEM((npix, quarter), bf16),
        pltpu.VMEM((ngal, npix), bf16),
        pltpu.VMEM((shifts, ngal), bf16),
        pltpu.VMEM((2, 2, far, 2 * TP, quarter), bf16),
        pltpu.VMEM((2, 2, far - 1, 2 * TP, quarter), bf16),
        pltpu.VMEM((2, NX, TP, quarter), bf16),
        pltpu.VMEM((zpix, quarter), bf16),
        pltpu.VMEM((NX, TP, quarter), bf16),
        pltpu.VMEM((NX, 1, 2 * SW), f32),
        pltpu.VMEM((chan_size, 1, 2 * SW), f32),
        pltpu.VMEM((nz, 1, 2 * SW), f32),
        dma((2,)),
    ]
    for shape in ((NX,), (3, NX), (chan_size,), (chan_size,), (NX,)):
        scratch += [dma(shape), dma(shape)]
    scratch += [dma((2, 2, far)), dma((2, 2, far - 1)), dma((2, NX)), dma((2, NX))]
    for shape in ((NX,), (NX,), (chan_size,), (nz,)):
        scratch += [dma(shape), dma(shape)]
    return kernel, scratch


def solution(mesh):
    tm_size, chan_size = mesh.shape["tm"], mesh.shape["chan"]

    def per_device(spectra, chan_weight, routes, offsets, taps, gal_pix, gal_chan):
        rows, width = spectra.shape
        nblocks = routes.shape[0]
        kernel, scratch = make_kernel(
            tm_size, chan_size, rows, width, nblocks, gal_pix.shape[0]
        )
        vmem = pl.BlockSpec(memory_space=pltpu.VMEM)
        sky, stacked = pl.pallas_call(
            kernel,
            out_shape=(
                jax.ShapeDtypeStruct((TP, width), bf16),
                jax.ShapeDtypeStruct((1, 2 * SW), f32),
            ),
            in_specs=[pl.BlockSpec(memory_space=pl.ANY)] * 2 + [vmem] * 6,
            out_specs=(vmem, vmem),
            scratch_shapes=scratch,
            compiler_params=pltpu.CompilerParams(
                collective_id=0, has_side_effects=True, vmem_limit_bytes=54880 * 1024
            ),
        )(
            spectra, jnp.asarray(basis_table(width * chan_size)), chan_weight[None, :],
            routes.reshape(1, nblocks), offsets[None, :], taps[None, :], gal_pix[None, :],
            gal_chan[None, :],
        )
        return sky, stacked[0]

    in_specs = (
        P("tm", "chan"), P("chan"), P("tm", None), P("tm"), P(None), P(None), P(None)
    )
    return jax.shard_map(
        per_device, mesh=mesh, in_specs=in_specs, out_specs=(P("tm", "chan"), P(None)),
        check_vma=False,
    )
```
